32 devices in a mesh: chain: 8 (over z, y), sub: 4 (over x, core).
Axes of the slice: x: 2, y: 2, z: 4, core: 2. Of those that a mesh axis runs over, the one named last changes fastest.
Arguments:
- rhs: float32 [192, 5, 8, 512], P('chain', None, None, 'sub'), may hold values from -100 to 100
- diag_block: float32 [192, 5, 5, 512], P('chain', None, None, 'sub')
- diag_inverse: float32 [192, 5, 5, 512], P('chain', None, None, 'sub'), as said below
- lower_coef: float32 [192, 2, 5, 5, 512], P('chain', None, None, None, 'sub')
- upper_coef: float32 [192, 2, 5, 5, 512], P('chain', None, None, None, 'sub')
- side_coef: float32 [192, 2, 5, 5, 512], P('chain', None, None, None, 'sub')
- lower_cols: int32 [192, 2], P('chain'), may hold values from -3 to 190, as said below
- upper_cols: int32 [192, 2], P('chain'), may hold values from 1 to 194, as said below
- counts: int32 [192, 2], P('chain'), may hold values from 1 to 2
Outputs:
- correction: float32 [192, 5, 8, 512], P('chain', None, None, 'sub')
- residual_unit: float32 [192, 5, 8, 512], P('chain', None, None, 'sub')
The draws below stay inside these ranges and needn't reach their ends.
Inputs may be any that keep to these rules, and one draw needn't show every extreme that they name: lower_cols[b, k] = b - d with d from 1 to 3, the two slots of a block differ, and some block has d = 3. upper_cols[b, k] = b + d with d from 1 to 3, the two slots of a block differ, and some block has d = 3. diag_inverse is the inverse of diag_block at every block and cell.
All inputs are finite; a program needn't handle non-finite values.
Results may differ from the reference program's by a relative error of at most 0.0003.
Values sent between devices are 32-bit elements; how exact they have to be, the bound alone decides.
No kernel may reach another device: no remote copies, remote signals or barrier semaphores. Data moves between devices by JAX's collectives and lax.ppermute only.
A program may use at most 128 MiB of HBM per device.

```python
import math
import jax
import jax.numpy as jnp
from jax import lax

VARS = 5
RHS = 8
REACH = 3
SLOTS = 2
BLOCK_TOTAL = 192
NCELL = 512


def layout_ints(key):
    random_keys = jax.random.split(jax.random.fold_in(key, 11), 4)
    rows = jnp.arange(BLOCK_TOTAL, dtype=jnp.int32)

    def offsets(subkey):
        key_a, key_b, key_c, key_d = jax.random.split(subkey, 4)
        omit = jax.random.randint(key_a, (BLOCK_TOTAL,), 0, 3)
        first = (omit + 1) % 3 + 1
        second = (omit + 2) % 3 + 1
        flip = jax.random.randint(key_b, (BLOCK_TOTAL,), 0, 2)
        slot_one = jnp.where(flip == 1, second, first)
        slot_two = jnp.where(flip == 1, first, second)
        forced = (jax.random.randint(key_c, (BLOCK_TOTAL,), 0, 7) == 0) | (rows == BLOCK_TOTAL // 2)
        other = jax.random.randint(key_d, (BLOCK_TOTAL,), 1, REACH)
        slot_one = jnp.where(forced, REACH, slot_one)
        slot_two = jnp.where(forced, other, slot_two)
        return jnp.stack([slot_one, slot_two], 1).astype(jnp.int32)
    low_off = offsets(random_keys[0])
    up_off = offsets(random_keys[1])
    level = 1 + rows // 16 % 3
    count_low = 1 + (jax.random.randint(random_keys[2], (BLOCK_TOTAL,), 0, 4) < level).astype(jnp.int32)
    count_up = 1 + (jax.random.randint(random_keys[3], (BLOCK_TOTAL,), 0, 4) < level).astype(jnp.int32)
    return (low_off, up_off, jnp.stack([count_low, count_up], 1).astype(jnp.int32))


def decay(key, tag):
    random_keys = jax.random.split(jax.random.fold_in(key, tag), 5)
    share = 0.5
    slow = jax.random.uniform(random_keys[0], (NCELL,)) < share
    long_horizon = BLOCK_TOTAL * jnp.exp(jax.random.uniform(random_keys[1], (NCELL,), minval=0.0, maxval=math.log(4.0)))
    short_t = jnp.exp(jax.random.uniform(random_keys[2], (NCELL,), minval=math.log(30.0), maxval=math.log(50.0)))
    base = jnp.where(slow, long_horizon, short_t)
    factor = jnp.exp(jax.random.uniform(random_keys[3], (BLOCK_TOTAL, NCELL), minval=math.log(0.7), maxval=math.log(1.4)))
    tau = base[None, :] * factor
    grouped_rows = jax.random.randint(random_keys[4], (3,), 0, BLOCK_TOTAL)
    block_touched = jnp.any(jnp.arange(BLOCK_TOTAL)[:, None] == grouped_rows[None, :], axis=1)
    rho = jnp.exp(-1.0 / tau) * jnp.where(block_touched, 0.65, 1.0)[:, None]
    return (rho, tau)


def diag_pair(key):
    rho, tau = decay(key, 21)
    scale = jnp.sqrt(tau)
    noise = 0.1 * jax.random.normal(jax.random.fold_in(key, 22), (BLOCK_TOTAL, NCELL, 5, 5))
    dmat = scale[:, :, None, None] * (jnp.eye(5, dtype=jnp.float32) + noise)
    return (dmat, jnp.linalg.inv(dmat))


def to_layout(matrix):
    return jnp.transpose(matrix, (0, 2, 3, 1))


def couplings(key, tag, sign, column):
    dmat, unused = diag_pair(key)
    rho, tau = decay(key, tag)
    count = layout_ints(key)[2][:, column]
    random_keys = jax.random.split(jax.random.fold_in(key, tag + 5), 4)
    two = (count == 2)[:, None]
    weight_one = jnp.where(two, jax.random.uniform(random_keys[0], (BLOCK_TOTAL, NCELL), minval=0.5, maxval=0.8), 1.0)
    weight_two = jnp.where(two, 1.0 - weight_one, jax.random.uniform(random_keys[1], (BLOCK_TOTAL, NCELL), minval=0.2, maxval=0.5))
    result = []
    for slot, weight in enumerate([weight_one, weight_two]):
        jitter = 0.015 * jax.random.normal(random_keys[2 + slot], (BLOCK_TOTAL, NCELL, 5, 5))
        target = sign * (weight * rho)[:, :, None, None] * (jnp.eye(5, dtype=jnp.float32) + jitter)
        result.append(to_layout(jnp.matmul(dmat, target, precision=lax.Precision.HIGHEST)))
    return jnp.stack(result, 1).astype(jnp.float32)


def draw_rhs(key, part):
    random_keys = jax.random.split(jax.random.fold_in(key, 41), 1)
    rows = jnp.arange(BLOCK_TOTAL, dtype=jnp.float32)
    cells = jnp.arange(NCELL, dtype=jnp.float32)
    ramp = (1.0 + 2.0 * rows / max(BLOCK_TOTAL - 1, 1))[:, None, None, None] * (1.0 + 0.5 * cells / max(NCELL - 1, 1))[None, None, None, :]
    values = jnp.clip(jax.random.normal(random_keys[0], (BLOCK_TOTAL, VARS, RHS, NCELL)), -6.0, 6.0) * ramp
    return values.astype(jnp.float32)


def draw_diag_block(key, part):
    dmat, dinv = diag_pair(key)
    return to_layout(dmat).astype(jnp.float32)


def draw_diag_inverse(key, part):
    dmat, dinv = diag_pair(key)
    return to_layout(dinv).astype(jnp.float32)


def draw_lower_coef(key, part):
    return couplings(key, 21, -1.0, 0)


def draw_upper_coef(key, part):
    return couplings(key, 31, 1.0, 1)


def draw_side_coef(key, part):
    dmat, unused = diag_pair(key)
    random_keys = jax.random.split(jax.random.fold_in(key, 51), 2)
    result = []
    for side in range(2):
        target = 0.2 * jax.random.normal(random_keys[side], (BLOCK_TOTAL, NCELL, 5, 5))
        result.append(to_layout(jnp.matmul(dmat, target, precision=lax.Precision.HIGHEST)))
    return jnp.stack(result, 1).astype(jnp.float32)


def draw_lower_cols(key, part):
    low_off, up_off, count = layout_ints(key)
    rows = jnp.arange(BLOCK_TOTAL, dtype=jnp.int32)
    return (rows[:, None] - low_off).astype(jnp.int32)


def draw_upper_cols(key, part):
    low_off, up_off, count = layout_ints(key)
    rows = jnp.arange(BLOCK_TOTAL, dtype=jnp.int32)
    return (rows[:, None] + up_off).astype(jnp.int32)


def draw_counts(key, part):
    low_off, up_off, count = layout_ints(key)
    return count


def setup_inputs(seed: int = 0) -> dict:
    splits = jax.random.split(jax.random.key(seed), 10)
    return {
        "rhs": draw_rhs(jax.random.fold_in(splits[9], 71), 0),
        "diag_block": draw_diag_block(jax.random.fold_in(splits[9], 71), 0),
        "diag_inverse": draw_diag_inverse(jax.random.fold_in(splits[9], 71), 0),
        "lower_coef": draw_lower_coef(jax.random.fold_in(splits[9], 71), 0),
        "upper_coef": draw_upper_coef(jax.random.fold_in(splits[9], 71), 0),
        "side_coef": draw_side_coef(jax.random.fold_in(splits[9], 71), 0),
        "lower_cols": draw_lower_cols(jax.random.fold_in(splits[9], 71), 0),
        "upper_cols": draw_upper_cols(jax.random.fold_in(splits[9], 71), 0),
        "counts": draw_counts(jax.random.fold_in(splits[9], 71), 0),
    }


def mat_apply(matrix, vector):
    return jnp.einsum('ijc,jqc->iqc', matrix, vector, precision=lax.Precision.HIGHEST)

def sweep_all(coef, inverse, source, offsets, active, forward):
    start = jnp.zeros((REACH,) + source.shape[1:], jnp.float32)

    def step(window, item):
        mats, inv, src, off, act = item
        acc = jnp.zeros_like(src)
        for slot in range(SLOTS):
            near = lax.dynamic_index_in_dim(window, (off[slot] - 1).astype(jnp.int32), 0, keepdims=False)
            acc = acc + act[slot] * mat_apply(mats[slot], near)
        if forward:
            out = mat_apply(inv, src - acc)
        else:
            out = src - mat_apply(inv, acc)
        return (jnp.concatenate([out[None], window[:-1]], 0), out)
    _, outs = lax.scan(step, start, (coef, inverse, source, offsets, active), reverse=not forward)
    return outs

def reference(rhs, diag_block, diag_inverse, lower_coef, upper_coef, side_coef, lower_cols, upper_cols, counts):
    rows = jnp.arange(rhs.shape[0], dtype=jnp.int32)
    slot_ids = jnp.arange(SLOTS, dtype=jnp.int32)
    lower_off = (rows[:, None] - lower_cols).astype(jnp.int32)
    upper_off = (upper_cols - rows[:, None]).astype(jnp.int32)
    act_low = (slot_ids[None, :] < counts[:, 0:1]).astype(jnp.float32)
    act_up = (slot_ids[None, :] < counts[:, 1:2]).astype(jnp.float32)
    ysweep = sweep_all(lower_coef, diag_inverse, rhs, lower_off, act_low, True)
    correction = sweep_all(upper_coef, diag_inverse, ysweep, upper_off, act_up, False)
    hi = lax.Precision.HIGHEST
    image = jnp.einsum('bijc,bjqc->biqc', diag_block, correction, precision=hi)
    padded = jnp.pad(correction, ((REACH, REACH), (0, 0), (0, 0), (0, 0)))
    for slot in range(SLOTS):
        near = padded[(lower_cols[:, slot] + REACH).astype(jnp.int32)]
        image = image + act_low[:, slot, None, None, None] * jnp.einsum('bijc,bjqc->biqc', lower_coef[:, slot], near, precision=hi)
        near = padded[(upper_cols[:, slot] + REACH).astype(jnp.int32)]
        image = image + act_up[:, slot, None, None, None] * jnp.einsum('bijc,bjqc->biqc', upper_coef[:, slot], near, precision=hi)
    zeros = jnp.zeros(correction.shape[:3] + (1,), jnp.float32)
    west = jnp.concatenate([zeros, correction[..., :-1]], 3)
    east = jnp.concatenate([correction[..., 1:], zeros], 3)
    image = image + jnp.einsum('bijc,bjqc->biqc', side_coef[:, 0], west, precision=hi)
    image = image + jnp.einsum('bijc,bjqc->biqc', side_coef[:, 1], east, precision=hi)
    resid = rhs - image
    msq = lax.optimization_barrier(jnp.mean(resid * resid, axis=(0, 1, 3)))
    residual_unit = resid / jnp.sqrt(msq + 1e-06)[None, None, :, None]
    return (correction, residual_unit)
```

```python
import functools

import jax
import jax.numpy as jnp
from jax import lax
from jax.experimental import pallas as pl
from jax.experimental.pallas import tpu as pltpu
from jax.sharding import PartitionSpec as P

VARS = 5
REACH = 3
SLOTS = 2
STATE = REACH * VARS
WIDE = 16
GROUPS = 8
VMEM_LIMIT = 40 * 1024 * 1024

VMEM = pltpu.VMEM
SMEM = pltpu.SMEM


def lanes_of(cells):
    return lax.broadcasted_iota(jnp.int32, (8, cells), 1)


def block_transpose(items, width, cells):
    count = len(items)
    lane = lanes_of(cells)
    half = 1
    while half < count:
        bit = (lane // (half * width)) % 2 == 1
        out = list(items)
        for a in range(count):
            if a & half:
                continue
            b = a + half
            out[a] = jnp.where(bit, pltpu.roll(items[b], half * width, 1), items[a])
            out[b] = jnp.where(bit, items[b], pltpu.roll(items[a], cells - half * width, 1))
        items = out
        half *= 2
    return items


def mul_rows(rows, near):
    total = rows[0] * near[0]
    for j in range(1, len(near)):
        total = total + rows[j] * near[j]
    return total


def inv_rows(inv, b, i):
    return [inv[i, j, pl.ds(b, 1), :] for j in range(VARS)]


def coef_rows(coef, b, i, k):
    return [coef[b, i, j, pl.ds(k, 1), :] for j in range(VARS)]


def apply_coef(coef, b, nears):
    out = []
    for i in range(VARS):
        parts = [mul_rows(coef_rows(coef, b, i, k), nears[k]) for k in range(SLOTS)]
        out.append(parts[0] + parts[1])
    return out


def slots(cols, counts, side, b, shift, empty):
    return [jnp.where(k < counts[side, b], cols[k, b] + shift, empty) for k in range(SLOTS)]


def read_block(buf, place):
    return [buf[place, v] for v in range(VARS)]


def steps(blocks, body, unroll):
    def chunk(o, carry):
        for u in range(unroll):
            body(o * unroll, u)
        return carry

    lax.fori_loop(0, blocks // unroll, chunk, 0)


def local_kernel(
    n, rhs, inv, low, upp, lcols, ucols, counts, out, ybuf, zbuf, hbuf
):
    blocks, _, nrhs, cells = rhs.shape
    base = lax.axis_index("chain") * blocks
    wide_y = nrhs + WIDE
    row = lax.broadcasted_iota(jnp.int32, (WIDE, cells), 0)
    row_y = lax.broadcasted_iota(jnp.int32, (wide_y, cells), 0)
    for m in range(REACH):
        for v in range(VARS):
            ybuf[REACH - 1 - m, v] = (row_y == nrhs + VARS * m + v).astype(jnp.float32)
            hbuf[blocks + m, v] = (row == VARS * m + v).astype(jnp.float32)
            zbuf[blocks + m, v] = jnp.zeros((wide_y, cells), jnp.float32)
    for v in range(VARS):
        ybuf[blocks + REACH, v] = jnp.zeros((wide_y, cells), jnp.float32)
        zbuf[blocks + REACH, v] = jnp.zeros((wide_y, cells), jnp.float32)
        hbuf[blocks + REACH, v] = jnp.zeros((WIDE, cells), jnp.float32)
    empty = blocks + REACH
    pad = jnp.zeros((WIDE, cells), jnp.float32)
    unroll = 2

    def first(start, u):
        b = start + u
        nears = [read_block(ybuf, s) for s in slots(lcols, counts, 0, b, REACH - base, empty)]
        acc = apply_coef(low, b, nears)
        t = [jnp.concatenate([rhs[b, i], pad], 0) - acc[i] for i in range(VARS)]
        for i in range(VARS):
            ybuf[b + REACH, i] = mul_rows(inv_rows(inv, b, i), t)
        c = blocks - 1 - b
        nears = [read_block(hbuf, s) for s in slots(ucols, counts, 1, c, -base, empty)]
        acc = apply_coef(upp, c, nears)
        for i in range(VARS):
            hbuf[c, i] = -mul_rows(inv_rows(inv, c, i), acc)

    steps(blocks, first, unroll)

    def second(start, u):
        c = blocks - 1 - start - u
        nears = [read_block(zbuf, s) for s in slots(ucols, counts, 1, c, -base, empty)]
        acc = apply_coef(upp, c, nears)
        for i in range(VARS):
            zbuf[c, i] = ybuf[c + REACH, i] - mul_rows(inv_rows(inv, c, i), acc)

    steps(blocks, second, unroll)

    items = []
    for m in range(REACH):
        for v in range(VARS):
            y = ybuf[blocks + REACH - 1 - m, v]
            z = zbuf[m, v]
            h = hbuf[m, v]
            items += [y[8:16], z[8:16], y[0:8], z[0:8], y[16:24], z[16:24], h[0:8], h[8:16]]
    width = cells // n
    parts = out.shape[1]
    items += [jnp.zeros((8, cells), jnp.float32)] * (parts * n - len(items))
    for r in range(parts):
        for k, item in enumerate(block_transpose(items[r * n : (r + 1) * n], width, cells)):
            out[k, r] = item


def solve_kernel(n, x, out, g0, g1, h0, h1, kq, sbuf):
    cells = x.shape[3]
    width = cells // n
    lane = lanes_of(cells)
    at_0 = lane < width
    at_1 = (lane >= width) & (lane < 2 * width)

    def spot(d, i, g):
        m = GROUPS * i + g
        shift = (m % n) * width
        value = x[d, m // n]
        return value if shift == 0 else pltpu.roll(value, cells - shift, 1)

    def unpack(d, carry):
        for i in range(STATE):
            g0[d, i] = spot(d, i, 0)
            kq[d, i] = spot(d, i, 2)
            g1[d, i] = spot(d, i, 4)
            h0[d, i] = spot(d, i, 6)
            h1[d, i] = spot(d, i, 7)
        return carry

    lax.fori_loop(0, n, unpack, 0)

    def rows(first, second, d, i):
        return [
            first[d, i, pl.ds(j, 1), :] if j < 8 else second[d, i, pl.ds(j - 8, 1), :]
            for j in range(STATE)
        ]

    def ahead(d, state):
        for i in range(STATE):
            sbuf[d, i] = jnp.where(at_0, state[i], 0.0)
        fresh = []
        for i in range(STATE):
            total = kq[d, i] + mul_rows(rows(g0, g1, d, i), state)
            kq[d, i] = pltpu.roll(total, cells - width, 1)
            fresh.append(jnp.where(at_1, pltpu.roll(total, width, 1), total))
        return tuple(fresh)

    zeros = tuple(jnp.zeros((8, cells), jnp.float32) for _ in range(STATE))
    lax.fori_loop(0, n, ahead, zeros)

    def back(e, state):
        d = n - 1 - e
        fresh = []
        for i in range(STATE):
            sbuf[d, STATE + i] = jnp.where(at_0, state[i], 0.0)
            fresh.append(kq[d, i] + mul_rows(rows(h0, h1, d, i), state))
        return tuple(fresh)

    lax.fori_loop(0, n, back, zeros)

    def pack(d, carry):
        for r in range(out.shape[1]):
            total = jnp.zeros((8, cells), jnp.float32)
            for m in range(r * n, min((r + 1) * n, 2 * STATE)):
                value = sbuf[d, m]
                shift = (m % n) * width
                total = total + (value if shift == 0 else pltpu.roll(value, shift, 1))
            out[d, r] = total
        return carry

    lax.fori_loop(0, n, pack, 0)


def sweep_kernel(
    n, states, rhs, inv, low, upp, lcols, ucols, counts, zout, wout, tail, west, east, ybuf, zbuf
):
    blocks, _, nrhs, cells = rhs.shape
    base = lax.axis_index("chain") * blocks
    width = cells // n
    zero = jnp.zeros((nrhs, cells), jnp.float32)
    for r in range(states.shape[1]):
        items = block_transpose([states[k, r] for k in range(n)], width, cells)
        for g in range(n):
            m = r * n + g
            if m < STATE:
                ybuf[REACH - 1 - m // VARS, m % VARS] = items[g]
            elif m < 2 * STATE:
                q = m - STATE
                zbuf[blocks + q // VARS, q % VARS] = items[g]
    empty = blocks + REACH
    for v in range(VARS):
        ybuf[empty, v] = zero
        zbuf[empty, v] = zero
    west[...] = jnp.zeros_like(west)
    east[...] = jnp.zeros_like(east)
    lane = lanes_of(cells)

    def first(start, u):
        b = start + u
        nears = [read_block(ybuf, s) for s in slots(lcols, counts, 0, b, REACH - base, empty)]
        acc = apply_coef(low, b, nears)
        t = [rhs[b, i] - acc[i] for i in range(VARS)]
        for i in range(VARS):
            ybuf[b + REACH, i] = mul_rows(inv_rows(inv, b, i), t)

    steps(blocks, first, 2)

    def second(start, u):
        c = blocks - 1 - start - u
        nears = [read_block(zbuf, s) for s in slots(ucols, counts, 1, c, -base, empty)]
        acc = apply_coef(upp, c, nears)
        for i in range(VARS):
            w = mul_rows(inv_rows(inv, c, i), acc)
            z = ybuf[c + REACH, i] - w
            zbuf[c, i] = z
            zout[c, i] = z
            wout[c, i] = w
            m = c * VARS + i
            page, spot = m // cells, m % cells
            here = lane == spot
            west[page] = jnp.where(here, pltpu.roll(z, spot, 1), west[page])
            east[page] = jnp.where(here, pltpu.roll(z, spot + 1, 1), east[page])

    steps(blocks, second, 2)
    for m in range(REACH):
        for v in range(VARS):
            tail[m, v] = wout[blocks - REACH + m, v]


def resid_kernel(z, w, tail, from_west, from_east, low, side, lcols, counts, resid, squares, wbuf):
    blocks, _, nrhs, cells = z.shape
    base = lax.axis_index("chain") * blocks
    empty = blocks + REACH
    lane = lanes_of(cells)
    for m in range(REACH):
        for v in range(VARS):
            wbuf[m, v] = tail[m, v]
    for v in range(VARS):
        wbuf[empty, v] = jnp.zeros((nrhs, cells), jnp.float32)

    def fill(b, carry):
        for v in range(VARS):
            wbuf[b + REACH, v] = w[b, v]
        return carry

    lax.fori_loop(0, blocks, fill, 0)

    def block(b, total):
        nears = [read_block(wbuf, s) for s in slots(lcols, counts, 0, b, REACH - base, empty)]
        acc = apply_coef(low, b, nears)
        left, right = [], []
        for v in range(VARS):
            m = b * VARS + v
            page, spot = m // cells, m % cells
            here = z[b, v]
            left.append(
                jnp.where(
                    lane == 0,
                    pltpu.roll(from_west[page], cells - spot, 1),
                    pltpu.roll(here, 1, 1),
                )
            )
            right.append(
                jnp.where(
                    lane == cells - 1,
                    pltpu.roll(from_east[page], cells - 1 - spot, 1),
                    pltpu.roll(here, cells - 1, 1),
                )
            )
        beside = apply_coef(side, b, [left, right])
        for i in range(VARS):
            r = acc[i] - beside[i]
            resid[b, i] = r
            total = total + r * r
        return total

    squares[...] = lax.fori_loop(0, blocks, block, jnp.zeros((nrhs, cells), jnp.float32))


def scale_kernel(entries, resid, squares, out):
    msq = jnp.sum(squares[...], axis=1, keepdims=True) / entries
    factor = jnp.broadcast_to(lax.rsqrt(msq + 1e-06), squares.shape)

    def block(b, carry):
        for v in range(VARS):
            out[b, v] = resid[b, v] * factor
        return carry

    lax.fori_loop(0, resid.shape[0], block, 0)


def call(kernel, out_shape, args, smem, scratch):
    kinds = [pl.BlockSpec(memory_space=SMEM if s else VMEM) for s in smem]
    single = isinstance(out_shape[0], int)
    shapes = [out_shape] if single else list(out_shape)
    outs = pl.pallas_call(
        kernel,
        out_shape=[jax.ShapeDtypeStruct(s, jnp.float32) for s in shapes],
        in_specs=kinds,
        out_specs=[pl.BlockSpec(memory_space=VMEM)] * len(shapes),
        scratch_shapes=[VMEM(s, jnp.float32) for s in scratch],
        compiler_params=pltpu.CompilerParams(vmem_limit_bytes=VMEM_LIMIT),
    )(*args)
    return outs[0] if single else outs


def total_over(value, axis):
    count = lax.axis_size(axis)
    if count & (count - 1):
        return lax.psum(value, axis)
    hop = 1
    while hop < count:
        value = value + lax.ppermute(value, axis, [(i, i ^ hop) for i in range(count)])
        hop *= 2
    return value


def shards(
    rhs, diag_block, diag_inverse, lower_coef, upper_coef, side_coef, lower_cols, upper_cols, counts
):
    blocks, nvars, nrhs, cells = rhs.shape
    n = lax.axis_size("chain")
    inv = jnp.transpose(diag_inverse, (1, 2, 0, 3))
    low, upp, side = (
        jnp.transpose(a, (0, 2, 3, 1, 4)) for a in (lower_coef, upper_coef, side_coef)
    )
    lcols, ucols, used = lower_cols.T, upper_cols.T, counts.T
    rows = blocks + REACH + 1
    parts = -(-STATE * GROUPS // n)
    back = -(-2 * STATE // n)
    tile = (nrhs, cells)
    pages = -(-blocks * VARS // cells)

    maps = call(
        functools.partial(local_kernel, n),
        (n, parts) + tile,
        (rhs, inv, low, upp, lcols, ucols, used),
        (0, 0, 0, 0, 1, 1, 1),
        [(rows, VARS, nrhs + WIDE, cells)] * 2 + [(rows, VARS, WIDE, cells)],
    )
    maps = lax.all_to_all(maps, "chain", 0, 0, tiled=True)
    states = call(
        functools.partial(solve_kernel, n),
        (n, back) + tile,
        (maps,),
        (0,),
        [(n, STATE) + tile] * 5 + [(n, 2 * STATE) + tile],
    )
    states = lax.all_to_all(states, "chain", 0, 0, tiled=True)
    correction, w, tail, west, east = call(
        functools.partial(sweep_kernel, n),
        [rhs.shape, rhs.shape, (REACH, VARS) + tile, (pages,) + tile, (pages,) + tile],
        (states, rhs, inv, low, upp, lcols, ucols, used),
        (0, 0, 0, 0, 0, 1, 1, 1),
        [(rows, VARS) + tile] * 2,
    )
    m = lax.axis_size("sub")
    from_west = lax.ppermute(east, "sub", [(i, i + 1) for i in range(m - 1)])
    from_east = lax.ppermute(west, "sub", [(i + 1, i) for i in range(m - 1)])
    tail = lax.ppermute(tail, "chain", [(i, i + 1) for i in range(n - 1)])
    resid, squares = call(
        resid_kernel,
        [rhs.shape, tile],
        (correction, w, tail, from_west, from_east, low, side, lcols, used),
        (0, 0, 0, 0, 0, 0, 0, 1, 1),
        [(rows, VARS) + tile],
    )
    squares = total_over(total_over(squares, "sub"), "chain")
    entries = blocks * VARS * cells * n * m
    residual_unit = call(
        functools.partial(scale_kernel, entries), rhs.shape, (resid, squares), (0, 0), []
    )
    return (correction, residual_unit)


def solution(mesh):
    in_specs = (
        P("chain", None, None, "sub"),
        P("chain", None, None, "sub"),
        P("chain", None, None, "sub"),
        P("chain", None, None, None, "sub"),
        P("chain", None, None, None, "sub"),
        P("chain", None, None, None, "sub"),
        P("chain", None),
        P("chain", None),
        P("chain", None),
    )
    out_specs = (P("chain", None, None, "sub"), P("chain", None, None, "sub"))
    return jax.shard_map(shards, mesh=mesh, in_specs=in_specs, out_specs=out_specs, check_vma=False)
```

```python
import functools

import jax
import jax.numpy as jnp
from jax import lax
from jax.experimental import pallas as pl
from jax.experimental.pallas import tpu as pltpu
from jax.sharding import PartitionSpec as P

VARS = 5
REACH = 3
SLOTS = 2
STATE = REACH * VARS
WIDE = 16
GROUPS = 8
VMEM_LIMIT = 40 * 1024 * 1024

VMEM = pltpu.VMEM
SMEM = pltpu.SMEM
HBM = pltpu.HBM


def lanes_of(cells):
    return lax.broadcasted_iota(jnp.int32, (8, cells), 1)


def block_transpose(items, width, cells):
    count = len(items)
    lane = lanes_of(cells)
    half = 1
    while half < count:
        bit = (lane // (half * width)) % 2 == 1
        out = list(items)
        for a in range(count):
            if a & half:
                continue
            b = a + half
            out[a] = jnp.where(bit, pltpu.roll(items[b], half * width, 1), items[a])
            out[b] = jnp.where(bit, items[b], pltpu.roll(items[a], cells - half * width, 1))
        items = out
        half *= 2
    return items


def mul_rows(rows, near):
    total = rows[0] * near[0]
    for j in range(1, len(near)):
        total = total + rows[j] * near[j]
    return total


def inv_rows(inv, b, i):
    return [inv[i, j, pl.ds(b, 1), :] for j in range(VARS)]


def coef_rows(coef, b, i, k):
    return [coef[b, i, j, pl.ds(k, 1), :] for j in range(VARS)]


def apply_coef(coef, b, nears):
    out = []
    for i in range(VARS):
        parts = [mul_rows(coef_rows(coef, b, i, k), nears[k]) for k in range(SLOTS)]
        out.append(parts[0] + parts[1])
    return out


def slots(cols, counts, side, b, shift, empty):
    return [jnp.where(k < counts[side, b], cols[k, b] + shift, empty) for k in range(SLOTS)]


def read_block(buf, place):
    return [buf[place, v] for v in range(VARS)]


def steps(count, most, body, carry=0):
    unroll = max(u for u in range(1, most + 1) if count % u == 0)

    def chunk(o, carry):
        for u in range(unroll):
            carry = body(o * unroll + u, carry)
        return carry

    return lax.fori_loop(0, count // unroll, chunk, carry)


def local_kernel(
    n, rhs_h, inv_h, low_h, upp_h, lcols, ucols, counts, out, rhs, inv, low, upp, ybuf, zbuf, sems
):
    copies = [
        pltpu.make_async_copy(src, dst, sems.at[k])
        for k, (src, dst) in enumerate(((low_h, low), (rhs_h, rhs), (inv_h, inv), (upp_h, upp)))
    ]
    for copy in copies:
        copy.start()
    blocks, _, nrhs, cells = rhs.shape
    base = lax.axis_index("chain") * blocks
    wide_y = nrhs + WIDE
    wide_z = wide_y + WIDE
    row_y = lax.broadcasted_iota(jnp.int32, (wide_y, cells), 0)
    row_z = lax.broadcasted_iota(jnp.int32, (wide_z, cells), 0)
    for m in range(REACH):
        for v in range(VARS):
            q = VARS * m + v
            ybuf[REACH - 1 - m, v] = (row_y == nrhs + q).astype(jnp.float32)
            zbuf[blocks + m, v] = (row_z == wide_y + q).astype(jnp.float32)
    for v in range(VARS):
        ybuf[blocks + REACH, v] = jnp.zeros((wide_y, cells), jnp.float32)
        zbuf[blocks + REACH, v] = jnp.zeros((wide_z, cells), jnp.float32)
    empty = blocks + REACH
    pad = jnp.zeros((WIDE, cells), jnp.float32)
    for copy in copies[:3]:
        copy.wait()

    def first(b, carry):
        nears = [read_block(ybuf, s) for s in slots(lcols, counts, 0, b, REACH - base, empty)]
        acc = apply_coef(low, b, nears)
        t = [jnp.concatenate([rhs[b, i], pad], 0) - acc[i] for i in range(VARS)]
        for i in range(VARS):
            ybuf[b + REACH, i] = mul_rows(inv_rows(inv, b, i), t)
        return carry

    steps(blocks, 2, first)
    copies[3].wait()

    def second(e, carry):
        c = blocks - 1 - e
        nears = [read_block(zbuf, s) for s in slots(ucols, counts, 1, c, -base, empty)]
        acc = apply_coef(upp, c, nears)
        for i in range(VARS):
            source = jnp.concatenate([ybuf[c + REACH, i], pad], 0)
            zbuf[c, i] = source - mul_rows(inv_rows(inv, c, i), acc)
        return carry

    steps(blocks, 2, second)

    items = []
    for m in range(REACH):
        for v in range(VARS):
            y = ybuf[blocks + REACH - 1 - m, v]
            z = zbuf[m, v]
            items += [y[8:16], z[8:16], z[24:32], y[0:8], y[16:24], z[16:24], z[32:40], z[0:8]]
    width = cells // n
    parts = out.shape[1]
    items += [jnp.zeros((8, cells), jnp.float32)] * (parts * n - len(items))
    for r in range(parts):
        for k, item in enumerate(block_transpose(items[r * n : (r + 1) * n], width, cells)):
            out[k, r] = item


def solve_kernel(n, x, out, kq, sbuf, tbuf):
    cells = x.shape[3]
    width = cells // n
    lane = lanes_of(cells)
    at_0 = lane < width
    at_2 = (lane >= 2 * width) & (lane < 3 * width)
    zero = jnp.zeros((8, cells), jnp.float32)

    def turn(value, groups):
        shift = groups * width % cells
        return value if shift == 0 else pltpu.roll(value, shift, 1)

    def rows(d, i):
        place, spot = GROUPS * i // n, GROUPS * i % n
        value = turn(x[d, place], -spot)
        if spot:
            return value, [value[j : j + 1] for j in range(8)]
        return value, [x[d, place, pl.ds(j, 1), :] for j in range(8)]

    def spread(total, here):
        fresh = []
        for j in range(8):
            c = jnp.where(here, total[j], 0.0)
            if j + 8 < STATE:
                c = c + turn(jnp.where(here, total[j + 8], 0.0), 4)
            fresh.append(c)
        return fresh

    def ahead(d, state):
        for j in range(8):
            sbuf[d, j] = state[j]
        both = [c + turn(c, 1) for c in state]
        total = []
        for i in range(STATE):
            value, row = rows(d, i)
            acc = mul_rows(row, both)
            source = jnp.where(at_0, turn(value, -3), turn(value, -6))
            total.append(acc + turn(acc, -4) + source)
            kq[d, i] = turn(total[i], 1)
        return tuple(spread(total, at_0))

    lax.fori_loop(0, n, ahead, (zero,) * 8)

    def back(e, state):
        d = n - 1 - e
        for j in range(8):
            tbuf[d, j] = state[j]
        total = []
        for i in range(STATE):
            acc = mul_rows(rows(d, i)[1], state)
            total.append(acc + turn(acc, -4) + kq[d, i])
        return tuple(spread(total, at_2))

    lax.fori_loop(0, n, back, (zero,) * 8)

    def pack(d, carry):
        total = [zero] * out.shape[1]
        for r in range(4):
            value = sbuf[d, r] + tbuf[d, r] + turn(sbuf[d, r + 4] + tbuf[d, r + 4], 1)
            total[GROUPS * r // n] += turn(value, GROUPS * r % n)
        for r in range(out.shape[1]):
            out[d, r] = total[r]
        return carry

    lax.fori_loop(0, n, pack, 0)


def sweep_kernel(
    n, states, rhs, inv, low, upp, lcols, ucols, counts, zout, wout, tail, west, east, ybuf, zbuf
):
    blocks, _, nrhs, cells = rhs.shape
    base = lax.axis_index("chain") * blocks
    width = cells // n
    zero = jnp.zeros((nrhs, cells), jnp.float32)
    items = []
    for r in range(states.shape[1]):
        items += block_transpose([states[k, r] for k in range(n)], width, cells)
    for r in range(4):
        for g in range(GROUPS):
            q = r + 4 * (g % 2) + 8 * (g // 4)
            if q >= STATE:
                continue
            m, v = q // VARS, q % VARS
            if g // 2 % 2 == 0:
                ybuf[REACH - 1 - m, v] = items[GROUPS * r + g]
            else:
                zbuf[blocks + m, v] = items[GROUPS * r + g]
    empty = blocks + REACH
    for v in range(VARS):
        ybuf[empty, v] = zero
        zbuf[empty, v] = zero
        wout[blocks, v] = zero
    lane = lanes_of(cells)

    def first(b, carry):
        nears = [read_block(ybuf, s) for s in slots(lcols, counts, 0, b, REACH - base, empty)]
        acc = apply_coef(low, b, nears)
        t = [rhs[b, i] - acc[i] for i in range(VARS)]
        for i in range(VARS):
            ybuf[b + REACH, i] = mul_rows(inv_rows(inv, b, i), t)
        return carry

    steps(blocks, 2, first)

    def second(e, edges):
        c = blocks - 1 - e
        nears = [read_block(zbuf, s) for s in slots(ucols, counts, 1, c, -base, empty)]
        acc = apply_coef(upp, c, nears)
        edges = list(edges)
        for i in range(VARS):
            w = mul_rows(inv_rows(inv, c, i), acc)
            z = ybuf[c + REACH, i] - w
            zbuf[c, i] = z
            zout[c, i] = z
            wout[c, i] = w
            m = c * VARS + i
            spot = m % cells
            first_lane, last_lane = pltpu.roll(z, spot, 1), pltpu.roll(z, (spot + 1) % cells, 1)
            for page in range(len(edges) // 2):
                here = lane == m - page * cells
                edges[2 * page] = jnp.where(here, first_lane, edges[2 * page])
                edges[2 * page + 1] = jnp.where(here, last_lane, edges[2 * page + 1])
        return tuple(edges)

    edges = steps(blocks, 2, second, (zero,) * (2 * west.shape[0]))
    for page in range(west.shape[0]):
        west[page] = edges[2 * page]
        east[page] = edges[2 * page + 1]
    for m in range(REACH):
        for v in range(VARS):
            tail[m, v] = wout[blocks - REACH + m, v]


def resid_kernel(
    z, w, tail, from_west, from_east, low, side, lcols, counts, resid, squares, correction, wbuf, sem
):
    store = pltpu.make_async_copy(z, correction, sem)
    store.start()
    blocks, _, nrhs, cells = z.shape
    base = lax.axis_index("chain") * blocks
    lane = lanes_of(cells)
    for v in range(VARS):
        for m in range(REACH):
            wbuf[m, v] = tail[m, v]
            wbuf[m + REACH, v] = w[m, v]
        wbuf[2 * REACH, v] = jnp.zeros((nrhs, cells), jnp.float32)

    def block(b, total, buf, shift, empty):
        nears = [read_block(buf, s) for s in slots(lcols, counts, 0, b, shift - base, empty)]
        acc = apply_coef(low, b, nears)
        left, right = [], []
        for v in range(VARS):
            m = b * VARS + v
            page, spot = m // cells, m % cells
            here = z[b, v]
            edge = pltpu.roll(from_west[page], (cells - spot) % cells, 1)
            left.append(jnp.where(lane == 0, edge, pltpu.roll(here, 1, 1)))
            edge = pltpu.roll(from_east[page], cells - 1 - spot, 1)
            right.append(jnp.where(lane == cells - 1, edge, pltpu.roll(here, cells - 1, 1)))
        beside = apply_coef(side, b, [left, right])
        for i in range(VARS):
            r = acc[i] - beside[i]
            resid[b, i] = r
            total = total + r * r
        return total

    total = jnp.zeros((nrhs, cells), jnp.float32)
    for b in range(REACH):
        total = block(b, total, wbuf, REACH, 2 * REACH)

    def inner(b, total):
        return block(b + REACH, total, w, 0, blocks)

    total = steps(blocks - REACH, 3, inner, total)
    sums = jnp.broadcast_to(jnp.sum(total, axis=1, keepdims=True), total.shape)
    row = lax.broadcasted_iota(jnp.int32, total.shape, 0)
    line = jnp.sum(jnp.where(lane == row, sums, 0.0), axis=0, keepdims=True)
    for p in range(squares.shape[0]):
        squares[p] = line
    store.wait()


def scale_kernel(entries, resid, squares, out):
    blocks, _, nrhs, cells = resid.shape
    line = squares[0]
    for p in range(1, squares.shape[0]):
        line = line + squares[p]
    lane = lanes_of(cells)
    row = lax.broadcasted_iota(jnp.int32, (nrhs, cells), 0)
    line = jnp.where(lane == row, jnp.broadcast_to(line, (nrhs, cells)), 0.0)
    msq = jnp.sum(line, axis=1, keepdims=True) / entries
    factor = jnp.broadcast_to(lax.rsqrt(msq + 1e-06), (nrhs, cells))

    def block(b, carry):
        for v in range(VARS):
            out[b, v] = resid[b, v] * factor
        return carry

    steps(blocks, 4, block)


def call(kernel, outs, args, places, scratch):
    shapes = [o[0] for o in outs]
    result = pl.pallas_call(
        kernel,
        out_shape=[jax.ShapeDtypeStruct(s, jnp.float32) for s in shapes],
        in_specs=[pl.BlockSpec(memory_space=p) for p in places],
        out_specs=[pl.BlockSpec(memory_space=o[1]) for o in outs],
        scratch_shapes=[s if not isinstance(s, tuple) else VMEM(s, jnp.float32) for s in scratch],
        compiler_params=pltpu.CompilerParams(vmem_limit_bytes=VMEM_LIMIT),
    )(*args)
    return result


def shards(
    rhs, diag_block, diag_inverse, lower_coef, upper_coef, side_coef, lower_cols, upper_cols, counts
):
    blocks, nvars, nrhs, cells = rhs.shape
    n = lax.axis_size("chain")
    inv = jnp.transpose(diag_inverse, (1, 2, 0, 3))
    low, upp, side = (
        jnp.transpose(a, (0, 2, 3, 1, 4)) for a in (lower_coef, upper_coef, side_coef)
    )
    lcols, ucols, used = lower_cols.T, upper_cols.T, counts.T
    m = lax.axis_size("sub")
    rows = blocks + REACH + 1
    parts = -(-STATE * GROUPS // n)
    back = -(-4 * GROUPS // n)
    tile = (nrhs, cells)
    pages = -(-blocks * VARS // cells)

    (maps,) = call(
        functools.partial(local_kernel, n),
        [((n, parts) + tile, VMEM)],
        (rhs, inv, low, upp, lcols, ucols, used),
        (HBM,) * 4 + (SMEM,) * 3,
        [rhs.shape, inv.shape, low.shape, upp.shape]
        + [(rows, VARS, nrhs + WIDE, cells), (rows, VARS, nrhs + 2 * WIDE, cells)]
        + [pltpu.SemaphoreType.DMA((4,))],
    )
    maps = lax.all_to_all(maps, "chain", 0, 0, tiled=True)
    (states,) = call(
        functools.partial(solve_kernel, n),
        [((n, back) + tile, VMEM)],
        (maps,),
        (VMEM,),
        [(n, STATE) + tile, (n, 8) + tile, (n, 8) + tile],
    )
    states = lax.all_to_all(states, "chain", 0, 0, tiled=True)
    z, w, tail, west, east = call(
        functools.partial(sweep_kernel, n),
        [
            (rhs.shape, VMEM),
            ((blocks + 1, VARS) + tile, VMEM),
            ((REACH, VARS) + tile, VMEM),
            ((pages,) + tile, VMEM),
            ((pages,) + tile, VMEM),
        ],
        (states, rhs, inv, low, upp, lcols, ucols, used),
        (VMEM,) * 5 + (SMEM,) * 3,
        [(rows, VARS) + tile] * 2,
    )
    from_west = lax.ppermute(east, "sub", [(i, i + 1) for i in range(m - 1)])
    from_east = lax.ppermute(west, "sub", [(i + 1, i) for i in range(m - 1)])
    tail = lax.ppermute(tail, "chain", [(i, i + 1) for i in range(n - 1)])
    resid, squares, correction = call(
        resid_kernel,
        [(rhs.shape, VMEM), ((n * m, 1, cells), VMEM), (rhs.shape, HBM)],
        (z, w, tail, from_west, from_east, low, side, lcols, used),
        (VMEM,) * 7 + (SMEM,) * 2,
        [(2 * REACH + 1, VARS) + tile, pltpu.SemaphoreType.DMA],
    )
    squares = lax.all_to_all(squares, ("chain", "sub"), 0, 0, tiled=True)
    entries = blocks * VARS * cells * n * m
    (residual_unit,) = call(
        functools.partial(scale_kernel, entries),
        [(rhs.shape, VMEM)],
        (resid, squares),
        (VMEM, VMEM),
        [],
    )
    return (correction, residual_unit)


def solution(mesh):
    in_specs = (
        P("chain", None, None, "sub"),
        P("chain", None, None, "sub"),
        P("chain", None, None, "sub"),
        P("chain", None, None, None, "sub"),
        P("chain", None, None, None, "sub"),
        P("chain", None, None, None, "sub"),
        P("chain", None),
        P("chain", None),
        P("chain", None),
    )
    out_specs = (P("chain", None, None, "sub"), P("chain", None, None, "sub"))
    return jax.shard_map(shards, mesh=mesh, in_specs=in_specs, out_specs=out_specs, check_vma=False)
```

```python
import functools

import jax
import jax.numpy as jnp
from jax import lax
from jax.experimental import pallas as pl
from jax.experimental.pallas import tpu as pltpu
from jax.sharding import PartitionSpec as P

VARS = 5
REACH = 3
SLOTS = 2
STATE = REACH * VARS
WIDE = 16
GROUPS = 8
VMEM_LIMIT = 40 * 1024 * 1024

VMEM = pltpu.VMEM
SMEM = pltpu.SMEM
HBM = pltpu.HBM


def lanes_of(cells):
    return lax.broadcasted_iota(jnp.int32, (8, cells), 1)


def block_transpose(items, width, cells):
    count = len(items)
    lane = lanes_of(cells)
    half = 1
    while half < count:
        bit = (lane // (half * width)) % 2 == 1
        out = list(items)
        for a in range(count):
            if a & half:
                continue
            b = a + half
            out[a] = jnp.where(bit, pltpu.roll(items[b], half * width, 1), items[a])
            out[b] = jnp.where(bit, items[b], pltpu.roll(items[a], cells - half * width, 1))
        items = out
        half *= 2
    return items


def mul_rows(rows, near):
    total = rows[0] * near[0]
    for j in range(1, len(near)):
        total = total + rows[j] * near[j]
    return total


def product_rows(mats, b, i, k):
    return [mats[i, j, k, pl.ds(b, 1), :] for j in range(VARS)]


def couple(mats, b, nears):
    out = []
    for i in range(VARS):
        parts = [mul_rows(product_rows(mats, b, i, k), nears[k]) for k in range(SLOTS)]
        out.append(parts[0] + parts[1])
    return out


def coef_rows(coef, b, i, k):
    place = (b * VARS + i) * VARS * SLOTS + k
    return [coef[pl.ds(place + SLOTS * j, 1), :] for j in range(VARS)]


def apply_coef(coef, b, nears):
    out = []
    for i in range(VARS):
        parts = [mul_rows(coef_rows(coef, b, i, k), nears[k]) for k in range(SLOTS)]
        out.append(parts[0] + parts[1])
    return out


def products(inv, coef, out):
    blocks = inv.shape[2]
    stride = VARS * VARS * SLOTS

    def some(o, carry):
        start = o * 8
        left = [[inv[i, m, pl.ds(start, 8), :] for m in range(VARS)] for i in range(VARS)]
        for k in range(SLOTS):
            for j in range(VARS):
                place = start * stride + j * SLOTS + k
                right = [
                    coef[pl.ds(place + m * VARS * SLOTS, 8, stride=stride), :] for m in range(VARS)
                ]
                for i in range(VARS):
                    out[i, j, k, pl.ds(start, 8), :] = mul_rows(left[i], right)
        return carry

    lax.fori_loop(0, blocks // 8, some, 0)


def slots(cols, counts, side, b, shift, empty):
    return [jnp.where(k < counts[side, b], cols[k, b] + shift, empty) for k in range(SLOTS)]


def read_block(buf, place):
    return [buf[place, v] for v in range(VARS)]


def steps(count, most, body, carry=0):
    unroll = max(u for u in range(1, most + 1) if count % u == 0)

    def chunk(o, carry):
        for u in range(unroll):
            carry = body(o * unroll + u, carry)
        return carry

    return lax.fori_loop(0, count // unroll, chunk, carry)


def local_kernel(
    n,
    rhs_h,
    inv_h,
    low_h,
    upp_h,
    lcols_h,
    ucols_h,
    counts_h,
    out,
    source,
    mlow,
    mupp,
    rhs,
    inv,
    low,
    upp,
    lcols,
    ucols,
    counts,
    ybuf,
    zbuf,
    sems,
):
    copies = [
        pltpu.make_async_copy(src, dst, sems.at[k])
        for k, (src, dst) in enumerate(
            (
                (inv_h, inv),
                (low_h, low),
                (lcols_h, lcols),
                (counts_h, counts),
                (ucols_h, ucols),
                (rhs_h, rhs),
                (upp_h, upp),
            )
        )
    ]
    for copy in copies:
        copy.start()
    blocks, _, nrhs, cells = rhs.shape
    base = lax.axis_index("chain") * blocks
    wide_y = nrhs + WIDE
    wide_z = wide_y + WIDE
    row_y = lax.broadcasted_iota(jnp.int32, (wide_y, cells), 0)
    row_z = lax.broadcasted_iota(jnp.int32, (wide_z, cells), 0)
    for m in range(REACH):
        for v in range(VARS):
            q = VARS * m + v
            ybuf[REACH - 1 - m, v] = (row_y == nrhs + q).astype(jnp.float32)
            zbuf[blocks + m, v] = (row_z == wide_y + q).astype(jnp.float32)
    for v in range(VARS):
        ybuf[blocks + REACH, v] = jnp.zeros((wide_y, cells), jnp.float32)
        zbuf[blocks + REACH, v] = jnp.zeros((wide_z, cells), jnp.float32)
    empty = blocks + REACH
    pad = jnp.zeros((WIDE, cells), jnp.float32)
    copies[0].wait()
    copies[1].wait()
    products(inv, low, mlow)
    for copy in copies[2:6]:
        copy.wait()

    def first(b, carry):
        nears = [read_block(ybuf, s) for s in slots(lcols, counts, 0, b, REACH - base, empty)]
        acc = couple(mlow, b, nears)
        right = [rhs[b, i] for i in range(VARS)]
        for i in range(VARS):
            own = mul_rows([inv[i, j, pl.ds(b, 1), :] for j in range(VARS)], right)
            source[b, i] = own
            ybuf[b + REACH, i] = jnp.concatenate([own, pad], 0) - acc[i]
        return carry

    steps(blocks, 2, first)
    copies[6].wait()
    products(inv, upp, mupp)

    def second(e, carry):
        c = blocks - 1 - e
        nears = [read_block(zbuf, s) for s in slots(ucols, counts, 1, c, -base, empty)]
        acc = couple(mupp, c, nears)
        for i in range(VARS):
            zbuf[c, i] = jnp.concatenate([ybuf[c + REACH, i], pad], 0) - acc[i]
        return carry

    steps(blocks, 2, second)

    items = []
    for m in range(REACH):
        for v in range(VARS):
            y = ybuf[blocks + REACH - 1 - m, v]
            z = zbuf[m, v]
            items += [y[8:16], z[8:16], z[24:32], y[0:8], y[16:24], z[16:24], z[32:40], z[0:8]]
    width = cells // n
    parts = out.shape[1]
    items += [jnp.zeros((8, cells), jnp.float32)] * (parts * n - len(items))
    for r in range(parts):
        for k, item in enumerate(block_transpose(items[r * n : (r + 1) * n], width, cells)):
            out[k, r] = item


def solve_kernel(n, x, out, g1, p, kq, sbuf, tbuf):
    cells = x.shape[3]
    width = cells // n
    lane = lanes_of(cells)
    zero = jnp.zeros((8, cells), jnp.float32)

    def at(group):
        return (lane >= group * width) & (lane < (group + 1) * width)

    def turn(value, groups):
        shift = groups * width % cells
        return value if shift == 0 else pltpu.roll(value, shift, 1)

    def place(i):
        return GROUPS * i // n, GROUPS * i % n

    def unpack(d, carry):
        for i in range(STATE):
            page, spot = place(i)
            value = x[d, page]
            if spot:
                value = turn(value, -spot)
            g1[d, i] = turn(value, -4)
            p[d, i] = turn(value, -3)
            kq[d, i] = turn(value, -5)
        return carry

    lax.fori_loop(0, n, unpack, 0)

    def rows(d, i, state):
        page, spot = place(i)
        if spot:
            value = turn(x[d, page], -spot)
            low = [value[j : j + 1] for j in range(8)]
        else:
            low = [x[d, page, pl.ds(j, 1), :] for j in range(8)]
        high = [g1[d, i, pl.ds(j, 1), :] for j in range(STATE - 8)]
        return mul_rows(low, state[:8]) + mul_rows(high, state[8:])

    def ahead(d, state):
        for i in range(STATE):
            sbuf[d, i] = state[i]
        return tuple(p[d, i] + rows(d, i, state) for i in range(STATE))

    lax.fori_loop(0, n, ahead, (zero,) * STATE)

    def couple_both(d, carry):
        state = []
        for i in range(STATE):
            sbuf[d, i] = jnp.where(at(0), sbuf[d, i], 0.0)
            state.append(turn(sbuf[d, i], 1))
        for i in range(STATE):
            kq[d, i] = turn(rows(d, i, state), 1) + kq[d, i]
        return carry

    lax.fori_loop(0, n, couple_both, 0)

    def back(e, state):
        d = n - 1 - e
        for i in range(STATE):
            tbuf[d, i] = jnp.where(at(2), state[i], 0.0)
        return tuple(kq[d, i] + rows(d, i, state) for i in range(STATE))

    lax.fori_loop(0, n, back, (zero,) * STATE)

    def pack(d, carry):
        total = [zero] * out.shape[1]
        mixed = [sbuf[d, j] + tbuf[d, j] for j in range(STATE)] + [zero]
        for r in range(4):
            value = mixed[r] + turn(mixed[r + 4], 1)
            value = value + turn(mixed[r + 8], 4) + turn(mixed[r + 12], 5)
            total[GROUPS * r // n] += turn(value, GROUPS * r % n)
        for r in range(out.shape[1]):
            out[d, r] = total[r]
        return carry

    lax.fori_loop(0, n, pack, 0)


def sweep_kernel(
    n, states, source, mlow, mupp, lcols, ucols, counts, zout, wout, tail, west, east, ybuf, zbuf
):
    blocks, _, nrhs, cells = source.shape
    base = lax.axis_index("chain") * blocks
    width = cells // n
    zero = jnp.zeros((nrhs, cells), jnp.float32)
    items = []
    for r in range(states.shape[1]):
        items += block_transpose([states[k, r] for k in range(n)], width, cells)
    for r in range(4):
        for g in range(GROUPS):
            q = r + 4 * (g % 2) + 8 * (g // 4)
            if q >= STATE:
                continue
            m, v = q // VARS, q % VARS
            if g // 2 % 2 == 0:
                ybuf[REACH - 1 - m, v] = items[GROUPS * r + g]
            else:
                zbuf[blocks + m, v] = items[GROUPS * r + g]
    empty = blocks + REACH
    for v in range(VARS):
        ybuf[empty, v] = zero
        zbuf[empty, v] = zero
        wout[blocks, v] = zero
    lane = lanes_of(cells)

    def first(b, carry):
        nears = [read_block(ybuf, s) for s in slots(lcols, counts, 0, b, REACH - base, empty)]
        acc = couple(mlow, b, nears)
        for i in range(VARS):
            ybuf[b + REACH, i] = source[b, i] - acc[i]
        return carry

    steps(blocks, 4, first)

    def second(e, edges):
        c = blocks - 1 - e
        nears = [read_block(zbuf, s) for s in slots(ucols, counts, 1, c, -base, empty)]
        acc = couple(mupp, c, nears)
        edges = list(edges)
        for i in range(VARS):
            w = acc[i]
            z = ybuf[c + REACH, i] - w
            zbuf[c, i] = z
            zout[c, i] = z
            wout[c, i] = w
            m = c * VARS + i
            spot = m % cells
            first_lane, last_lane = pltpu.roll(z, spot, 1), pltpu.roll(z, (spot + 1) % cells, 1)
            for page in range(len(edges) // 2):
                here = lane == m - page * cells
                edges[2 * page] = jnp.where(here, first_lane, edges[2 * page])
                edges[2 * page + 1] = jnp.where(here, last_lane, edges[2 * page + 1])
        return tuple(edges)

    edges = steps(blocks, 4, second, (zero,) * (2 * west.shape[0]))
    for page in range(west.shape[0]):
        west[page] = edges[2 * page]
        east[page] = edges[2 * page + 1]
    for m in range(REACH):
        for v in range(VARS):
            tail[m, v] = wout[blocks - REACH + m, v]


def resid_kernel(
    z, w, tail, from_west, from_east, low, side, lcols, counts, resid, squares, correction, wbuf, sem
):
    store = pltpu.make_async_copy(z, correction, sem)
    store.start()
    blocks, _, nrhs, cells = z.shape
    base = lax.axis_index("chain") * blocks
    lane = lanes_of(cells)
    for v in range(VARS):
        for m in range(REACH):
            wbuf[m, v] = tail[m, v]
            wbuf[m + REACH, v] = w[m, v]
        wbuf[2 * REACH, v] = jnp.zeros((nrhs, cells), jnp.float32)

    def block(b, total, buf, shift, empty):
        nears = [read_block(buf, s) for s in slots(lcols, counts, 0, b, shift - base, empty)]
        acc = apply_coef(low, b, nears)
        left, right = [], []
        for v in range(VARS):
            m = b * VARS + v
            page, spot = m // cells, m % cells
            here = z[b, v]
            edge = pltpu.roll(from_west[page], (cells - spot) % cells, 1)
            left.append(jnp.where(lane == 0, edge, pltpu.roll(here, 1, 1)))
            edge = pltpu.roll(from_east[page], cells - 1 - spot, 1)
            right.append(jnp.where(lane == cells - 1, edge, pltpu.roll(here, cells - 1, 1)))
        beside = apply_coef(side, b, [left, right])
        for i in range(VARS):
            r = acc[i] - beside[i]
            resid[b, i] = r
            total = total + r * r
        return total

    total = jnp.zeros((nrhs, cells), jnp.float32)
    for b in range(REACH):
        total = block(b, total, wbuf, REACH, 2 * REACH)

    def inner(b, total):
        return block(b + REACH, total, w, 0, blocks)

    total = steps(blocks - REACH, 3, inner, total)
    sums = jnp.broadcast_to(jnp.sum(total, axis=1, keepdims=True), total.shape)
    row = lax.broadcasted_iota(jnp.int32, total.shape, 0)
    line = jnp.sum(jnp.where(lane == row, sums, 0.0), axis=0, keepdims=True)
    for p in range(squares.shape[0]):
        squares[p] = line
    store.wait()


def scale_kernel(entries, resid, squares, out):
    blocks, _, nrhs, cells = resid.shape
    line = squares[0]
    for p in range(1, squares.shape[0]):
        line = line + squares[p]
    lane = lanes_of(cells)
    row = lax.broadcasted_iota(jnp.int32, (nrhs, cells), 0)
    line = jnp.where(lane == row, jnp.broadcast_to(line, (nrhs, cells)), 0.0)
    msq = jnp.sum(line, axis=1, keepdims=True) / entries
    factor = jnp.broadcast_to(lax.rsqrt(msq + 1e-06), (nrhs, cells))

    def block(b, carry):
        for v in range(VARS):
            out[b, v] = resid[b, v] * factor
        return carry

    steps(blocks, 4, block)


def call(kernel, outs, args, places, scratch):
    args = [
        pltpu.with_memory_space_constraint(a, p) if p is HBM else a for a, p in zip(args, places)
    ]
    return pl.pallas_call(
        kernel,
        out_shape=[jax.ShapeDtypeStruct(shape, jnp.float32) for shape, _ in outs],
        in_specs=[pl.BlockSpec(memory_space=p) for p in places],
        out_specs=[pl.BlockSpec(memory_space=p) for _, p in outs],
        scratch_shapes=[VMEM(s, jnp.float32) if isinstance(s, tuple) else s for s in scratch],
        compiler_params=pltpu.CompilerParams(vmem_limit_bytes=VMEM_LIMIT),
    )(*args)


def shards(
    rhs, diag_block, diag_inverse, lower_coef, upper_coef, side_coef, lower_cols, upper_cols, counts
):
    blocks, nvars, nrhs, cells = rhs.shape
    n = lax.axis_size("chain")
    inv = jnp.transpose(diag_inverse, (1, 2, 0, 3))
    low, upp, side = (
        jnp.transpose(a, (0, 2, 3, 1, 4)).reshape(-1, cells)
        for a in (lower_coef, upper_coef, side_coef)
    )
    lcols, ucols, used = lower_cols.T, upper_cols.T, counts.T
    m = lax.axis_size("sub")
    rows = blocks + REACH + 1
    parts = -(-STATE * GROUPS // n)
    back = -(-4 * GROUPS // n)
    tile = (nrhs, cells)
    pages = -(-blocks * VARS // cells)

    mats = (VARS, VARS, SLOTS, blocks, cells)

    maps, source, mlow, mupp = call(
        functools.partial(local_kernel, n),
        [((n, parts) + tile, VMEM), (rhs.shape, VMEM), (mats, VMEM), (mats, VMEM)],
        (rhs, inv, low, upp, lcols, ucols, used),
        (HBM,) * 7,
        [rhs.shape, inv.shape, low.shape, upp.shape]
        + [pltpu.SMEM(lcols.shape, jnp.int32)] * 3
        + [(rows, VARS, nrhs + WIDE, cells), (rows, VARS, nrhs + 2 * WIDE, cells)]
        + [pltpu.SemaphoreType.DMA((7,))],
    )
    maps = lax.all_to_all(maps, "chain", 0, 0, tiled=True)
    (states,) = call(
        functools.partial(solve_kernel, n),
        [((n, back) + tile, VMEM)],
        (maps,),
        (VMEM,),
        [(n, STATE) + tile] * 5,
    )
    states = lax.all_to_all(states, "chain", 0, 0, tiled=True)
    z, w, tail, west, east = call(
        functools.partial(sweep_kernel, n),
        [
            (rhs.shape, VMEM),
            ((blocks + 1, VARS) + tile, VMEM),
            ((REACH, VARS) + tile, VMEM),
            ((pages,) + tile, VMEM),
            ((pages,) + tile, VMEM),
        ],
        (states, source, mlow, mupp, lcols, ucols, used),
        (VMEM,) * 4 + (SMEM,) * 3,
        [(rows, VARS) + tile] * 2,
    )
    from_west = lax.ppermute(east, "sub", [(i, i + 1) for i in range(m - 1)])
    from_east = lax.ppermute(west, "sub", [(i + 1, i) for i in range(m - 1)])
    tail = lax.ppermute(tail, "chain", [(i, i + 1) for i in range(n - 1)])
    resid, squares, correction = call(
        resid_kernel,
        [(rhs.shape, VMEM), ((n * m, 1, cells), VMEM), (rhs.shape, HBM)],
        (z, w, tail, from_west, from_east, low, side, lcols, used),
        (VMEM,) * 7 + (SMEM,) * 2,
        [(2 * REACH + 1, VARS) + tile, pltpu.SemaphoreType.DMA],
    )
    squares = lax.all_to_all(squares, ("chain", "sub"), 0, 0, tiled=True)
    entries = blocks * VARS * cells * n * m
    (residual_unit,) = call(
        functools.partial(scale_kernel, entries),
        [(rhs.shape, VMEM)],
        (resid, squares),
        (VMEM, VMEM),
        [],
    )
    return (correction, residual_unit)


def solution(mesh):
    in_specs = (
        P("chain", None, None, "sub"),
        P("chain", None, None, "sub"),
        P("chain", None, None, "sub"),
        P("chain", None, None, None, "sub"),
        P("chain", None, None, None, "sub"),
        P("chain", None, None, None, "sub"),
        P("chain", None),
        P("chain", None),
        P("chain", None),
    )
    out_specs = (P("chain", None, None, "sub"), P("chain", None, None, "sub"))
    return jax.shard_map(shards, mesh=mesh, in_specs=in_specs, out_specs=out_specs, check_vma=False)
```

```python
import functools

import jax
import jax.numpy as jnp
from jax import lax
from jax.experimental import pallas as pl
from jax.experimental.pallas import tpu as pltpu
from jax.sharding import PartitionSpec as P

VARS = 5
REACH = 3
SLOTS = 2
STATE = REACH * VARS
WIDE = 16
PAD = 8
GROUPS = 8
VMEM_LIMIT = 40 * 1024 * 1024

VMEM = pltpu.VMEM
SMEM = pltpu.SMEM
HBM = pltpu.HBM


def lanes_of(cells):
    return lax.broadcasted_iota(jnp.int32, (8, cells), 1)


def block_transpose(items, width, cells):
    count = len(items)
    lane = lanes_of(cells)
    half = 1
    while half < count:
        bit = (lane // (half * width)) % 2 == 1
        out = list(items)
        for a in range(count):
            if a & half:
                continue
            b = a + half
            out[a] = jnp.where(bit, pltpu.roll(items[b], half * width, 1), items[a])
            out[b] = jnp.where(bit, items[b], pltpu.roll(items[a], cells - half * width, 1))
        items = out
        half *= 2
    return items


def spread(ref, place, row):
    return ref[place + (pl.ds(row, 8, stride=0), slice(None))]


def mul_rows(rows, near):
    total = rows[0] * near[0]
    for j in range(1, len(near)):
        total = total + rows[j] * near[j]
    return total


def mul_groups(rows, nears):
    return [mul_rows(rows, [near[g] for near in nears]) for g in range(len(nears[0]))]


def couple(mats, b, nears):
    out = []
    for i in range(VARS):
        parts = [
            mul_groups([spread(mats, (i, j, k), b) for j in range(VARS)], nears[k])
            for k in range(SLOTS)
        ]
        out.append([x + y for x, y in zip(*parts)])
    return out


def apply_coef(coef, b, nears):
    out = []
    for i in range(VARS):
        parts = []
        for k in range(SLOTS):
            place = (b * VARS + i) * VARS * SLOTS + k
            parts.append(
                mul_rows([spread(coef, (), place + SLOTS * j) for j in range(VARS)], nears[k])
            )
        out.append(parts[0] + parts[1])
    return out


def products(inv, coef, out):
    blocks = out.shape[3] - PAD
    stride = VARS * VARS * SLOTS

    def some(o, carry):
        start = o * 8
        left = [[inv[i, m, pl.ds(start, 8), :] for m in range(VARS)] for i in range(VARS)]
        for k in range(SLOTS):
            for j in range(VARS):
                place = start * stride + j * SLOTS + k
                right = [
                    coef[pl.ds(place + m * VARS * SLOTS, 8, stride=stride), :] for m in range(VARS)
                ]
                for i in range(VARS):
                    out[i, j, k, pl.ds(start, 8), :] = mul_rows(left[i], right)
        return carry

    lax.fori_loop(0, blocks // 8, some, 0)


def slots(cols, counts, side, b, shift, empty):
    return [jnp.where(k < counts[side, b], cols[k, b] + shift, empty) for k in range(SLOTS)]


def read_block(buf, place):
    return [buf[place, v] for v in range(VARS)]


def read_groups(buf, place):
    count = buf.shape[2] // 8
    return [[buf[place, v, pl.ds(8 * g, 8), :] for g in range(count)] for v in range(VARS)]


def steps(count, most, body, carry=0):
    unroll = max(u for u in range(1, most + 1) if count % u == 0)

    def chunk(o, carry):
        for u in range(unroll):
            carry = body(o * unroll + u, carry)
        return carry

    return lax.fori_loop(0, count // unroll, chunk, carry)


def local_kernel(
    n,
    rhs_h,
    inv_h,
    low_h,
    upp_h,
    lcols_h,
    ucols_h,
    counts_h,
    out,
    source,
    mlow,
    mupp,
    rhs,
    inv,
    low,
    upp,
    lcols,
    ucols,
    counts,
    ybuf,
    zbuf,
    sems,
):
    copies = [
        pltpu.make_async_copy(src, dst, sems.at[k])
        for k, (src, dst) in enumerate(
            (
                (inv_h, inv.at[:, :, pl.ds(0, rhs.shape[0]), :]),
                (low_h, low),
                (lcols_h, lcols),
                (counts_h, counts),
                (ucols_h, ucols),
                (rhs_h, rhs),
                (upp_h, upp),
            )
        )
    ]
    for copy in copies:
        copy.start()
    blocks, _, nrhs, cells = rhs.shape
    base = lax.axis_index("chain") * blocks
    wide_y = nrhs + WIDE
    wide_z = wide_y + WIDE
    row_y = lax.broadcasted_iota(jnp.int32, (wide_y, cells), 0)
    row_z = lax.broadcasted_iota(jnp.int32, (wide_z, cells), 0)
    for m in range(REACH):
        for v in range(VARS):
            q = VARS * m + v
            ybuf[REACH - 1 - m, v] = (row_y == nrhs + q).astype(jnp.float32)
            zbuf[blocks + m, v] = (row_z == wide_y + q).astype(jnp.float32)
    for v in range(VARS):
        ybuf[blocks + REACH, v] = jnp.zeros((wide_y, cells), jnp.float32)
        zbuf[blocks + REACH, v] = jnp.zeros((wide_z, cells), jnp.float32)
    empty = blocks + REACH
    copies[0].wait()
    copies[1].wait()
    products(inv, low, mlow)
    for copy in copies[2:6]:
        copy.wait()

    def first(b, carry):
        nears = [read_groups(ybuf, s) for s in slots(lcols, counts, 0, b, REACH - base, empty)]
        acc = couple(mlow, b, nears)
        right = [rhs[b, i] for i in range(VARS)]
        for i in range(VARS):
            own = mul_rows([spread(inv, (i, j), b) for j in range(VARS)], right)
            source[b, i] = own
            ybuf[b + REACH, i, 0:8] = own - acc[i][0]
            for g in range(1, len(acc[i])):
                ybuf[b + REACH, i, 8 * g : 8 * g + 8] = -acc[i][g]
        return carry

    steps(blocks, 2, first)
    copies[6].wait()
    products(inv, upp, mupp)

    def second(e, carry):
        c = blocks - 1 - e
        nears = [read_groups(zbuf, s) for s in slots(ucols, counts, 1, c, -base, empty)]
        acc = couple(mupp, c, nears)
        for i in range(VARS):
            for g in range(len(acc[i])):
                if g < wide_y // 8:
                    value = ybuf[c + REACH, i, 8 * g : 8 * g + 8] - acc[i][g]
                else:
                    value = -acc[i][g]
                zbuf[c, i, 8 * g : 8 * g + 8] = value
        return carry

    steps(blocks, 2, second)

    items = []
    for m in range(REACH):
        for v in range(VARS):
            y = ybuf[blocks + REACH - 1 - m, v]
            z = zbuf[m, v]
            items += [y[8:16], z[8:16], z[24:32], y[0:8], y[16:24], z[16:24], z[32:40], z[0:8]]
    width = cells // n
    parts = out.shape[1]
    items += [jnp.zeros((8, cells), jnp.float32)] * (parts * n - len(items))
    for r in range(parts):
        for k, item in enumerate(block_transpose(items[r * n : (r + 1) * n], width, cells)):
            out[k, r] = item


def solve_kernel(n, x, out, g0, g1, p, kq, sbuf, tbuf):
    cells = x.shape[3]
    width = cells // n
    lane = lanes_of(cells)
    zero = jnp.zeros((8, cells), jnp.float32)

    def at(group):
        return (lane >= group * width) & (lane < (group + 1) * width)

    def turn(value, groups):
        shift = groups * width % cells
        return value if shift == 0 else pltpu.roll(value, shift, 1)

    def place(i):
        return GROUPS * i // n, GROUPS * i % n

    def unpack(d, carry):
        for i in range(STATE):
            page, spot = place(i)
            value = x[d, page]
            if spot:
                value = turn(value, -spot)
            here = pl.ds((d * STATE + i) * 8, 8)
            g0[here, :] = value
            g1[here, :] = turn(value, -4)
            p[d, i] = turn(value, -3)
            kq[d, i] = turn(value, -5)
        return carry

    lax.fori_loop(0, n, unpack, 0)

    def rows(d, i, state):
        start = (d * STATE + i) * 8
        low = [spread(g0, (), start + j) for j in range(8)]
        high = [spread(g1, (), start + j) for j in range(STATE - 8)]
        return mul_rows(low, state[:8]) + mul_rows(high, state[8:])

    def ahead(d, state):
        for i in range(STATE):
            sbuf[d, i] = state[i]
        return tuple(p[d, i] + rows(d, i, state) for i in range(STATE))

    lax.fori_loop(0, n, ahead, (zero,) * STATE)

    def couple_both(d, carry):
        state = []
        for i in range(STATE):
            sbuf[d, i] = jnp.where(at(0), sbuf[d, i], 0.0)
            state.append(turn(sbuf[d, i], 1))
        for i in range(STATE):
            kq[d, i] = turn(rows(d, i, state), 1) + kq[d, i]
        return carry

    lax.fori_loop(0, n, couple_both, 0)

    def back(e, state):
        d = n - 1 - e
        for i in range(STATE):
            tbuf[d, i] = jnp.where(at(2), state[i], 0.0)
        return tuple(kq[d, i] + rows(d, i, state) for i in range(STATE))

    lax.fori_loop(0, n, back, (zero,) * STATE)

    def pack(d, carry):
        total = [zero] * out.shape[1]
        mixed = [sbuf[d, j] + tbuf[d, j] for j in range(STATE)] + [zero]
        for r in range(4):
            value = mixed[r] + turn(mixed[r + 4], 1)
            value = value + turn(mixed[r + 8], 4) + turn(mixed[r + 12], 5)
            total[GROUPS * r // n] += turn(value, GROUPS * r % n)
        for r in range(out.shape[1]):
            out[d, r] = total[r]
        return carry

    lax.fori_loop(0, n, pack, 0)


def sweep_kernel(
    n,
    states,
    source,
    mlow,
    mupp,
    lcols,
    ucols,
    counts,
    low_h,
    side_h,
    zout,
    wout,
    tail,
    west,
    east,
    low,
    side,
    ybuf,
    zbuf,
    sems,
):
    total = low_h.shape[0]
    copies = [
        pltpu.make_async_copy(src, dst.at[pl.ds(0, total), :], sems.at[k])
        for k, (src, dst) in enumerate(((low_h, low), (side_h, side)))
    ]
    for copy in copies:
        copy.start()
    blocks, _, nrhs, cells = source.shape
    base = lax.axis_index("chain") * blocks
    width = cells // n
    zero = jnp.zeros((nrhs, cells), jnp.float32)
    items = []
    for r in range(states.shape[1]):
        items += block_transpose([states[k, r] for k in range(n)], width, cells)
    for r in range(4):
        for g in range(GROUPS):
            q = r + 4 * (g % 2) + 8 * (g // 4)
            if q >= STATE:
                continue
            m, v = q // VARS, q % VARS
            if g // 2 % 2 == 0:
                ybuf[REACH - 1 - m, v] = items[GROUPS * r + g]
            else:
                zbuf[blocks + m, v] = items[GROUPS * r + g]
    empty = blocks + REACH
    for v in range(VARS):
        ybuf[empty, v] = zero
        zbuf[empty, v] = zero
        wout[blocks, v] = zero
    lane = lanes_of(cells)

    def first(b, carry):
        nears = [read_groups(ybuf, s) for s in slots(lcols, counts, 0, b, REACH - base, empty)]
        acc = couple(mlow, b, nears)
        for i in range(VARS):
            ybuf[b + REACH, i] = source[b, i] - acc[i][0]
        return carry

    steps(blocks, 4, first)

    def second(e, edges):
        c = blocks - 1 - e
        nears = [read_groups(zbuf, s) for s in slots(ucols, counts, 1, c, -base, empty)]
        acc = couple(mupp, c, nears)
        edges = list(edges)
        for i in range(VARS):
            w = acc[i][0]
            z = ybuf[c + REACH, i] - w
            zbuf[c, i] = z
            zout[c, i] = z
            wout[c, i] = w
            m = c * VARS + i
            spot = m % cells
            first_lane, last_lane = pltpu.roll(z, spot, 1), pltpu.roll(z, (spot + 1) % cells, 1)
            for page in range(len(edges) // 2):
                here = lane == m - page * cells
                edges[2 * page] = jnp.where(here, first_lane, edges[2 * page])
                edges[2 * page + 1] = jnp.where(here, last_lane, edges[2 * page + 1])
        return tuple(edges)

    edges = steps(blocks, 4, second, (zero,) * (2 * west.shape[0]))
    for page in range(west.shape[0]):
        west[page] = edges[2 * page]
        east[page] = edges[2 * page + 1]
    for m in range(REACH):
        for v in range(VARS):
            tail[m, v] = wout[blocks - REACH + m, v]
    for copy in copies:
        copy.wait()


def resid_kernel(
    z, w, tail, from_west, from_east, low, side, lcols, counts, resid, squares, correction, wbuf, sem
):
    store = pltpu.make_async_copy(z, correction, sem)
    store.start()
    blocks, _, nrhs, cells = z.shape
    base = lax.axis_index("chain") * blocks
    lane = lanes_of(cells)
    for v in range(VARS):
        for m in range(REACH):
            wbuf[m, v] = tail[m, v]
            wbuf[m + REACH, v] = w[m, v]
        wbuf[2 * REACH, v] = jnp.zeros((nrhs, cells), jnp.float32)

    def block(b, total, buf, shift, empty):
        nears = [read_block(buf, s) for s in slots(lcols, counts, 0, b, shift - base, empty)]
        acc = apply_coef(low, b, nears)
        left, right = [], []
        for v in range(VARS):
            m = b * VARS + v
            page, spot = m // cells, m % cells
            here = z[b, v]
            edge = pltpu.roll(from_west[page], (cells - spot) % cells, 1)
            left.append(jnp.where(lane == 0, edge, pltpu.roll(here, 1, 1)))
            edge = pltpu.roll(from_east[page], cells - 1 - spot, 1)
            right.append(jnp.where(lane == cells - 1, edge, pltpu.roll(here, cells - 1, 1)))
        beside = apply_coef(side, b, [left, right])
        for i in range(VARS):
            r = acc[i] - beside[i]
            resid[b, i] = r
            total = total + r * r
        return total

    total = jnp.zeros((nrhs, cells), jnp.float32)
    for b in range(REACH):
        total = block(b, total, wbuf, REACH, 2 * REACH)

    def inner(b, total):
        return block(b + REACH, total, w, 0, blocks)

    total = steps(blocks - REACH, 3, inner, total)
    sums = jnp.broadcast_to(jnp.sum(total, axis=1, keepdims=True), total.shape)
    row = lax.broadcasted_iota(jnp.int32, total.shape, 0)
    line = jnp.sum(jnp.where(lane == row, sums, 0.0), axis=0, keepdims=True)
    for p in range(squares.shape[0]):
        squares[p] = line
    store.wait()


def scale_kernel(entries, resid, squares, out):
    blocks, _, nrhs, cells = resid.shape
    line = squares[0]
    for p in range(1, squares.shape[0]):
        line = line + squares[p]
    lane = lanes_of(cells)
    row = lax.broadcasted_iota(jnp.int32, (nrhs, cells), 0)
    line = jnp.where(lane == row, jnp.broadcast_to(line, (nrhs, cells)), 0.0)
    msq = jnp.sum(line, axis=1, keepdims=True) / entries
    factor = jnp.broadcast_to(lax.rsqrt(msq + 1e-06), (nrhs, cells))

    def block(b, carry):
        for v in range(VARS):
            out[b, v] = resid[b, v] * factor
        return carry

    steps(blocks, 4, block)


def call(kernel, outs, args, places, scratch):
    args = [
        pltpu.with_memory_space_constraint(a, p) if p is HBM else a for a, p in zip(args, places)
    ]
    return pl.pallas_call(
        kernel,
        out_shape=[jax.ShapeDtypeStruct(shape, jnp.float32) for shape, _ in outs],
        in_specs=[pl.BlockSpec(memory_space=p) for p in places],
        out_specs=[pl.BlockSpec(memory_space=p) for _, p in outs],
        scratch_shapes=[VMEM(s, jnp.float32) if isinstance(s, tuple) else s for s in scratch],
        compiler_params=pltpu.CompilerParams(vmem_limit_bytes=VMEM_LIMIT),
    )(*args)


def shards(
    rhs, diag_block, diag_inverse, lower_coef, upper_coef, side_coef, lower_cols, upper_cols, counts
):
    blocks, nvars, nrhs, cells = rhs.shape
    n = lax.axis_size("chain")
    inv = jnp.transpose(diag_inverse, (1, 2, 0, 3))
    low, upp, side = (
        jnp.transpose(a, (0, 2, 3, 1, 4)).reshape(-1, cells)
        for a in (lower_coef, upper_coef, side_coef)
    )
    lcols, ucols, used = lower_cols.T, upper_cols.T, counts.T
    m = lax.axis_size("sub")
    rows = blocks + REACH + 1
    parts = -(-STATE * GROUPS // n)
    back = -(-4 * GROUPS // n)
    tile = (nrhs, cells)
    pages = -(-blocks * VARS // cells)

    mats = (VARS, VARS, SLOTS, blocks + PAD, cells)
    padded = (low.shape[0] + PAD, cells)

    maps, source, mlow, mupp = call(
        functools.partial(local_kernel, n),
        [((n, parts) + tile, VMEM), (rhs.shape, VMEM), (mats, VMEM), (mats, VMEM)],
        (rhs, inv, low, upp, lcols, ucols, used),
        (HBM,) * 7,
        [rhs.shape, (VARS, VARS, blocks + PAD, cells), low.shape, upp.shape]
        + [pltpu.SMEM(lcols.shape, jnp.int32)] * 3
        + [(rows, VARS, nrhs + WIDE, cells), (rows, VARS, nrhs + 2 * WIDE, cells)]
        + [pltpu.SemaphoreType.DMA((7,))],
    )
    maps = lax.all_to_all(maps, "chain", 0, 0, tiled=True)
    (states,) = call(
        functools.partial(solve_kernel, n),
        [((n, back) + tile, VMEM)],
        (maps,),
        (VMEM,),
        [(n * STATE * 8 + PAD, cells)] * 2 + [(n, STATE) + tile] * 4,
    )
    states = lax.all_to_all(states, "chain", 0, 0, tiled=True)
    z, w, tail, west, east, low, side = call(
        functools.partial(sweep_kernel, n),
        [
            (rhs.shape, VMEM),
            ((blocks + 1, VARS) + tile, VMEM),
            ((REACH, VARS) + tile, VMEM),
            ((pages,) + tile, VMEM),
            ((pages,) + tile, VMEM),
            (padded, VMEM),
            (padded, VMEM),
        ],
        (states, source, mlow, mupp, lcols, ucols, used, low, side),
        (VMEM,) * 4 + (SMEM,) * 3 + (HBM,) * 2,
        [(rows, VARS) + tile] * 2 + [pltpu.SemaphoreType.DMA((2,))],
    )
    from_west = lax.ppermute(east, "sub", [(i, i + 1) for i in range(m - 1)])
    from_east = lax.ppermute(west, "sub", [(i + 1, i) for i in range(m - 1)])
    tail = lax.ppermute(tail, "chain", [(i, i + 1) for i in range(n - 1)])
    resid, squares, correction = call(
        resid_kernel,
        [(rhs.shape, VMEM), ((n * m, 1, cells), VMEM), (rhs.shape, HBM)],
        (z, w, tail, from_west, from_east, low, side, lcols, used),
        (VMEM,) * 7 + (SMEM,) * 2,
        [(2 * REACH + 1, VARS) + tile, pltpu.SemaphoreType.DMA],
    )
    squares = lax.all_to_all(squares, ("chain", "sub"), 0, 0, tiled=True)
    entries = blocks * VARS * cells * n * m
    (residual_unit,) = call(
        functools.partial(scale_kernel, entries),
        [(rhs.shape, VMEM)],
        (resid, squares),
        (VMEM, VMEM),
        [],
    )
    return (correction, residual_unit)


def solution(mesh):
    in_specs = (
        P("chain", None, None, "sub"),
        P("chain", None, None, "sub"),
        P("chain", None, None, "sub"),
        P("chain", None, None, None, "sub"),
        P("chain", None, None, None, "sub"),
        P("chain", None, None, None, "sub"),
        P("chain", None),
        P("chain", None),
        P("chain", None),
    )
    out_specs = (P("chain", None, None, "sub"), P("chain", None, None, "sub"))
    return jax.shard_map(shards, mesh=mesh, in_specs=in_specs, out_specs=out_specs, check_vma=False)
```

```python
import functools

import jax
import jax.numpy as jnp
from jax import lax
from jax.experimental import pallas as pl
from jax.experimental.pallas import tpu as pltpu
from jax.sharding import PartitionSpec as P

VARS = 5
REACH = 3
SLOTS = 2
STATE = REACH * VARS
WIDE = 16
PAD = 8
GROUPS = 8
VMEM_LIMIT = 40 * 1024 * 1024

VMEM = pltpu.VMEM
SMEM = pltpu.SMEM
HBM = pltpu.HBM


def lanes_of(cells):
    return lax.broadcasted_iota(jnp.int32, (8, cells), 1)


def block_transpose(items, width, cells):
    count = len(items)
    lane = lanes_of(cells)
    half = 1
    while half < count:
        bit = (lane // (half * width)) % 2 == 1
        out = list(items)
        for a in range(count):
            if a & half:
                continue
            b = a + half
            out[a] = jnp.where(bit, pltpu.roll(items[b], half * width, 1), items[a])
            out[b] = jnp.where(bit, items[b], pltpu.roll(items[a], cells - half * width, 1))
        items = out
        half *= 2
    return items


def spread(ref, place, row):
    return ref[place + (pl.ds(row, 8, stride=0), slice(None))]


def mul_rows(rows, near):
    total = rows[0] * near[0]
    for j in range(1, len(near)):
        total = total + rows[j] * near[j]
    return total


def mul_groups(rows, nears):
    return [mul_rows(rows, [near[g] for near in nears]) for g in range(len(nears[0]))]


def couple(mats, b, nears):
    out = []
    for i in range(VARS):
        parts = [
            mul_groups([spread(mats, (i, j, k), b) for j in range(VARS)], nears[k])
            for k in range(SLOTS)
        ]
        out.append([x + y for x, y in zip(*parts)])
    return out


def apply_coef(coef, b, nears):
    out = []
    for i in range(VARS):
        parts = []
        for k in range(SLOTS):
            place = (b * VARS + i) * VARS * SLOTS + k
            parts.append(
                mul_rows([spread(coef, (), place + SLOTS * j) for j in range(VARS)], nears[k])
            )
        out.append(parts[0] + parts[1])
    return out


def products(inv, coef, out):
    blocks = out.shape[3] - PAD
    stride = VARS * VARS * SLOTS

    def some(o, carry):
        start = o * 8
        left = [[inv[i, m, pl.ds(start, 8), :] for m in range(VARS)] for i in range(VARS)]
        for k in range(SLOTS):
            for j in range(VARS):
                place = start * stride + j * SLOTS + k
                right = [
                    coef[pl.ds(place + m * VARS * SLOTS, 8, stride=stride), :] for m in range(VARS)
                ]
                for i in range(VARS):
                    out[i, j, k, pl.ds(start, 8), :] = mul_rows(left[i], right)
        return carry

    lax.fori_loop(0, blocks // 8, some, 0)


def slots(cols, counts, side, b, shift, empty):
    return [jnp.where(k < counts[side, b], cols[k, b] + shift, empty) for k in range(SLOTS)]


def read_block(buf, place):
    return [buf[place, v] for v in range(VARS)]


def read_groups(buf, place):
    count = buf.shape[2] // 8
    return [[buf[place, v, pl.ds(8 * g, 8), :] for g in range(count)] for v in range(VARS)]


def steps(count, most, body, carry=0):
    unroll = max(u for u in range(1, most + 1) if count % u == 0)

    def chunk(o, carry):
        for u in range(unroll):
            carry = body(o * unroll + u, carry)
        return carry

    return lax.fori_loop(0, count // unroll, chunk, carry)


def local_kernel(
    n,
    rhs_h,
    inv_h,
    low_h,
    upp_h,
    lcols_h,
    ucols_h,
    counts_h,
    out,
    source,
    mlow,
    mupp,
    lcols_v,
    ucols_v,
    counts_v,
    rhs,
    inv,
    low,
    upp,
    lcols,
    ucols,
    counts,
    ybuf,
    zbuf,
    sems,
):
    copies = [
        pltpu.make_async_copy(src, dst, sems.at[k])
        for k, (src, dst) in enumerate(
            (
                (inv_h, inv.at[:, :, pl.ds(0, rhs.shape[0]), :]),
                (low_h, low),
                (lcols_h, lcols),
                (counts_h, counts),
                (ucols_h, ucols),
                (rhs_h, rhs),
                (upp_h, upp),
                (lcols_h, lcols_v),
                (ucols_h, ucols_v),
                (counts_h, counts_v),
            )
        )
    ]
    for copy in copies:
        copy.start()
    blocks, _, nrhs, cells = rhs.shape
    base = lax.axis_index("chain") * blocks
    wide_y = nrhs + WIDE
    wide_z = wide_y + WIDE
    row_y = lax.broadcasted_iota(jnp.int32, (wide_y, cells), 0)
    row_z = lax.broadcasted_iota(jnp.int32, (wide_z, cells), 0)
    for m in range(REACH):
        for v in range(VARS):
            q = VARS * m + v
            ybuf[REACH - 1 - m, v] = (row_y == nrhs + q).astype(jnp.float32)
            zbuf[blocks + m, v] = (row_z == wide_y + q).astype(jnp.float32)
    for v in range(VARS):
        ybuf[blocks + REACH, v] = jnp.zeros((wide_y, cells), jnp.float32)
        zbuf[blocks + REACH, v] = jnp.zeros((wide_z, cells), jnp.float32)
    empty = blocks + REACH
    copies[0].wait()
    copies[1].wait()
    products(inv, low, mlow)
    for copy in copies[2:6]:
        copy.wait()

    def first(b, carry):
        nears = [read_groups(ybuf, s) for s in slots(lcols, counts, 0, b, REACH - base, empty)]
        acc = couple(mlow, b, nears)
        right = [rhs[b, i] for i in range(VARS)]
        for i in range(VARS):
            own = mul_rows([spread(inv, (i, j), b) for j in range(VARS)], right)
            source[b, i] = own
            ybuf[b + REACH, i, 0:8] = own - acc[i][0]
            for g in range(1, len(acc[i])):
                ybuf[b + REACH, i, 8 * g : 8 * g + 8] = -acc[i][g]
        return carry

    steps(blocks, 2, first)
    for copy in copies[6:]:
        copy.wait()
    products(inv, upp, mupp)

    def second(e, carry):
        c = blocks - 1 - e
        nears = [read_groups(zbuf, s) for s in slots(ucols, counts, 1, c, -base, empty)]
        acc = couple(mupp, c, nears)
        for i in range(VARS):
            for g in range(len(acc[i])):
                if g < wide_y // 8:
                    value = ybuf[c + REACH, i, 8 * g : 8 * g + 8] - acc[i][g]
                else:
                    value = -acc[i][g]
                zbuf[c, i, 8 * g : 8 * g + 8] = value
        return carry

    steps(blocks, 2, second)

    items = []
    for m in range(REACH):
        for v in range(VARS):
            y = ybuf[blocks + REACH - 1 - m, v]
            z = zbuf[m, v]
            items += [y[8:16], z[8:16], z[24:32], y[0:8], y[16:24], z[16:24], z[32:40], z[0:8]]
    width = cells // n
    parts = out.shape[1]
    items += [jnp.zeros((8, cells), jnp.float32)] * (parts * n - len(items))
    for r in range(parts):
        for k, item in enumerate(block_transpose(items[r * n : (r + 1) * n], width, cells)):
            out[k, r] = item


def solve_kernel(n, x, out, g0, g1, p, kq, sbuf, tbuf):
    cells = x.shape[3]
    width = cells // n
    lane = lanes_of(cells)
    zero = jnp.zeros((8, cells), jnp.float32)

    def at(group):
        return (lane >= group * width) & (lane < (group + 1) * width)

    def turn(value, groups):
        shift = groups * width % cells
        return value if shift == 0 else pltpu.roll(value, shift, 1)

    def place(i):
        return GROUPS * i // n, GROUPS * i % n

    def unpack(d, carry):
        for i in range(STATE):
            page, spot = place(i)
            value = x[d, page]
            if spot:
                value = turn(value, -spot)
            here = pl.ds((d * STATE + i) * 8, 8)
            g0[here, :] = value
            g1[here, :] = turn(value, -4)
            p[d, i] = turn(value, -3)
            kq[d, i] = turn(value, -5)
        return carry

    lax.fori_loop(0, n, unpack, 0)

    def rows(d, i, state):
        start = (d * STATE + i) * 8
        low = [spread(g0, (), start + j) for j in range(8)]
        high = [spread(g1, (), start + j) for j in range(STATE - 8)]
        return mul_rows(low, state[:8]) + mul_rows(high, state[8:])

    def ahead(d, state):
        for i in range(STATE):
            sbuf[d, i] = state[i]
        return tuple(p[d, i] + rows(d, i, state) for i in range(STATE))

    lax.fori_loop(0, n, ahead, (zero,) * STATE)

    def couple_both(d, carry):
        state = []
        for i in range(STATE):
            sbuf[d, i] = jnp.where(at(0), sbuf[d, i], 0.0)
            state.append(turn(sbuf[d, i], 1))
        for i in range(STATE):
            kq[d, i] = turn(rows(d, i, state), 1) + kq[d, i]
        return carry

    lax.fori_loop(0, n, couple_both, 0)

    def back(e, state):
        d = n - 1 - e
        for i in range(STATE):
            tbuf[d, i] = jnp.where(at(2), state[i], 0.0)
        return tuple(kq[d, i] + rows(d, i, state) for i in range(STATE))

    lax.fori_loop(0, n, back, (zero,) * STATE)

    def pack(d, carry):
        total = [zero] * out.shape[1]
        mixed = [sbuf[d, j] + tbuf[d, j] for j in range(STATE)] + [zero]
        for r in range(4):
            value = mixed[r] + turn(mixed[r + 4], 1)
            value = value + turn(mixed[r + 8], 4) + turn(mixed[r + 12], 5)
            total[GROUPS * r // n] += turn(value, GROUPS * r % n)
        for r in range(out.shape[1]):
            out[d, r] = total[r]
        return carry

    lax.fori_loop(0, n, pack, 0)


def sweep_kernel(
    n,
    states,
    source,
    mlow,
    mupp,
    lcols,
    ucols,
    counts,
    low_h,
    side_h,
    zout,
    wout,
    tail,
    edge,
    low,
    side,
    ybuf,
    zbuf,
    sems,
):
    total = low_h.shape[0]
    copies = [
        pltpu.make_async_copy(src, dst.at[pl.ds(0, total), :], sems.at[k])
        for k, (src, dst) in enumerate(((low_h, low), (side_h, side)))
    ]
    for copy in copies:
        copy.start()
    blocks, _, nrhs, cells = source.shape
    base = lax.axis_index("chain") * blocks
    width = cells // n
    zero = jnp.zeros((nrhs, cells), jnp.float32)
    items = []
    for r in range(states.shape[1]):
        items += block_transpose([states[k, r] for k in range(n)], width, cells)
    for r in range(4):
        for g in range(GROUPS):
            q = r + 4 * (g % 2) + 8 * (g // 4)
            if q >= STATE:
                continue
            m, v = q // VARS, q % VARS
            if g // 2 % 2 == 0:
                ybuf[REACH - 1 - m, v] = items[GROUPS * r + g]
            else:
                zbuf[blocks + m, v] = items[GROUPS * r + g]
    empty = blocks + REACH
    for v in range(VARS):
        ybuf[empty, v] = zero
        zbuf[empty, v] = zero
        wout[blocks, v] = zero
    lane = lanes_of(cells)

    def first(b, carry):
        nears = [read_groups(ybuf, s) for s in slots(lcols, counts, 0, b, REACH - base, empty)]
        acc = couple(mlow, b, nears)
        for i in range(VARS):
            ybuf[b + REACH, i] = source[b, i] - acc[i][0]
        return carry

    steps(blocks, 4, first)

    def second(e, edges):
        c = blocks - 1 - e
        nears = [read_groups(zbuf, s) for s in slots(ucols, counts, 1, c, -base, empty)]
        acc = couple(mupp, c, nears)
        edges = list(edges)
        for i in range(VARS):
            w = acc[i][0]
            z = ybuf[c + REACH, i] - w
            zbuf[c, i] = z
            zout[c, i] = z
            wout[c, i] = w
            here = (lane == 2 * c) | (lane == (2 * c + cells - 1) % cells)
            edges[i] = jnp.where(here, pltpu.roll(z, 2 * c, 1), edges[i])
        return tuple(edges)

    edges = steps(blocks, 4, second, (zero,) * VARS)
    for v in range(VARS):
        edge[v] = edges[v]
    for m in range(REACH):
        for v in range(VARS):
            tail[m, v] = wout[blocks - REACH + m, v]
    for copy in copies:
        copy.wait()


def inner_kernel(z, w, low, side, lcols, counts, resid, coef, correction, wbuf, sem):
    store = pltpu.make_async_copy(z, correction, sem)
    store.start()
    blocks, _, nrhs, cells = z.shape
    base = lax.axis_index("chain") * blocks
    lane = lanes_of(cells)
    zero = jnp.zeros((nrhs, cells), jnp.float32)
    for v in range(VARS):
        for m in range(REACH):
            wbuf[m, v] = zero
            wbuf[m + REACH, v] = w[m, v]
        wbuf[2 * REACH, v] = zero
    pages = coef.shape[0]
    size = VARS * VARS * SLOTS
    row = lax.broadcasted_iota(jnp.int32, (8, cells), 0)

    def block(b, found, buf, shift, empty):
        nears = [read_block(buf, s) for s in slots(lcols, counts, 0, b, shift - base, empty)]
        acc = apply_coef(low, b, nears)
        left, right = [], []
        for v in range(VARS):
            here = z[b, v]
            left.append(jnp.where(lane == 0, 0.0, pltpu.roll(here, 1, 1)))
            right.append(jnp.where(lane == cells - 1, 0.0, pltpu.roll(here, cells - 1, 1)))
        beside = apply_coef(side, b, [left, right])
        for i in range(VARS):
            resid[b, i] = acc[i] - beside[i]
        here = (lane + row % 2) % cells == 2 * b
        return tuple(
            jnp.where(here, pltpu.roll(side[pl.ds(b * size + 8 * r, 8), :], 2 * b, 1), found[r])
            for r in range(pages)
        )

    found = (jnp.zeros((8, cells), jnp.float32),) * pages
    for b in range(REACH):
        found = block(b, found, wbuf, REACH, 2 * REACH)

    def inner(b, found):
        return block(b + REACH, found, w, 0, blocks)

    found = steps(blocks - REACH, 3, inner, found)
    for r in range(pages):
        coef[r] = found[r]
    store.wait()


def outer_kernel(
    inner, coef, low, tail, swap_a, swap_b, lcols, counts, resid, squares, wbuf, cbuf
):
    blocks, _, nrhs, cells = inner.shape
    base = lax.axis_index("chain") * blocks
    odd = lax.axis_index("sub") % 2 == 1
    lane = lanes_of(cells)
    zero = jnp.zeros((nrhs, cells), jnp.float32)
    near = []
    for v in range(VARS):
        west = pltpu.roll(jnp.where(odd, swap_a[v], swap_b[v]), 1, 1)
        east = pltpu.roll(jnp.where(odd, swap_b[v], swap_a[v]), cells - 1, 1)
        near.append(jnp.where(lane % 2 == 0, west, east))
    for i in range(VARS):
        rows = []
        for j in range(VARS):
            k = (i * VARS + j) * SLOTS
            rows.append(coef[k // 8, pl.ds(k % 8, 1), :] + coef[(k + 1) // 8, pl.ds((k + 1) % 8, 1), :])
        cbuf[i] = mul_rows(rows, near)
    for v in range(VARS):
        for m in range(REACH):
            wbuf[m, v] = tail[m, v]
        wbuf[REACH, v] = zero
    ends = (lane == 0) | (lane == cells - 1)

    def add(b, i, value, total):
        value = value - jnp.where(ends, pltpu.roll(cbuf[i], (cells - 2 * b) % cells, 1), 0.0)
        resid[b, i] = value
        return total + value * value

    total = zero
    for b in range(REACH):
        places = [
            jnp.where(s < REACH, s, REACH) for s in slots(lcols, counts, 0, b, REACH - base, REACH)
        ]
        acc = apply_coef(low, b, [read_block(wbuf, s) for s in places])
        for i in range(VARS):
            total = add(b, i, inner[b, i] + acc[i], total)

    def rest(b, total):
        for i in range(VARS):
            total = add(b + REACH, i, inner[b + REACH, i], total)
        return total

    total = steps(blocks - REACH, 3, rest, total)
    sums = jnp.broadcast_to(jnp.sum(total, axis=1, keepdims=True), total.shape)
    row = lax.broadcasted_iota(jnp.int32, total.shape, 0)
    line = jnp.sum(jnp.where(lane == row, sums, 0.0), axis=0, keepdims=True)
    for p in range(squares.shape[0]):
        squares[p] = line


def scale_kernel(entries, resid, squares, out):
    blocks, _, nrhs, cells = resid.shape
    line = squares[0]
    for p in range(1, squares.shape[0]):
        line = line + squares[p]
    lane = lanes_of(cells)
    row = lax.broadcasted_iota(jnp.int32, (nrhs, cells), 0)
    line = jnp.where(lane == row, jnp.broadcast_to(line, (nrhs, cells)), 0.0)
    msq = jnp.sum(line, axis=1, keepdims=True) / entries
    factor = jnp.broadcast_to(lax.rsqrt(msq + 1e-06), (nrhs, cells))

    def block(b, carry):
        for v in range(VARS):
            out[b, v] = resid[b, v] * factor
        return carry

    steps(blocks, 4, block)


def call(kernel, outs, args, places, scratch):
    args = [
        pltpu.with_memory_space_constraint(a, p) if p is HBM else a for a, p in zip(args, places)
    ]
    return pl.pallas_call(
        kernel,
        out_shape=[jax.ShapeDtypeStruct(o[0], (o + (jnp.float32,))[2]) for o in outs],
        in_specs=[pl.BlockSpec(memory_space=p) for p in places],
        out_specs=[pl.BlockSpec(memory_space=p) for p in (o[1] for o in outs)],
        scratch_shapes=[VMEM(s, jnp.float32) if isinstance(s, tuple) else s for s in scratch],
        compiler_params=pltpu.CompilerParams(vmem_limit_bytes=VMEM_LIMIT),
    )(*args)


def shards(
    rhs, diag_block, diag_inverse, lower_coef, upper_coef, side_coef, lower_cols, upper_cols, counts
):
    blocks, nvars, nrhs, cells = rhs.shape
    n = lax.axis_size("chain")
    inv = jnp.transpose(diag_inverse, (1, 2, 0, 3))
    low, upp, side = (
        jnp.transpose(a, (0, 2, 3, 1, 4)).reshape(-1, cells)
        for a in (lower_coef, upper_coef, side_coef)
    )
    lcols, ucols, used = lower_cols.T, upper_cols.T, counts.T
    m = lax.axis_size("sub")
    rows = blocks + REACH + 1
    parts = -(-STATE * GROUPS // n)
    back = -(-4 * GROUPS // n)
    tile = (nrhs, cells)

    mats = (VARS, VARS, SLOTS, blocks + PAD, cells)
    padded = (low.shape[0] + PAD, cells)

    maps, source, mlow, mupp, lcols, ucols, used = call(
        functools.partial(local_kernel, n),
        [((n, parts) + tile, VMEM), (rhs.shape, VMEM), (mats, VMEM), (mats, VMEM)]
        + [(lcols.shape, VMEM, jnp.int32)] * 3,
        (rhs, inv, low, upp, lcols, ucols, used),
        (HBM,) * 7,
        [rhs.shape, (VARS, VARS, blocks + PAD, cells), low.shape, upp.shape]
        + [pltpu.SMEM(lcols.shape, jnp.int32)] * 3
        + [(rows, VARS, nrhs + WIDE, cells), (rows, VARS, nrhs + 2 * WIDE, cells)]
        + [pltpu.SemaphoreType.DMA((10,))],
    )
    maps = lax.all_to_all(maps, "chain", 0, 0, tiled=True)
    (states,) = call(
        functools.partial(solve_kernel, n),
        [((n, back) + tile, VMEM)],
        (maps,),
        (VMEM,),
        [(n * STATE * 8 + PAD, cells)] * 2 + [(n, STATE) + tile] * 4,
    )
    states = lax.all_to_all(states, "chain", 0, 0, tiled=True)
    z, w, tail, edge, low, side = call(
        functools.partial(sweep_kernel, n),
        [
            (rhs.shape, VMEM),
            ((blocks + 1, VARS) + tile, VMEM),
            ((REACH, VARS) + tile, VMEM),
            ((VARS,) + tile, VMEM),
            (padded, VMEM),
            (padded, VMEM),
        ],
        (states, source, mlow, mupp, lcols, ucols, used, low, side),
        (VMEM,) * 4 + (SMEM,) * 3 + (HBM,) * 2,
        [(rows, VARS) + tile] * 2 + [pltpu.SemaphoreType.DMA((2,))],
    )
    tail = lax.ppermute(tail, "chain", [(i, i + 1) for i in range(n - 1)])
    swap_a, swap_b = (
        lax.ppermute(
            edge, "sub", [p for i in range(first, m - 1, 2) for p in ((i, i + 1), (i + 1, i))]
        )
        for first in (0, 1)
    )
    inner, coef, correction = call(
        inner_kernel,
        [
            (rhs.shape, VMEM),
            ((-(-VARS * VARS * SLOTS // 8),) + (8, cells), VMEM),
            (rhs.shape, HBM),
        ],
        (z, w, low, side, lcols, used),
        (VMEM,) * 4 + (SMEM,) * 2,
        [(2 * REACH + 1, VARS) + tile, pltpu.SemaphoreType.DMA],
    )
    resid, squares = call(
        outer_kernel,
        [(rhs.shape, VMEM), ((n * m, 1, cells), VMEM)],
        (inner, coef, low, tail, swap_a, swap_b, lcols, used),
        (VMEM,) * 6 + (SMEM,) * 2,
        [(REACH + 1, VARS) + tile, (VARS,) + tile],
    )
    squares = lax.all_to_all(squares, ("chain", "sub"), 0, 0, tiled=True)
    entries = blocks * VARS * cells * n * m
    (residual_unit,) = call(
        functools.partial(scale_kernel, entries),
        [(rhs.shape, VMEM)],
        (resid, squares),
        (VMEM, VMEM),
        [],
    )
    return (correction, residual_unit)


def solution(mesh):
    in_specs = (
        P("chain", None, None, "sub"),
        P("chain", None, None, "sub"),
        P("chain", None, None, "sub"),
        P("chain", None, None, None, "sub"),
        P("chain", None, None, None, "sub"),
        P("chain", None, None, None, "sub"),
        P("chain", None),
        P("chain", None),
        P("chain", None),
    )
    out_specs = (P("chain", None, None, "sub"), P("chain", None, None, "sub"))
    return jax.shard_map(shards, mesh=mesh, in_specs=in_specs, out_specs=out_specs, check_vma=False)
```

```python
import functools

import jax
import jax.numpy as jnp
from jax import lax
from jax.experimental import pallas as pl
from jax.experimental.pallas import tpu as pltpu
from jax.sharding import PartitionSpec as P

VARS = 5
REACH = 3
SLOTS = 2
STATE = REACH * VARS
WIDE = 16
PAD = 8
SPACE = 72
GROUPS = 8
VMEM_LIMIT = 40 * 1024 * 1024

VMEM = pltpu.VMEM
SMEM = pltpu.SMEM
HBM = pltpu.HBM


def lanes_of(cells):
    return lax.broadcasted_iota(jnp.int32, (8, cells), 1)


def block_transpose(items, width, cells):
    count = len(items)
    lane = lanes_of(cells)
    half = 1
    while half < count:
        bit = (lane // (half * width)) % 2 == 1
        out = list(items)
        for a in range(count):
            if a & half:
                continue
            b = a + half
            out[a] = jnp.where(bit, pltpu.roll(items[b], half * width, 1), items[a])
            out[b] = jnp.where(bit, items[b], pltpu.roll(items[a], cells - half * width, 1))
        items = out
        half *= 2
    return items


def spread(ref, place, row):
    return ref[place + (pl.ds(row, 8, stride=0), slice(None))]


def mul_rows(rows, near):
    total = rows[0] * near[0]
    for j in range(1, len(near)):
        total = total + rows[j] * near[j]
    return total


def mul_groups(rows, nears):
    return [mul_rows(rows, [near[g] for near in nears]) for g in range(len(nears[0]))]


def couple(mats, b, nears):
    out = []
    for i in range(VARS):
        parts = [
            mul_groups([spread(mats, (i, j, k), b) for j in range(VARS)], nears[k])
            for k in range(SLOTS)
        ]
        out.append([x + y for x, y in zip(*parts)])
    return out


def apply_coef(coef, b, nears):
    out = []
    for i in range(VARS):
        parts = []
        for k in range(SLOTS):
            place = (b * VARS + i) * VARS * SLOTS + k
            parts.append(
                mul_rows([spread(coef, (), place + SLOTS * j) for j in range(VARS)], nears[k])
            )
        out.append(parts[0] + parts[1])
    return out


def products(inv, coef, out):
    blocks = out.shape[3] - PAD
    stride = VARS * VARS * SLOTS

    def some(o, carry):
        start = o * 8
        left = [[inv[i, m, pl.ds(start, 8), :] for m in range(VARS)] for i in range(VARS)]
        for k in range(SLOTS):
            for j in range(VARS):
                place = start * stride + j * SLOTS + k
                right = [
                    coef[pl.ds(place + m * VARS * SLOTS, 8, stride=stride), :] for m in range(VARS)
                ]
                for i in range(VARS):
                    out[i, j, k, pl.ds(start, 8), :] = mul_rows(left[i], right)
        return carry

    lax.fori_loop(0, blocks // 8, some, 0)


def slots(cols, counts, side, b, shift, empty):
    return [jnp.where(k < counts[side, b], cols[k, b] + shift, empty) for k in range(SLOTS)]


def read_block(buf, place):
    return [buf[place, v] for v in range(VARS)]


def read_groups(buf, place):
    count = buf.shape[2] // 8
    return [[buf[place, v, pl.ds(8 * g, 8), :] for g in range(count)] for v in range(VARS)]


def steps(count, most, body, carry=0):
    unroll = max(u for u in range(1, most + 1) if count % u == 0)

    def chunk(o, carry):
        for u in range(unroll):
            carry = body(o * unroll + u, carry)
        return carry

    return lax.fori_loop(0, count // unroll, chunk, carry)


def prepare_kernel(
    rhs_h,
    inv_h,
    low_h,
    upp_h,
    lcols_h,
    ucols_h,
    counts_h,
    rhs,
    inv,
    mlow,
    mupp,
    last,
    lcols_v,
    ucols_v,
    counts_v,
    low,
    upp,
    ucols,
    counts,
    sems,
):
    blocks = rhs.shape[0]
    pairs = (
        (inv_h, inv.at[:, :, pl.ds(0, blocks), :]),
        (upp_h, upp),
        (ucols_h, ucols),
        (counts_h, counts),
        (low_h, low),
        (rhs_h, rhs),
        (lcols_h, lcols_v),
        (ucols_h, ucols_v),
        (counts_h, counts_v),
    )
    copies = [pltpu.make_async_copy(src, dst, sems.at[k]) for k, (src, dst) in enumerate(pairs)]
    for copy in copies:
        copy.start()
    base = lax.axis_index("chain") * blocks
    for copy in copies[:4]:
        copy.wait()
    products(inv, upp, mupp)
    for m in range(REACH):
        b = blocks - REACH + m
        offs = [ucols[k, b] - base - b for k in range(SLOTS)]
        for i in range(VARS):
            for j in range(VARS):
                rows = [mupp[i, j, k, pl.ds(b, 1), :] for k in range(SLOTS)]
                for d in range(REACH):
                    total = jnp.zeros_like(rows[0])
                    for k in range(SLOTS):
                        hit = (offs[k] == d + 1) & (k < counts[1, b])
                        total = jnp.where(hit, rows[k], total)
                    last[pl.ds(((m * VARS + i) * VARS + j) * REACH + d, 1), :] = total
    copies[4].wait()
    products(inv, low, mlow)
    for copy in copies[5:]:
        copy.wait()


def local_kernel(n, rhs, inv, mlow, mupp, lcols, ucols, counts, out, source, ybuf, zbuf, stage):
    blocks, _, nrhs, cells = rhs.shape
    base = lax.axis_index("chain") * blocks
    wide_y = nrhs + WIDE
    wide_z = wide_y + WIDE
    row_y = lax.broadcasted_iota(jnp.int32, (wide_y, cells), 0)
    row_z = lax.broadcasted_iota(jnp.int32, (wide_z, cells), 0)
    for m in range(REACH):
        for v in range(VARS):
            q = VARS * m + v
            ybuf[REACH - 1 - m, v] = (row_y == nrhs + q).astype(jnp.float32)
            zbuf[blocks + m, v] = (row_z == wide_y + q).astype(jnp.float32)
    for v in range(VARS):
        ybuf[blocks + REACH, v] = jnp.zeros((wide_y, cells), jnp.float32)
        zbuf[blocks + REACH, v] = jnp.zeros((wide_z, cells), jnp.float32)
    empty = blocks + REACH

    def first(b, carry):
        nears = [read_groups(ybuf, s) for s in slots(lcols, counts, 0, b, REACH - base, empty)]
        acc = couple(mlow, b, nears)
        right = [rhs[b, i] for i in range(VARS)]
        for i in range(VARS):
            own = mul_rows([spread(inv, (i, j), b) for j in range(VARS)], right)
            source[b, i] = own
            ybuf[b + REACH, i, 0:8] = own - acc[i][0]
            for g in range(1, len(acc[i])):
                ybuf[b + REACH, i, 8 * g : 8 * g + 8] = -acc[i][g]
        return carry

    steps(blocks, 2, first)

    def second(e, carry):
        c = blocks - 1 - e
        nears = [read_groups(zbuf, s) for s in slots(ucols, counts, 1, c, -base, empty)]
        acc = couple(mupp, c, nears)
        for i in range(VARS):
            for g in range(len(acc[i])):
                if g < wide_y // 8:
                    value = ybuf[c + REACH, i, 8 * g : 8 * g + 8] - acc[i][g]
                else:
                    value = -acc[i][g]
                zbuf[c, i, 8 * g : 8 * g + 8] = value
        return carry

    steps(blocks, 2, second)

    for i in range(WIDE):
        m, v = i // VARS, i % VARS
        for g in range((wide_y + wide_z) // 8):
            if i == STATE:
                value = jnp.zeros((8, cells), jnp.float32)
            elif g < wide_y // 8:
                value = ybuf[blocks + REACH - 1 - m, v, 8 * g : 8 * g + 8]
            else:
                value = zbuf[m, v, 8 * g - wide_y : 8 * g - wide_y + 8]
            stage[pl.ds(i * SPACE + 8 * g, 8), :] = value
    order = []
    for first_column in (nrhs, wide_y + nrhs, 2 * wide_y):
        for half in range(2):
            order += [(half, first_column + j) for j in range(WIDE)]
    for first_column in (0, wide_y):
        for half in range(2):
            order += [(half, first_column + q) for q in range(nrhs)]
    width = cells // n
    for page in range(out.shape[1]):
        items = [
            stage[pl.ds(half * 8 * SPACE + column, 8, stride=SPACE), :]
            for half, column in order[page * n : (page + 1) * n]
        ]
        for k, item in enumerate(block_transpose(items, width, cells)):
            out[k, page] = item


def split(value, period, stop, width, cells):
    items = [value]
    lane = lanes_of(cells)
    while period > stop:
        half = period // 2 * width
        bit = lane // half % 2 == 1
        fresh = []
        for item in items:
            other = pltpu.roll(item, half, 1)
            fresh += [jnp.where(bit, other, item), jnp.where(bit, item, other)]
        items = fresh
        period //= 2
    return items


def solve_kernel(n, x, out, kq, states):
    cells = x.shape[3]
    width = cells // n
    zero = jnp.zeros((8, cells), jnp.float32)

    def piece(d, at):
        page, spot = GROUPS * at // n, GROUPS * at % n // GROUPS
        return split(x[d, page], n, GROUPS, width, cells)[spot]

    def spread_rows(state):
        return [state[j // 8][j % 8 : j % 8 + 1] for j in range(STATE)]

    def apply(d, first, rows):
        total = []
        for half in range(2):
            columns = []
            for part in range(2):
                columns += split(piece(d, first + 2 * half + part), GROUPS, 1, width, cells)
            sums = [columns[j] * rows[j] for j in range(STATE)]
            while len(sums) > 1:
                sums = [
                    sums[k] + sums[k + 1] if k + 1 < len(sums) else sums[k]
                    for k in range(0, len(sums), 2)
                ]
            total.append(sums[0])
        return total

    def ahead(d, state):
        rows = spread_rows(state)
        fresh = apply(d, 0, rows)
        both = apply(d, 4, rows)
        for half in range(2):
            states[d, half] = state[half]
            kq[d, half] = both[half] + piece(d, 14 + half)
        return tuple(fresh[half] + piece(d, 12 + half) for half in range(2))

    lax.fori_loop(0, n, ahead, (zero, zero))

    def back(e, state):
        d = n - 1 - e
        fresh = apply(d, 8, spread_rows(state))
        for half in range(2):
            states[d, 2 + half] = state[half]
        return tuple(fresh[half] + kq[d, half] for half in range(2))

    lax.fori_loop(0, n, back, (zero, zero))
    block = lanes_of(cells) // (GROUPS * width)

    def pack(d, carry):
        for page in range(out.shape[1]):
            total = zero
            for r in range(4):
                if GROUPS * r // n == page:
                    here = block == GROUPS * r % n // GROUPS
                    total = jnp.where(here, states[d, r], total)
            out[d, page] = total
        return carry

    lax.fori_loop(0, n, pack, 0)


def sweep_kernel(
    n,
    states,
    source,
    mlow,
    mupp,
    last,
    lcols,
    ucols,
    counts,
    low_h,
    side_h,
    zout,
    wout,
    edge,
    low,
    side,
    ybuf,
    zbuf,
    stage,
    sems,
):
    total = low_h.shape[0]
    copies = [
        pltpu.make_async_copy(src, dst.at[pl.ds(0, total), :], sems.at[k])
        for k, (src, dst) in enumerate(((low_h, low), (side_h, side)))
    ]
    for copy in copies:
        copy.start()
    blocks, _, nrhs, cells = source.shape
    base = lax.axis_index("chain") * blocks
    width = cells // n
    zero = jnp.zeros((nrhs, cells), jnp.float32)
    items = []
    for r in range(states.shape[1]):
        items += block_transpose([states[k, r] for k in range(n)], width, cells)
    for e in range(4 * GROUPS):
        stage[pl.ds(8 * e, 8), :] = items[e]
    for q in range(STATE):
        m, v = q // VARS, q % VARS
        start = q // 8 * 64 + q % 8
        ybuf[REACH - 1 - m, v] = stage[pl.ds(start, 8, stride=8), :]
        zbuf[blocks + m, v] = stage[pl.ds(start + 128, 8, stride=8), :]
    empty = blocks + REACH
    for v in range(VARS):
        ybuf[empty, v] = zero
        zbuf[empty, v] = zero
        wout[empty, v] = zero
    lane = lanes_of(cells)

    def first(b, carry):
        nears = [read_groups(ybuf, s) for s in slots(lcols, counts, 0, b, REACH - base, empty)]
        acc = couple(mlow, b, nears)
        for i in range(VARS):
            ybuf[b + REACH, i] = source[b, i] - acc[i][0]
        return carry

    steps(blocks, 4, first)

    def second(e, edges):
        c = blocks - 1 - e
        nears = [read_groups(zbuf, s) for s in slots(ucols, counts, 1, c, -base, empty)]
        acc = couple(mupp, c, nears)
        edges = list(edges)
        for i in range(VARS):
            w = acc[i][0]
            z = ybuf[c + REACH, i] - w
            zbuf[c, i] = z
            zout[c, i] = z
            wout[c + REACH, i] = w
            here = (lane == 2 * c) | (lane == (2 * c + cells - 1) % cells)
            edges[i] = jnp.where(here, pltpu.roll(z, 2 * c, 1), edges[i])
        return tuple(edges)

    edges = steps(blocks, 4, second, (zero,) * VARS)
    for v in range(VARS):
        edge[v] = edges[v]
    window = [read_block(zbuf, d) for d in range(REACH)]
    for m in reversed(range(REACH)):
        fresh = []
        for i in range(VARS):
            parts = []
            for d in range(REACH):
                place = (m * VARS + i) * VARS * REACH + d
                parts.append(
                    mul_rows([spread(last, (), place + REACH * j) for j in range(VARS)], window[d])
                )
            w = parts[0] + parts[1] + parts[2]
            wout[m, i] = w
            fresh.append(ybuf[m, i] - w)
        window = [fresh] + window[:-1]
    for copy in copies:
        copy.wait()


def inner_kernel(z, w, low, side, lcols, counts, resid, coef, correction, sem):
    store = pltpu.make_async_copy(z, correction, sem)
    store.start()
    blocks, _, nrhs, cells = z.shape
    base = lax.axis_index("chain") * blocks
    lane = lanes_of(cells)
    pages = coef.shape[0]
    size = VARS * VARS * SLOTS
    row = lax.broadcasted_iota(jnp.int32, (8, cells), 0)

    def block(b, found):
        nears = [
            read_block(w, s) for s in slots(lcols, counts, 0, b, REACH - base, blocks + REACH)
        ]
        acc = apply_coef(low, b, nears)
        left, right = [], []
        for v in range(VARS):
            here = z[b, v]
            left.append(jnp.where(lane == 0, 0.0, pltpu.roll(here, 1, 1)))
            right.append(jnp.where(lane == cells - 1, 0.0, pltpu.roll(here, cells - 1, 1)))
        beside = apply_coef(side, b, [left, right])
        for i in range(VARS):
            resid[b, i] = acc[i] - beside[i]
        here = (lane + row % 2) % cells == 2 * b
        return tuple(
            jnp.where(here, pltpu.roll(side[pl.ds(b * size + 8 * r, 8), :], 2 * b, 1), found[r])
            for r in range(pages)
        )

    found = steps(blocks, 4, block, (jnp.zeros((8, cells), jnp.float32),) * pages)
    for r in range(pages):
        coef[r] = found[r]
    store.wait()


def outer_kernel(inner, coef, swap_a, swap_b, resid, squares, cbuf):
    blocks, _, nrhs, cells = inner.shape
    odd = lax.axis_index("sub") % 2 == 1
    lane = lanes_of(cells)
    zero = jnp.zeros((nrhs, cells), jnp.float32)
    near = []
    for v in range(VARS):
        west = pltpu.roll(jnp.where(odd, swap_a[v], swap_b[v]), 1, 1)
        east = pltpu.roll(jnp.where(odd, swap_b[v], swap_a[v]), cells - 1, 1)
        near.append(jnp.where(lane % 2 == 0, west, east))
    for i in range(VARS):
        rows = []
        for j in range(VARS):
            k = (i * VARS + j) * SLOTS
            rows.append(coef[k // 8, pl.ds(k % 8, 1), :] + coef[(k + 1) // 8, pl.ds((k + 1) % 8, 1), :])
        cbuf[i] = mul_rows(rows, near)
    ends = (lane == 0) | (lane == cells - 1)

    def add(b, total):
        for i in range(VARS):
            other = pltpu.roll(cbuf[i], (cells - 2 * b) % cells, 1)
            value = inner[b, i] - jnp.where(ends, other, 0.0)
            resid[b, i] = value
            total = total + value * value
        return total

    total = steps(blocks, 4, add, zero)
    sums = jnp.broadcast_to(jnp.sum(total, axis=1, keepdims=True), total.shape)
    row = lax.broadcasted_iota(jnp.int32, total.shape, 0)
    line = jnp.sum(jnp.where(lane == row, sums, 0.0), axis=0, keepdims=True)
    for p in range(squares.shape[0]):
        squares[p] = line


def scale_kernel(entries, resid, squares, out):
    blocks, _, nrhs, cells = resid.shape
    line = squares[0]
    for p in range(1, squares.shape[0]):
        line = line + squares[p]
    lane = lanes_of(cells)
    row = lax.broadcasted_iota(jnp.int32, (nrhs, cells), 0)
    line = jnp.where(lane == row, jnp.broadcast_to(line, (nrhs, cells)), 0.0)
    msq = jnp.sum(line, axis=1, keepdims=True) / entries
    factor = jnp.broadcast_to(lax.rsqrt(msq + 1e-06), (nrhs, cells))

    def block(b, carry):
        for v in range(VARS):
            out[b, v] = resid[b, v] * factor
        return carry

    steps(blocks, 4, block)


def call(kernel, outs, args, places, scratch):
    args = [
        pltpu.with_memory_space_constraint(a, p) if p is HBM else a for a, p in zip(args, places)
    ]
    return pl.pallas_call(
        kernel,
        out_shape=[jax.ShapeDtypeStruct(o[0], (o + (jnp.float32,))[2]) for o in outs],
        in_specs=[pl.BlockSpec(memory_space=p) for p in places],
        out_specs=[pl.BlockSpec(memory_space=p) for p in (o[1] for o in outs)],
        scratch_shapes=[VMEM(s, jnp.float32) if isinstance(s, tuple) else s for s in scratch],
        compiler_params=pltpu.CompilerParams(vmem_limit_bytes=VMEM_LIMIT),
    )(*args)


def shards(
    rhs, diag_block, diag_inverse, lower_coef, upper_coef, side_coef, lower_cols, upper_cols, counts
):
    blocks, nvars, nrhs, cells = rhs.shape
    n = lax.axis_size("chain")
    inv = jnp.transpose(diag_inverse, (1, 2, 0, 3))
    low, upp, side = (
        jnp.transpose(a, (0, 2, 3, 1, 4)).reshape(-1, cells)
        for a in (lower_coef, upper_coef, side_coef)
    )
    lcols, ucols, used = lower_cols.T, upper_cols.T, counts.T
    m = lax.axis_size("sub")
    rows = blocks + REACH + 1
    parts = 16 * GROUPS // n
    back = -(-4 * GROUPS // n)
    tile = (nrhs, cells)

    mats = (VARS, VARS, SLOTS, blocks + PAD, cells)
    padded = (low.shape[0] + PAD, cells)

    count = REACH * REACH * VARS * VARS
    ints = (lcols.shape, VMEM, jnp.int32)
    own, inv, mlow, mupp, last, lcols, ucols, used = call(
        prepare_kernel,
        [
            (rhs.shape, VMEM),
            ((VARS, VARS, blocks + PAD, cells), VMEM),
            (mats, VMEM),
            (mats, VMEM),
            ((-(-count // 8) * 8 + PAD, cells), VMEM),
            ints,
            ints,
            ints,
        ],
        (rhs, inv, low, upp, lcols, ucols, used),
        (HBM,) * 7,
        [low.shape, upp.shape]
        + [pltpu.SMEM(lcols.shape, jnp.int32)] * 2
        + [pltpu.SemaphoreType.DMA((9,))],
    )
    last = lax.ppermute(last, "chain", [(i, i + 1) for i in range(n - 1)])
    maps, source = call(
        functools.partial(local_kernel, n),
        [((n, parts) + tile, VMEM), (rhs.shape, VMEM)],
        (own, inv, mlow, mupp, lcols, ucols, used),
        (VMEM,) * 4 + (SMEM,) * 3,
        [(rows, VARS, nrhs + WIDE, cells), (rows, VARS, nrhs + 2 * WIDE, cells)]
        + [(WIDE * SPACE, cells)],
    )
    maps = lax.all_to_all(maps, "chain", 0, 0, tiled=True)
    (states,) = call(
        functools.partial(solve_kernel, n),
        [((n, back) + tile, VMEM)],
        (maps,),
        (VMEM,),
        [(n, 2) + tile, (n, 4) + tile],
    )
    states = lax.all_to_all(states, "chain", 0, 0, tiled=True)
    z, w, edge, low, side = call(
        functools.partial(sweep_kernel, n),
        [
            (rhs.shape, VMEM),
            ((rows, VARS) + tile, VMEM),
            ((VARS,) + tile, VMEM),
            (padded, VMEM),
            (padded, VMEM),
        ],
        (states, source, mlow, mupp, last, lcols, ucols, used, low, side),
        (VMEM,) * 5 + (SMEM,) * 3 + (HBM,) * 2,
        [(rows, VARS) + tile] * 2 + [(4 * GROUPS * 8, cells), pltpu.SemaphoreType.DMA((2,))],
    )
    swap_a, swap_b = (
        lax.ppermute(
            edge, "sub", [p for i in range(first, m - 1, 2) for p in ((i, i + 1), (i + 1, i))]
        )
        for first in (0, 1)
    )
    inner, coef, correction = call(
        inner_kernel,
        [
            (rhs.shape, VMEM),
            ((-(-VARS * VARS * SLOTS // 8),) + (8, cells), VMEM),
            (rhs.shape, HBM),
        ],
        (z, w, low, side, lcols, used),
        (VMEM,) * 4 + (SMEM,) * 2,
        [pltpu.SemaphoreType.DMA],
    )
    resid, squares = call(
        outer_kernel,
        [(rhs.shape, VMEM), ((n * m, 1, cells), VMEM)],
        (inner, coef, swap_a, swap_b),
        (VMEM,) * 4,
        [(VARS,) + tile],
    )
    squares = lax.all_to_all(squares, ("chain", "sub"), 0, 0, tiled=True)
    entries = blocks * VARS * cells * n * m
    (residual_unit,) = call(
        functools.partial(scale_kernel, entries),
        [(rhs.shape, VMEM)],
        (resid, squares),
        (VMEM, VMEM),
        [],
    )
    return (correction, residual_unit)


def solution(mesh):
    in_specs = (
        P("chain", None, None, "sub"),
        P("chain", None, None, "sub"),
        P("chain", None, None, "sub"),
        P("chain", None, None, None, "sub"),
        P("chain", None, None, None, "sub"),
        P("chain", None, None, None, "sub"),
        P("chain", None),
        P("chain", None),
        P("chain", None),
    )
    out_specs = (P("chain", None, None, "sub"), P("chain", None, None, "sub"))
    return jax.shard_map(shards, mesh=mesh, in_specs=in_specs, out_specs=out_specs, check_vma=False)
```

```python
import functools

import jax
import jax.numpy as jnp
from jax import lax
from jax.experimental import pallas as pl
from jax.experimental.pallas import tpu as pltpu
from jax.sharding import PartitionSpec as P

VARS = 5
REACH = 3
SLOTS = 2
STATE = REACH * VARS
WIDE = 16
PAD = 8
SPACE = 72
GROUPS = 8
VMEM_LIMIT = 40 * 1024 * 1024

VMEM = pltpu.VMEM
SMEM = pltpu.SMEM
HBM = pltpu.HBM


def lanes_of(cells):
    return lax.broadcasted_iota(jnp.int32, (8, cells), 1)


def block_transpose(items, width, cells):
    count = len(items)
    lane = lanes_of(cells)
    half = 1
    while half < count:
        bit = (lane // (half * width)) % 2 == 1
        out = list(items)
        for a in range(count):
            if a & half:
                continue
            b = a + half
            out[a] = jnp.where(bit, pltpu.roll(items[b], half * width, 1), items[a])
            out[b] = jnp.where(bit, items[b], pltpu.roll(items[a], cells - half * width, 1))
        items = out
        half *= 2
    return items


def spread(ref, place, row):
    return ref[place + (pl.ds(row, 8, stride=0), slice(None))]


def mul_rows(rows, near):
    total = rows[0] * near[0]
    for j in range(1, len(near)):
        total = total + rows[j] * near[j]
    return total


def mul_groups(rows, nears):
    return [mul_rows(rows, [near[g] for near in nears]) for g in range(len(nears[0]))]


def couple(mats, b, nears):
    out = []
    for i in range(VARS):
        parts = [
            mul_groups([spread(mats, (i, j, k), b) for j in range(VARS)], nears[k])
            for k in range(SLOTS)
        ]
        out.append([x + y for x, y in zip(*parts)])
    return out


def apply_coef(coef, b, nears):
    out = []
    for i in range(VARS):
        parts = []
        for k in range(SLOTS):
            place = (b * VARS + i) * VARS * SLOTS + k
            parts.append(
                mul_rows([spread(coef, (), place + SLOTS * j) for j in range(VARS)], nears[k])
            )
        out.append(parts[0] + parts[1])
    return out


def products(inv, coef, out):
    blocks = out.shape[3] - PAD
    stride = VARS * VARS * SLOTS

    def some(o, carry):
        start = o * 8
        left = [[inv[i, m, pl.ds(start, 8), :] for m in range(VARS)] for i in range(VARS)]
        for k in range(SLOTS):
            for j in range(VARS):
                place = start * stride + j * SLOTS + k
                right = [
                    coef[pl.ds(place + m * VARS * SLOTS, 8, stride=stride), :] for m in range(VARS)
                ]
                for i in range(VARS):
                    out[i, j, k, pl.ds(start, 8), :] = mul_rows(left[i], right)
        return carry

    lax.fori_loop(0, blocks // 8, some, 0)


def slots(cols, counts, side, b, shift, empty):
    return [jnp.where(k < counts[side, b], cols[k, b] + shift, empty) for k in range(SLOTS)]


def read_block(buf, place):
    return [buf[place, v] for v in range(VARS)]


def read_groups(buf, place):
    count = buf.shape[2] // 8
    return [[buf[place, v, pl.ds(8 * g, 8), :] for g in range(count)] for v in range(VARS)]


def steps(count, most, body, carry=0):
    unroll = max(u for u in range(1, most + 1) if count % u == 0)

    def chunk(o, carry):
        for u in range(unroll):
            carry = body(o * unroll + u, carry)
        return carry

    return lax.fori_loop(0, count // unroll, chunk, carry)


def prepare_kernel(
    rhs_h,
    inv_h,
    low_h,
    upp_h,
    lcols_h,
    ucols_h,
    counts_h,
    rhs,
    inv,
    mlow,
    mupp,
    last,
    lcols_v,
    ucols_v,
    counts_v,
    low,
    upp,
    ucols,
    counts,
    sems,
):
    blocks = rhs.shape[0]
    pairs = (
        (inv_h, inv.at[:, :, pl.ds(0, blocks), :]),
        (upp_h, upp),
        (ucols_h, ucols),
        (counts_h, counts),
        (low_h, low),
        (rhs_h, rhs),
        (lcols_h, lcols_v),
        (ucols_h, ucols_v),
        (counts_h, counts_v),
    )
    copies = [pltpu.make_async_copy(src, dst, sems.at[k]) for k, (src, dst) in enumerate(pairs)]
    for copy in copies:
        copy.start()
    base = lax.axis_index("chain") * blocks
    for copy in copies[:4]:
        copy.wait()
    products(inv, upp, mupp)
    for m in range(REACH):
        b = blocks - REACH + m
        offs = [ucols[k, b] - base - b for k in range(SLOTS)]
        for i in range(VARS):
            for j in range(VARS):
                rows = [mupp[i, j, k, pl.ds(b, 1), :] for k in range(SLOTS)]
                for d in range(REACH):
                    total = jnp.zeros_like(rows[0])
                    for k in range(SLOTS):
                        hit = (offs[k] == d + 1) & (k < counts[1, b])
                        total = jnp.where(hit, rows[k], total)
                    last[pl.ds(((m * VARS + i) * VARS + j) * REACH + d, 1), :] = total
    copies[4].wait()
    products(inv, low, mlow)
    for copy in copies[5:]:
        copy.wait()


def forward_kernel(rhs, inv, mlow, lcols, counts, source, ybuf):
    blocks, _, nrhs, cells = rhs.shape
    base = lax.axis_index("chain") * blocks
    wide_y = nrhs + WIDE
    row_y = lax.broadcasted_iota(jnp.int32, (wide_y, cells), 0)
    empty = blocks + REACH
    for v in range(VARS):
        for m in range(REACH):
            ybuf[REACH - 1 - m, v] = (row_y == nrhs + VARS * m + v).astype(jnp.float32)
        ybuf[empty, v] = jnp.zeros((wide_y, cells), jnp.float32)

    def first(b, carry):
        nears = [read_groups(ybuf, s) for s in slots(lcols, counts, 0, b, REACH - base, empty)]
        acc = couple(mlow, b, nears)
        right = [rhs[b, i] for i in range(VARS)]
        for i in range(VARS):
            own = mul_rows([spread(inv, (i, j), b) for j in range(VARS)], right)
            source[b, i] = own
            ybuf[b + REACH, i, 0:8] = own - acc[i][0]
            for g in range(1, len(acc[i])):
                ybuf[b + REACH, i, 8 * g : 8 * g + 8] = -acc[i][g]
        return carry

    steps(blocks, 2, first)


def column_order(nrhs):
    wide_y = nrhs + WIDE
    order = []
    for first, count in ((nrhs, STATE), (wide_y + nrhs, STATE - 1), (wide_y + nrhs + WIDE, STATE)):
        order += [(half, first + j) for half in range(2) for j in range(count)]
    for first in (0, wide_y):
        order += [(half, first + q) for half in range(2) for q in range(nrhs)]
    return order


def backward_kernel(n, ybuf, mupp, last, ucols, counts, out, zbuf, stage):
    blocks, nrhs, cells = ybuf.shape[0] - REACH - 1, ybuf.shape[2] - WIDE, ybuf.shape[3]
    base = lax.axis_index("chain") * blocks
    wide_y, wide_z = zbuf.shape[2] - WIDE, zbuf.shape[2]
    row_z = lax.broadcasted_iota(jnp.int32, (wide_z, cells), 0)
    empty = blocks + REACH
    for v in range(VARS):
        for m in range(REACH):
            zbuf[blocks + m, v] = (row_z == wide_y + VARS * m + v).astype(jnp.float32)
        zbuf[empty, v] = jnp.zeros((wide_z, cells), jnp.float32)

    def second(e, carry):
        c = blocks - 1 - e
        nears = [read_groups(zbuf, s) for s in slots(ucols, counts, 1, c, -base, empty)]
        acc = couple(mupp, c, nears)
        for i in range(VARS):
            for g in range(len(acc[i])):
                if g < wide_y // 8:
                    value = ybuf[c + REACH, i, 8 * g : 8 * g + 8] - acc[i][g]
                else:
                    value = -acc[i][g]
                zbuf[c, i, 8 * g : 8 * g + 8] = value
        return carry

    steps(blocks, 2, second)

    zero = jnp.zeros((8, cells), jnp.float32)
    for i in range(WIDE):
        m, v = i // VARS, i % VARS
        for g in range((wide_y + wide_z) // 8):
            if i == STATE:
                value = zero
            elif g < wide_y // 8:
                value = ybuf[blocks + REACH - 1 - m, v, 8 * g : 8 * g + 8]
            else:
                value = zbuf[m, v, 8 * g - wide_y : 8 * g - wide_y + 8]
            stage[pl.ds(i * SPACE + 8 * g, 8), :] = value

    def column(half, index):
        return stage[pl.ds(half * 8 * SPACE + index, 8, stride=SPACE), :]

    for half in range(2):
        place = STATE * SPACE + nrhs + 8 * half
        stage[pl.ds(place, 8), :] = column(half, wide_y + nrhs + STATE - 1)
    order = column_order(nrhs)
    width = cells // n
    for page in range(out.shape[1]):
        items = [column(*at) for at in order[page * n : (page + 1) * n]]
        items += [zero] * (n - len(items))
        for k, item in enumerate(block_transpose(items, width, cells)):
            out[k, page] = item


def split(value, period, stop, width, cells):
    items = [value]
    lane = lanes_of(cells)
    while period > stop:
        half = period // 2 * width
        bit = lane // half % 2 == 1
        fresh = []
        for item in items:
            other = pltpu.roll(item, half, 1)
            fresh += [jnp.where(bit, other, item), jnp.where(bit, item, other)]
        items = fresh
        period //= 2
    return items


def solve_kernel(n, x, out, cols, sides, kq, states):
    cells = x.shape[3]
    width = cells // n
    zero = jnp.zeros((8, cells), jnp.float32)
    count = 6 * STATE - 2

    def unpack(d, carry):
        for page in range(x.shape[1]):
            for k, block in enumerate(split(x[d, page], n, GROUPS, width, cells)):
                e = page * n + k * GROUPS
                if e < count:
                    for g, value in enumerate(split(block, GROUPS, 1, width, cells)):
                        cols[pl.ds((d * count + e + g) * 8, 8), :] = value
                elif e < count + 4 * GROUPS:
                    sides[d, (e - count) // GROUPS] = block
        return carry

    steps(n, 2, unpack)

    def column(d, e):
        return cols[pl.ds((d * count + e) * 8, 8), :]

    def total_of(terms):
        while len(terms) > 1:
            pairs = [terms[k] + terms[k + 1] for k in range(0, len(terms) - 1, 2)]
            terms = pairs + terms[len(terms) - len(terms) % 2 :]
        return terms[0]

    def rows_of(place):
        return [spread(states, (), place * 8 + j) for j in range(STATE)]

    def ahead(d, state):
        for half in range(2):
            states[pl.ds((d * 4 + half) * 8, 8), :] = state[half]
        rows = rows_of(d * 4)
        fresh = []
        for half in range(2):
            terms = [column(d, half * STATE + j) * rows[j] for j in range(STATE)]
            fresh.append(total_of(terms) + sides[d, half])
            first = 2 * STATE + half * (STATE - 1)
            terms = [column(d, first + j) * rows[j] for j in range(STATE - 1)]
            start = (d * count + STATE + 8 * half) * 8 + 7
            terms.append(cols[pl.ds(start, 8, stride=8), :] * rows[STATE - 1])
            kq[d, half] = total_of(terms) + sides[d, 2 + half]
        return tuple(fresh)

    steps(n, 4, ahead, (zero, zero))

    def back(e, state):
        d = n - 1 - e
        for half in range(2):
            states[pl.ds((d * 4 + 2 + half) * 8, 8), :] = state[half]
        rows = rows_of(d * 4 + 2)
        fresh = []
        for half in range(2):
            first = 4 * STATE - 2 + half * STATE
            terms = [column(d, first + j) * rows[j] for j in range(STATE)]
            fresh.append(total_of(terms) + kq[d, half])
        return tuple(fresh)

    steps(n, 4, back, (zero, zero))
    block = lanes_of(cells) // (GROUPS * width)

    def pack(d, carry):
        for page in range(out.shape[1]):
            total = zero
            for r in range(4):
                if GROUPS * r // n == page:
                    here = block == GROUPS * r % n // GROUPS
                    total = jnp.where(here, states[pl.ds((d * 4 + r) * 8, 8), :], total)
            out[d, page] = total
        return carry

    steps(n, 4, pack)


def sweep_kernel(
    n,
    states,
    source,
    mlow,
    mupp,
    last,
    lcols,
    ucols,
    counts,
    low_h,
    side_h,
    zout,
    wout,
    edge,
    low,
    side,
    ybuf,
    zbuf,
    stage,
    sems,
):
    total = low_h.shape[0]
    copies = [
        pltpu.make_async_copy(src, dst.at[pl.ds(0, total), :], sems.at[k])
        for k, (src, dst) in enumerate(((low_h, low), (side_h, side)))
    ]
    for copy in copies:
        copy.start()
    blocks, _, nrhs, cells = source.shape
    base = lax.axis_index("chain") * blocks
    width = cells // n
    zero = jnp.zeros((nrhs, cells), jnp.float32)
    items = []
    for r in range(states.shape[1]):
        items += block_transpose([states[k, r] for k in range(n)], width, cells)
    for e in range(4 * GROUPS):
        stage[pl.ds(8 * e, 8), :] = items[e]
    for q in range(STATE):
        m, v = q // VARS, q % VARS
        start = q // 8 * 64 + q % 8
        ybuf[REACH - 1 - m, v] = stage[pl.ds(start, 8, stride=8), :]
        zbuf[blocks + m, v] = stage[pl.ds(start + 128, 8, stride=8), :]
    empty = blocks + REACH
    for v in range(VARS):
        ybuf[empty, v] = zero
        zbuf[empty, v] = zero
        wout[empty, v] = zero
    lane = lanes_of(cells)

    def first(b, carry):
        nears = [read_groups(ybuf, s) for s in slots(lcols, counts, 0, b, REACH - base, empty)]
        acc = couple(mlow, b, nears)
        for i in range(VARS):
            ybuf[b + REACH, i] = source[b, i] - acc[i][0]
        return carry

    steps(blocks, 4, first)

    def second(e, edges):
        c = blocks - 1 - e
        nears = [read_groups(zbuf, s) for s in slots(ucols, counts, 1, c, -base, empty)]
        acc = couple(mupp, c, nears)
        edges = list(edges)
        for i in range(VARS):
            w = acc[i][0]
            z = ybuf[c + REACH, i] - w
            zbuf[c, i] = z
            zout[c, i] = z
            wout[c + REACH, i] = w
            here = (lane == 2 * c) | (lane == (2 * c + cells - 1) % cells)
            edges[i] = jnp.where(here, pltpu.roll(z, 2 * c, 1), edges[i])
        return tuple(edges)

    edges = steps(blocks, 4, second, (zero,) * VARS)
    for v in range(VARS):
        edge[v] = edges[v]
    window = [read_block(zbuf, d) for d in range(REACH)]
    for m in reversed(range(REACH)):
        fresh = []
        for i in range(VARS):
            parts = []
            for d in range(REACH):
                place = (m * VARS + i) * VARS * REACH + d
                parts.append(
                    mul_rows([spread(last, (), place + REACH * j) for j in range(VARS)], window[d])
                )
            w = parts[0] + parts[1] + parts[2]
            wout[m, i] = w
            fresh.append(ybuf[m, i] - w)
        window = [fresh] + window[:-1]
    for copy in copies:
        copy.wait()


def inner_kernel(z, w, low, side, lcols, counts, resid, coef, correction, sem):
    store = pltpu.make_async_copy(z, correction, sem)
    store.start()
    blocks, _, nrhs, cells = z.shape
    base = lax.axis_index("chain") * blocks
    lane = lanes_of(cells)
    pages = coef.shape[0]
    size = VARS * VARS * SLOTS
    row = lax.broadcasted_iota(jnp.int32, (8, cells), 0)

    def block(b, found):
        nears = [
            read_block(w, s) for s in slots(lcols, counts, 0, b, REACH - base, blocks + REACH)
        ]
        acc = apply_coef(low, b, nears)
        left, right = [], []
        for v in range(VARS):
            here = z[b, v]
            left.append(jnp.where(lane == 0, 0.0, pltpu.roll(here, 1, 1)))
            right.append(jnp.where(lane == cells - 1, 0.0, pltpu.roll(here, cells - 1, 1)))
        beside = apply_coef(side, b, [left, right])
        for i in range(VARS):
            resid[b, i] = acc[i] - beside[i]
        here = (lane + row % 2) % cells == 2 * b
        return tuple(
            jnp.where(here, pltpu.roll(side[pl.ds(b * size + 8 * r, 8), :], 2 * b, 1), found[r])
            for r in range(pages)
        )

    found = steps(blocks, 4, block, (jnp.zeros((8, cells), jnp.float32),) * pages)
    for r in range(pages):
        coef[r] = found[r]
    store.wait()


def outer_kernel(inner, coef, swap_a, swap_b, resid, squares, cbuf):
    blocks, _, nrhs, cells = inner.shape
    odd = lax.axis_index("sub") % 2 == 1
    lane = lanes_of(cells)
    zero = jnp.zeros((nrhs, cells), jnp.float32)
    near = []
    for v in range(VARS):
        west = pltpu.roll(jnp.where(odd, swap_a[v], swap_b[v]), 1, 1)
        east = pltpu.roll(jnp.where(odd, swap_b[v], swap_a[v]), cells - 1, 1)
        near.append(jnp.where(lane % 2 == 0, west, east))
    for i in range(VARS):
        rows = []
        for j in range(VARS):
            k = (i * VARS + j) * SLOTS
            rows.append(coef[k // 8, pl.ds(k % 8, 1), :] + coef[(k + 1) // 8, pl.ds((k + 1) % 8, 1), :])
        cbuf[i] = mul_rows(rows, near)
    ends = (lane == 0) | (lane == cells - 1)

    def add(b, total):
        for i in range(VARS):
            other = pltpu.roll(cbuf[i], (cells - 2 * b) % cells, 1)
            value = inner[b, i] - jnp.where(ends, other, 0.0)
            resid[b, i] = value
            total = total + value * value
        return total

    total = steps(blocks, 4, add, zero)
    sums = jnp.broadcast_to(jnp.sum(total, axis=1, keepdims=True), total.shape)
    row = lax.broadcasted_iota(jnp.int32, total.shape, 0)
    line = jnp.sum(jnp.where(lane == row, sums, 0.0), axis=0, keepdims=True)
    for p in range(squares.shape[0]):
        squares[p] = line


def scale_kernel(entries, resid, squares, out):
    blocks, _, nrhs, cells = resid.shape
    line = squares[0]
    for p in range(1, squares.shape[0]):
        line = line + squares[p]
    lane = lanes_of(cells)
    row = lax.broadcasted_iota(jnp.int32, (nrhs, cells), 0)
    line = jnp.where(lane == row, jnp.broadcast_to(line, (nrhs, cells)), 0.0)
    msq = jnp.sum(line, axis=1, keepdims=True) / entries
    factor = jnp.broadcast_to(lax.rsqrt(msq + 1e-06), (nrhs, cells))

    def block(b, carry):
        for v in range(VARS):
            out[b, v] = resid[b, v] * factor
        return carry

    steps(blocks, 4, block)


def call(kernel, outs, args, places, scratch):
    args = [
        pltpu.with_memory_space_constraint(a, p) if p is HBM else a for a, p in zip(args, places)
    ]
    return pl.pallas_call(
        kernel,
        out_shape=[jax.ShapeDtypeStruct(o[0], (o + (jnp.float32,))[2]) for o in outs],
        in_specs=[pl.BlockSpec(memory_space=p) for p in places],
        out_specs=[pl.BlockSpec(memory_space=p) for p in (o[1] for o in outs)],
        scratch_shapes=[VMEM(s, jnp.float32) if isinstance(s, tuple) else s for s in scratch],
        compiler_params=pltpu.CompilerParams(vmem_limit_bytes=VMEM_LIMIT),
    )(*args)


def shards(
    rhs, diag_block, diag_inverse, lower_coef, upper_coef, side_coef, lower_cols, upper_cols, counts
):
    blocks, nvars, nrhs, cells = rhs.shape
    n = lax.axis_size("chain")
    inv = jnp.transpose(diag_inverse, (1, 2, 0, 3))
    low, upp, side = (
        jnp.transpose(a, (0, 2, 3, 1, 4)).reshape(-1, cells)
        for a in (lower_coef, upper_coef, side_coef)
    )
    lcols, ucols, used = lower_cols.T, upper_cols.T, counts.T
    m = lax.axis_size("sub")
    rows = blocks + REACH + 1
    parts = -(-len(column_order(nrhs)) // n)
    back = -(-4 * GROUPS // n)
    tile = (nrhs, cells)

    mats = (VARS, VARS, SLOTS, blocks + PAD, cells)
    padded = (low.shape[0] + PAD, cells)

    count = REACH * REACH * VARS * VARS
    ints = (lcols.shape, VMEM, jnp.int32)
    own, inv, mlow, mupp, last, lcols, ucols, used = call(
        prepare_kernel,
        [
            (rhs.shape, VMEM),
            ((VARS, VARS, blocks + PAD, cells), VMEM),
            (mats, VMEM),
            (mats, VMEM),
            ((-(-count // 8) * 8 + PAD, cells), VMEM),
            ints,
            ints,
            ints,
        ],
        (rhs, inv, low, upp, lcols, ucols, used),
        (HBM,) * 7,
        [low.shape, upp.shape]
        + [pltpu.SMEM(lcols.shape, jnp.int32)] * 2
        + [pltpu.SemaphoreType.DMA((9,))],
    )
    last = lax.ppermute(last, "chain", [(i, i + 1) for i in range(n - 1)])
    source, ybuf = call(
        forward_kernel,
        [(rhs.shape, VMEM), ((rows, VARS, nrhs + WIDE, cells), VMEM)],
        (own, inv, mlow, lcols, used),
        (VMEM,) * 3 + (SMEM,) * 2,
        [],
    )
    (maps,) = call(
        functools.partial(backward_kernel, n),
        [((n, parts) + tile, VMEM)],
        (ybuf, mupp, last, ucols, used),
        (VMEM, VMEM, pl.ANY) + (SMEM,) * 2,
        [(rows, VARS, nrhs + 2 * WIDE, cells), (WIDE * SPACE, cells)],
    )
    maps = lax.all_to_all(maps, "chain", 0, 0, tiled=True)
    (states,) = call(
        functools.partial(solve_kernel, n),
        [((n, back) + tile, VMEM)],
        (maps,),
        (VMEM,),
        [(n * (6 * STATE - 2) * 8 + PAD, cells), (n, 4) + tile, (n, 2) + tile]
        + [(n * 4 * 8 + PAD, cells)],
    )
    states = lax.all_to_all(states, "chain", 0, 0, tiled=True)
    z, w, edge, low, side = call(
        functools.partial(sweep_kernel, n),
        [
            (rhs.shape, VMEM),
            ((rows, VARS) + tile, VMEM),
            ((VARS,) + tile, VMEM),
            (padded, VMEM),
            (padded, VMEM),
        ],
        (states, source, mlow, mupp, last, lcols, ucols, used, low, side),
        (VMEM,) * 5 + (SMEM,) * 3 + (HBM,) * 2,
        [(rows, VARS) + tile] * 2 + [(4 * GROUPS * 8, cells), pltpu.SemaphoreType.DMA((2,))],
    )
    swap_a, swap_b = (
        lax.ppermute(
            edge, "sub", [p for i in range(first, m - 1, 2) for p in ((i, i + 1), (i + 1, i))]
        )
        for first in (0, 1)
    )
    inner, coef, correction = call(
        inner_kernel,
        [
            (rhs.shape, VMEM),
            ((-(-VARS * VARS * SLOTS // 8),) + (8, cells), VMEM),
            (rhs.shape, HBM),
        ],
        (z, w, low, side, lcols, used),
        (VMEM,) * 4 + (SMEM,) * 2,
        [pltpu.SemaphoreType.DMA],
    )
    resid, squares = call(
        outer_kernel,
        [(rhs.shape, VMEM), ((n * m, 1, cells), VMEM)],
        (inner, coef, swap_a, swap_b),
        (VMEM,) * 4,
        [(VARS,) + tile],
    )
    squares = lax.all_to_all(squares, ("chain", "sub"), 0, 0, tiled=True)
    entries = blocks * VARS * cells * n * m
    (residual_unit,) = call(
        functools.partial(scale_kernel, entries),
        [(rhs.shape, VMEM)],
        (resid, squares),
        (VMEM, VMEM),
        [],
    )
    return (correction, residual_unit)


def solution(mesh):
    in_specs = (
        P("chain", None, None, "sub"),
        P("chain", None, None, "sub"),
        P("chain", None, None, "sub"),
        P("chain", None, None, None, "sub"),
        P("chain", None, None, None, "sub"),
        P("chain", None, None, None, "sub"),
        P("chain", None),
        P("chain", None),
        P("chain", None),
    )
    out_specs = (P("chain", None, None, "sub"), P("chain", None, None, "sub"))
    return jax.shard_map(shards, mesh=mesh, in_specs=in_specs, out_specs=out_specs, check_vma=False)
```

```python
import functools

import jax
import jax.numpy as jnp
from jax import lax
from jax.experimental import pallas as pl
from jax.experimental.pallas import tpu as pltpu
from jax.sharding import PartitionSpec as P

VARS = 5
REACH = 3
SLOTS = 2
STATE = REACH * VARS
WIDE = 16
PAD = 8
SPACE = 72
GROUPS = 8
VMEM_LIMIT = 40 * 1024 * 1024

VMEM = pltpu.VMEM
SMEM = pltpu.SMEM
HBM = pltpu.HBM


def lanes_of(cells):
    return lax.broadcasted_iota(jnp.int32, (8, cells), 1)


def block_transpose(items, width, cells):
    count = len(items)
    lane = lanes_of(cells)
    half = 1
    while half < count:
        bit = (lane // (half * width)) % 2 == 1
        out = list(items)
        for a in range(count):
            if a & half:
                continue
            b = a + half
            out[a] = jnp.where(bit, pltpu.roll(items[b], half * width, 1), items[a])
            out[b] = jnp.where(bit, items[b], pltpu.roll(items[a], cells - half * width, 1))
        items = out
        half *= 2
    return items


def spread(ref, place, row):
    return ref[place + (pl.ds(row, 8, stride=0), slice(None))]


def mul_rows(rows, near):
    total = rows[0] * near[0]
    for j in range(1, len(near)):
        total = total + rows[j] * near[j]
    return total


def mul_groups(rows, nears):
    return [mul_rows(rows, [near[g] for near in nears]) for g in range(len(nears[0]))]


def couple(mats, b, nears):
    out = []
    for i in range(VARS):
        parts = [
            mul_groups([spread(mats, (i, j, k), b) for j in range(VARS)], nears[k])
            for k in range(SLOTS)
        ]
        out.append([x + y for x, y in zip(*parts)])
    return out


def apply_coef(coef, b, nears):
    out = []
    for i in range(VARS):
        parts = []
        for k in range(SLOTS):
            place = (b * VARS + i) * VARS * SLOTS + k
            parts.append(
                mul_rows([spread(coef, (), place + SLOTS * j) for j in range(VARS)], nears[k])
            )
        out.append(parts[0] + parts[1])
    return out


def products(inv, coef, out):
    blocks = out.shape[3] - PAD
    stride = VARS * VARS * SLOTS

    def some(o, carry):
        start = o * 8
        left = [[inv[i, m, pl.ds(start, 8), :] for m in range(VARS)] for i in range(VARS)]
        for k in range(SLOTS):
            for j in range(VARS):
                place = start * stride + j * SLOTS + k
                right = [
                    coef[pl.ds(place + m * VARS * SLOTS, 8, stride=stride), :] for m in range(VARS)
                ]
                for i in range(VARS):
                    out[i, j, k, pl.ds(start, 8), :] = mul_rows(left[i], right)
        return carry

    lax.fori_loop(0, blocks // 8, some, 0)


def slots(cols, counts, side, b, shift, empty):
    return [jnp.where(k < counts[side, b], cols[k, b] + shift, empty) for k in range(SLOTS)]


def read_block(buf, place):
    return [buf[place, v] for v in range(VARS)]


def read_groups(buf, place):
    count = buf.shape[2] // 8
    return [[buf[place, v, pl.ds(8 * g, 8), :] for g in range(count)] for v in range(VARS)]


def steps(count, most, body, carry=0):
    unroll = max(u for u in range(1, most + 1) if count % u == 0)

    def chunk(o, carry):
        for u in range(unroll):
            carry = body(o * unroll + u, carry)
        return carry

    return lax.fori_loop(0, count // unroll, chunk, carry)


def column_order(nrhs):
    wide_y = nrhs + WIDE
    order = []
    for first, count in ((nrhs, STATE), (wide_y + nrhs, STATE - 1), (wide_y + nrhs + WIDE, STATE)):
        order += [(half, first + j) for half in range(2) for j in range(count)]
    for first in (0, wide_y):
        order += [(half, first + q) for half in range(2) for q in range(nrhs)]
    return order


def local_kernel(
    n,
    rhs_h,
    inv_h,
    low_h,
    upp_h,
    lcols_h,
    ucols_h,
    counts_h,
    out,
    source,
    mlow,
    mupp,
    lcols_v,
    ucols_v,
    counts_v,
    rhs,
    inv,
    low,
    upp,
    lcols,
    ucols,
    counts,
    ybuf,
    zbuf,
    stage,
    sems,
):
    copies = [
        pltpu.make_async_copy(src, dst, sems.at[k])
        for k, (src, dst) in enumerate(
            (
                (inv_h, inv.at[:, :, pl.ds(0, rhs.shape[0]), :]),
                (low_h, low),
                (lcols_h, lcols),
                (counts_h, counts),
                (ucols_h, ucols),
                (rhs_h, rhs),
                (upp_h, upp),
                (lcols_h, lcols_v),
                (ucols_h, ucols_v),
                (counts_h, counts_v),
            )
        )
    ]
    for copy in copies:
        copy.start()
    blocks, _, nrhs, cells = rhs.shape
    base = lax.axis_index("chain") * blocks
    wide_y = nrhs + WIDE
    wide_z = wide_y + WIDE
    row_y = lax.broadcasted_iota(jnp.int32, (wide_y, cells), 0)
    row_z = lax.broadcasted_iota(jnp.int32, (wide_z, cells), 0)
    for m in range(REACH):
        for v in range(VARS):
            q = VARS * m + v
            ybuf[REACH - 1 - m, v] = (row_y == nrhs + q).astype(jnp.float32)
            zbuf[blocks + m, v] = (row_z == wide_y + q).astype(jnp.float32)
    for v in range(VARS):
        ybuf[blocks + REACH, v] = jnp.zeros((wide_y, cells), jnp.float32)
        zbuf[blocks + REACH, v] = jnp.zeros((wide_z, cells), jnp.float32)
    empty = blocks + REACH
    copies[0].wait()
    copies[1].wait()
    products(inv, low, mlow)
    for copy in copies[2:6]:
        copy.wait()

    def first(b, carry):
        nears = [read_groups(ybuf, s) for s in slots(lcols, counts, 0, b, REACH - base, empty)]
        acc = couple(mlow, b, nears)
        right = [rhs[b, i] for i in range(VARS)]
        for i in range(VARS):
            own = mul_rows([spread(inv, (i, j), b) for j in range(VARS)], right)
            source[b, i] = own
            ybuf[b + REACH, i, 0:8] = own - acc[i][0]
            for g in range(1, len(acc[i])):
                ybuf[b + REACH, i, 8 * g : 8 * g + 8] = -acc[i][g]
        return carry

    steps(blocks, 2, first)
    for copy in copies[6:]:
        copy.wait()
    products(inv, upp, mupp)

    def second(e, carry):
        c = blocks - 1 - e
        nears = [read_groups(zbuf, s) for s in slots(ucols, counts, 1, c, -base, empty)]
        acc = couple(mupp, c, nears)
        for i in range(VARS):
            for g in range(len(acc[i])):
                if g < wide_y // 8:
                    value = ybuf[c + REACH, i, 8 * g : 8 * g + 8] - acc[i][g]
                else:
                    value = -acc[i][g]
                zbuf[c, i, 8 * g : 8 * g + 8] = value
        return carry

    steps(blocks, 2, second)

    zero = jnp.zeros((8, cells), jnp.float32)
    for i in range(WIDE):
        m, v = i // VARS, i % VARS
        for g in range((wide_y + wide_z) // 8):
            if i == STATE:
                value = zero
            elif g < wide_y // 8:
                value = ybuf[blocks + REACH - 1 - m, v, 8 * g : 8 * g + 8]
            else:
                value = zbuf[m, v, 8 * g - wide_y : 8 * g - wide_y + 8]
            stage[pl.ds(i * SPACE + 8 * g, 8), :] = value

    def column(half, index):
        return stage[pl.ds(half * 8 * SPACE + index, 8, stride=SPACE), :]

    for half in range(2):
        place = STATE * SPACE + nrhs + 8 * half
        stage[pl.ds(place, 8), :] = column(half, wide_y + nrhs + STATE - 1)
    order = column_order(nrhs)
    width = cells // n
    for page in range(out.shape[1]):
        items = [column(*at) for at in order[page * n : (page + 1) * n]]
        items += [zero] * (n - len(items))
        for k, item in enumerate(block_transpose(items, width, cells)):
            out[k, page] = item


def split(value, period, stop, width, cells):
    items = [value]
    lane = lanes_of(cells)
    while period > stop:
        half = period // 2 * width
        bit = lane // half % 2 == 1
        fresh = []
        for item in items:
            other = pltpu.roll(item, half, 1)
            fresh += [jnp.where(bit, other, item), jnp.where(bit, item, other)]
        items = fresh
        period //= 2
    return items


def solve_kernel(n, x, out, cols, sides, kq, states):
    cells = x.shape[3]
    width = cells // n
    zero = jnp.zeros((8, cells), jnp.float32)
    count = 6 * STATE - 2

    def unpack(d, carry):
        for page in range(x.shape[1]):
            for k, block in enumerate(split(x[d, page], n, GROUPS, width, cells)):
                e = page * n + k * GROUPS
                if e < count:
                    for g, value in enumerate(split(block, GROUPS, 1, width, cells)):
                        cols[pl.ds((d * count + e + g) * 8, 8), :] = value
                elif e < count + 4 * GROUPS:
                    sides[d, (e - count) // GROUPS] = block
        return carry

    steps(n, 2, unpack)

    def column(d, e):
        return cols[pl.ds((d * count + e) * 8, 8), :]

    def total_of(terms):
        while len(terms) > 1:
            pairs = [terms[k] + terms[k + 1] for k in range(0, len(terms) - 1, 2)]
            terms = pairs + terms[len(terms) - len(terms) % 2 :]
        return terms[0]

    def rows_of(place):
        return [spread(states, (), place * 8 + j) for j in range(STATE)]

    def ahead(d, state):
        for half in range(2):
            states[pl.ds((d * 4 + half) * 8, 8), :] = state[half]
        rows = rows_of(d * 4)
        fresh = []
        for half in range(2):
            terms = [column(d, half * STATE + j) * rows[j] for j in range(STATE)]
            fresh.append(total_of(terms) + sides[d, half])
            first = 2 * STATE + half * (STATE - 1)
            terms = [column(d, first + j) * rows[j] for j in range(STATE - 1)]
            start = (d * count + STATE + 8 * half) * 8 + 7
            terms.append(cols[pl.ds(start, 8, stride=8), :] * rows[STATE - 1])
            kq[d, half] = total_of(terms) + sides[d, 2 + half]
        return tuple(fresh)

    steps(n, 4, ahead, (zero, zero))

    def back(e, state):
        d = n - 1 - e
        for half in range(2):
            states[pl.ds((d * 4 + 2 + half) * 8, 8), :] = state[half]
        rows = rows_of(d * 4 + 2)
        fresh = []
        for half in range(2):
            first = 4 * STATE - 2 + half * STATE
            terms = [column(d, first + j) * rows[j] for j in range(STATE)]
            fresh.append(total_of(terms) + kq[d, half])
        return tuple(fresh)

    steps(n, 4, back, (zero, zero))
    block = lanes_of(cells) // (GROUPS * width)

    def pack(d, carry):
        for page in range(out.shape[1]):
            total = zero
            for r in range(4):
                if GROUPS * r // n == page:
                    here = block == GROUPS * r % n // GROUPS
                    total = jnp.where(here, states[pl.ds((d * 4 + r) * 8, 8), :], total)
            out[d, page] = total
        return carry

    steps(n, 4, pack)


def sweep_kernel(
    n,
    states,
    source,
    mlow,
    mupp,
    lcols,
    ucols,
    counts,
    low_h,
    side_h,
    zout,
    wout,
    tail,
    edge,
    low,
    side,
    ybuf,
    stage,
    sems,
):
    total = low_h.shape[0]
    copies = [
        pltpu.make_async_copy(src, dst.at[pl.ds(0, total), :], sems.at[k])
        for k, (src, dst) in enumerate(((low_h, low), (side_h, side)))
    ]
    for copy in copies:
        copy.start()
    blocks, _, nrhs, cells = source.shape
    base = lax.axis_index("chain") * blocks
    width = cells // n
    zero = jnp.zeros((nrhs, cells), jnp.float32)
    items = []
    for r in range(states.shape[1]):
        items += block_transpose([states[k, r] for k in range(n)], width, cells)
    for e in range(4 * GROUPS):
        stage[pl.ds(8 * e, 8), :] = items[e]

    def entering(start):
        rows = [stage[pl.ds(start + q // 8 * 64 + q % 8, 8, stride=8), :] for q in range(STATE)]
        return tuple(rows)

    lane = lanes_of(cells)
    for v in range(VARS):
        wout[blocks, v] = zero

    def near(window, b, sign, cols, side):
        nears = []
        for k in range(SLOTS):
            off = sign * (cols[k, b] - base - b)
            picks = []
            for v in range(VARS):
                value = window[(REACH - 1) * VARS + v]
                for d in range(REACH - 1):
                    value = jnp.where(off == d + 1, window[d * VARS + v], value)
                picks.append(value if k == 0 else jnp.where(k < counts[side, b], value, 0.0))
            nears.append([[value] for value in picks])
        return nears

    def first(b, window):
        acc = couple(mlow, b, near(window, b, -1, lcols, 0))
        fresh = tuple(source[b, i] - acc[i][0] for i in range(VARS))
        for i in range(VARS):
            ybuf[b, i] = fresh[i]
        return fresh + window[: STATE - VARS]

    steps(blocks, 4, first, entering(0))

    def second(e, carry):
        c = blocks - 1 - e
        window, edges = carry[:STATE], list(carry[STATE:])
        acc = couple(mupp, c, near(window, c, 1, ucols, 1))
        fresh = tuple(ybuf[c, i] - acc[i][0] for i in range(VARS))
        here = (lane == 2 * c) | (lane == (2 * c + cells - 1) % cells)
        for i in range(VARS):
            zout[c, i] = fresh[i]
            wout[c, i] = acc[i][0]
            edges[i] = jnp.where(here, pltpu.roll(fresh[i], 2 * c, 1), edges[i])
        return fresh + window[: STATE - VARS] + tuple(edges)

    carry = steps(blocks, 4, second, entering(128) + (zero,) * VARS)
    for v in range(VARS):
        edge[v] = carry[STATE + v]
    for m in range(REACH):
        for v in range(VARS):
            tail[m, v] = wout[blocks - REACH + m, v]
    for copy in copies:
        copy.wait()


def inner_kernel(z, w, low, side, lcols, counts, resid, coef, correction, wbuf, sem):
    store = pltpu.make_async_copy(z, correction, sem)
    store.start()
    blocks, _, nrhs, cells = z.shape
    base = lax.axis_index("chain") * blocks
    lane = lanes_of(cells)
    zero = jnp.zeros((nrhs, cells), jnp.float32)
    for v in range(VARS):
        for m in range(REACH):
            wbuf[m, v] = zero
            wbuf[m + REACH, v] = w[m, v]
        wbuf[2 * REACH, v] = zero
    pages = coef.shape[0]
    size = VARS * VARS * SLOTS
    row = lax.broadcasted_iota(jnp.int32, (8, cells), 0)

    def block(b, found, buf, shift, empty):
        nears = [read_block(buf, s) for s in slots(lcols, counts, 0, b, shift - base, empty)]
        acc = apply_coef(low, b, nears)
        left, right = [], []
        for v in range(VARS):
            here = z[b, v]
            left.append(jnp.where(lane == 0, 0.0, pltpu.roll(here, 1, 1)))
            right.append(jnp.where(lane == cells - 1, 0.0, pltpu.roll(here, cells - 1, 1)))
        beside = apply_coef(side, b, [left, right])
        for i in range(VARS):
            resid[b, i] = acc[i] - beside[i]
        here = (lane + row % 2) % cells == 2 * b
        return tuple(
            jnp.where(here, pltpu.roll(side[pl.ds(b * size + 8 * r, 8), :], 2 * b, 1), found[r])
            for r in range(pages)
        )

    found = (jnp.zeros((8, cells), jnp.float32),) * pages
    for b in range(REACH):
        found = block(b, found, wbuf, REACH, 2 * REACH)

    def inner(b, found):
        return block(b + REACH, found, w, 0, blocks)

    found = steps(blocks - REACH, 3, inner, found)
    for r in range(pages):
        coef[r] = found[r]
    store.wait()


def outer_kernel(
    inner, coef, low, tail, swap_a, swap_b, lcols, counts, resid, squares, wbuf, cbuf
):
    blocks, _, nrhs, cells = inner.shape
    base = lax.axis_index("chain") * blocks
    odd = lax.axis_index("sub") % 2 == 1
    lane = lanes_of(cells)
    zero = jnp.zeros((nrhs, cells), jnp.float32)
    near = []
    for v in range(VARS):
        west = pltpu.roll(jnp.where(odd, swap_a[v], swap_b[v]), 1, 1)
        east = pltpu.roll(jnp.where(odd, swap_b[v], swap_a[v]), cells - 1, 1)
        near.append(jnp.where(lane % 2 == 0, west, east))
    for i in range(VARS):
        rows = []
        for j in range(VARS):
            k = (i * VARS + j) * SLOTS
            rows.append(coef[k // 8, pl.ds(k % 8, 1), :] + coef[(k + 1) // 8, pl.ds((k + 1) % 8, 1), :])
        cbuf[i] = mul_rows(rows, near)
    for v in range(VARS):
        for m in range(REACH):
            wbuf[m, v] = tail[m, v]
        wbuf[REACH, v] = zero
    ends = (lane == 0) | (lane == cells - 1)

    def add(b, i, value, total):
        value = value - jnp.where(ends, pltpu.roll(cbuf[i], (cells - 2 * b) % cells, 1), 0.0)
        resid[b, i] = value
        return total + value * value

    total = zero
    for b in range(REACH):
        places = [
            jnp.where(s < REACH, s, REACH) for s in slots(lcols, counts, 0, b, REACH - base, REACH)
        ]
        acc = apply_coef(low, b, [read_block(wbuf, s) for s in places])
        for i in range(VARS):
            total = add(b, i, inner[b, i] + acc[i], total)

    def rest(b, total):
        for i in range(VARS):
            total = add(b + REACH, i, inner[b + REACH, i], total)
        return total

    total = steps(blocks - REACH, 3, rest, total)
    sums = jnp.broadcast_to(jnp.sum(total, axis=1, keepdims=True), total.shape)
    row = lax.broadcasted_iota(jnp.int32, total.shape, 0)
    line = jnp.sum(jnp.where(lane == row, sums, 0.0), axis=0, keepdims=True)
    for p in range(squares.shape[0]):
        squares[p] = line


def scale_kernel(entries, resid, squares, out):
    blocks, _, nrhs, cells = resid.shape
    line = squares[0]
    for p in range(1, squares.shape[0]):
        line = line + squares[p]
    lane = lanes_of(cells)
    row = lax.broadcasted_iota(jnp.int32, (nrhs, cells), 0)
    line = jnp.where(lane == row, jnp.broadcast_to(line, (nrhs, cells)), 0.0)
    msq = jnp.sum(line, axis=1, keepdims=True) / entries
    factor = jnp.broadcast_to(lax.rsqrt(msq + 1e-06), (nrhs, cells))

    def block(b, carry):
        for v in range(VARS):
            out[b, v] = resid[b, v] * factor
        return carry

    steps(blocks, 4, block)


def call(kernel, outs, args, places, scratch):
    args = [
        pltpu.with_memory_space_constraint(a, p) if p is HBM else a for a, p in zip(args, places)
    ]
    return pl.pallas_call(
        kernel,
        out_shape=[jax.ShapeDtypeStruct(o[0], (o + (jnp.float32,))[2]) for o in outs],
        in_specs=[pl.BlockSpec(memory_space=p) for p in places],
        out_specs=[pl.BlockSpec(memory_space=p) for p in (o[1] for o in outs)],
        scratch_shapes=[VMEM(s, jnp.float32) if isinstance(s, tuple) else s for s in scratch],
        compiler_params=pltpu.CompilerParams(vmem_limit_bytes=VMEM_LIMIT),
    )(*args)


def shards(
    rhs, diag_block, diag_inverse, lower_coef, upper_coef, side_coef, lower_cols, upper_cols, counts
):
    blocks, nvars, nrhs, cells = rhs.shape
    n = lax.axis_size("chain")
    inv = jnp.transpose(diag_inverse, (1, 2, 0, 3))
    low, upp, side = (
        jnp.transpose(a, (0, 2, 3, 1, 4)).reshape(-1, cells)
        for a in (lower_coef, upper_coef, side_coef)
    )
    lcols, ucols, used = lower_cols.T, upper_cols.T, counts.T
    m = lax.axis_size("sub")
    rows = blocks + REACH + 1
    parts = -(-len(column_order(nrhs)) // n)
    back = -(-4 * GROUPS // n)
    tile = (nrhs, cells)

    mats = (VARS, VARS, SLOTS, blocks + PAD, cells)
    padded = (low.shape[0] + PAD, cells)

    maps, source, mlow, mupp, lcols, ucols, used = call(
        functools.partial(local_kernel, n),
        [((n, parts) + tile, VMEM), (rhs.shape, VMEM), (mats, VMEM), (mats, VMEM)]
        + [(lcols.shape, VMEM, jnp.int32)] * 3,
        (rhs, inv, low, upp, lcols, ucols, used),
        (HBM,) * 7,
        [rhs.shape, (VARS, VARS, blocks + PAD, cells), low.shape, upp.shape]
        + [pltpu.SMEM(lcols.shape, jnp.int32)] * 3
        + [(rows, VARS, nrhs + WIDE, cells), (rows, VARS, nrhs + 2 * WIDE, cells)]
        + [(WIDE * SPACE, cells), pltpu.SemaphoreType.DMA((10,))],
    )
    maps = lax.all_to_all(maps, "chain", 0, 0, tiled=True)
    (states,) = call(
        functools.partial(solve_kernel, n),
        [((n, back) + tile, VMEM)],
        (maps,),
        (VMEM,),
        [(n * (6 * STATE - 2) * 8 + PAD, cells), (n, 4) + tile, (n, 2) + tile]
        + [(n * 4 * 8 + PAD, cells)],
    )
    states = lax.all_to_all(states, "chain", 0, 0, tiled=True)
    z, w, tail, edge, low, side = call(
        functools.partial(sweep_kernel, n),
        [
            (rhs.shape, VMEM),
            ((blocks + 1, VARS) + tile, VMEM),
            ((REACH, VARS) + tile, VMEM),
            ((VARS,) + tile, VMEM),
            (padded, VMEM),
            (padded, VMEM),
        ],
        (states, source, mlow, mupp, lcols, ucols, used, low, side),
        (VMEM,) * 4 + (SMEM,) * 3 + (HBM,) * 2,
        [rhs.shape, (4 * GROUPS * 8, cells), pltpu.SemaphoreType.DMA((2,))],
    )
    tail = lax.ppermute(tail, "chain", [(i, i + 1) for i in range(n - 1)])
    swap_a, swap_b = (
        lax.ppermute(
            edge, "sub", [p for i in range(first, m - 1, 2) for p in ((i, i + 1), (i + 1, i))]
        )
        for first in (0, 1)
    )
    inner, coef, correction = call(
        inner_kernel,
        [
            (rhs.shape, VMEM),
            ((-(-VARS * VARS * SLOTS // 8),) + (8, cells), VMEM),
            (rhs.shape, HBM),
        ],
        (z, w, low, side, lcols, used),
        (VMEM,) * 4 + (SMEM,) * 2,
        [(2 * REACH + 1, VARS) + tile, pltpu.SemaphoreType.DMA],
    )
    resid, squares = call(
        outer_kernel,
        [(rhs.shape, VMEM), ((n * m, 1, cells), VMEM)],
        (inner, coef, low, tail, swap_a, swap_b, lcols, used),
        (VMEM,) * 6 + (SMEM,) * 2,
        [(REACH + 1, VARS) + tile, (VARS,) + tile],
    )
    squares = lax.all_to_all(squares, ("chain", "sub"), 0, 0, tiled=True)
    entries = blocks * VARS * cells * n * m
    (residual_unit,) = call(
        functools.partial(scale_kernel, entries),
        [(rhs.shape, VMEM)],
        (resid, squares),
        (VMEM, VMEM),
        [],
    )
    return (correction, residual_unit)


def solution(mesh):
    in_specs = (
        P("chain", None, None, "sub"),
        P("chain", None, None, "sub"),
        P("chain", None, None, "sub"),
        P("chain", None, None, None, "sub"),
        P("chain", None, None, None, "sub"),
        P("chain", None, None, None, "sub"),
        P("chain", None),
        P("chain", None),
        P("chain", None),
    )
    out_specs = (P("chain", None, None, "sub"), P("chain", None, None, "sub"))
    return jax.shard_map(shards, mesh=mesh, in_specs=in_specs, out_specs=out_specs, check_vma=False)
```

```python
import functools

import jax
import jax.numpy as jnp
from jax import lax
from jax.experimental import pallas as pl
from jax.experimental.pallas import tpu as pltpu
from jax.sharding import PartitionSpec as P

VARS = 5
REACH = 3
SLOTS = 2
STATE = REACH * VARS
WIDE = 16
PAD = 8
SPACE = 72
GROUPS = 8
VMEM_LIMIT = 40 * 1024 * 1024

VMEM = pltpu.VMEM
SMEM = pltpu.SMEM
HBM = pltpu.HBM


def lanes_of(cells):
    return lax.broadcasted_iota(jnp.int32, (8, cells), 1)


def block_transpose(items, width, cells):
    count = len(items)
    lane = lanes_of(cells)
    half = 1
    while half < count:
        bit = (lane // (half * width)) % 2 == 1
        out = list(items)
        for a in range(count):
            if a & half:
                continue
            b = a + half
            out[a] = jnp.where(bit, pltpu.roll(items[b], half * width, 1), items[a])
            out[b] = jnp.where(bit, items[b], pltpu.roll(items[a], cells - half * width, 1))
        items = out
        half *= 2
    return items


def spread(ref, place, row):
    return ref[place + (pl.ds(row, 8, stride=0), slice(None))]


def mul_rows(rows, near):
    total = rows[0] * near[0]
    for j in range(1, len(near)):
        total = total + rows[j] * near[j]
    return total


def mul_groups(rows, nears):
    return [mul_rows(rows, [near[g] for near in nears]) for g in range(len(nears[0]))]


def couple(mats, b, nears):
    out = []
    for i in range(VARS):
        parts = [
            mul_groups([spread(mats, (i, j, k), b) for j in range(VARS)], nears[k])
            for k in range(SLOTS)
        ]
        out.append([x + y for x, y in zip(*parts)])
    return out


def apply_coef(coef, b, nears):
    out = []
    for i in range(VARS):
        parts = []
        for k in range(SLOTS):
            place = (b * VARS + i) * VARS * SLOTS + k
            parts.append(
                mul_rows([spread(coef, (), place + SLOTS * j) for j in range(VARS)], nears[k])
            )
        out.append(parts[0] + parts[1])
    return out


def products(inv, coef, out):
    blocks = out.shape[3] - PAD
    stride = VARS * VARS * SLOTS

    def some(o, carry):
        start = o * 8
        left = [[inv[i, m, pl.ds(start, 8), :] for m in range(VARS)] for i in range(VARS)]
        for k in range(SLOTS):
            stores = []
            for j in range(VARS):
                place = start * stride + j * SLOTS + k
                right = [
                    coef[pl.ds(place + m * VARS * SLOTS, 8, stride=stride), :] for m in range(VARS)
                ]
                for i in range(VARS):
                    here = (i, j, k, pl.ds(start, 8))
                    stores.append((out, here, mul_rows(left[i], right)))
            store_all(stores)
        return carry

    lax.fori_loop(0, blocks // 8, some, 0)


def slots(cols, counts, side, b, shift, empty):
    return [jnp.where(k < counts[side, b], cols[k, b] + shift, empty) for k in range(SLOTS)]


def read_block(buf, place):
    return [buf[place, v] for v in range(VARS)]


def read_groups(buf, place):
    count = buf.shape[2] // 8
    return [[buf[place, v, pl.ds(8 * g, 8), :] for g in range(count)] for v in range(VARS)]


class Kept:
    def __init__(self, carry, stores):
        self.carry, self.stores = carry, stores


def store_all(stores):
    for ref, place, value in stores:
        ref[place] = value


def steps(count, most, body, carry=0):
    unroll = max(u for u in range(1, most + 1) if count % u == 0)

    def chunk(o, carry):
        kept = []
        for u in range(unroll):
            carry = body(o * unroll + u, carry)
            if isinstance(carry, Kept):
                kept += carry.stores
                carry = carry.carry
        store_all(kept)
        return carry

    return lax.fori_loop(0, count // unroll, chunk, carry)


def column_order(nrhs):
    wide_y = nrhs + WIDE
    order = []
    for first, count in ((nrhs, STATE), (wide_y + nrhs, STATE - 1), (wide_y + nrhs + WIDE, STATE)):
        order += [(half, first + j) for half in range(2) for j in range(count)]
    for first in (0, wide_y):
        order += [(half, first + q) for half in range(2) for q in range(nrhs)]
    return order


def local_kernel(
    n,
    rhs_h,
    inv_h,
    low_h,
    upp_h,
    lcols_h,
    ucols_h,
    counts_h,
    out,
    source,
    mlow,
    mupp,
    lcols_v,
    ucols_v,
    counts_v,
    rhs,
    inv,
    low,
    upp,
    lcols,
    ucols,
    counts,
    ybuf,
    zbuf,
    stage,
    sems,
):
    copies = [
        pltpu.make_async_copy(src, dst, sems.at[k])
        for k, (src, dst) in enumerate(
            (
                (inv_h, inv.at[:, :, pl.ds(0, rhs.shape[0]), :]),
                (low_h, low),
                (lcols_h, lcols),
                (counts_h, counts),
                (ucols_h, ucols),
                (rhs_h, rhs),
                (upp_h, upp),
                (lcols_h, lcols_v),
                (ucols_h, ucols_v),
                (counts_h, counts_v),
            )
        )
    ]
    for copy in copies:
        copy.start()
    blocks, _, nrhs, cells = rhs.shape
    base = lax.axis_index("chain") * blocks
    wide_y = nrhs + WIDE
    wide_z = wide_y + WIDE
    row_y = lax.broadcasted_iota(jnp.int32, (wide_y, cells), 0)
    row_z = lax.broadcasted_iota(jnp.int32, (wide_z, cells), 0)
    for m in range(REACH):
        for v in range(VARS):
            q = VARS * m + v
            ybuf[REACH - 1 - m, v] = (row_y == nrhs + q).astype(jnp.float32)
            zbuf[blocks + m, v] = (row_z == wide_y + q).astype(jnp.float32)
    for v in range(VARS):
        ybuf[blocks + REACH, v] = jnp.zeros((wide_y, cells), jnp.float32)
        zbuf[blocks + REACH, v] = jnp.zeros((wide_z, cells), jnp.float32)
    empty = blocks + REACH
    copies[0].wait()
    copies[1].wait()
    products(inv, low, mlow)
    for copy in copies[2:6]:
        copy.wait()

    def first(b, carry):
        nears = [read_groups(ybuf, s) for s in slots(lcols, counts, 0, b, REACH - base, empty)]
        acc = couple(mlow, b, nears)
        right = [rhs[b, i] for i in range(VARS)]
        stores = []
        for i in range(VARS):
            own = mul_rows([spread(inv, (i, j), b) for j in range(VARS)], right)
            stores.append((source, (b, i), own))
            for g in range(len(acc[i])):
                value = own - acc[i][0] if g == 0 else -acc[i][g]
                stores.append((ybuf, (b + REACH, i, pl.ds(8 * g, 8)), value))
        store_all(stores)
        return carry

    steps(blocks, 2, first)
    for copy in copies[6:]:
        copy.wait()
    products(inv, upp, mupp)

    def second(e, carry):
        c = blocks - 1 - e
        nears = [read_groups(zbuf, s) for s in slots(ucols, counts, 1, c, -base, empty)]
        acc = couple(mupp, c, nears)
        stores = []
        for i in range(VARS):
            for g in range(len(acc[i])):
                if g < wide_y // 8:
                    value = ybuf[c + REACH, i, 8 * g : 8 * g + 8] - acc[i][g]
                else:
                    value = -acc[i][g]
                stores.append((zbuf, (c, i, pl.ds(8 * g, 8)), value))
        store_all(stores)
        return carry

    steps(blocks, 2, second)

    zero = jnp.zeros((8, cells), jnp.float32)
    for i in range(WIDE):
        m, v = i // VARS, i % VARS
        for g in range((wide_y + wide_z) // 8):
            if i == STATE:
                value = zero
            elif g < wide_y // 8:
                value = ybuf[blocks + REACH - 1 - m, v, 8 * g : 8 * g + 8]
            else:
                value = zbuf[m, v, 8 * g - wide_y : 8 * g - wide_y + 8]
            stage[pl.ds(i * SPACE + 8 * g, 8), :] = value

    def column(half, index):
        return stage[pl.ds(half * 8 * SPACE + index, 8, stride=SPACE), :]

    for half in range(2):
        place = STATE * SPACE + nrhs + 8 * half
        stage[pl.ds(place, 8), :] = column(half, wide_y + nrhs + STATE - 1)
    order = column_order(nrhs)
    width = cells // n
    for page in range(out.shape[1]):
        items = [column(*at) for at in order[page * n : (page + 1) * n]]
        items += [zero] * (n - len(items))
        for k, item in enumerate(block_transpose(items, width, cells)):
            out[k, page] = item


def split(value, period, stop, width, cells):
    items = [value]
    lane = lanes_of(cells)
    while period > stop:
        half = period // 2 * width
        bit = lane // half % 2 == 1
        fresh = []
        for item in items:
            other = pltpu.roll(item, half, 1)
            fresh += [jnp.where(bit, other, item), jnp.where(bit, item, other)]
        items = fresh
        period //= 2
    return items


def solve_kernel(n, x, out, cols, sides, kq, states):
    cells = x.shape[3]
    width = cells // n
    zero = jnp.zeros((8, cells), jnp.float32)
    count = 6 * STATE - 2

    def unpack(d, carry):
        values = [x[d, page] for page in range(x.shape[1])]
        for page, value in enumerate(values):
            for k, block in enumerate(split(value, n, GROUPS, width, cells)):
                e = page * n + k * GROUPS
                if e < count:
                    for g, item in enumerate(split(block, GROUPS, 1, width, cells)):
                        cols[pl.ds((d * count + e + g) * 8, 8), :] = item
                elif e < count + 4 * GROUPS:
                    sides[d, (e - count) // GROUPS] = block
        return carry

    steps(n, 2, unpack)

    def column(d, e):
        return cols[pl.ds((d * count + e) * 8, 8), :]

    def total_of(terms):
        while len(terms) > 1:
            pairs = [terms[k] + terms[k + 1] for k in range(0, len(terms) - 1, 2)]
            terms = pairs + terms[len(terms) - len(terms) % 2 :]
        return terms[0]

    def rows_of(place):
        return [spread(states, (), place * 8 + j) for j in range(STATE)]

    def ahead(d, state):
        for half in range(2):
            states[pl.ds((d * 4 + half) * 8, 8), :] = state[half]
        rows = rows_of(d * 4)
        fresh = []
        for half in range(2):
            terms = [column(d, half * STATE + j) * rows[j] for j in range(STATE)]
            fresh.append(total_of(terms) + sides[d, half])
            first = 2 * STATE + half * (STATE - 1)
            terms = [column(d, first + j) * rows[j] for j in range(STATE - 1)]
            start = (d * count + STATE + 8 * half) * 8 + 7
            terms.append(cols[pl.ds(start, 8, stride=8), :] * rows[STATE - 1])
            kq[d, half] = total_of(terms) + sides[d, 2 + half]
        return tuple(fresh)

    steps(n, 4, ahead, (zero, zero))

    def back(e, state):
        d = n - 1 - e
        for half in range(2):
            states[pl.ds((d * 4 + 2 + half) * 8, 8), :] = state[half]
        rows = rows_of(d * 4 + 2)
        fresh = []
        for half in range(2):
            first = 4 * STATE - 2 + half * STATE
            terms = [column(d, first + j) * rows[j] for j in range(STATE)]
            fresh.append(total_of(terms) + kq[d, half])
        return tuple(fresh)

    steps(n, 4, back, (zero, zero))
    block = lanes_of(cells) // (GROUPS * width)

    def pack(d, carry):
        for page in range(out.shape[1]):
            total = zero
            for r in range(4):
                if GROUPS * r // n == page:
                    here = block == GROUPS * r % n // GROUPS
                    total = jnp.where(here, states[pl.ds((d * 4 + r) * 8, 8), :], total)
            out[d, page] = total
        return carry

    steps(n, 4, pack)


def sweep_kernel(
    n,
    states,
    source,
    mlow,
    mupp,
    lcols,
    ucols,
    counts,
    low_h,
    side_h,
    zout,
    wout,
    tail,
    edge,
    low,
    side,
    ybuf,
    stage,
    sems,
):
    total = low_h.shape[0]
    copies = [
        pltpu.make_async_copy(src, dst.at[pl.ds(0, total), :], sems.at[k])
        for k, (src, dst) in enumerate(((low_h, low), (side_h, side)))
    ]
    for copy in copies:
        copy.start()
    blocks, _, nrhs, cells = source.shape
    base = lax.axis_index("chain") * blocks
    width = cells // n
    zero = jnp.zeros((nrhs, cells), jnp.float32)
    items = []
    for r in range(states.shape[1]):
        items += block_transpose([states[k, r] for k in range(n)], width, cells)
    for e in range(4 * GROUPS):
        stage[pl.ds(8 * e, 8), :] = items[e]

    def entering(start):
        rows = [stage[pl.ds(start + q // 8 * 64 + q % 8, 8, stride=8), :] for q in range(STATE)]
        return tuple(rows)

    lane = lanes_of(cells)
    for v in range(VARS):
        wout[blocks, v] = zero

    def near(window, b, sign, cols, side):
        nears = []
        for k in range(SLOTS):
            off = sign * (cols[k, b] - base - b)
            picks = []
            for v in range(VARS):
                value = window[(REACH - 1) * VARS + v]
                for d in range(REACH - 1):
                    value = jnp.where(off == d + 1, window[d * VARS + v], value)
                picks.append(value if k == 0 else jnp.where(k < counts[side, b], value, 0.0))
            nears.append([[value] for value in picks])
        return nears

    def first(b, window):
        acc = couple(mlow, b, near(window, b, -1, lcols, 0))
        fresh = tuple(source[b, i] - acc[i][0] for i in range(VARS))
        return Kept(fresh + window[: STATE - VARS], [(ybuf, (b, i), fresh[i]) for i in range(VARS)])

    steps(blocks, 4, first, entering(0))

    def second(e, carry):
        c = blocks - 1 - e
        window, edges = carry[:STATE], list(carry[STATE:])
        acc = couple(mupp, c, near(window, c, 1, ucols, 1))
        fresh = tuple(ybuf[c, i] - acc[i][0] for i in range(VARS))
        here = (lane == 2 * c) | (lane == (2 * c + cells - 1) % cells)
        stores = []
        for i in range(VARS):
            stores += [(zout, (c, i), fresh[i]), (wout, (c, i), acc[i][0])]
            edges[i] = jnp.where(here, pltpu.roll(fresh[i], 2 * c, 1), edges[i])
        return Kept(fresh + window[: STATE - VARS] + tuple(edges), stores)

    carry = steps(blocks, 4, second, entering(128) + (zero,) * VARS)
    for v in range(VARS):
        edge[v] = carry[STATE + v]
    for m in range(REACH):
        for v in range(VARS):
            tail[m, v] = wout[blocks - REACH + m, v]
    for copy in copies:
        copy.wait()


def inner_kernel(z, w, low, side, lcols, counts, resid, coef, correction, wbuf, sem):
    store = pltpu.make_async_copy(z, correction, sem)
    store.start()
    blocks, _, nrhs, cells = z.shape
    base = lax.axis_index("chain") * blocks
    lane = lanes_of(cells)
    zero = jnp.zeros((nrhs, cells), jnp.float32)
    for v in range(VARS):
        for m in range(REACH):
            wbuf[m, v] = zero
            wbuf[m + REACH, v] = w[m, v]
        wbuf[2 * REACH, v] = zero
    pages = coef.shape[0]
    size = VARS * VARS * SLOTS
    row = lax.broadcasted_iota(jnp.int32, (8, cells), 0)

    def block(b, found, buf, shift, empty):
        nears = [read_block(buf, s) for s in slots(lcols, counts, 0, b, shift - base, empty)]
        acc = apply_coef(low, b, nears)
        left, right = [], []
        for v in range(VARS):
            here = z[b, v]
            left.append(jnp.where(lane == 0, 0.0, pltpu.roll(here, 1, 1)))
            right.append(jnp.where(lane == cells - 1, 0.0, pltpu.roll(here, cells - 1, 1)))
        beside = apply_coef(side, b, [left, right])
        here = (lane + row % 2) % cells == 2 * b
        found = tuple(
            jnp.where(here, pltpu.roll(side[pl.ds(b * size + 8 * r, 8), :], 2 * b, 1), found[r])
            for r in range(pages)
        )
        return Kept(found, [(resid, (b, i), acc[i] - beside[i]) for i in range(VARS)])

    found = (jnp.zeros((8, cells), jnp.float32),) * pages
    for b in range(REACH):
        kept = block(b, found, wbuf, REACH, 2 * REACH)
        store_all(kept.stores)
        found = kept.carry

    def inner(b, found):
        return block(b + REACH, found, w, 0, blocks)

    found = steps(blocks - REACH, 3, inner, found)
    for r in range(pages):
        coef[r] = found[r]
    store.wait()


def outer_kernel(
    inner, coef, low, tail, swap_a, swap_b, lcols, counts, resid, squares, wbuf
):
    blocks, _, nrhs, cells = inner.shape
    base = lax.axis_index("chain") * blocks
    odd = lax.axis_index("sub") % 2 == 1
    lane = lanes_of(cells)
    zero = jnp.zeros((nrhs, cells), jnp.float32)
    near = []
    for v in range(VARS):
        west = pltpu.roll(jnp.where(odd, swap_a[v], swap_b[v]), 1, 1)
        east = pltpu.roll(jnp.where(odd, swap_b[v], swap_a[v]), cells - 1, 1)
        near.append(jnp.where(lane % 2 == 0, west, east))
    edge = []
    for i in range(VARS):
        rows = []
        for j in range(VARS):
            k = (i * VARS + j) * SLOTS
            rows.append(coef[k // 8, pl.ds(k % 8, 1), :] + coef[(k + 1) // 8, pl.ds((k + 1) % 8, 1), :])
        edge.append(mul_rows(rows, near))
    for v in range(VARS):
        for m in range(REACH):
            wbuf[m, v] = tail[m, v]
        wbuf[REACH, v] = zero
    ends = (lane == 0) | (lane == cells - 1)

    def add(b, values, totals):
        stores, fresh = [], []
        for i in range(VARS):
            other = pltpu.roll(edge[i], (cells - 2 * b) % cells, 1)
            value = values[i] - jnp.where(ends, other, 0.0)
            stores.append((resid, (b, i), value))
            fresh.append(totals[i] + value * value)
        return Kept(tuple(fresh), stores)

    totals = (zero,) * VARS
    stores = []
    for b in range(REACH):
        places = [
            jnp.where(s < REACH, s, REACH) for s in slots(lcols, counts, 0, b, REACH - base, REACH)
        ]
        acc = apply_coef(low, b, [read_block(wbuf, s) for s in places])
        kept = add(b, [inner[b, i] + acc[i] for i in range(VARS)], totals)
        stores += kept.stores
        totals = kept.carry
    store_all(stores)

    def rest(b, totals):
        return add(b + REACH, [inner[b + REACH, i] for i in range(VARS)], totals)

    totals = steps(blocks - REACH, 7, rest, totals)
    total = totals[0]
    for i in range(1, VARS):
        total = total + totals[i]
    sums = jnp.broadcast_to(jnp.sum(total, axis=1, keepdims=True), total.shape)
    row = lax.broadcasted_iota(jnp.int32, total.shape, 0)
    line = jnp.sum(jnp.where(lane == row, sums, 0.0), axis=0, keepdims=True)
    for p in range(squares.shape[0]):
        squares[p] = line


def scale_kernel(entries, resid, squares, out):
    blocks, _, nrhs, cells = resid.shape
    line = squares[0]
    for p in range(1, squares.shape[0]):
        line = line + squares[p]
    lane = lanes_of(cells)
    row = lax.broadcasted_iota(jnp.int32, (nrhs, cells), 0)
    line = jnp.where(lane == row, jnp.broadcast_to(line, (nrhs, cells)), 0.0)
    msq = jnp.sum(line, axis=1, keepdims=True) / entries
    factor = jnp.broadcast_to(lax.rsqrt(msq + 1e-06), (nrhs, cells))

    def block(b, carry):
        return Kept(carry, [(out, (b, v), resid[b, v] * factor) for v in range(VARS)])

    steps(blocks, 6, block)


def call(kernel, outs, args, places, scratch):
    args = [
        pltpu.with_memory_space_constraint(a, p) if p is HBM else a for a, p in zip(args, places)
    ]
    return pl.pallas_call(
        kernel,
        out_shape=[jax.ShapeDtypeStruct(o[0], (o + (jnp.float32,))[2]) for o in outs],
        in_specs=[pl.BlockSpec(memory_space=p) for p in places],
        out_specs=[pl.BlockSpec(memory_space=p) for p in (o[1] for o in outs)],
        scratch_shapes=[VMEM(s, jnp.float32) if isinstance(s, tuple) else s for s in scratch],
        compiler_params=pltpu.CompilerParams(vmem_limit_bytes=VMEM_LIMIT),
    )(*args)


def shards(
    rhs, diag_block, diag_inverse, lower_coef, upper_coef, side_coef, lower_cols, upper_cols, counts
):
    blocks, nvars, nrhs, cells = rhs.shape
    n = lax.axis_size("chain")
    inv = jnp.transpose(diag_inverse, (1, 2, 0, 3))
    low, upp, side = (
        jnp.transpose(a, (0, 2, 3, 1, 4)).reshape(-1, cells)
        for a in (lower_coef, upper_coef, side_coef)
    )
    lcols, ucols, used = lower_cols.T, upper_cols.T, counts.T
    m = lax.axis_size("sub")
    rows = blocks + REACH + 1
    parts = -(-len(column_order(nrhs)) // n)
    back = -(-4 * GROUPS // n)
    tile = (nrhs, cells)

    mats = (VARS, VARS, SLOTS, blocks + PAD, cells)
    padded = (low.shape[0] + PAD, cells)

    maps, source, mlow, mupp, lcols, ucols, used = call(
        functools.partial(local_kernel, n),
        [((n, parts) + tile, VMEM), (rhs.shape, VMEM), (mats, VMEM), (mats, VMEM)]
        + [(lcols.shape, VMEM, jnp.int32)] * 3,
        (rhs, inv, low, upp, lcols, ucols, used),
        (HBM,) * 7,
        [rhs.shape, (VARS, VARS, blocks + PAD, cells), low.shape, upp.shape]
        + [pltpu.SMEM(lcols.shape, jnp.int32)] * 3
        + [(rows, VARS, nrhs + WIDE, cells), (rows, VARS, nrhs + 2 * WIDE, cells)]
        + [(WIDE * SPACE, cells), pltpu.SemaphoreType.DMA((10,))],
    )
    maps = lax.all_to_all(maps, "chain", 0, 0, tiled=True)
    (states,) = call(
        functools.partial(solve_kernel, n),
        [((n, back) + tile, VMEM)],
        (maps,),
        (VMEM,),
        [(n * (6 * STATE - 2) * 8 + PAD, cells), (n, 4) + tile, (n, 2) + tile]
        + [(n * 4 * 8 + PAD, cells)],
    )
    states = lax.all_to_all(states, "chain", 0, 0, tiled=True)
    z, w, tail, edge, low, side = call(
        functools.partial(sweep_kernel, n),
        [
            (rhs.shape, VMEM),
            ((blocks + 1, VARS) + tile, VMEM),
            ((REACH, VARS) + tile, VMEM),
            ((VARS,) + tile, VMEM),
            (padded, VMEM),
            (padded, VMEM),
        ],
        (states, source, mlow, mupp, lcols, ucols, used, low, side),
        (VMEM,) * 4 + (SMEM,) * 3 + (HBM,) * 2,
        [rhs.shape, (4 * GROUPS * 8, cells), pltpu.SemaphoreType.DMA((2,))],
    )
    tail = lax.ppermute(tail, "chain", [(i, i + 1) for i in range(n - 1)])
    swap_a, swap_b = (
        lax.ppermute(
            edge, "sub", [p for i in range(first, m - 1, 2) for p in ((i, i + 1), (i + 1, i))]
        )
        for first in (0, 1)
    )
    inner, coef, correction = call(
        inner_kernel,
        [
            (rhs.shape, VMEM),
            ((-(-VARS * VARS * SLOTS // 8),) + (8, cells), VMEM),
            (rhs.shape, HBM),
        ],
        (z, w, low, side, lcols, used),
        (VMEM,) * 4 + (SMEM,) * 2,
        [(2 * REACH + 1, VARS) + tile, pltpu.SemaphoreType.DMA],
    )
    resid, squares = call(
        outer_kernel,
        [(rhs.shape, VMEM), ((n * m, 1, cells), VMEM)],
        (inner, coef, low, tail, swap_a, swap_b, lcols, used),
        (VMEM,) * 6 + (SMEM,) * 2,
        [(REACH + 1, VARS) + tile],
    )
    squares = lax.all_to_all(squares, ("chain", "sub"), 0, 0, tiled=True)
    entries = blocks * VARS * cells * n * m
    (residual_unit,) = call(
        functools.partial(scale_kernel, entries),
        [(rhs.shape, VMEM)],
        (resid, squares),
        (VMEM, VMEM),
        [],
    )
    return (correction, residual_unit)


def solution(mesh):
    in_specs = (
        P("chain", None, None, "sub"),
        P("chain", None, None, "sub"),
        P("chain", None, None, "sub"),
        P("chain", None, None, None, "sub"),
        P("chain", None, None, None, "sub"),
        P("chain", None, None, None, "sub"),
        P("chain", None),
        P("chain", None),
        P("chain", None),
    )
    out_specs = (P("chain", None, None, "sub"), P("chain", None, None, "sub"))
    return jax.shard_map(shards, mesh=mesh, in_specs=in_specs, out_specs=out_specs, check_vma=False)
```

```python
import functools

import jax
import jax.numpy as jnp
from jax import lax
from jax.experimental import pallas as pl
from jax.experimental.pallas import tpu as pltpu
from jax.sharding import PartitionSpec as P

VARS = 5
REACH = 3
SLOTS = 2
STATE = REACH * VARS
WIDE = 16
PAD = 8
SPACE = 72
VMEM_LIMIT = 40 * 1024 * 1024

VMEM = pltpu.VMEM
SMEM = pltpu.SMEM
HBM = pltpu.HBM


def lanes_of(cells):
    return lax.broadcasted_iota(jnp.int32, (8, cells), 1)


def block_transpose(items, width, cells):
    count = len(items)
    lane = lanes_of(cells)
    half = 1
    while half < count:
        bit = (lane // (half * width)) % 2 == 1
        out = list(items)
        for a in range(count):
            if a & half:
                continue
            b = a + half
            out[a] = jnp.where(bit, pltpu.roll(items[b], half * width, 1), items[a])
            out[b] = jnp.where(bit, items[b], pltpu.roll(items[a], cells - half * width, 1))
        items = out
        half *= 2
    return items


def spread(ref, place, row):
    return ref[place + (pl.ds(row, 8, stride=0), slice(None))]


def mul_rows(rows, near):
    total = rows[0] * near[0]
    for j in range(1, len(near)):
        total = total + rows[j] * near[j]
    return total


def mul_groups(rows, nears):
    return [mul_rows(rows, [near[g] for near in nears]) for g in range(len(nears[0]))]


def couple(mats, b, nears):
    out = []
    for i in range(VARS):
        parts = [
            mul_groups([spread(mats, (i, j, k), b) for j in range(VARS)], nears[k])
            for k in range(SLOTS)
        ]
        out.append([x + y for x, y in zip(*parts)])
    return out


def apply_coef(coef, b, nears):
    out = []
    for i in range(VARS):
        parts = []
        for k in range(SLOTS):
            place = (b * VARS + i) * VARS * SLOTS + k
            parts.append(
                mul_rows([spread(coef, (), place + SLOTS * j) for j in range(VARS)], nears[k])
            )
        out.append(parts[0] + parts[1])
    return out


def products(inv, coef, out):
    blocks = out.shape[3] - PAD
    stride = VARS * VARS * SLOTS

    def some(o, carry):
        start = o * 8
        left = [[inv[i, m, pl.ds(start, 8), :] for m in range(VARS)] for i in range(VARS)]
        for k in range(SLOTS):
            stores = []
            for j in range(VARS):
                place = start * stride + j * SLOTS + k
                right = [
                    coef[pl.ds(place + m * VARS * SLOTS, 8, stride=stride), :] for m in range(VARS)
                ]
                for i in range(VARS):
                    here = (i, j, k, pl.ds(start, 8))
                    stores.append((out, here, mul_rows(left[i], right)))
            store_all(stores)
        return carry

    lax.fori_loop(0, blocks // 8, some, 0)


def slots(cols, counts, side, b, shift, empty):
    return [jnp.where(k < counts[side, b], cols[k, b] + shift, empty) for k in range(SLOTS)]


def read_block(buf, place):
    return [buf[place, v] for v in range(VARS)]


def read_groups(buf, place):
    count = buf.shape[2] // 8
    return [[buf[place, v, pl.ds(8 * g, 8), :] for g in range(count)] for v in range(VARS)]


class Kept:
    def __init__(self, carry, stores):
        self.carry, self.stores = carry, stores


def store_all(stores):
    for ref, place, value in stores:
        ref[place] = value


def steps(count, most, body, carry=0):
    unroll = max(u for u in range(1, most + 1) if count % u == 0)

    def chunk(o, carry):
        kept = []
        for u in range(unroll):
            carry = body(o * unroll + u, carry)
            if isinstance(carry, Kept):
                kept += carry.stores
                carry = carry.carry
        store_all(kept)
        return carry

    return lax.fori_loop(0, count // unroll, chunk, carry)


def column_order(nrhs):
    wide_y = nrhs + WIDE
    order = []
    for first, count in ((nrhs, STATE), (wide_y + nrhs, STATE - 1), (wide_y + nrhs + WIDE, STATE)):
        order += [(half, first + j) for half in range(2) for j in range(count)]
    for first in (0, wide_y):
        order += [(half, first + q) for half in range(2) for q in range(nrhs)]
    return order


def local_kernel(
    n,
    rhs_h,
    inv_h,
    low_h,
    upp_h,
    lcols_h,
    ucols_h,
    counts_h,
    out,
    source,
    mlow,
    mupp,
    lcols_v,
    ucols_v,
    counts_v,
    rhs,
    inv,
    low,
    upp,
    lcols,
    ucols,
    counts,
    ybuf,
    zbuf,
    stage,
    sems,
):
    copies = [
        pltpu.make_async_copy(src, dst, sems.at[k])
        for k, (src, dst) in enumerate(
            (
                (inv_h, inv.at[:, :, pl.ds(0, rhs.shape[0]), :]),
                (low_h, low),
                (lcols_h, lcols),
                (counts_h, counts),
                (ucols_h, ucols),
                (rhs_h, rhs),
                (upp_h, upp),
                (lcols_h, lcols_v),
                (ucols_h, ucols_v),
                (counts_h, counts_v),
            )
        )
    ]
    for copy in copies:
        copy.start()
    blocks, _, nrhs, cells = rhs.shape
    base = lax.axis_index("chain") * blocks
    wide_y = nrhs + WIDE
    wide_z = wide_y + WIDE
    row_y = lax.broadcasted_iota(jnp.int32, (wide_y, cells), 0)
    row_z = lax.broadcasted_iota(jnp.int32, (wide_z, cells), 0)
    for m in range(REACH):
        for v in range(VARS):
            q = VARS * m + v
            ybuf[REACH - 1 - m, v] = (row_y == nrhs + q).astype(jnp.float32)
            zbuf[blocks + m, v] = (row_z == wide_y + q).astype(jnp.float32)
    for v in range(VARS):
        ybuf[blocks + REACH, v] = jnp.zeros((wide_y, cells), jnp.float32)
        zbuf[blocks + REACH, v] = jnp.zeros((wide_z, cells), jnp.float32)
    empty = blocks + REACH
    copies[0].wait()
    copies[1].wait()
    products(inv, low, mlow)
    for copy in copies[2:6]:
        copy.wait()

    def first(b, carry):
        nears = [read_groups(ybuf, s) for s in slots(lcols, counts, 0, b, REACH - base, empty)]
        acc = couple(mlow, b, nears)
        right = [rhs[b, i] for i in range(VARS)]
        stores = []
        for i in range(VARS):
            own = mul_rows([spread(inv, (i, j), b) for j in range(VARS)], right)
            stores.append((source, (b, i), own))
            for g in range(len(acc[i])):
                value = own - acc[i][0] if g == 0 else -acc[i][g]
                stores.append((ybuf, (b + REACH, i, pl.ds(8 * g, 8)), value))
        store_all(stores)
        return carry

    steps(blocks, 2, first)
    for copy in copies[6:]:
        copy.wait()
    products(inv, upp, mupp)

    def second(e, carry):
        c = blocks - 1 - e
        nears = [read_groups(zbuf, s) for s in slots(ucols, counts, 1, c, -base, empty)]
        acc = couple(mupp, c, nears)
        stores = []
        for i in range(VARS):
            for g in range(len(acc[i])):
                if g < wide_y // 8:
                    value = ybuf[c + REACH, i, 8 * g : 8 * g + 8] - acc[i][g]
                else:
                    value = -acc[i][g]
                stores.append((zbuf, (c, i, pl.ds(8 * g, 8)), value))
        store_all(stores)
        return carry

    steps(blocks, 2, second)

    zero = jnp.zeros((8, cells), jnp.float32)
    for i in range(WIDE):
        m, v = i // VARS, i % VARS
        for g in range((wide_y + wide_z) // 8):
            if i == STATE:
                value = zero
            elif g < wide_y // 8:
                value = ybuf[blocks + REACH - 1 - m, v, 8 * g : 8 * g + 8]
            else:
                value = zbuf[m, v, 8 * g - wide_y : 8 * g - wide_y + 8]
            stage[pl.ds(i * SPACE + 8 * g, 8), :] = value

    def column(half, index):
        return stage[pl.ds(half * 8 * SPACE + index, 8, stride=SPACE), :]

    for half in range(2):
        place = STATE * SPACE + nrhs + 8 * half
        stage[pl.ds(place, 8), :] = column(half, wide_y + nrhs + STATE - 1)
    order = column_order(nrhs)
    width = cells // n
    for page in range(out.shape[1]):
        items = [column(*at) for at in order[page * n : (page + 1) * n]]
        items += [zero] * (n - len(items))
        for k, item in enumerate(block_transpose(items, width, cells)):
            out[k, page] = item


def split(value, period, stop, width, cells):
    items = [value]
    lane = lanes_of(cells)
    while period > stop:
        half = period // 2 * width
        bit = lane // half % 2 == 1
        fresh = []
        for item in items:
            other = pltpu.roll(item, half, 1)
            fresh += [jnp.where(bit, other, item), jnp.where(bit, item, other)]
        items = fresh
        period //= 2
    return items


def total_of(terms):
    while len(terms) > 1:
        pairs = [terms[k] + terms[k + 1] for k in range(0, len(terms) - 1, 2)]
        terms = pairs + terms[len(terms) - len(terms) % 2 :]
    return terms[0]


COLUMNS = 6 * STATE - 2


def store_state(buf, state):
    for half in range(2):
        for g, value in enumerate(state[half]):
            buf[pl.ds(g * WIDE + 8 * half, 8), :] = value


def state_rows(buf, count):
    return [[spread(buf, (), g * WIDE + j) for j in range(STATE)] for g in range(count)]


def pass_forward(d, cols, sides, state, buf, keep):
    groups, extra = len(state[0]), sides.shape[1] // 4
    store_state(buf, state)
    rows = state_rows(buf, groups)
    fresh = []
    for half in range(2):
        columns = [cols[pl.ds((d * COLUMNS + half * STATE + j) * 8, 8), :] for j in range(STATE)]
        fresh.append([])
        for g in range(groups):
            total = total_of([c * r for c, r in zip(columns, rows[g])])
            fresh[half].append(total + sides[d, half * extra + g] if g < extra else total)
        first = d * COLUMNS + 2 * STATE + half * (STATE - 1)
        columns = [cols[pl.ds((first + j) * 8, 8), :] for j in range(STATE - 1)]
        start = (d * COLUMNS + STATE + 8 * half) * 8 + 7
        columns.append(cols[pl.ds(start, 8, stride=8), :])
        for g in range(groups):
            total = total_of([c * r for c, r in zip(columns, rows[g])])
            if g < extra:
                total = total + sides[d, (2 + half) * extra + g]
            keep[d, half * groups + g] = total
    return fresh


def pass_back(d, cols, state, buf, keep):
    groups = len(state[0])
    store_state(buf, state)
    rows = state_rows(buf, groups)
    fresh = []
    for half in range(2):
        first = d * COLUMNS + 4 * STATE - 2 + half * STATE
        columns = [cols[pl.ds((first + j) * 8, 8), :] for j in range(STATE)]
        fresh.append(
            [
                total_of([c * r for c, r in zip(columns, rows[g])]) + keep[d, half * groups + g]
                for g in range(groups)
            ]
        )
    return fresh


def flat(state):
    return tuple(state[0] + state[1])


def folded(values):
    groups = len(values) // 2
    return [list(values[:groups]), list(values[groups:])]


def first_solve_kernel(x, cols, sides, offer, keep, buf):
    n, cells = x.shape[0], x.shape[3]
    width = cells // n
    packed = min(8, n)
    extra, groups = sides.shape[1] // 4, offer.shape[0] // 2
    zero = jnp.zeros((8, cells), jnp.float32)

    def unpack(d, carry):
        values = [x[d, page] for page in range(x.shape[1])]
        for page, value in enumerate(values):
            for k, block in enumerate(split(value, n, packed, width, cells)):
                e = page * n + k * packed
                if e < COLUMNS:
                    for g, item in enumerate(split(block, packed, 1, width, cells)):
                        cols[pl.ds((d * COLUMNS + e + g) * 8, 8), :] = item
                elif e < COLUMNS + 4 * 8:
                    sides[d, (e - COLUMNS) // packed] = block
        return carry

    steps(n, 2, unpack)
    lane = lanes_of(cells)
    row = lax.broadcasted_iota(jnp.int32, (8, cells), 0)
    start = []
    for half in range(2):
        start.append([zero] * extra)
        for g in range(groups - extra):
            column = lane // width % packed + g * packed
            start[half].append((column == row + 8 * half).astype(jnp.float32))

    def ahead(d, state):
        return flat(pass_forward(d, cols, sides, folded(state), buf, keep))

    leaving = steps(n, 2, ahead, flat(start))

    def back(e, state):
        return flat(pass_back(n - 1 - e, cols, folded(state), buf, keep))

    left = steps(n, 2, back, (zero,) * (2 * groups))
    is_left = lax.axis_index("chain") < n
    for e in range(2 * groups):
        offer[e] = jnp.where(is_left, leaving[e], left[e])


def second_solve_kernel(cols, sides, mine, got, out, keep, buf, states):
    n, cells = out.shape[0], out.shape[3]
    width = cells // n
    packed = min(8, n)
    extra, groups = sides.shape[1] // 4, mine.shape[0] // 2
    zero = jnp.zeros((8, cells), jnp.float32)
    is_left = lax.axis_index("chain") < n
    store_state(buf, [[mine[half * groups + g] for g in range(extra)] for half in range(2)])
    rows = state_rows(buf, extra)
    entering, far = [], []
    for half in range(2):
        columns = []
        for g in range(extra, groups):
            columns += split(got[half * groups + g], packed, 1, width, cells)
        for g in range(extra):
            known = got[half * groups + g]
            total = total_of([c * r for c, r in zip(columns, rows[g])])
            entering.append(jnp.where(is_left, 0.0, known))
            far.append(jnp.where(is_left, known + total, 0.0))

    def ahead(d, state):
        for e in range(2 * extra):
            states[d, e] = state[e]
        return flat(pass_forward(d, cols, sides, folded(state), buf, keep))

    steps(n, 4, ahead, tuple(entering))

    def back(e, state):
        d = n - 1 - e
        for e in range(2 * extra):
            states[d, 2 * extra + e] = state[e]
        return flat(pass_back(d, cols, folded(state), buf, keep))

    steps(n, 4, back, tuple(far))
    block = lanes_of(cells) // (packed * width)

    def pack(d, carry):
        for page in range(out.shape[1]):
            total = zero
            for r in range(4 * extra):
                if packed * r // n == page:
                    total = jnp.where(block == packed * r % n // packed, states[d, r], total)
            out[d, page] = total
        return carry

    steps(n, 4, pack)


def sweep_kernel(
    n,
    states,
    source,
    mlow,
    mupp,
    lcols,
    ucols,
    counts,
    low_h,
    side_h,
    zout,
    wout,
    tail,
    edge,
    low,
    side,
    ybuf,
    stage,
    sems,
):
    total = low_h.shape[0]
    copies = [
        pltpu.make_async_copy(src, dst.at[pl.ds(0, total), :], sems.at[k])
        for k, (src, dst) in enumerate(((low_h, low), (side_h, side)))
    ]
    for copy in copies:
        copy.start()
    blocks, _, nrhs, cells = source.shape
    base = lax.axis_index("chain") * blocks
    width = cells // n
    zero = jnp.zeros((nrhs, cells), jnp.float32)
    items = []
    for r in range(states.shape[1]):
        items += block_transpose([states[k, r] for k in range(n)], width, cells)
    for e in range(32):
        stage[pl.ds(8 * e, 8), :] = items[e]

    def entering(start):
        rows = [stage[pl.ds(start + q // 8 * 64 + q % 8, 8, stride=8), :] for q in range(STATE)]
        return tuple(rows)

    lane = lanes_of(cells)
    for v in range(VARS):
        wout[blocks, v] = zero

    def near(window, b, sign, cols, side):
        nears = []
        for k in range(SLOTS):
            off = sign * (cols[k, b] - base - b)
            picks = []
            for v in range(VARS):
                value = window[(REACH - 1) * VARS + v]
                for d in range(REACH - 1):
                    value = jnp.where(off == d + 1, window[d * VARS + v], value)
                picks.append(value if k == 0 else jnp.where(k < counts[side, b], value, 0.0))
            nears.append([[value] for value in picks])
        return nears

    def first(b, window):
        acc = couple(mlow, b, near(window, b, -1, lcols, 0))
        fresh = tuple(source[b, i] - acc[i][0] for i in range(VARS))
        return Kept(fresh + window[: STATE - VARS], [(ybuf, (b, i), fresh[i]) for i in range(VARS)])

    steps(blocks, 4, first, entering(0))

    def second(e, carry):
        c = blocks - 1 - e
        window, edges = carry[:STATE], list(carry[STATE:])
        acc = couple(mupp, c, near(window, c, 1, ucols, 1))
        fresh = tuple(ybuf[c, i] - acc[i][0] for i in range(VARS))
        here = (lane == 2 * c) | (lane == (2 * c + cells - 1) % cells)
        stores = []
        for i in range(VARS):
            stores += [(zout, (c, i), fresh[i]), (wout, (c, i), acc[i][0])]
            edges[i] = jnp.where(here, pltpu.roll(fresh[i], 2 * c, 1), edges[i])
        return Kept(fresh + window[: STATE - VARS] + tuple(edges), stores)

    carry = steps(blocks, 4, second, entering(128) + (zero,) * VARS)
    for v in range(VARS):
        edge[v] = carry[STATE + v]
    for m in range(REACH):
        for v in range(VARS):
            tail[m, v] = wout[blocks - REACH + m, v]
    for copy in copies:
        copy.wait()


def inner_kernel(z, w, low, side, lcols, counts, resid, coef, correction, wbuf, sem):
    store = pltpu.make_async_copy(z, correction, sem)
    store.start()
    blocks, _, nrhs, cells = z.shape
    base = lax.axis_index("chain") * blocks
    lane = lanes_of(cells)
    zero = jnp.zeros((nrhs, cells), jnp.float32)
    for v in range(VARS):
        for m in range(REACH):
            wbuf[m, v] = zero
            wbuf[m + REACH, v] = w[m, v]
        wbuf[2 * REACH, v] = zero
    pages = coef.shape[0]
    size = VARS * VARS * SLOTS
    row = lax.broadcasted_iota(jnp.int32, (8, cells), 0)

    def block(b, found, buf, shift, empty):
        nears = [read_block(buf, s) for s in slots(lcols, counts, 0, b, shift - base, empty)]
        acc = apply_coef(low, b, nears)
        left, right = [], []
        for v in range(VARS):
            here = z[b, v]
            left.append(jnp.where(lane == 0, 0.0, pltpu.roll(here, 1, 1)))
            right.append(jnp.where(lane == cells - 1, 0.0, pltpu.roll(here, cells - 1, 1)))
        beside = apply_coef(side, b, [left, right])
        here = (lane + row % 2) % cells == 2 * b
        found = tuple(
            jnp.where(here, pltpu.roll(side[pl.ds(b * size + 8 * r, 8), :], 2 * b, 1), found[r])
            for r in range(pages)
        )
        return Kept(found, [(resid, (b, i), acc[i] - beside[i]) for i in range(VARS)])

    found = (jnp.zeros((8, cells), jnp.float32),) * pages
    for b in range(REACH):
        kept = block(b, found, wbuf, REACH, 2 * REACH)
        store_all(kept.stores)
        found = kept.carry

    def inner(b, found):
        return block(b + REACH, found, w, 0, blocks)

    found = steps(blocks - REACH, 3, inner, found)
    for r in range(pages):
        coef[r] = found[r]
    store.wait()


def outer_kernel(
    inner, coef, low, tail, swap_a, swap_b, lcols, counts, resid, squares, wbuf
):
    blocks, _, nrhs, cells = inner.shape
    base = lax.axis_index("chain") * blocks
    odd = lax.axis_index("sub") % 2 == 1
    lane = lanes_of(cells)
    zero = jnp.zeros((nrhs, cells), jnp.float32)
    near = []
    for v in range(VARS):
        west = pltpu.roll(jnp.where(odd, swap_a[v], swap_b[v]), 1, 1)
        east = pltpu.roll(jnp.where(odd, swap_b[v], swap_a[v]), cells - 1, 1)
        near.append(jnp.where(lane % 2 == 0, west, east))
    edge = []
    for i in range(VARS):
        rows = []
        for j in range(VARS):
            k = (i * VARS + j) * SLOTS
            rows.append(coef[k // 8, pl.ds(k % 8, 1), :] + coef[(k + 1) // 8, pl.ds((k + 1) % 8, 1), :])
        edge.append(mul_rows(rows, near))
    for v in range(VARS):
        for m in range(REACH):
            wbuf[m, v] = tail[m, v]
        wbuf[REACH, v] = zero
    ends = (lane == 0) | (lane == cells - 1)

    def add(b, values, totals):
        stores, fresh = [], []
        for i in range(VARS):
            other = pltpu.roll(edge[i], (cells - 2 * b) % cells, 1)
            value = values[i] - jnp.where(ends, other, 0.0)
            stores.append((resid, (b, i), value))
            fresh.append(totals[i] + value * value)
        return Kept(tuple(fresh), stores)

    totals = (zero,) * VARS
    stores = []
    for b in range(REACH):
        places = [
            jnp.where(s < REACH, s, REACH) for s in slots(lcols, counts, 0, b, REACH - base, REACH)
        ]
        acc = apply_coef(low, b, [read_block(wbuf, s) for s in places])
        kept = add(b, [inner[b, i] + acc[i] for i in range(VARS)], totals)
        stores += kept.stores
        totals = kept.carry
    store_all(stores)

    def rest(b, totals):
        return add(b + REACH, [inner[b + REACH, i] for i in range(VARS)], totals)

    totals = steps(blocks - REACH, 7, rest, totals)
    total = totals[0]
    for i in range(1, VARS):
        total = total + totals[i]
    sums = jnp.broadcast_to(jnp.sum(total, axis=1, keepdims=True), total.shape)
    row = lax.broadcasted_iota(jnp.int32, total.shape, 0)
    line = jnp.sum(jnp.where(lane == row, sums, 0.0), axis=0, keepdims=True)
    for p in range(squares.shape[0]):
        squares[p] = line


def scale_kernel(entries, resid, squares, out):
    blocks, _, nrhs, cells = resid.shape
    line = squares[0]
    for p in range(1, squares.shape[0]):
        line = line + squares[p]
    lane = lanes_of(cells)
    row = lax.broadcasted_iota(jnp.int32, (nrhs, cells), 0)
    line = jnp.where(lane == row, jnp.broadcast_to(line, (nrhs, cells)), 0.0)
    msq = jnp.sum(line, axis=1, keepdims=True) / entries
    factor = jnp.broadcast_to(lax.rsqrt(msq + 1e-06), (nrhs, cells))

    def block(b, carry):
        return Kept(carry, [(out, (b, v), resid[b, v] * factor) for v in range(VARS)])

    steps(blocks, 6, block)


def call(kernel, outs, args, places, scratch):
    args = [
        pltpu.with_memory_space_constraint(a, p) if p is HBM else a for a, p in zip(args, places)
    ]
    return pl.pallas_call(
        kernel,
        out_shape=[jax.ShapeDtypeStruct(o[0], (o + (jnp.float32,))[2]) for o in outs],
        in_specs=[pl.BlockSpec(memory_space=p) for p in places],
        out_specs=[pl.BlockSpec(memory_space=p) for p in (o[1] for o in outs)],
        scratch_shapes=[VMEM(s, jnp.float32) if isinstance(s, tuple) else s for s in scratch],
        compiler_params=pltpu.CompilerParams(vmem_limit_bytes=VMEM_LIMIT),
    )(*args)


def shards(
    rhs, diag_block, diag_inverse, lower_coef, upper_coef, side_coef, lower_cols, upper_cols, counts
):
    blocks, nvars, nrhs, cells = rhs.shape
    n = lax.axis_size("chain")
    inv = jnp.transpose(diag_inverse, (1, 2, 0, 3))
    low, upp, side = (
        jnp.transpose(a, (0, 2, 3, 1, 4)).reshape(-1, cells)
        for a in (lower_coef, upper_coef, side_coef)
    )
    lcols, ucols, used = lower_cols.T, upper_cols.T, counts.T
    m = lax.axis_size("sub")
    rows = blocks + REACH + 1
    half = n // 2
    parts = -(-len(column_order(nrhs)) // half)
    back = -(-32 // half)
    packed = min(8, half)
    extra = 8 // packed
    wide = 2 * (extra + WIDE // packed)
    sides = [list(range(half)), list(range(half, n))]
    tile = (nrhs, cells)

    mats = (VARS, VARS, SLOTS, blocks + PAD, cells)
    padded = (low.shape[0] + PAD, cells)

    maps, source, mlow, mupp, lcols, ucols, used = call(
        functools.partial(local_kernel, half),
        [((half, parts) + tile, VMEM), (rhs.shape, VMEM), (mats, VMEM), (mats, VMEM)]
        + [(lcols.shape, VMEM, jnp.int32)] * 3,
        (rhs, inv, low, upp, lcols, ucols, used),
        (HBM,) * 7,
        [rhs.shape, (VARS, VARS, blocks + PAD, cells), low.shape, upp.shape]
        + [pltpu.SMEM(lcols.shape, jnp.int32)] * 3
        + [(rows, VARS, nrhs + WIDE, cells), (rows, VARS, nrhs + 2 * WIDE, cells)]
        + [(WIDE * SPACE, cells), pltpu.SemaphoreType.DMA((10,))],
    )
    maps = lax.all_to_all(maps, "chain", 0, 0, tiled=True, axis_index_groups=sides)
    cols, ends, offer = call(
        first_solve_kernel,
        [
            ((half * COLUMNS * 8, cells), VMEM),
            ((half, 4 * extra) + tile, VMEM),
            ((wide,) + tile, VMEM),
        ],
        (maps,),
        (VMEM,),
        [(half, wide) + tile, (wide // 2 * WIDE + PAD, cells)],
    )
    got = lax.ppermute(
        offer, "chain", [p for i in range(half) for p in ((i, i + half), (i + half, i))]
    )
    (states,) = call(
        second_solve_kernel,
        [((half, back) + tile, VMEM)],
        (cols, ends, offer, got),
        (VMEM,) * 4,
        [(half, 2 * extra) + tile, (extra * WIDE + PAD, cells), (half, 4 * extra) + tile],
    )
    states = lax.all_to_all(states, "chain", 0, 0, tiled=True, axis_index_groups=sides)
    z, w, tail, edge, low, side = call(
        functools.partial(sweep_kernel, half),
        [
            (rhs.shape, VMEM),
            ((blocks + 1, VARS) + tile, VMEM),
            ((REACH, VARS) + tile, VMEM),
            ((VARS,) + tile, VMEM),
            (padded, VMEM),
            (padded, VMEM),
        ],
        (states, source, mlow, mupp, lcols, ucols, used, low, side),
        (VMEM,) * 4 + (SMEM,) * 3 + (HBM,) * 2,
        [rhs.shape, (32 * 8, cells), pltpu.SemaphoreType.DMA((2,))],
    )
    tail = lax.ppermute(tail, "chain", [(i, i + 1) for i in range(n - 1)])
    swap_a, swap_b = (
        lax.ppermute(
            edge, "sub", [p for i in range(first, m - 1, 2) for p in ((i, i + 1), (i + 1, i))]
        )
        for first in (0, 1)
    )
    inner, coef, correction = call(
        inner_kernel,
        [
            (rhs.shape, VMEM),
            ((-(-VARS * VARS * SLOTS // 8),) + (8, cells), VMEM),
            (rhs.shape, HBM),
        ],
        (z, w, low, side, lcols, used),
        (VMEM,) * 4 + (SMEM,) * 2,
        [(2 * REACH + 1, VARS) + tile, pltpu.SemaphoreType.DMA],
    )
    resid, squares = call(
        outer_kernel,
        [(rhs.shape, VMEM), ((n * m, 1, cells), VMEM)],
        (inner, coef, low, tail, swap_a, swap_b, lcols, used),
        (VMEM,) * 6 + (SMEM,) * 2,
        [(REACH + 1, VARS) + tile],
    )
    squares = lax.all_to_all(squares, ("chain", "sub"), 0, 0, tiled=True)
    entries = blocks * VARS * cells * n * m
    (residual_unit,) = call(
        functools.partial(scale_kernel, entries),
        [(rhs.shape, VMEM)],
        (resid, squares),
        (VMEM, VMEM),
        [],
    )
    return (correction, residual_unit)


def solution(mesh):
    in_specs = (
        P("chain", None, None, "sub"),
        P("chain", None, None, "sub"),
        P("chain", None, None, "sub"),
        P("chain", None, None, None, "sub"),
        P("chain", None, None, None, "sub"),
        P("chain", None, None, None, "sub"),
        P("chain", None),
        P("chain", None),
        P("chain", None),
    )
    out_specs = (P("chain", None, None, "sub"), P("chain", None, None, "sub"))
    return jax.shard_map(shards, mesh=mesh, in_specs=in_specs, out_specs=out_specs, check_vma=False)
```

```python
import functools

import jax
import jax.numpy as jnp
from jax import lax
from jax.experimental import pallas as pl
from jax.experimental.pallas import tpu as pltpu
from jax.sharding import PartitionSpec as P

VARS = 5
REACH = 3
SLOTS = 2
STATE = REACH * VARS
WIDE = 16
PAD = 8
SPACE = 72
VMEM_LIMIT = 40 * 1024 * 1024

VMEM = pltpu.VMEM
SMEM = pltpu.SMEM
HBM = pltpu.HBM


def lanes_of(cells):
    return lax.broadcasted_iota(jnp.int32, (8, cells), 1)


def block_transpose(items, width, cells):
    count = len(items)
    lane = lanes_of(cells)
    half = 1
    while half < count:
        bit = (lane // (half * width)) % 2 == 1
        out = list(items)
        for a in range(count):
            if a & half:
                continue
            b = a + half
            out[a] = jnp.where(bit, pltpu.roll(items[b], half * width, 1), items[a])
            out[b] = jnp.where(bit, items[b], pltpu.roll(items[a], cells - half * width, 1))
        items = out
        half *= 2
    return items


def spread(ref, place, row):
    return ref[place + (pl.ds(row, 8, stride=0), slice(None))]


def mul_rows(rows, near):
    total = rows[0] * near[0]
    for j in range(1, len(near)):
        total = total + rows[j] * near[j]
    return total


def mul_groups(rows, nears):
    return [mul_rows(rows, [near[g] for near in nears]) for g in range(len(nears[0]))]


def couple(mats, b, nears):
    out = []
    for i in range(VARS):
        parts = [
            mul_groups([spread(mats, (i, j, k), b) for j in range(VARS)], nears[k])
            for k in range(SLOTS)
        ]
        out.append([x + y for x, y in zip(*parts)])
    return out


def apply_coef(coef, b, nears):
    out = []
    for i in range(VARS):
        parts = []
        for k in range(SLOTS):
            place = (b * VARS + i) * VARS * SLOTS + k
            parts.append(
                mul_rows([spread(coef, (), place + SLOTS * j) for j in range(VARS)], nears[k])
            )
        out.append(parts[0] + parts[1])
    return out


def products(inv, coef, out):
    blocks = out.shape[3] - PAD
    stride = VARS * VARS * SLOTS

    def some(o, carry):
        start = o * 8
        left = [[-inv[i, m, pl.ds(start, 8), :] for m in range(VARS)] for i in range(VARS)]
        for k in range(SLOTS):
            stores = []
            for j in range(VARS):
                place = start * stride + j * SLOTS + k
                right = [
                    coef[pl.ds(place + m * VARS * SLOTS, 8, stride=stride), :] for m in range(VARS)
                ]
                for i in range(VARS):
                    here = (i, j, k, pl.ds(start, 8))
                    stores.append((out, here, mul_rows(left[i], right)))
            store_all(stores)
        return carry

    lax.fori_loop(0, blocks // 8, some, 0)


def slots(cols, counts, side, b, shift, empty):
    return [jnp.where(k < counts[side, b], cols[k, b] + shift, empty) for k in range(SLOTS)]


def read_block(buf, place):
    return [buf[place, v] for v in range(VARS)]


def read_groups(buf, place):
    count = buf.shape[2] // 8
    return [[buf[place, v, pl.ds(8 * g, 8), :] for g in range(count)] for v in range(VARS)]


class Kept:
    def __init__(self, carry, stores):
        self.carry, self.stores = carry, stores


def store_all(stores):
    for ref, place, value in stores:
        ref[place] = value


def steps(count, most, body, carry=0):
    unroll = max(u for u in range(1, most + 1) if count % u == 0)

    def chunk(o, carry):
        kept = []
        for u in range(unroll):
            carry = body(o * unroll + u, carry)
            if isinstance(carry, Kept):
                kept += carry.stores
                carry = carry.carry
        store_all(kept)
        return carry

    return lax.fori_loop(0, count // unroll, chunk, carry)


def column_order(nrhs):
    wide_y = nrhs + WIDE
    order = []
    for first, count in ((nrhs, STATE), (wide_y + nrhs, STATE - 1), (wide_y + nrhs + WIDE, STATE)):
        order += [(half, first + j) for half in range(2) for j in range(count)]
    for first in (0, wide_y):
        order += [(half, first + q) for half in range(2) for q in range(nrhs)]
    return order


def local_kernel(
    n,
    rhs_h,
    inv_h,
    low_h,
    upp_h,
    lcols_h,
    ucols_h,
    counts_h,
    out,
    source,
    mlow,
    mupp,
    lcols_v,
    ucols_v,
    counts_v,
    rhs,
    inv,
    low,
    upp,
    lcols,
    ucols,
    counts,
    ybuf,
    zbuf,
    stage,
    sems,
):
    copies = [
        pltpu.make_async_copy(src, dst, sems.at[k])
        for k, (src, dst) in enumerate(
            (
                (inv_h, inv.at[:, :, pl.ds(0, rhs.shape[0]), :]),
                (low_h, low),
                (lcols_h, lcols),
                (counts_h, counts),
                (ucols_h, ucols),
                (rhs_h, rhs),
                (upp_h, upp),
                (lcols_h, lcols_v),
                (ucols_h, ucols_v),
                (counts_h, counts_v),
            )
        )
    ]
    for copy in copies:
        copy.start()
    blocks, _, nrhs, cells = rhs.shape
    base = lax.axis_index("chain") * blocks
    wide_y = nrhs + WIDE
    wide_z = wide_y + WIDE
    row_y = lax.broadcasted_iota(jnp.int32, (wide_y, cells), 0)
    row_z = lax.broadcasted_iota(jnp.int32, (wide_z, cells), 0)
    for m in range(REACH):
        for v in range(VARS):
            q = VARS * m + v
            ybuf[REACH - 1 - m, v] = (row_y == nrhs + q).astype(jnp.float32)
            zbuf[blocks + m, v] = (row_z == wide_y + q).astype(jnp.float32)
    for v in range(VARS):
        ybuf[blocks + REACH, v] = jnp.zeros((wide_y, cells), jnp.float32)
        zbuf[blocks + REACH, v] = jnp.zeros((wide_z, cells), jnp.float32)
    empty = blocks + REACH
    copies[0].wait()
    copies[1].wait()
    products(inv, low, mlow)
    for copy in copies[2:6]:
        copy.wait()

    def first(b, carry):
        nears = [read_groups(ybuf, s) for s in slots(lcols, counts, 0, b, REACH - base, empty)]
        acc = couple(mlow, b, nears)
        right = [rhs[b, i] for i in range(VARS)]
        stores = []
        for i in range(VARS):
            own = mul_rows([spread(inv, (i, j), b) for j in range(VARS)], right)
            stores.append((source, (b, i), own))
            for g in range(len(acc[i])):
                value = own + acc[i][0] if g == 0 else acc[i][g]
                stores.append((ybuf, (b + REACH, i, pl.ds(8 * g, 8)), value))
        store_all(stores)
        return carry

    steps(blocks, 2, first)
    for copy in copies[6:]:
        copy.wait()
    products(inv, upp, mupp)

    def second(e, carry):
        c = blocks - 1 - e
        nears = [read_groups(zbuf, s) for s in slots(ucols, counts, 1, c, -base, empty)]
        acc = couple(mupp, c, nears)
        stores = []
        for i in range(VARS):
            for g in range(len(acc[i])):
                if g < wide_y // 8:
                    value = ybuf[c + REACH, i, 8 * g : 8 * g + 8] + acc[i][g]
                else:
                    value = acc[i][g]
                stores.append((zbuf, (c, i, pl.ds(8 * g, 8)), value))
        store_all(stores)
        return carry

    steps(blocks, 2, second)

    zero = jnp.zeros((8, cells), jnp.float32)
    for i in range(WIDE):
        m, v = i // VARS, i % VARS
        for g in range((wide_y + wide_z) // 8):
            if i == STATE:
                value = zero
            elif g < wide_y // 8:
                value = ybuf[blocks + REACH - 1 - m, v, 8 * g : 8 * g + 8]
            else:
                value = zbuf[m, v, 8 * g - wide_y : 8 * g - wide_y + 8]
            stage[pl.ds(i * SPACE + 8 * g, 8), :] = value

    def column(half, index):
        return stage[pl.ds(half * 8 * SPACE + index, 8, stride=SPACE), :]

    for half in range(2):
        place = STATE * SPACE + nrhs + 8 * half
        stage[pl.ds(place, 8), :] = column(half, wide_y + nrhs + STATE - 1)
    order = column_order(nrhs)
    width = cells // n
    for page in range(out.shape[1]):
        items = [column(*at) for at in order[page * n : (page + 1) * n]]
        items += [zero] * (n - len(items))
        for k, item in enumerate(block_transpose(items, width, cells)):
            out[k, page] = item


def split(value, period, stop, width, cells):
    items = [value]
    lane = lanes_of(cells)
    while period > stop:
        half = period // 2 * width
        bit = lane // half % 2 == 1
        fresh = []
        for item in items:
            other = pltpu.roll(item, half, 1)
            fresh += [jnp.where(bit, other, item), jnp.where(bit, item, other)]
        items = fresh
        period //= 2
    return items


def total_of(terms):
    while len(terms) > 1:
        pairs = [terms[k] + terms[k + 1] for k in range(0, len(terms) - 1, 2)]
        terms = pairs + terms[len(terms) - len(terms) % 2 :]
    return terms[0]


COLUMNS = 6 * STATE - 2


def store_state(buf, state):
    for half in range(2):
        for g, value in enumerate(state[half]):
            buf[pl.ds(g * WIDE + 8 * half, 8), :] = value


def state_rows(buf, count):
    return [[spread(buf, (), g * WIDE + j) for j in range(STATE)] for g in range(count)]


def pass_forward(d, cols, sides, state, buf, keep):
    groups, extra = len(state[0]), sides.shape[1] // 4
    store_state(buf, state)
    rows = state_rows(buf, groups)
    fresh = []
    for half in range(2):
        columns = [cols[pl.ds((d * COLUMNS + half * STATE + j) * 8, 8), :] for j in range(STATE)]
        fresh.append([])
        for g in range(groups):
            total = total_of([c * r for c, r in zip(columns, rows[g])])
            fresh[half].append(total + sides[d, half * extra + g] if g < extra else total)
        first = d * COLUMNS + 2 * STATE + half * (STATE - 1)
        columns = [cols[pl.ds((first + j) * 8, 8), :] for j in range(STATE - 1)]
        start = (d * COLUMNS + STATE + 8 * half) * 8 + 7
        columns.append(cols[pl.ds(start, 8, stride=8), :])
        for g in range(groups):
            total = total_of([c * r for c, r in zip(columns, rows[g])])
            if g < extra:
                total = total + sides[d, (2 + half) * extra + g]
            keep[d, half * groups + g] = total
    return fresh


def pass_back(d, cols, state, buf, keep):
    groups = len(state[0])
    store_state(buf, state)
    rows = state_rows(buf, groups)
    fresh = []
    for half in range(2):
        first = d * COLUMNS + 4 * STATE - 2 + half * STATE
        columns = [cols[pl.ds((first + j) * 8, 8), :] for j in range(STATE)]
        fresh.append(
            [
                total_of([c * r for c, r in zip(columns, rows[g])]) + keep[d, half * groups + g]
                for g in range(groups)
            ]
        )
    return fresh


def flat(state):
    return tuple(state[0] + state[1])


def folded(values):
    groups = len(values) // 2
    return [list(values[:groups]), list(values[groups:])]


def first_solve_kernel(x, cols, sides, leaving, behind, keep, buf):
    n, cells = x.shape[0], x.shape[3]
    width = cells // n
    packed = min(8, n)
    extra, groups = sides.shape[1] // 4, behind.shape[0] // 2
    zero = jnp.zeros((8, cells), jnp.float32)

    def unpack(d, carry):
        values = [x[d, page] for page in range(x.shape[1])]
        for page, value in enumerate(values):
            for k, block in enumerate(split(value, n, packed, width, cells)):
                e = page * n + k * packed
                if e < COLUMNS:
                    for g, item in enumerate(split(block, packed, 1, width, cells)):
                        cols[pl.ds((d * COLUMNS + e + g) * 8, 8), :] = item
                elif e < COLUMNS + 4 * 8:
                    sides[d, (e - COLUMNS) // packed] = block
        return carry

    steps(n, 2, unpack)
    lane = lanes_of(cells)
    row = lax.broadcasted_iota(jnp.int32, (8, cells), 0)
    start = []
    for half in range(2):
        start.append([zero] * extra)
        for g in range(groups - extra):
            column = lane // width % packed + g * packed
            start[half].append((column == row + 8 * half).astype(jnp.float32))

    def ahead(d, state):
        return flat(pass_forward(d, cols, sides, folded(state), buf, keep))

    state = folded(steps(n, 2, ahead, flat(start)))
    for half in range(2):
        for g in range(extra):
            leaving[half * extra + g] = state[half][g]

    def back(e, state):
        return flat(pass_back(n - 1 - e, cols, folded(state), buf, keep))

    state = steps(n, 2, back, (zero,) * (2 * groups))
    for e in range(2 * groups):
        behind[e] = state[e]


def second_solve_kernel(cols, sides, leaving, entering, behind, out, keep, buf, states):
    n, cells = out.shape[0], out.shape[3]
    width = cells // n
    packed = min(8, n)
    extra, groups = sides.shape[1] // 4, behind.shape[0] // 2
    zero = jnp.zeros((8, cells), jnp.float32)
    store_state(buf, folded([leaving[e] for e in range(2 * extra)]))
    rows = state_rows(buf, extra)
    far = []
    for half in range(2):
        columns = []
        for g in range(extra, groups):
            columns += split(behind[half * groups + g], packed, 1, width, cells)
        for g in range(extra):
            total = total_of([c * r for c, r in zip(columns, rows[g])])
            far.append(behind[half * groups + g] + total)

    def ahead(d, state):
        for e in range(2 * extra):
            states[d, e] = state[e]
        return flat(pass_forward(d, cols, sides, folded(state), buf, keep))

    steps(n, 4, ahead, tuple(entering[e] for e in range(2 * extra)))

    def back(e, state):
        d = n - 1 - e
        for e in range(2 * extra):
            states[d, 2 * extra + e] = state[e]
        return flat(pass_back(d, cols, folded(state), buf, keep))

    steps(n, 4, back, tuple(far))
    block = lanes_of(cells) // (packed * width)

    def pack(d, carry):
        for page in range(out.shape[1]):
            total = zero
            for r in range(4 * extra):
                if packed * r // n == page:
                    total = jnp.where(block == packed * r % n // packed, states[d, r], total)
            out[d, page] = total
        return carry

    steps(n, 4, pack)


def sweep_kernel(
    n,
    states,
    source,
    mlow,
    mupp,
    lcols,
    ucols,
    counts,
    low_h,
    side_h,
    zout,
    wout,
    tail,
    edge,
    low,
    side,
    ybuf,
    stage,
    sems,
):
    total = low_h.shape[0]
    copies = [
        pltpu.make_async_copy(src, dst.at[pl.ds(0, total), :], sems.at[k])
        for k, (src, dst) in enumerate(((low_h, low), (side_h, side)))
    ]
    for copy in copies:
        copy.start()
    blocks, _, nrhs, cells = source.shape
    base = lax.axis_index("chain") * blocks
    width = cells // n
    zero = jnp.zeros((nrhs, cells), jnp.float32)
    items = []
    for r in range(states.shape[1]):
        items += block_transpose([states[k, r] for k in range(n)], width, cells)
    for e in range(32):
        stage[pl.ds(8 * e, 8), :] = items[e]

    def entering(start):
        rows = [stage[pl.ds(start + q // 8 * 64 + q % 8, 8, stride=8), :] for q in range(STATE)]
        return tuple(rows)

    lane = lanes_of(cells)
    for v in range(VARS):
        wout[blocks, v] = zero

    def near(window, b, sign, cols, side):
        nears = []
        for k in range(SLOTS):
            off = sign * (cols[k, b] - base - b)
            picks = []
            for v in range(VARS):
                value = window[(REACH - 1) * VARS + v]
                for d in range(REACH - 1):
                    value = jnp.where(off == d + 1, window[d * VARS + v], value)
                picks.append(value if k == 0 else jnp.where(k < counts[side, b], value, 0.0))
            nears.append([[value] for value in picks])
        return nears

    def first(b, window):
        acc = couple(mlow, b, near(window, b, -1, lcols, 0))
        fresh = tuple(source[b, i] + acc[i][0] for i in range(VARS))
        return Kept(fresh + window[: STATE - VARS], [(ybuf, (b, i), fresh[i]) for i in range(VARS)])

    steps(blocks, 4, first, entering(0))

    def second(e, carry):
        c = blocks - 1 - e
        window, edges = carry[:STATE], list(carry[STATE:])
        acc = couple(mupp, c, near(window, c, 1, ucols, 1))
        fresh = tuple(ybuf[c, i] + acc[i][0] for i in range(VARS))
        here = (lane == 2 * c) | (lane == (2 * c + cells - 1) % cells)
        stores = []
        for i in range(VARS):
            stores += [(zout, (c, i), fresh[i]), (wout, (c, i), acc[i][0])]
            edges[i] = jnp.where(here, pltpu.roll(fresh[i], 2 * c, 1), edges[i])
        return Kept(fresh + window[: STATE - VARS] + tuple(edges), stores)

    carry = steps(blocks, 4, second, entering(128) + (zero,) * VARS)
    for v in range(VARS):
        edge[v] = carry[STATE + v]
    for m in range(REACH):
        for v in range(VARS):
            tail[m, v] = wout[blocks - REACH + m, v]
    for copy in copies:
        copy.wait()


def inner_kernel(z, w, low, side, lcols, counts, resid, coef, correction, wbuf, sem):
    store = pltpu.make_async_copy(z, correction, sem)
    store.start()
    blocks, _, nrhs, cells = z.shape
    base = lax.axis_index("chain") * blocks
    lane = lanes_of(cells)
    zero = jnp.zeros((nrhs, cells), jnp.float32)
    for v in range(VARS):
        for m in range(REACH):
            wbuf[m, v] = zero
            wbuf[m + REACH, v] = w[m, v]
        wbuf[2 * REACH, v] = zero
    pages = coef.shape[0]
    size = VARS * VARS * SLOTS
    row = lax.broadcasted_iota(jnp.int32, (8, cells), 0)

    def block(b, found, buf, shift, empty):
        nears = [read_block(buf, s) for s in slots(lcols, counts, 0, b, shift - base, empty)]
        acc = apply_coef(low, b, nears)
        left, right = [], []
        for v in range(VARS):
            here = z[b, v]
            left.append(jnp.where(lane == 0, 0.0, pltpu.roll(here, 1, 1)))
            right.append(jnp.where(lane == cells - 1, 0.0, pltpu.roll(here, cells - 1, 1)))
        beside = apply_coef(side, b, [left, right])
        here = (lane + row % 2) % cells == 2 * b
        found = tuple(
            jnp.where(here, pltpu.roll(side[pl.ds(b * size + 8 * r, 8), :], 2 * b, 1), found[r])
            for r in range(pages)
        )
        return Kept(found, [(resid, (b, i), acc[i] + beside[i]) for i in range(VARS)])

    found = (jnp.zeros((8, cells), jnp.float32),) * pages
    for b in range(REACH):
        kept = block(b, found, wbuf, REACH, 2 * REACH)
        store_all(kept.stores)
        found = kept.carry

    def inner(b, found):
        return block(b + REACH, found, w, 0, blocks)

    found = steps(blocks - REACH, 3, inner, found)
    for r in range(pages):
        coef[r] = found[r]
    store.wait()


def outer_kernel(
    inner, coef, low, tail, swap_a, swap_b, lcols, counts, resid, squares, wbuf
):
    blocks, _, nrhs, cells = inner.shape
    base = lax.axis_index("chain") * blocks
    odd = lax.axis_index("sub") % 2 == 1
    lane = lanes_of(cells)
    zero = jnp.zeros((nrhs, cells), jnp.float32)
    near = []
    for v in range(VARS):
        west = pltpu.roll(jnp.where(odd, swap_a[v], swap_b[v]), 1, 1)
        east = pltpu.roll(jnp.where(odd, swap_b[v], swap_a[v]), cells - 1, 1)
        near.append(jnp.where(lane % 2 == 0, west, east))
    edge = []
    for i in range(VARS):
        rows = []
        for j in range(VARS):
            k = (i * VARS + j) * SLOTS
            rows.append(coef[k // 8, pl.ds(k % 8, 1), :] + coef[(k + 1) // 8, pl.ds((k + 1) % 8, 1), :])
        edge.append(mul_rows(rows, near))
    for v in range(VARS):
        for m in range(REACH):
            wbuf[m, v] = tail[m, v]
        wbuf[REACH, v] = zero
    ends = (lane == 0) | (lane == cells - 1)

    def add(b, values, totals):
        stores, fresh = [], []
        for i in range(VARS):
            other = pltpu.roll(edge[i], (cells - 2 * b) % cells, 1)
            value = values[i] + jnp.where(ends, other, 0.0)
            stores.append((resid, (b, i), value))
            fresh.append(totals[i] + value * value)
        return Kept(tuple(fresh), stores)

    totals = (zero,) * VARS
    stores = []
    for b in range(REACH):
        places = [
            jnp.where(s < REACH, s, REACH) for s in slots(lcols, counts, 0, b, REACH - base, REACH)
        ]
        acc = apply_coef(low, b, [read_block(wbuf, s) for s in places])
        kept = add(b, [inner[b, i] + acc[i] for i in range(VARS)], totals)
        stores += kept.stores
        totals = kept.carry
    store_all(stores)

    def rest(b, totals):
        return add(b + REACH, [inner[b + REACH, i] for i in range(VARS)], totals)

    totals = steps(blocks - REACH, 7, rest, totals)
    total = totals[0]
    for i in range(1, VARS):
        total = total + totals[i]
    sums = jnp.broadcast_to(jnp.sum(total, axis=1, keepdims=True), total.shape)
    row = lax.broadcasted_iota(jnp.int32, total.shape, 0)
    line = jnp.sum(jnp.where(lane == row, sums, 0.0), axis=0, keepdims=True)
    for p in range(squares.shape[0]):
        squares[p] = line


def scale_kernel(entries, resid, squares, out):
    blocks, _, nrhs, cells = resid.shape
    line = squares[0]
    for p in range(1, squares.shape[0]):
        line = line + squares[p]
    lane = lanes_of(cells)
    row = lax.broadcasted_iota(jnp.int32, (nrhs, cells), 0)
    line = jnp.where(lane == row, jnp.broadcast_to(line, (nrhs, cells)), 0.0)
    msq = jnp.sum(line, axis=1, keepdims=True) / entries
    factor = jnp.broadcast_to(-lax.rsqrt(msq + 1e-06), (nrhs, cells))

    def block(b, carry):
        return Kept(carry, [(out, (b, v), resid[b, v] * factor) for v in range(VARS)])

    steps(blocks, 6, block)


def call(kernel, outs, args, places, scratch):
    args = [
        pltpu.with_memory_space_constraint(a, p) if p is HBM else a for a, p in zip(args, places)
    ]
    return pl.pallas_call(
        kernel,
        out_shape=[jax.ShapeDtypeStruct(o[0], (o + (jnp.float32,))[2]) for o in outs],
        in_specs=[pl.BlockSpec(memory_space=p) for p in places],
        out_specs=[pl.BlockSpec(memory_space=p) for p in (o[1] for o in outs)],
        scratch_shapes=[VMEM(s, jnp.float32) if isinstance(s, tuple) else s for s in scratch],
        compiler_params=pltpu.CompilerParams(vmem_limit_bytes=VMEM_LIMIT),
    )(*args)


def shards(
    rhs, diag_block, diag_inverse, lower_coef, upper_coef, side_coef, lower_cols, upper_cols, counts
):
    blocks, nvars, nrhs, cells = rhs.shape
    n = lax.axis_size("chain")
    inv = jnp.transpose(diag_inverse, (1, 2, 0, 3))
    low, upp, side = (
        jnp.transpose(a, (0, 2, 3, 1, 4)).reshape(-1, cells)
        for a in (lower_coef, upper_coef, side_coef)
    )
    lcols, ucols, used = lower_cols.T, upper_cols.T, counts.T
    m = lax.axis_size("sub")
    rows = blocks + REACH + 1
    half = n // 2
    parts = -(-len(column_order(nrhs)) // half)
    back = -(-32 // half)
    packed = min(8, half)
    extra = 8 // packed
    wide = 2 * (extra + WIDE // packed)
    sides = [list(range(half)), list(range(half, n))]
    tile = (nrhs, cells)

    mats = (VARS, VARS, SLOTS, blocks + PAD, cells)
    padded = (low.shape[0] + PAD, cells)

    maps, source, mlow, mupp, lcols, ucols, used = call(
        functools.partial(local_kernel, half),
        [((half, parts) + tile, VMEM), (rhs.shape, VMEM), (mats, VMEM), (mats, VMEM)]
        + [(lcols.shape, VMEM, jnp.int32)] * 3,
        (rhs, inv, low, upp, lcols, ucols, used),
        (HBM,) * 7,
        [rhs.shape, (VARS, VARS, blocks + PAD, cells), low.shape, upp.shape]
        + [pltpu.SMEM(lcols.shape, jnp.int32)] * 3
        + [(rows, VARS, nrhs + WIDE, cells), (rows, VARS, nrhs + 2 * WIDE, cells)]
        + [(WIDE * SPACE, cells), pltpu.SemaphoreType.DMA((10,))],
    )
    maps = lax.all_to_all(maps, "chain", 0, 0, tiled=True, axis_index_groups=sides)
    cols, ends, leaving, behind = call(
        first_solve_kernel,
        [
            ((half * COLUMNS * 8, cells), VMEM),
            ((half, 4 * extra) + tile, VMEM),
            ((2 * extra,) + tile, VMEM),
            ((wide,) + tile, VMEM),
        ],
        (maps,),
        (VMEM,),
        [(half, wide) + tile, (wide // 2 * WIDE + PAD, cells)],
    )
    entering = lax.ppermute(leaving, "chain", [(i, i + half) for i in range(half)])
    behind = lax.ppermute(behind, "chain", [(i + half, i) for i in range(half)])
    (states,) = call(
        second_solve_kernel,
        [((half, back) + tile, VMEM)],
        (cols, ends, leaving, entering, behind),
        (VMEM,) * 5,
        [(half, 2 * extra) + tile, (extra * WIDE + PAD, cells), (half, 4 * extra) + tile],
    )
    states = lax.all_to_all(states, "chain", 0, 0, tiled=True, axis_index_groups=sides)
    z, w, tail, edge, low, side = call(
        functools.partial(sweep_kernel, half),
        [
            (rhs.shape, VMEM),
            ((blocks + 1, VARS) + tile, VMEM),
            ((REACH, VARS) + tile, VMEM),
            ((VARS,) + tile, VMEM),
            (padded, VMEM),
            (padded, VMEM),
        ],
        (states, source, mlow, mupp, lcols, ucols, used, low, side),
        (VMEM,) * 4 + (SMEM,) * 3 + (HBM,) * 2,
        [rhs.shape, (32 * 8, cells), pltpu.SemaphoreType.DMA((2,))],
    )
    tail = lax.ppermute(tail, "chain", [(i, i + 1) for i in range(n - 1)])
    swap_b, swap_a = (
        lax.ppermute(
            edge, "sub", [p for i in range(first, m - 1, 2) for p in ((i, i + 1), (i + 1, i))]
        )
        for first in (1, 0)
    )
    inner, coef, correction = call(
        inner_kernel,
        [
            (rhs.shape, VMEM),
            ((-(-VARS * VARS * SLOTS // 8),) + (8, cells), VMEM),
            (rhs.shape, HBM),
        ],
        (z, w, low, side, lcols, used),
        (VMEM,) * 4 + (SMEM,) * 2,
        [(2 * REACH + 1, VARS) + tile, pltpu.SemaphoreType.DMA],
    )
    resid, squares = call(
        outer_kernel,
        [(rhs.shape, VMEM), ((n * m, 1, cells), VMEM)],
        (inner, coef, low, tail, swap_a, swap_b, lcols, used),
        (VMEM,) * 6 + (SMEM,) * 2,
        [(REACH + 1, VARS) + tile],
    )
    squares = lax.all_to_all(squares, ("chain", "sub"), 0, 0, tiled=True)
    entries = blocks * VARS * cells * n * m
    (residual_unit,) = call(
        functools.partial(scale_kernel, entries),
        [(rhs.shape, VMEM)],
        (resid, squares),
        (VMEM, VMEM),
        [],
    )
    return (correction, residual_unit)


def solution(mesh):
    in_specs = (
        P("chain", None, None, "sub"),
        P("chain", None, None, "sub"),
        P("chain", None, None, "sub"),
        P("chain", None, None, None, "sub"),
        P("chain", None, None, None, "sub"),
        P("chain", None, None, None, "sub"),
        P("chain", None),
        P("chain", None),
        P("chain", None),
    )
    out_specs = (P("chain", None, None, "sub"), P("chain", None, None, "sub"))
    return jax.shard_map(shards, mesh=mesh, in_specs=in_specs, out_specs=out_specs, check_vma=False)
```

```python
import functools

import jax
import jax.numpy as jnp
from jax import lax
from jax.experimental import pallas as pl
from jax.experimental.pallas import tpu as pltpu
from jax.sharding import PartitionSpec as P

VARS = 5
REACH = 3
SLOTS = 2
STATE = REACH * VARS
WIDE = 16
PAD = 8
SPACE = 72
VMEM_LIMIT = 40 * 1024 * 1024

VMEM = pltpu.VMEM
SMEM = pltpu.SMEM
HBM = pltpu.HBM


def lanes_of(cells):
    return lax.broadcasted_iota(jnp.int32, (8, cells), 1)


def block_transpose(items, width, cells):
    count = len(items)
    lane = lanes_of(cells)
    half = 1
    while half < count:
        bit = (lane // (half * width)) % 2 == 1
        out = list(items)
        for a in range(count):
            if a & half:
                continue
            b = a + half
            out[a] = jnp.where(bit, pltpu.roll(items[b], half * width, 1), items[a])
            out[b] = jnp.where(bit, items[b], pltpu.roll(items[a], cells - half * width, 1))
        items = out
        half *= 2
    return items


def spread(ref, place, row):
    return ref[place + (pl.ds(row, 8, stride=0), slice(None))]


def mul_rows(rows, near):
    total = rows[0] * near[0]
    for j in range(1, len(near)):
        total = total + rows[j] * near[j]
    return total


def mul_groups(rows, nears):
    return [mul_rows(rows, [near[g] for near in nears]) for g in range(len(nears[0]))]


def couple(mats, b, nears):
    out = []
    for i in range(VARS):
        parts = [
            mul_groups([spread(mats, (i, j, k), b) for j in range(VARS)], nears[k])
            for k in range(SLOTS)
        ]
        out.append([x + y for x, y in zip(*parts)])
    return out


def apply_coef(coef, b, nears):
    out = []
    for i in range(VARS):
        parts = []
        for k in range(SLOTS):
            place = (b * VARS + i) * VARS * SLOTS + k
            parts.append(
                mul_rows([spread(coef, (), place + SLOTS * j) for j in range(VARS)], nears[k])
            )
        out.append(parts[0] + parts[1])
    return out


def products(inv, coef, out):
    blocks = out.shape[3] - PAD
    stride = VARS * VARS * SLOTS

    def some(o, carry):
        start = o * 8
        left = [[-inv[i, m, pl.ds(start, 8), :] for m in range(VARS)] for i in range(VARS)]
        for k in range(SLOTS):
            stores = []
            for j in range(VARS):
                place = start * stride + j * SLOTS + k
                right = [
                    coef[pl.ds(place + m * VARS * SLOTS, 8, stride=stride), :] for m in range(VARS)
                ]
                for i in range(VARS):
                    here = (i, j, k, pl.ds(start, 8))
                    stores.append((out, here, mul_rows(left[i], right)))
            store_all(stores)
        return carry

    lax.fori_loop(0, blocks // 8, some, 0)


def slots(cols, counts, side, b, shift, empty):
    return [jnp.where(k < counts[side, b], cols[k, b] + shift, empty) for k in range(SLOTS)]


def read_block(buf, place):
    return [buf[place, v] for v in range(VARS)]


def read_groups(buf, place):
    count = buf.shape[2] // 8
    return [[buf[place, v, pl.ds(8 * g, 8), :] for g in range(count)] for v in range(VARS)]


class Kept:
    def __init__(self, carry, stores):
        self.carry, self.stores = carry, stores


def store_all(stores):
    for ref, place, value in stores:
        ref[place] = value


def steps(count, most, body, carry=0):
    unroll = max(u for u in range(1, most + 1) if count % u == 0)

    def chunk(o, carry):
        kept = []
        for u in range(unroll):
            carry = body(o * unroll + u, carry)
            if isinstance(carry, Kept):
                kept += carry.stores
                carry = carry.carry
        store_all(kept)
        return carry

    return lax.fori_loop(0, count // unroll, chunk, carry)


def column_order(nrhs):
    wide_y = nrhs + WIDE
    order = []
    for first, count in ((nrhs, STATE), (wide_y + nrhs, STATE - 1), (wide_y + nrhs + WIDE, STATE)):
        order += [(half, first + j) for half in range(2) for j in range(count)]
    for first in (0, wide_y):
        order += [(half, first + q) for half in range(2) for q in range(nrhs)]
    return order


def local_kernel(
    n,
    rhs_h,
    inv_h,
    low_h,
    upp_h,
    lcols_h,
    ucols_h,
    counts_h,
    out,
    source,
    mlow,
    mupp,
    lcols_v,
    ucols_v,
    counts_v,
    rhs,
    inv,
    low,
    upp,
    lcols,
    ucols,
    counts,
    ybuf,
    zbuf,
    stage,
    sems,
):
    copies = [
        pltpu.make_async_copy(src, dst, sems.at[k])
        for k, (src, dst) in enumerate(
            (
                (inv_h, inv.at[:, :, pl.ds(0, rhs.shape[0]), :]),
                (low_h, low),
                (lcols_h, lcols),
                (counts_h, counts),
                (ucols_h, ucols),
                (rhs_h, rhs),
                (upp_h, upp),
                (lcols_h, lcols_v),
                (ucols_h, ucols_v),
                (counts_h, counts_v),
            )
        )
    ]
    for copy in copies:
        copy.start()
    blocks, _, nrhs, cells = rhs.shape
    base = lax.axis_index("chain") * blocks
    wide_y = nrhs + WIDE
    wide_z = wide_y + WIDE
    row_y = lax.broadcasted_iota(jnp.int32, (wide_y, cells), 0)
    row_z = lax.broadcasted_iota(jnp.int32, (wide_z, cells), 0)
    for m in range(REACH):
        for v in range(VARS):
            q = VARS * m + v
            ybuf[REACH - 1 - m, v] = (row_y == nrhs + q).astype(jnp.float32)
            zbuf[blocks + m, v] = (row_z == wide_y + q).astype(jnp.float32)
    for v in range(VARS):
        ybuf[blocks + REACH, v] = jnp.zeros((wide_y, cells), jnp.float32)
        zbuf[blocks + REACH, v] = jnp.zeros((wide_z, cells), jnp.float32)
    empty = blocks + REACH
    copies[0].wait()
    copies[1].wait()
    products(inv, low, mlow)
    for copy in copies[2:6]:
        copy.wait()

    def first(b, carry):
        nears = [read_groups(ybuf, s) for s in slots(lcols, counts, 0, b, REACH - base, empty)]
        acc = couple(mlow, b, nears)
        right = [rhs[b, i] for i in range(VARS)]
        stores = []
        for i in range(VARS):
            own = mul_rows([spread(inv, (i, j), b) for j in range(VARS)], right)
            stores.append((source, (b, i), own))
            for g in range(len(acc[i])):
                value = own + acc[i][0] if g == 0 else acc[i][g]
                stores.append((ybuf, (b + REACH, i, pl.ds(8 * g, 8)), value))
        store_all(stores)
        return carry

    steps(blocks, 2, first)
    for copy in copies[6:]:
        copy.wait()
    products(inv, upp, mupp)

    def second(e, carry):
        c = blocks - 1 - e
        nears = [read_groups(zbuf, s) for s in slots(ucols, counts, 1, c, -base, empty)]
        acc = couple(mupp, c, nears)
        stores = []
        for i in range(VARS):
            for g in range(len(acc[i])):
                if g < wide_y // 8:
                    value = ybuf[c + REACH, i, 8 * g : 8 * g + 8] + acc[i][g]
                else:
                    value = acc[i][g]
                stores.append((zbuf, (c, i, pl.ds(8 * g, 8)), value))
        store_all(stores)
        return carry

    steps(blocks, 2, second)

    zero = jnp.zeros((8, cells), jnp.float32)
    for i in range(WIDE):
        m, v = i // VARS, i % VARS
        for g in range((wide_y + wide_z) // 8):
            if i == STATE:
                value = zero
            elif g < wide_y // 8:
                value = ybuf[blocks + REACH - 1 - m, v, 8 * g : 8 * g + 8]
            else:
                value = zbuf[m, v, 8 * g - wide_y : 8 * g - wide_y + 8]
            stage[pl.ds(i * SPACE + 8 * g, 8), :] = value

    def column(half, index):
        return stage[pl.ds(half * 8 * SPACE + index, 8, stride=SPACE), :]

    for half in range(2):
        place = STATE * SPACE + nrhs + 8 * half
        stage[pl.ds(place, 8), :] = column(half, wide_y + nrhs + STATE - 1)
    order = column_order(nrhs)
    width = cells // n
    for page in range(out.shape[1]):
        items = [column(*at) for at in order[page * n : (page + 1) * n]]
        items += [zero] * (n - len(items))
        for k, item in enumerate(block_transpose(items, width, cells)):
            out[k, page] = item


def split(value, period, stop, width, cells):
    items = [value]
    lane = lanes_of(cells)
    while period > stop:
        half = period // 2 * width
        bit = lane // half % 2 == 1
        fresh = []
        for item in items:
            other = pltpu.roll(item, half, 1)
            fresh += [jnp.where(bit, other, item), jnp.where(bit, item, other)]
        items = fresh
        period //= 2
    return items


def total_of(terms):
    while len(terms) > 1:
        pairs = [terms[k] + terms[k + 1] for k in range(0, len(terms) - 1, 2)]
        terms = pairs + terms[len(terms) - len(terms) % 2 :]
    return terms[0]


COLUMNS = 6 * STATE - 2


def store_state(buf, state):
    for half in range(2):
        for g, value in enumerate(state[half]):
            buf[pl.ds(g * WIDE + 8 * half, 8), :] = value


def state_rows(buf, count):
    return [[spread(buf, (), g * WIDE + j) for j in range(STATE)] for g in range(count)]


def pass_forward(d, cols, sides, state, buf, keep):
    groups, extra = len(state[0]), sides.shape[1] // 4
    store_state(buf, state)
    rows = state_rows(buf, groups)
    fresh = []
    for half in range(2):
        columns = [cols[pl.ds((d * COLUMNS + half * STATE + j) * 8, 8), :] for j in range(STATE)]
        fresh.append([])
        for g in range(groups):
            total = total_of([c * r for c, r in zip(columns, rows[g])])
            fresh[half].append(total + sides[d, half * extra + g] if g < extra else total)
        first = d * COLUMNS + 2 * STATE + half * (STATE - 1)
        columns = [cols[pl.ds((first + j) * 8, 8), :] for j in range(STATE - 1)]
        start = (d * COLUMNS + STATE + 8 * half) * 8 + 7
        columns.append(cols[pl.ds(start, 8, stride=8), :])
        for g in range(groups):
            total = total_of([c * r for c, r in zip(columns, rows[g])])
            if g < extra:
                total = total + sides[d, (2 + half) * extra + g]
            keep[d, half * groups + g] = total
    return fresh


def pass_back(d, cols, state, buf, keep):
    groups = len(state[0])
    store_state(buf, state)
    rows = state_rows(buf, groups)
    fresh = []
    for half in range(2):
        first = d * COLUMNS + 4 * STATE - 2 + half * STATE
        columns = [cols[pl.ds((first + j) * 8, 8), :] for j in range(STATE)]
        fresh.append(
            [
                total_of([c * r for c, r in zip(columns, rows[g])]) + keep[d, half * groups + g]
                for g in range(groups)
            ]
        )
    return fresh


def flat(state):
    return tuple(state[0] + state[1])


def folded(values):
    groups = len(values) // 2
    return [list(values[:groups]), list(values[groups:])]


def first_solve_kernel(x, cols, sides, offer, keep, buf):
    n, cells = x.shape[0], x.shape[3]
    width = cells // n
    packed = min(8, n)
    extra, groups = sides.shape[1] // 4, offer.shape[0] // 2
    zero = jnp.zeros((8, cells), jnp.float32)

    def unpack(d, carry):
        values = [x[d, page] for page in range(x.shape[1])]
        for page, value in enumerate(values):
            for k, block in enumerate(split(value, n, packed, width, cells)):
                e = page * n + k * packed
                if e < COLUMNS:
                    for g, item in enumerate(split(block, packed, 1, width, cells)):
                        cols[pl.ds((d * COLUMNS + e + g) * 8, 8), :] = item
                elif e < COLUMNS + 4 * 8:
                    sides[d, (e - COLUMNS) // packed] = block
        return carry

    steps(n, 2, unpack)
    lane = lanes_of(cells)
    row = lax.broadcasted_iota(jnp.int32, (8, cells), 0)
    start = []
    for half in range(2):
        start.append([zero] * extra)
        for g in range(groups - extra):
            column = lane // width % packed + g * packed
            start[half].append((column == row + 8 * half).astype(jnp.float32))

    def ahead(d, state):
        return flat(pass_forward(d, cols, sides, folded(state), buf, keep))

    leaving = steps(n, 2, ahead, flat(start))

    def back(e, state):
        return flat(pass_back(n - 1 - e, cols, folded(state), buf, keep))

    left = steps(n, 2, back, (zero,) * (2 * groups))
    is_left = lax.axis_index("chain") < n
    for e in range(2 * groups):
        offer[e] = jnp.where(is_left, leaving[e], left[e])


def second_solve_kernel(cols, sides, mine, got, out, keep, buf, states):
    n, cells = out.shape[0], out.shape[3]
    width = cells // n
    packed = min(8, n)
    extra, groups = sides.shape[1] // 4, mine.shape[0] // 2
    zero = jnp.zeros((8, cells), jnp.float32)
    is_left = lax.axis_index("chain") < n
    store_state(buf, [[mine[half * groups + g] for g in range(extra)] for half in range(2)])
    rows = state_rows(buf, extra)
    entering, far = [], []
    for half in range(2):
        columns = []
        for g in range(extra, groups):
            columns += split(got[half * groups + g], packed, 1, width, cells)
        for g in range(extra):
            known = got[half * groups + g]
            total = total_of([c * r for c, r in zip(columns, rows[g])])
            entering.append(jnp.where(is_left, 0.0, known))
            far.append(jnp.where(is_left, known + total, 0.0))

    def ahead(d, state):
        for e in range(2 * extra):
            states[d, e] = state[e]
        return flat(pass_forward(d, cols, sides, folded(state), buf, keep))

    steps(n, 4, ahead, tuple(entering))

    def back(e, state):
        d = n - 1 - e
        for e in range(2 * extra):
            states[d, 2 * extra + e] = state[e]
        return flat(pass_back(d, cols, folded(state), buf, keep))

    steps(n, 4, back, tuple(far))
    block = lanes_of(cells) // (packed * width)

    def pack(d, carry):
        for page in range(out.shape[1]):
            total = zero
            for r in range(4 * extra):
                if packed * r // n == page:
                    total = jnp.where(block == packed * r % n // packed, states[d, r], total)
            out[d, page] = total
        return carry

    steps(n, 4, pack)


def sweep_kernel(
    n,
    states,
    source,
    mlow,
    mupp,
    lcols,
    ucols,
    counts,
    low_h,
    side_h,
    zout,
    wout,
    tail,
    edge,
    low,
    side,
    ybuf,
    stage,
    sems,
):
    total = low_h.shape[0]
    copies = [
        pltpu.make_async_copy(src, dst.at[pl.ds(0, total), :], sems.at[k])
        for k, (src, dst) in enumerate(((low_h, low), (side_h, side)))
    ]
    for copy in copies:
        copy.start()
    blocks, _, nrhs, cells = source.shape
    base = lax.axis_index("chain") * blocks
    width = cells // n
    zero = jnp.zeros((nrhs, cells), jnp.float32)
    items = []
    for r in range(states.shape[1]):
        items += block_transpose([states[k, r] for k in range(n)], width, cells)
    for e in range(32):
        stage[pl.ds(8 * e, 8), :] = items[e]

    def entering(start):
        rows = [stage[pl.ds(start + q // 8 * 64 + q % 8, 8, stride=8), :] for q in range(STATE)]
        return tuple(rows)

    lane = lanes_of(cells)
    for v in range(VARS):
        wout[blocks, v] = zero

    def near(window, b, sign, cols, side):
        nears = []
        for k in range(SLOTS):
            off = sign * (cols[k, b] - base - b)
            picks = []
            for v in range(VARS):
                value = window[(REACH - 1) * VARS + v]
                for d in range(REACH - 1):
                    value = jnp.where(off == d + 1, window[d * VARS + v], value)
                picks.append(value if k == 0 else jnp.where(k < counts[side, b], value, 0.0))
            nears.append([[value] for value in picks])
        return nears

    def first(b, window):
        acc = couple(mlow, b, near(window, b, -1, lcols, 0))
        fresh = tuple(source[b, i] + acc[i][0] for i in range(VARS))
        return Kept(fresh + window[: STATE - VARS], [(ybuf, (b, i), fresh[i]) for i in range(VARS)])

    steps(blocks, 4, first, entering(0))

    def second(e, carry):
        c = blocks - 1 - e
        window, edges = carry[:STATE], list(carry[STATE:])
        acc = couple(mupp, c, near(window, c, 1, ucols, 1))
        fresh = tuple(ybuf[c, i] + acc[i][0] for i in range(VARS))
        here = (lane == 2 * c) | (lane == (2 * c + cells - 1) % cells)
        stores = []
        for i in range(VARS):
            stores += [(zout, (c, i), fresh[i]), (wout, (c, i), acc[i][0])]
            edges[i] = jnp.where(here, pltpu.roll(fresh[i], 2 * c, 1), edges[i])
        return Kept(fresh + window[: STATE - VARS] + tuple(edges), stores)

    carry = steps(blocks, 4, second, entering(128) + (zero,) * VARS)
    for v in range(VARS):
        edge[v] = carry[STATE + v]
    for m in range(REACH):
        for v in range(VARS):
            tail[m, v] = wout[blocks - REACH + m, v]
    for copy in copies:
        copy.wait()


def inner_kernel(z, w, low, side, lcols, counts, resid, coef, correction, wbuf, sem):
    store = pltpu.make_async_copy(z, correction, sem)
    store.start()
    blocks, _, nrhs, cells = z.shape
    base = lax.axis_index("chain") * blocks
    lane = lanes_of(cells)
    zero = jnp.zeros((nrhs, cells), jnp.float32)
    for v in range(VARS):
        for m in range(REACH):
            wbuf[m, v] = zero
            wbuf[m + REACH, v] = w[m, v]
        wbuf[2 * REACH, v] = zero
    pages = coef.shape[0]
    size = VARS * VARS * SLOTS
    row = lax.broadcasted_iota(jnp.int32, (8, cells), 0)

    def block(b, found, buf, shift, empty):
        nears = [read_block(buf, s) for s in slots(lcols, counts, 0, b, shift - base, empty)]
        acc = apply_coef(low, b, nears)
        left, right = [], []
        for v in range(VARS):
            here = z[b, v]
            left.append(jnp.where(lane == 0, 0.0, pltpu.roll(here, 1, 1)))
            right.append(jnp.where(lane == cells - 1, 0.0, pltpu.roll(here, cells - 1, 1)))
        beside = apply_coef(side, b, [left, right])
        here = (lane + row % 2) % cells == 2 * b
        found = tuple(
            jnp.where(here, pltpu.roll(side[pl.ds(b * size + 8 * r, 8), :], 2 * b, 1), found[r])
            for r in range(pages)
        )
        return Kept(found, [(resid, (b, i), acc[i] + beside[i]) for i in range(VARS)])

    found = (jnp.zeros((8, cells), jnp.float32),) * pages
    for b in range(REACH):
        kept = block(b, found, wbuf, REACH, 2 * REACH)
        store_all(kept.stores)
        found = kept.carry

    def inner(b, found):
        return block(b + REACH, found, w, 0, blocks)

    found = steps(blocks - REACH, 3, inner, found)
    for r in range(pages):
        coef[r] = found[r]
    store.wait()


def outer_kernel(
    inner, coef, low, tail, swap_a, swap_b, lcols, counts, resid, squares, wbuf
):
    blocks, _, nrhs, cells = inner.shape
    base = lax.axis_index("chain") * blocks
    first_block = lax.axis_index("chain") == 0
    place = lax.axis_index("sub")
    odd = place % 2 == 1
    first, last = place == 0, place == lax.axis_size("sub") - 1
    lane = lanes_of(cells)
    zero = jnp.zeros((nrhs, cells), jnp.float32)
    near = []
    for v in range(VARS):
        west = jnp.where(first, 0.0, jnp.where(odd, swap_a[v], swap_b[v]))
        east = jnp.where(last, 0.0, jnp.where(odd, swap_b[v], swap_a[v]))
        west, east = pltpu.roll(west, 1, 1), pltpu.roll(east, cells - 1, 1)
        near.append(jnp.where(lane % 2 == 0, west, east))
    edge = []
    for i in range(VARS):
        rows = []
        for j in range(VARS):
            k = (i * VARS + j) * SLOTS
            rows.append(coef[k // 8, pl.ds(k % 8, 1), :] + coef[(k + 1) // 8, pl.ds((k + 1) % 8, 1), :])
        edge.append(mul_rows(rows, near))
    for v in range(VARS):
        for m in range(REACH):
            wbuf[m, v] = jnp.where(first_block, 0.0, tail[m, v])
        wbuf[REACH, v] = zero
    ends = (lane == 0) | (lane == cells - 1)

    def add(b, values, totals):
        stores, fresh = [], []
        for i in range(VARS):
            other = pltpu.roll(edge[i], (cells - 2 * b) % cells, 1)
            value = values[i] + jnp.where(ends, other, 0.0)
            stores.append((resid, (b, i), value))
            fresh.append(totals[i] + value * value)
        return Kept(tuple(fresh), stores)

    totals = (zero,) * VARS
    stores = []
    for b in range(REACH):
        places = [
            jnp.where(s < REACH, s, REACH) for s in slots(lcols, counts, 0, b, REACH - base, REACH)
        ]
        acc = apply_coef(low, b, [read_block(wbuf, s) for s in places])
        kept = add(b, [inner[b, i] + acc[i] for i in range(VARS)], totals)
        stores += kept.stores
        totals = kept.carry
    store_all(stores)

    def rest(b, totals):
        return add(b + REACH, [inner[b + REACH, i] for i in range(VARS)], totals)

    totals = steps(blocks - REACH, 7, rest, totals)
    total = totals[0]
    for i in range(1, VARS):
        total = total + totals[i]
    sums = jnp.broadcast_to(jnp.sum(total, axis=1, keepdims=True), total.shape)
    row = lax.broadcasted_iota(jnp.int32, total.shape, 0)
    line = jnp.sum(jnp.where(lane == row, sums, 0.0), axis=0, keepdims=True)
    for p in range(squares.shape[0]):
        squares[p] = line


def scale_kernel(entries, resid, squares, out):
    blocks, _, nrhs, cells = resid.shape
    line = squares[0]
    for p in range(1, squares.shape[0]):
        line = line + squares[p]
    lane = lanes_of(cells)
    row = lax.broadcasted_iota(jnp.int32, (nrhs, cells), 0)
    line = jnp.where(lane == row, jnp.broadcast_to(line, (nrhs, cells)), 0.0)
    msq = jnp.sum(line, axis=1, keepdims=True) / entries
    factor = jnp.broadcast_to(-lax.rsqrt(msq + 1e-06), (nrhs, cells))

    def block(b, carry):
        return Kept(carry, [(out, (b, v), resid[b, v] * factor) for v in range(VARS)])

    steps(blocks, 6, block)


def call(kernel, outs, args, places, scratch):
    args = [
        pltpu.with_memory_space_constraint(a, p) if p is HBM else a for a, p in zip(args, places)
    ]
    return pl.pallas_call(
        kernel,
        out_shape=[jax.ShapeDtypeStruct(o[0], (o + (jnp.float32,))[2]) for o in outs],
        in_specs=[pl.BlockSpec(memory_space=p) for p in places],
        out_specs=[pl.BlockSpec(memory_space=p) for p in (o[1] for o in outs)],
        scratch_shapes=[VMEM(s, jnp.float32) if isinstance(s, tuple) else s for s in scratch],
        compiler_params=pltpu.CompilerParams(vmem_limit_bytes=VMEM_LIMIT),
    )(*args)


def shards(
    rhs, diag_block, diag_inverse, lower_coef, upper_coef, side_coef, lower_cols, upper_cols, counts
):
    blocks, nvars, nrhs, cells = rhs.shape
    n = lax.axis_size("chain")
    inv = jnp.transpose(diag_inverse, (1, 2, 0, 3))
    low, upp, side = (
        jnp.transpose(a, (0, 2, 3, 1, 4)).reshape(-1, cells)
        for a in (lower_coef, upper_coef, side_coef)
    )
    lcols, ucols, used = lower_cols.T, upper_cols.T, counts.T
    m = lax.axis_size("sub")
    rows = blocks + REACH + 1
    half = n // 2
    parts = -(-len(column_order(nrhs)) // half)
    back = -(-32 // half)
    packed = min(8, half)
    extra = 8 // packed
    wide = 2 * (extra + WIDE // packed)
    sides = [list(range(half)), list(range(half, n))]
    tile = (nrhs, cells)

    mats = (VARS, VARS, SLOTS, blocks + PAD, cells)
    padded = (low.shape[0] + PAD, cells)

    maps, source, mlow, mupp, lcols, ucols, used = call(
        functools.partial(local_kernel, half),
        [((half, parts) + tile, VMEM), (rhs.shape, VMEM), (mats, VMEM), (mats, VMEM)]
        + [(lcols.shape, VMEM, jnp.int32)] * 3,
        (rhs, inv, low, upp, lcols, ucols, used),
        (HBM,) * 7,
        [rhs.shape, (VARS, VARS, blocks + PAD, cells), low.shape, upp.shape]
        + [pltpu.SMEM(lcols.shape, jnp.int32)] * 3
        + [(rows, VARS, nrhs + WIDE, cells), (rows, VARS, nrhs + 2 * WIDE, cells)]
        + [(WIDE * SPACE, cells), pltpu.SemaphoreType.DMA((10,))],
    )
    maps = lax.all_to_all(maps, "chain", 0, 0, tiled=True, axis_index_groups=sides)
    cols, ends, offer = call(
        first_solve_kernel,
        [
            ((half * COLUMNS * 8, cells), VMEM),
            ((half, 4 * extra) + tile, VMEM),
            ((wide,) + tile, VMEM),
        ],
        (maps,),
        (VMEM,),
        [(half, wide) + tile, (wide // 2 * WIDE + PAD, cells)],
    )
    got = lax.ppermute(
        offer, "chain", [p for i in range(half) for p in ((i, i + half), (i + half, i))]
    )
    (states,) = call(
        second_solve_kernel,
        [((half, back) + tile, VMEM)],
        (cols, ends, offer, got),
        (VMEM,) * 4,
        [(half, 2 * extra) + tile, (extra * WIDE + PAD, cells), (half, 4 * extra) + tile],
    )
    states = lax.all_to_all(states, "chain", 0, 0, tiled=True, axis_index_groups=sides)
    z, w, tail, edge, low, side = call(
        functools.partial(sweep_kernel, half),
        [
            (rhs.shape, VMEM),
            ((blocks + 1, VARS) + tile, VMEM),
            ((REACH, VARS) + tile, VMEM),
            ((VARS,) + tile, VMEM),
            (padded, VMEM),
            (padded, VMEM),
        ],
        (states, source, mlow, mupp, lcols, ucols, used, low, side),
        (VMEM,) * 4 + (SMEM,) * 3 + (HBM,) * 2,
        [rhs.shape, (32 * 8, cells), pltpu.SemaphoreType.DMA((2,))],
    )
    tail = lax.ppermute(tail, "chain", [(i, (i + 1) % n) for i in range(n)])
    swap_a, swap_b = (
        lax.ppermute(edge, "sub", [p for i, j in pairs for p in ((i, j), (j, i))])
        for pairs in (
            [(i, i + 1) for i in range(0, m - 1, 2)],
            [(i, i + 1) for i in range(1, m - 1, 2)] + [(0, m - 1)] * (m % 2 == 0),
        )
    )
    inner, coef, correction = call(
        inner_kernel,
        [
            (rhs.shape, VMEM),
            ((-(-VARS * VARS * SLOTS // 8),) + (8, cells), VMEM),
            (rhs.shape, HBM),
        ],
        (z, w, low, side, lcols, used),
        (VMEM,) * 4 + (SMEM,) * 2,
        [(2 * REACH + 1, VARS) + tile, pltpu.SemaphoreType.DMA],
    )
    resid, squares = call(
        outer_kernel,
        [(rhs.shape, VMEM), ((n * m, 1, cells), VMEM)],
        (inner, coef, low, tail, swap_a, swap_b, lcols, used),
        (VMEM,) * 6 + (SMEM,) * 2,
        [(REACH + 1, VARS) + tile],
    )
    squares = lax.all_to_all(squares, ("chain", "sub"), 0, 0, tiled=True)
    entries = blocks * VARS * cells * n * m
    (residual_unit,) = call(
        functools.partial(scale_kernel, entries),
        [(rhs.shape, VMEM)],
        (resid, squares),
        (VMEM, VMEM),
        [],
    )
    return (correction, residual_unit)


def solution(mesh):
    in_specs = (
        P("chain", None, None, "sub"),
        P("chain", None, None, "sub"),
        P("chain", None, None, "sub"),
        P("chain", None, None, None, "sub"),
        P("chain", None, None, None, "sub"),
        P("chain", None, None, None, "sub"),
        P("chain", None),
        P("chain", None),
        P("chain", None),
    )
    out_specs = (P("chain", None, None, "sub"), P("chain", None, None, "sub"))
    return jax.shard_map(shards, mesh=mesh, in_specs=in_specs, out_specs=out_specs, check_vma=False)
```

```python
import functools

import jax
import jax.numpy as jnp
from jax import lax
from jax.experimental import pallas as pl
from jax.experimental.pallas import tpu as pltpu
from jax.sharding import PartitionSpec as P

VARS = 5
REACH = 3
SLOTS = 2
STATE = REACH * VARS
WIDE = 16
PAD = 8
SPACE = 72
DIRECT = 4
VMEM_LIMIT = 40 * 1024 * 1024

VMEM = pltpu.VMEM
SMEM = pltpu.SMEM
HBM = pltpu.HBM


def lanes_of(cells):
    return lax.broadcasted_iota(jnp.int32, (8, cells), 1)


def block_transpose(items, width, cells):
    count = len(items)
    lane = lanes_of(cells)
    half = 1
    while half < count:
        bit = (lane // (half * width)) % 2 == 1
        out = list(items)
        for a in range(count):
            if a & half:
                continue
            b = a + half
            out[a] = jnp.where(bit, pltpu.roll(items[b], half * width, 1), items[a])
            out[b] = jnp.where(bit, items[b], pltpu.roll(items[a], cells - half * width, 1))
        items = out
        half *= 2
    return items


def spread(ref, place, row):
    return ref[place + (pl.ds(row, 8, stride=0), slice(None))]


def mul_rows(rows, near):
    total = rows[0] * near[0]
    for j in range(1, len(near)):
        total = total + rows[j] * near[j]
    return total


def mul_groups(rows, nears):
    return [mul_rows(rows, [near[g] for near in nears]) for g in range(len(nears[0]))]


def couple(mats, b, nears):
    out = []
    for i in range(VARS):
        parts = [
            mul_groups([spread(mats, (i, j, k), b) for j in range(VARS)], nears[k])
            for k in range(SLOTS)
        ]
        out.append([x + y for x, y in zip(*parts)])
    return out


def apply_coef(coef, b, nears):
    out = []
    for i in range(VARS):
        parts = []
        for k in range(SLOTS):
            place = (b * VARS + i) * VARS * SLOTS + k
            parts.append(
                mul_rows([spread(coef, (), place + SLOTS * j) for j in range(VARS)], nears[k])
            )
        out.append(parts[0] + parts[1])
    return out


def products(inv, coef, out):
    blocks = out.shape[3] - PAD
    stride = VARS * VARS * SLOTS

    def some(o, carry):
        start = o * 8
        left = [[-inv[i, m, pl.ds(start, 8), :] for m in range(VARS)] for i in range(VARS)]
        for k in range(SLOTS):
            stores = []
            for j in range(VARS):
                place = start * stride + j * SLOTS + k
                right = [
                    coef[pl.ds(place + m * VARS * SLOTS, 8, stride=stride), :] for m in range(VARS)
                ]
                for i in range(VARS):
                    here = (i, j, k, pl.ds(start, 8))
                    stores.append((out, here, mul_rows(left[i], right)))
            store_all(stores)
        return carry

    lax.fori_loop(0, blocks // 8, some, 0)


def slots(cols, counts, side, b, shift, empty):
    return [jnp.where(k < counts[side, b], cols[k, b] + shift, empty) for k in range(SLOTS)]


def read_block(buf, place):
    return [buf[place, v] for v in range(VARS)]


def read_groups(buf, place):
    count = buf.shape[2] // 8
    return [[buf[place, v, pl.ds(8 * g, 8), :] for g in range(count)] for v in range(VARS)]


class Kept:
    def __init__(self, carry, stores):
        self.carry, self.stores = carry, stores


def store_all(stores):
    for ref, place, value in stores:
        ref[place] = value


def steps(count, most, body, carry=0):
    unroll = max(u for u in range(1, most + 1) if count % u == 0)

    def chunk(o, carry):
        kept = []
        for u in range(unroll):
            carry = body(o * unroll + u, carry)
            if isinstance(carry, Kept):
                kept += carry.stores
                carry = carry.carry
        store_all(kept)
        return carry

    return lax.fori_loop(0, count // unroll, chunk, carry)


def column_order(nrhs):
    wide_y = nrhs + WIDE
    order = []
    for first, count in ((nrhs, STATE), (wide_y + nrhs, STATE - 1), (wide_y + nrhs + WIDE, STATE)):
        order += [(half, first + j) for half in range(2) for j in range(count)]
    for first in (0, wide_y):
        order += [(half, first + q) for half in range(2) for q in range(nrhs)]
    return order


def position(n):
    return lax.axis_index("chain") % n


def gather_parts(parts, buf):
    here = position(buf.shape[0])
    for x, part in enumerate(parts):
        for page in range(part.shape[0]):
            buf[here ^ x, page] = part[page]


def scatter_parts(buf, parts):
    here = position(buf.shape[0])
    for x, part in enumerate(parts):
        for page in range(part.shape[0]):
            part[page] = buf[here ^ x, page]


def parted(kernel, before, count, n, *refs):
    if count == 1:
        return kernel(*refs)
    outs, buf = refs[before : before + count], refs[-1]
    kernel(*refs[:before], buf, *refs[before + count : -1])
    scatter_parts(buf, outs)


def joined(kernel, count, n, *refs):
    if count == 1:
        return kernel(*refs)
    gather_parts(refs[:count], refs[-1])
    kernel(refs[-1], *refs[count:-1])


def exchange(parts, n, groups):
    if len(parts) == 1:
        return [lax.all_to_all(parts[0], "chain", 0, 0, tiled=True, axis_index_groups=groups)]
    count = lax.axis_size("chain")
    return [parts[0]] + [
        lax.ppermute(parts[x], "chain", [(i, i ^ x) for i in range(count)])
        for x in range(1, len(parts))
    ]


def local_kernel(
    n,
    rhs_h,
    inv_h,
    low_h,
    upp_h,
    lcols_h,
    ucols_h,
    counts_h,
    out,
    source,
    mlow,
    mupp,
    lcols_v,
    ucols_v,
    counts_v,
    rhs,
    inv,
    low,
    upp,
    lcols,
    ucols,
    counts,
    ybuf,
    zbuf,
    stage,
    sems,
):
    copies = [
        pltpu.make_async_copy(src, dst, sems.at[k])
        for k, (src, dst) in enumerate(
            (
                (inv_h, inv.at[:, :, pl.ds(0, rhs.shape[0]), :]),
                (low_h, low),
                (lcols_h, lcols),
                (counts_h, counts),
                (ucols_h, ucols),
                (rhs_h, rhs),
                (upp_h, upp),
                (lcols_h, lcols_v),
                (ucols_h, ucols_v),
                (counts_h, counts_v),
            )
        )
    ]
    for copy in copies:
        copy.start()
    blocks, _, nrhs, cells = rhs.shape
    base = lax.axis_index("chain") * blocks
    wide_y = nrhs + WIDE
    wide_z = wide_y + WIDE
    row_y = lax.broadcasted_iota(jnp.int32, (wide_y, cells), 0)
    row_z = lax.broadcasted_iota(jnp.int32, (wide_z, cells), 0)
    for m in range(REACH):
        for v in range(VARS):
            q = VARS * m + v
            ybuf[REACH - 1 - m, v] = (row_y == nrhs + q).astype(jnp.float32)
            zbuf[blocks + m, v] = (row_z == wide_y + q).astype(jnp.float32)
    for v in range(VARS):
        ybuf[blocks + REACH, v] = jnp.zeros((wide_y, cells), jnp.float32)
        zbuf[blocks + REACH, v] = jnp.zeros((wide_z, cells), jnp.float32)
    empty = blocks + REACH
    copies[0].wait()
    copies[1].wait()
    products(inv, low, mlow)
    for copy in copies[2:6]:
        copy.wait()

    def first(b, carry):
        nears = [read_groups(ybuf, s) for s in slots(lcols, counts, 0, b, REACH - base, empty)]
        acc = couple(mlow, b, nears)
        right = [rhs[b, i] for i in range(VARS)]
        stores = []
        for i in range(VARS):
            own = mul_rows([spread(inv, (i, j), b) for j in range(VARS)], right)
            stores.append((source, (b, i), own))
            for g in range(len(acc[i])):
                value = own + acc[i][0] if g == 0 else acc[i][g]
                stores.append((ybuf, (b + REACH, i, pl.ds(8 * g, 8)), value))
        store_all(stores)
        return carry

    steps(blocks, 2, first)
    for copy in copies[6:]:
        copy.wait()
    products(inv, upp, mupp)

    def second(e, carry):
        c = blocks - 1 - e
        nears = [read_groups(zbuf, s) for s in slots(ucols, counts, 1, c, -base, empty)]
        acc = couple(mupp, c, nears)
        stores = []
        for i in range(VARS):
            for g in range(len(acc[i])):
                if g < wide_y // 8:
                    value = ybuf[c + REACH, i, 8 * g : 8 * g + 8] + acc[i][g]
                else:
                    value = acc[i][g]
                stores.append((zbuf, (c, i, pl.ds(8 * g, 8)), value))
        store_all(stores)
        return carry

    steps(blocks, 2, second)

    zero = jnp.zeros((8, cells), jnp.float32)
    for i in range(WIDE):
        m, v = i // VARS, i % VARS
        for g in range((wide_y + wide_z) // 8):
            if i == STATE:
                value = zero
            elif g < wide_y // 8:
                value = ybuf[blocks + REACH - 1 - m, v, 8 * g : 8 * g + 8]
            else:
                value = zbuf[m, v, 8 * g - wide_y : 8 * g - wide_y + 8]
            stage[pl.ds(i * SPACE + 8 * g, 8), :] = value

    def column(half, index):
        return stage[pl.ds(half * 8 * SPACE + index, 8, stride=SPACE), :]

    for half in range(2):
        place = STATE * SPACE + nrhs + 8 * half
        stage[pl.ds(place, 8), :] = column(half, wide_y + nrhs + STATE - 1)
    order = column_order(nrhs)
    width = cells // n
    for page in range(out.shape[1]):
        items = [column(*at) for at in order[page * n : (page + 1) * n]]
        items += [zero] * (n - len(items))
        for k, item in enumerate(block_transpose(items, width, cells)):
            out[k, page] = item


def split(value, period, stop, width, cells):
    items = [value]
    lane = lanes_of(cells)
    while period > stop:
        half = period // 2 * width
        bit = lane // half % 2 == 1
        fresh = []
        for item in items:
            other = pltpu.roll(item, half, 1)
            fresh += [jnp.where(bit, other, item), jnp.where(bit, item, other)]
        items = fresh
        period //= 2
    return items


def total_of(terms):
    while len(terms) > 1:
        pairs = [terms[k] + terms[k + 1] for k in range(0, len(terms) - 1, 2)]
        terms = pairs + terms[len(terms) - len(terms) % 2 :]
    return terms[0]


COLUMNS = 6 * STATE - 2


def store_state(buf, state):
    for half in range(2):
        for g, value in enumerate(state[half]):
            buf[pl.ds(g * WIDE + 8 * half, 8), :] = value


def state_rows(buf, count):
    return [[spread(buf, (), g * WIDE + j) for j in range(STATE)] for g in range(count)]


def pass_forward(d, cols, sides, state, buf, keep):
    groups, extra = len(state[0]), sides.shape[1] // 4
    store_state(buf, state)
    rows = state_rows(buf, groups)
    fresh = []
    for half in range(2):
        columns = [cols[pl.ds((d * COLUMNS + half * STATE + j) * 8, 8), :] for j in range(STATE)]
        fresh.append([])
        for g in range(groups):
            total = total_of([c * r for c, r in zip(columns, rows[g])])
            fresh[half].append(total + sides[d, half * extra + g] if g < extra else total)
        first = d * COLUMNS + 2 * STATE + half * (STATE - 1)
        columns = [cols[pl.ds((first + j) * 8, 8), :] for j in range(STATE - 1)]
        start = (d * COLUMNS + STATE + 8 * half) * 8 + 7
        columns.append(cols[pl.ds(start, 8, stride=8), :])
        for g in range(groups):
            total = total_of([c * r for c, r in zip(columns, rows[g])])
            if g < extra:
                total = total + sides[d, (2 + half) * extra + g]
            keep[d, half * groups + g] = total
    return fresh


def pass_back(d, cols, state, buf, keep):
    groups = len(state[0])
    store_state(buf, state)
    rows = state_rows(buf, groups)
    fresh = []
    for half in range(2):
        first = d * COLUMNS + 4 * STATE - 2 + half * STATE
        columns = [cols[pl.ds((first + j) * 8, 8), :] for j in range(STATE)]
        fresh.append(
            [
                total_of([c * r for c, r in zip(columns, rows[g])]) + keep[d, half * groups + g]
                for g in range(groups)
            ]
        )
    return fresh


def flat(state):
    return tuple(state[0] + state[1])


def folded(values):
    groups = len(values) // 2
    return [list(values[:groups]), list(values[groups:])]


def first_solve_kernel(x, cols, sides, offer, keep, buf):
    n, cells = x.shape[0], x.shape[3]
    width = cells // n
    packed = min(8, n)
    extra, groups = sides.shape[1] // 4, offer.shape[0] // 2
    zero = jnp.zeros((8, cells), jnp.float32)

    def unpack(d, carry):
        values = [x[d, page] for page in range(x.shape[1])]
        for page, value in enumerate(values):
            for k, block in enumerate(split(value, n, packed, width, cells)):
                e = page * n + k * packed
                if e < COLUMNS:
                    for g, item in enumerate(split(block, packed, 1, width, cells)):
                        cols[pl.ds((d * COLUMNS + e + g) * 8, 8), :] = item
                elif e < COLUMNS + 4 * 8:
                    sides[d, (e - COLUMNS) // packed] = block
        return carry

    steps(n, 2, unpack)
    lane = lanes_of(cells)
    row = lax.broadcasted_iota(jnp.int32, (8, cells), 0)
    start = []
    for half in range(2):
        start.append([zero] * extra)
        for g in range(groups - extra):
            column = lane // width % packed + g * packed
            start[half].append((column == row + 8 * half).astype(jnp.float32))

    def ahead(d, state):
        return flat(pass_forward(d, cols, sides, folded(state), buf, keep))

    leaving = steps(n, 2, ahead, flat(start))

    def back(e, state):
        return flat(pass_back(n - 1 - e, cols, folded(state), buf, keep))

    left = steps(n, 2, back, (zero,) * (2 * groups))
    is_left = lax.axis_index("chain") < n
    for e in range(2 * groups):
        offer[e] = jnp.where(is_left, leaving[e], left[e])


def second_solve_kernel(cols, sides, mine, got, out, keep, buf, states):
    n, cells = out.shape[0], out.shape[3]
    width = cells // n
    packed = min(8, n)
    extra, groups = sides.shape[1] // 4, mine.shape[0] // 2
    zero = jnp.zeros((8, cells), jnp.float32)
    is_left = lax.axis_index("chain") < n
    store_state(buf, [[mine[half * groups + g] for g in range(extra)] for half in range(2)])
    rows = state_rows(buf, extra)
    entering, far = [], []
    for half in range(2):
        columns = []
        for g in range(extra, groups):
            columns += split(got[half * groups + g], packed, 1, width, cells)
        for g in range(extra):
            known = got[half * groups + g]
            total = total_of([c * r for c, r in zip(columns, rows[g])])
            entering.append(jnp.where(is_left, 0.0, known))
            far.append(jnp.where(is_left, known + total, 0.0))

    def ahead(d, state):
        for e in range(2 * extra):
            states[d, e] = state[e]
        return flat(pass_forward(d, cols, sides, folded(state), buf, keep))

    steps(n, 4, ahead, tuple(entering))

    def back(e, state):
        d = n - 1 - e
        for e in range(2 * extra):
            states[d, 2 * extra + e] = state[e]
        return flat(pass_back(d, cols, folded(state), buf, keep))

    steps(n, 4, back, tuple(far))
    block = lanes_of(cells) // (packed * width)

    def pack(d, carry):
        for page in range(out.shape[1]):
            total = zero
            for r in range(4 * extra):
                if packed * r // n == page:
                    total = jnp.where(block == packed * r % n // packed, states[d, r], total)
            out[d, page] = total
        return carry

    steps(n, 4, pack)


def sweep_kernel(
    n,
    states,
    source,
    mlow,
    mupp,
    lcols,
    ucols,
    counts,
    low_h,
    side_h,
    zout,
    wout,
    tail,
    edge,
    low,
    side,
    ybuf,
    stage,
    sems,
):
    total = low_h.shape[0]
    copies = [
        pltpu.make_async_copy(src, dst.at[pl.ds(0, total), :], sems.at[k])
        for k, (src, dst) in enumerate(((low_h, low), (side_h, side)))
    ]
    for copy in copies:
        copy.start()
    blocks, _, nrhs, cells = source.shape
    base = lax.axis_index("chain") * blocks
    width = cells // n
    zero = jnp.zeros((nrhs, cells), jnp.float32)
    items = []
    for r in range(states.shape[1]):
        items += block_transpose([states[k, r] for k in range(n)], width, cells)
    for e in range(32):
        stage[pl.ds(8 * e, 8), :] = items[e]

    def entering(start):
        rows = [stage[pl.ds(start + q // 8 * 64 + q % 8, 8, stride=8), :] for q in range(STATE)]
        return tuple(rows)

    lane = lanes_of(cells)
    for v in range(VARS):
        wout[blocks, v] = zero

    def near(window, b, sign, cols, side):
        nears = []
        for k in range(SLOTS):
            off = sign * (cols[k, b] - base - b)
            picks = []
            for v in range(VARS):
                value = window[(REACH - 1) * VARS + v]
                for d in range(REACH - 1):
                    value = jnp.where(off == d + 1, window[d * VARS + v], value)
                picks.append(value if k == 0 else jnp.where(k < counts[side, b], value, 0.0))
            nears.append([[value] for value in picks])
        return nears

    def first(b, window):
        acc = couple(mlow, b, near(window, b, -1, lcols, 0))
        fresh = tuple(source[b, i] + acc[i][0] for i in range(VARS))
        return Kept(fresh + window[: STATE - VARS], [(ybuf, (b, i), fresh[i]) for i in range(VARS)])

    steps(blocks, 4, first, entering(0))

    def second(e, carry):
        c = blocks - 1 - e
        window, edges = carry[:STATE], list(carry[STATE:])
        acc = couple(mupp, c, near(window, c, 1, ucols, 1))
        fresh = tuple(ybuf[c, i] + acc[i][0] for i in range(VARS))
        here = (lane == 2 * c) | (lane == (2 * c + cells - 1) % cells)
        stores = []
        for i in range(VARS):
            stores += [(zout, (c, i), fresh[i]), (wout, (c, i), acc[i][0])]
            edges[i] = jnp.where(here, pltpu.roll(fresh[i], 2 * c, 1), edges[i])
        return Kept(fresh + window[: STATE - VARS] + tuple(edges), stores)

    carry = steps(blocks, 4, second, entering(128) + (zero,) * VARS)
    for v in range(VARS):
        edge[v] = carry[STATE + v]
    for m in range(REACH):
        for v in range(VARS):
            tail[m, v] = wout[blocks - REACH + m, v]
    for copy in copies:
        copy.wait()


def inner_kernel(z, w, low, side, lcols, counts, resid, coef, correction, wbuf, sem):
    store = pltpu.make_async_copy(z, correction, sem)
    store.start()
    blocks, _, nrhs, cells = z.shape
    base = lax.axis_index("chain") * blocks
    lane = lanes_of(cells)
    zero = jnp.zeros((nrhs, cells), jnp.float32)
    for v in range(VARS):
        for m in range(REACH):
            wbuf[m, v] = zero
            wbuf[m + REACH, v] = w[m, v]
        wbuf[2 * REACH, v] = zero
    pages = coef.shape[0]
    size = VARS * VARS * SLOTS
    row = lax.broadcasted_iota(jnp.int32, (8, cells), 0)

    def block(b, found, buf, shift, empty):
        nears = [read_block(buf, s) for s in slots(lcols, counts, 0, b, shift - base, empty)]
        acc = apply_coef(low, b, nears)
        left, right = [], []
        for v in range(VARS):
            here = z[b, v]
            left.append(jnp.where(lane == 0, 0.0, pltpu.roll(here, 1, 1)))
            right.append(jnp.where(lane == cells - 1, 0.0, pltpu.roll(here, cells - 1, 1)))
        beside = apply_coef(side, b, [left, right])
        here = (lane + row % 2) % cells == 2 * b
        found = tuple(
            jnp.where(here, pltpu.roll(side[pl.ds(b * size + 8 * r, 8), :], 2 * b, 1), found[r])
            for r in range(pages)
        )
        return Kept(found, [(resid, (b, i), acc[i] + beside[i]) for i in range(VARS)])

    found = (jnp.zeros((8, cells), jnp.float32),) * pages
    for b in range(REACH):
        kept = block(b, found, wbuf, REACH, 2 * REACH)
        store_all(kept.stores)
        found = kept.carry

    def inner(b, found):
        return block(b + REACH, found, w, 0, blocks)

    found = steps(blocks - REACH, 3, inner, found)
    for r in range(pages):
        coef[r] = found[r]
    store.wait()


def outer_kernel(
    inner, coef, low, tail, swap_a, swap_b, lcols, counts, resid, squares, wbuf
):
    blocks, _, nrhs, cells = inner.shape
    base = lax.axis_index("chain") * blocks
    first_block = lax.axis_index("chain") == 0
    place = lax.axis_index("sub")
    odd = place % 2 == 1
    first, last = place == 0, place == lax.axis_size("sub") - 1
    lane = lanes_of(cells)
    zero = jnp.zeros((nrhs, cells), jnp.float32)
    near = []
    for v in range(VARS):
        west = jnp.where(first, 0.0, jnp.where(odd, swap_a[v], swap_b[v]))
        east = jnp.where(last, 0.0, jnp.where(odd, swap_b[v], swap_a[v]))
        west, east = pltpu.roll(west, 1, 1), pltpu.roll(east, cells - 1, 1)
        near.append(jnp.where(lane % 2 == 0, west, east))
    edge = []
    for i in range(VARS):
        rows = []
        for j in range(VARS):
            k = (i * VARS + j) * SLOTS
            rows.append(coef[k // 8, pl.ds(k % 8, 1), :] + coef[(k + 1) // 8, pl.ds((k + 1) % 8, 1), :])
        edge.append(mul_rows(rows, near))
    for v in range(VARS):
        for m in range(REACH):
            wbuf[m, v] = jnp.where(first_block, 0.0, tail[m, v])
        wbuf[REACH, v] = zero
    ends = (lane == 0) | (lane == cells - 1)

    def add(b, values, totals):
        stores, fresh = [], []
        for i in range(VARS):
            other = pltpu.roll(edge[i], (cells - 2 * b) % cells, 1)
            value = values[i] + jnp.where(ends, other, 0.0)
            stores.append((resid, (b, i), value))
            fresh.append(totals[i] + value * value)
        return Kept(tuple(fresh), stores)

    totals = (zero,) * VARS
    stores = []
    for b in range(REACH):
        places = [
            jnp.where(s < REACH, s, REACH) for s in slots(lcols, counts, 0, b, REACH - base, REACH)
        ]
        acc = apply_coef(low, b, [read_block(wbuf, s) for s in places])
        kept = add(b, [inner[b, i] + acc[i] for i in range(VARS)], totals)
        stores += kept.stores
        totals = kept.carry
    store_all(stores)

    def rest(b, totals):
        return add(b + REACH, [inner[b + REACH, i] for i in range(VARS)], totals)

    totals = steps(blocks - REACH, 7, rest, totals)
    total = totals[0]
    for i in range(1, VARS):
        total = total + totals[i]
    sums = jnp.broadcast_to(jnp.sum(total, axis=1, keepdims=True), total.shape)
    row = lax.broadcasted_iota(jnp.int32, total.shape, 0)
    line = jnp.sum(jnp.where(lane == row, sums, 0.0), axis=0, keepdims=True)
    for p in range(squares.shape[0]):
        squares[p] = line


def scale_kernel(entries, resid, squares, out):
    blocks, _, nrhs, cells = resid.shape
    line = squares[0]
    for p in range(1, squares.shape[0]):
        line = line + squares[p]
    lane = lanes_of(cells)
    row = lax.broadcasted_iota(jnp.int32, (nrhs, cells), 0)
    line = jnp.where(lane == row, jnp.broadcast_to(line, (nrhs, cells)), 0.0)
    msq = jnp.sum(line, axis=1, keepdims=True) / entries
    factor = jnp.broadcast_to(-lax.rsqrt(msq + 1e-06), (nrhs, cells))

    def block(b, carry):
        return Kept(carry, [(out, (b, v), resid[b, v] * factor) for v in range(VARS)])

    steps(blocks, 6, block)


def call(kernel, outs, args, places, scratch):
    args = [
        pltpu.with_memory_space_constraint(a, p) if p is HBM else a for a, p in zip(args, places)
    ]
    return pl.pallas_call(
        kernel,
        out_shape=[jax.ShapeDtypeStruct(o[0], (o + (jnp.float32,))[2]) for o in outs],
        in_specs=[pl.BlockSpec(memory_space=p) for p in places],
        out_specs=[pl.BlockSpec(memory_space=p) for p in (o[1] for o in outs)],
        scratch_shapes=[VMEM(s, jnp.float32) if isinstance(s, tuple) else s for s in scratch],
        compiler_params=pltpu.CompilerParams(vmem_limit_bytes=VMEM_LIMIT),
    )(*args)


def shards(
    rhs, diag_block, diag_inverse, lower_coef, upper_coef, side_coef, lower_cols, upper_cols, counts
):
    blocks, nvars, nrhs, cells = rhs.shape
    n = lax.axis_size("chain")
    inv = jnp.transpose(diag_inverse, (1, 2, 0, 3))
    low, upp, side = (
        jnp.transpose(a, (0, 2, 3, 1, 4)).reshape(-1, cells)
        for a in (lower_coef, upper_coef, side_coef)
    )
    lcols, ucols, used = lower_cols.T, upper_cols.T, counts.T
    m = lax.axis_size("sub")
    rows = blocks + REACH + 1
    half = n // 2
    parts = -(-len(column_order(nrhs)) // half)
    back = -(-32 // half)
    packed = min(8, half)
    extra = 8 // packed
    wide = 2 * (extra + WIDE // packed)
    sides = [list(range(half)), list(range(half, n))]
    tile = (nrhs, cells)

    mats = (VARS, VARS, SLOTS, blocks + PAD, cells)
    padded = (low.shape[0] + PAD, cells)

    count = half if half <= DIRECT else 1

    def pieces(pages):
        return [((pages,) + tile, VMEM)] * count if count > 1 else [((half, pages) + tile, VMEM)]

    def whole(pages):
        return [(half, pages) + tile] if count > 1 else []

    *maps, source, mlow, mupp, lcols, ucols, used = call(
        functools.partial(parted, functools.partial(local_kernel, half), 7, count, half),
        pieces(parts)
        + [(rhs.shape, VMEM), (mats, VMEM), (mats, VMEM)]
        + [(lcols.shape, VMEM, jnp.int32)] * 3,
        (rhs, inv, low, upp, lcols, ucols, used),
        (HBM,) * 7,
        [rhs.shape, (VARS, VARS, blocks + PAD, cells), low.shape, upp.shape]
        + [pltpu.SMEM(lcols.shape, jnp.int32)] * 3
        + [(rows, VARS, nrhs + WIDE, cells), (rows, VARS, nrhs + 2 * WIDE, cells)]
        + [(WIDE * SPACE, cells), pltpu.SemaphoreType.DMA((10,))]
        + whole(parts),
    )
    maps = exchange(maps, half, sides)
    cols, ends, offer = call(
        functools.partial(joined, first_solve_kernel, count, half),
        [
            ((half * COLUMNS * 8, cells), VMEM),
            ((half, 4 * extra) + tile, VMEM),
            ((wide,) + tile, VMEM),
        ],
        tuple(maps),
        (VMEM,) * count,
        [(half, wide) + tile, (wide // 2 * WIDE + PAD, cells)] + whole(parts),
    )
    got = lax.ppermute(
        offer, "chain", [p for i in range(half) for p in ((i, i + half), (i + half, i))]
    )
    states = call(
        functools.partial(parted, second_solve_kernel, 4, count, half),
        pieces(back),
        (cols, ends, offer, got),
        (VMEM,) * 4,
        [(half, 2 * extra) + tile, (extra * WIDE + PAD, cells), (half, 4 * extra) + tile]
        + whole(back),
    )
    states = exchange(states, half, sides)
    z, w, tail, edge, low, side = call(
        functools.partial(joined, functools.partial(sweep_kernel, half), count, half),
        [
            (rhs.shape, VMEM),
            ((blocks + 1, VARS) + tile, VMEM),
            ((REACH, VARS) + tile, VMEM),
            ((VARS,) + tile, VMEM),
            (padded, VMEM),
            (padded, VMEM),
        ],
        (*states, source, mlow, mupp, lcols, ucols, used, low, side),
        (VMEM,) * (3 + count) + (SMEM,) * 3 + (HBM,) * 2,
        [rhs.shape, (32 * 8, cells), pltpu.SemaphoreType.DMA((2,))] + whole(back),
    )
    tail = lax.ppermute(tail, "chain", [(i, (i + 1) % n) for i in range(n)])
    swap_a, swap_b = (
        lax.ppermute(edge, "sub", [p for i, j in pairs for p in ((i, j), (j, i))])
        for pairs in (
            [(i, i + 1) for i in range(0, m - 1, 2)],
            [(i, i + 1) for i in range(1, m - 1, 2)] + [(0, m - 1)] * (m % 2 == 0),
        )
    )
    inner, coef, correction = call(
        inner_kernel,
        [
            (rhs.shape, VMEM),
            ((-(-VARS * VARS * SLOTS // 8),) + (8, cells), VMEM),
            (rhs.shape, HBM),
        ],
        (z, w, low, side, lcols, used),
        (VMEM,) * 4 + (SMEM,) * 2,
        [(2 * REACH + 1, VARS) + tile, pltpu.SemaphoreType.DMA],
    )
    resid, squares = call(
        outer_kernel,
        [(rhs.shape, VMEM), ((n * m, 1, cells), VMEM)],
        (inner, coef, low, tail, swap_a, swap_b, lcols, used),
        (VMEM,) * 6 + (SMEM,) * 2,
        [(REACH + 1, VARS) + tile],
    )
    squares = lax.all_to_all(squares, ("chain", "sub"), 0, 0, tiled=True)
    entries = blocks * VARS * cells * n * m
    (residual_unit,) = call(
        functools.partial(scale_kernel, entries),
        [(rhs.shape, VMEM)],
        (resid, squares),
        (VMEM, VMEM),
        [],
    )
    return (correction, residual_unit)


def solution(mesh):
    in_specs = (
        P("chain", None, None, "sub"),
        P("chain", None, None, "sub"),
        P("chain", None, None, "sub"),
        P("chain", None, None, None, "sub"),
        P("chain", None, None, None, "sub"),
        P("chain", None, None, None, "sub"),
        P("chain", None),
        P("chain", None),
        P("chain", None),
    )
    out_specs = (P("chain", None, None, "sub"), P("chain", None, None, "sub"))
    return jax.shard_map(shards, mesh=mesh, in_specs=in_specs, out_specs=out_specs, check_vma=False)
```

```python
import functools

import jax
import jax.numpy as jnp
from jax import lax
from jax.experimental import pallas as pl
from jax.experimental.pallas import tpu as pltpu
from jax.sharding import PartitionSpec as P

VARS = 5
REACH = 3
SLOTS = 2
STATE = REACH * VARS
WIDE = 16
PAD = 8
SPACE = 72
DIRECT = 4
VMEM_LIMIT = 40 * 1024 * 1024

VMEM = pltpu.VMEM
SMEM = pltpu.SMEM
HBM = pltpu.HBM


def lanes_of(cells):
    return lax.broadcasted_iota(jnp.int32, (8, cells), 1)


def block_transpose(items, width, cells):
    count = len(items)
    lane = lanes_of(cells)
    half = 1
    while half < count:
        bit = (lane // (half * width)) % 2 == 1
        out = list(items)
        for a in range(count):
            if a & half:
                continue
            b = a + half
            out[a] = jnp.where(bit, pltpu.roll(items[b], half * width, 1), items[a])
            out[b] = jnp.where(bit, items[b], pltpu.roll(items[a], cells - half * width, 1))
        items = out
        half *= 2
    return items


def spread(ref, place, row):
    return ref[place + (pl.ds(row, 8, stride=0), slice(None))]


def mul_rows(rows, near):
    total = rows[0] * near[0]
    for j in range(1, len(near)):
        total = total + rows[j] * near[j]
    return total


def mul_groups(rows, nears):
    return [mul_rows(rows, [near[g] for near in nears]) for g in range(len(nears[0]))]


def couple(mats, b, nears):
    out = []
    for i in range(VARS):
        parts = [
            mul_groups([spread(mats, (i, j, k), b) for j in range(VARS)], nears[k])
            for k in range(SLOTS)
        ]
        out.append([x + y for x, y in zip(*parts)])
    return out


def apply_coef(coef, b, nears):
    out = []
    for i in range(VARS):
        parts = []
        for k in range(SLOTS):
            place = (b * VARS + i) * VARS * SLOTS + k
            parts.append(
                mul_rows([spread(coef, (), place + SLOTS * j) for j in range(VARS)], nears[k])
            )
        out.append(parts[0] + parts[1])
    return out


def products(inv, coef, out):
    blocks = out.shape[3] - PAD
    stride = VARS * VARS * SLOTS

    def some(o, carry):
        start = o * 8
        left = [[-inv[i, m, pl.ds(start, 8), :] for m in range(VARS)] for i in range(VARS)]
        for k in range(SLOTS):
            stores = []
            for j in range(VARS):
                place = start * stride + j * SLOTS + k
                right = [
                    coef[pl.ds(place + m * VARS * SLOTS, 8, stride=stride), :] for m in range(VARS)
                ]
                for i in range(VARS):
                    here = (i, j, k, pl.ds(start, 8))
                    stores.append((out, here, mul_rows(left[i], right)))
            store_all(stores)
        return carry

    steps(blocks // 8, 3, some)


def slots(cols, counts, side, b, shift, empty):
    return [jnp.where(k < counts[side, b], cols[k, b] + shift, empty) for k in range(SLOTS)]


def read_block(buf, place):
    return [buf[place, v] for v in range(VARS)]


def read_groups(buf, place):
    count = buf.shape[2] // 8
    return [[buf[place, v, pl.ds(8 * g, 8), :] for g in range(count)] for v in range(VARS)]


class Kept:
    def __init__(self, carry, stores):
        self.carry, self.stores = carry, stores


def store_all(stores):
    for ref, place, value in stores:
        ref[place] = value


def steps(count, most, body, carry=0):
    unroll = max(u for u in range(1, most + 1) if count % u == 0)

    def chunk(o, carry):
        kept = []
        for u in range(unroll):
            carry = body(o * unroll + u, carry)
            if isinstance(carry, Kept):
                kept += carry.stores
                carry = carry.carry
        store_all(kept)
        return carry

    return lax.fori_loop(0, count // unroll, chunk, carry)


def column_order(nrhs):
    wide_y = nrhs + WIDE
    order = []
    for first, count in ((nrhs, STATE), (wide_y + nrhs, STATE - 1), (wide_y + nrhs + WIDE, STATE)):
        order += [(half, first + j) for half in range(2) for j in range(count)]
    for first in (0, wide_y):
        order += [(half, first + q) for half in range(2) for q in range(nrhs)]
    return order


def position(n):
    return lax.axis_index("chain") % n


def gather_parts(parts, buf):
    here = position(buf.shape[0])
    for x, part in enumerate(parts):
        for page in range(part.shape[0]):
            buf[here ^ x, page] = part[page]


def scatter_parts(buf, parts):
    here = position(buf.shape[0])
    for x, part in enumerate(parts):
        for page in range(part.shape[0]):
            part[page] = buf[here ^ x, page]


def parted(kernel, before, count, n, *refs):
    if count == 1:
        return kernel(*refs)
    outs, buf = refs[before : before + count], refs[-1]
    kernel(*refs[:before], buf, *refs[before + count : -1])
    scatter_parts(buf, outs)


def joined(kernel, count, n, *refs):
    if count == 1:
        return kernel(*refs)
    gather_parts(refs[:count], refs[-1])
    kernel(refs[-1], *refs[count:-1])


def exchange(parts, n, groups):
    if len(parts) == 1:
        return [lax.all_to_all(parts[0], "chain", 0, 0, tiled=True, axis_index_groups=groups)]
    count = lax.axis_size("chain")
    return [parts[0]] + [
        lax.ppermute(parts[x], "chain", [(i, i ^ x) for i in range(count)])
        for x in range(1, len(parts))
    ]


def local_kernel(
    n,
    rhs_h,
    inv_h,
    low_h,
    upp_h,
    lcols_h,
    ucols_h,
    counts_h,
    out,
    source,
    mlow,
    mupp,
    lcols_v,
    ucols_v,
    counts_v,
    rhs,
    inv,
    low,
    upp,
    lcols,
    ucols,
    counts,
    ybuf,
    zbuf,
    stage,
    sems,
):
    copies = [
        pltpu.make_async_copy(src, dst, sems.at[k])
        for k, (src, dst) in enumerate(
            (
                (inv_h, inv.at[:, :, pl.ds(0, rhs.shape[0]), :]),
                (low_h, low),
                (lcols_h, lcols),
                (counts_h, counts),
                (ucols_h, ucols),
                (rhs_h, rhs),
                (upp_h, upp),
                (lcols_h, lcols_v),
                (ucols_h, ucols_v),
                (counts_h, counts_v),
            )
        )
    ]
    for copy in copies:
        copy.start()
    blocks, _, nrhs, cells = rhs.shape
    base = lax.axis_index("chain") * blocks
    wide_y = nrhs + WIDE
    wide_z = wide_y + WIDE
    row_y = lax.broadcasted_iota(jnp.int32, (wide_y, cells), 0)
    row_z = lax.broadcasted_iota(jnp.int32, (wide_z, cells), 0)
    for m in range(REACH):
        for v in range(VARS):
            q = VARS * m + v
            ybuf[REACH - 1 - m, v] = (row_y == nrhs + q).astype(jnp.float32)
            zbuf[blocks + m, v] = (row_z == wide_y + q).astype(jnp.float32)
    for v in range(VARS):
        ybuf[blocks + REACH, v] = jnp.zeros((wide_y, cells), jnp.float32)
        zbuf[blocks + REACH, v] = jnp.zeros((wide_z, cells), jnp.float32)
    empty = blocks + REACH
    copies[0].wait()
    copies[1].wait()
    products(inv, low, mlow)
    for copy in copies[2:6]:
        copy.wait()

    def first(b, carry):
        nears = [read_groups(ybuf, s) for s in slots(lcols, counts, 0, b, REACH - base, empty)]
        acc = couple(mlow, b, nears)
        right = [rhs[b, i] for i in range(VARS)]
        stores = []
        for i in range(VARS):
            own = mul_rows([spread(inv, (i, j), b) for j in range(VARS)], right)
            stores.append((source, (b, i), own))
            for g in range(len(acc[i])):
                value = own + acc[i][0] if g == 0 else acc[i][g]
                stores.append((ybuf, (b + REACH, i, pl.ds(8 * g, 8)), value))
        store_all(stores)
        return carry

    steps(blocks, 6, first)
    for copy in copies[6:]:
        copy.wait()
    products(inv, upp, mupp)

    def second(e, carry):
        c = blocks - 1 - e
        nears = [read_groups(zbuf, s) for s in slots(ucols, counts, 1, c, -base, empty)]
        acc = couple(mupp, c, nears)
        stores = []
        for i in range(VARS):
            for g in range(len(acc[i])):
                if g < wide_y // 8:
                    value = ybuf[c + REACH, i, 8 * g : 8 * g + 8] + acc[i][g]
                else:
                    value = acc[i][g]
                stores.append((zbuf, (c, i, pl.ds(8 * g, 8)), value))
        store_all(stores)
        return carry

    steps(blocks, 6, second)

    zero = jnp.zeros((8, cells), jnp.float32)
    for i in range(WIDE):
        m, v = i // VARS, i % VARS
        for g in range((wide_y + wide_z) // 8):
            if i == STATE:
                value = zero
            elif g < wide_y // 8:
                value = ybuf[blocks + REACH - 1 - m, v, 8 * g : 8 * g + 8]
            else:
                value = zbuf[m, v, 8 * g - wide_y : 8 * g - wide_y + 8]
            stage[pl.ds(i * SPACE + 8 * g, 8), :] = value

    def column(half, index):
        return stage[pl.ds(half * 8 * SPACE + index, 8, stride=SPACE), :]

    for half in range(2):
        place = STATE * SPACE + nrhs + 8 * half
        stage[pl.ds(place, 8), :] = column(half, wide_y + nrhs + STATE - 1)
    order = column_order(nrhs)
    width = cells // n
    for page in range(out.shape[1]):
        items = [column(*at) for at in order[page * n : (page + 1) * n]]
        items += [zero] * (n - len(items))
        for k, item in enumerate(block_transpose(items, width, cells)):
            out[k, page] = item


def split(value, period, stop, width, cells):
    items = [value]
    lane = lanes_of(cells)
    while period > stop:
        half = period // 2 * width
        bit = lane // half % 2 == 1
        fresh = []
        for item in items:
            other = pltpu.roll(item, half, 1)
            fresh += [jnp.where(bit, other, item), jnp.where(bit, item, other)]
        items = fresh
        period //= 2
    return items


def total_of(terms):
    while len(terms) > 1:
        pairs = [terms[k] + terms[k + 1] for k in range(0, len(terms) - 1, 2)]
        terms = pairs + terms[len(terms) - len(terms) % 2 :]
    return terms[0]


COLUMNS = 6 * STATE - 2


def store_state(buf, state):
    for half in range(2):
        for g, value in enumerate(state[half]):
            buf[pl.ds(g * WIDE + 8 * half, 8), :] = value


def state_rows(buf, count):
    return [[spread(buf, (), g * WIDE + j) for j in range(STATE)] for g in range(count)]


def pass_forward(d, cols, sides, state, buf, keep):
    groups, extra = len(state[0]), sides.shape[1] // 4
    store_state(buf, state)
    rows = state_rows(buf, groups)
    fresh = []
    for half in range(2):
        columns = [cols[pl.ds((d * COLUMNS + half * STATE + j) * 8, 8), :] for j in range(STATE)]
        fresh.append([])
        for g in range(groups):
            total = total_of([c * r for c, r in zip(columns, rows[g])])
            fresh[half].append(total + sides[d, half * extra + g] if g < extra else total)
        first = d * COLUMNS + 2 * STATE + half * (STATE - 1)
        columns = [cols[pl.ds((first + j) * 8, 8), :] for j in range(STATE - 1)]
        start = (d * COLUMNS + STATE + 8 * half) * 8 + 7
        columns.append(cols[pl.ds(start, 8, stride=8), :])
        for g in range(groups):
            total = total_of([c * r for c, r in zip(columns, rows[g])])
            if g < extra:
                total = total + sides[d, (2 + half) * extra + g]
            keep[d, half * groups + g] = total
    return fresh


def pass_back(d, cols, state, buf, keep):
    groups = len(state[0])
    store_state(buf, state)
    rows = state_rows(buf, groups)
    fresh = []
    for half in range(2):
        first = d * COLUMNS + 4 * STATE - 2 + half * STATE
        columns = [cols[pl.ds((first + j) * 8, 8), :] for j in range(STATE)]
        fresh.append(
            [
                total_of([c * r for c, r in zip(columns, rows[g])]) + keep[d, half * groups + g]
                for g in range(groups)
            ]
        )
    return fresh


def flat(state):
    return tuple(state[0] + state[1])


def folded(values):
    groups = len(values) // 2
    return [list(values[:groups]), list(values[groups:])]


def first_solve_kernel(x, cols, sides, offer, keep, buf):
    n, cells = x.shape[0], x.shape[3]
    width = cells // n
    packed = min(8, n)
    extra, groups = sides.shape[1] // 4, offer.shape[0] // 2
    zero = jnp.zeros((8, cells), jnp.float32)

    def unpack(d, carry):
        values = [x[d, page] for page in range(x.shape[1])]
        for page, value in enumerate(values):
            for k, block in enumerate(split(value, n, packed, width, cells)):
                e = page * n + k * packed
                if e < COLUMNS:
                    for g, item in enumerate(split(block, packed, 1, width, cells)):
                        cols[pl.ds((d * COLUMNS + e + g) * 8, 8), :] = item
                elif e < COLUMNS + 4 * 8:
                    sides[d, (e - COLUMNS) // packed] = block
        return carry

    steps(n, 4, unpack)
    lane = lanes_of(cells)
    row = lax.broadcasted_iota(jnp.int32, (8, cells), 0)
    start = []
    for half in range(2):
        start.append([zero] * extra)
        for g in range(groups - extra):
            column = lane // width % packed + g * packed
            start[half].append((column == row + 8 * half).astype(jnp.float32))

    def ahead(d, state):
        return flat(pass_forward(d, cols, sides, folded(state), buf, keep))

    leaving = steps(n, 4, ahead, flat(start))

    def back(e, state):
        return flat(pass_back(n - 1 - e, cols, folded(state), buf, keep))

    left = steps(n, 4, back, (zero,) * (2 * groups))
    is_left = lax.axis_index("chain") < n
    for e in range(2 * groups):
        offer[e] = jnp.where(is_left, leaving[e], left[e])


def second_solve_kernel(cols, sides, mine, got, out, keep, buf, states):
    n, cells = out.shape[0], out.shape[3]
    width = cells // n
    packed = min(8, n)
    extra, groups = sides.shape[1] // 4, mine.shape[0] // 2
    zero = jnp.zeros((8, cells), jnp.float32)
    is_left = lax.axis_index("chain") < n
    store_state(buf, [[mine[half * groups + g] for g in range(extra)] for half in range(2)])
    rows = state_rows(buf, extra)
    entering, far = [], []
    for half in range(2):
        columns = []
        for g in range(extra, groups):
            columns += split(got[half * groups + g], packed, 1, width, cells)
        for g in range(extra):
            known = got[half * groups + g]
            total = total_of([c * r for c, r in zip(columns, rows[g])])
            entering.append(jnp.where(is_left, 0.0, known))
            far.append(jnp.where(is_left, known + total, 0.0))

    def ahead(d, state):
        for e in range(2 * extra):
            states[d, e] = state[e]
        return flat(pass_forward(d, cols, sides, folded(state), buf, keep))

    steps(n, 4, ahead, tuple(entering))

    def back(e, state):
        d = n - 1 - e
        for e in range(2 * extra):
            states[d, 2 * extra + e] = state[e]
        return flat(pass_back(d, cols, folded(state), buf, keep))

    steps(n, 4, back, tuple(far))
    block = lanes_of(cells) // (packed * width)

    def pack(d, carry):
        for page in range(out.shape[1]):
            total = zero
            for r in range(4 * extra):
                if packed * r // n == page:
                    total = jnp.where(block == packed * r % n // packed, states[d, r], total)
            out[d, page] = total
        return carry

    steps(n, 4, pack)


def sweep_kernel(
    n,
    states,
    source,
    mlow,
    mupp,
    lcols,
    ucols,
    counts,
    low_h,
    side_h,
    zout,
    wout,
    tail,
    edge,
    low,
    side,
    ybuf,
    stage,
    sems,
):
    total = low_h.shape[0]
    copies = [
        pltpu.make_async_copy(src, dst.at[pl.ds(0, total), :], sems.at[k])
        for k, (src, dst) in enumerate(((low_h, low), (side_h, side)))
    ]
    for copy in copies:
        copy.start()
    blocks, _, nrhs, cells = source.shape
    base = lax.axis_index("chain") * blocks
    width = cells // n
    zero = jnp.zeros((nrhs, cells), jnp.float32)
    items = []
    for r in range(states.shape[1]):
        items += block_transpose([states[k, r] for k in range(n)], width, cells)
    for e in range(32):
        stage[pl.ds(8 * e, 8), :] = items[e]

    def entering(start):
        rows = [stage[pl.ds(start + q // 8 * 64 + q % 8, 8, stride=8), :] for q in range(STATE)]
        return tuple(rows)

    lane = lanes_of(cells)
    for v in range(VARS):
        wout[blocks, v] = zero

    def near(window, b, sign, cols, side):
        nears = []
        for k in range(SLOTS):
            off = sign * (cols[k, b] - base - b)
            picks = []
            for v in range(VARS):
                value = window[(REACH - 1) * VARS + v]
                for d in range(REACH - 1):
                    value = jnp.where(off == d + 1, window[d * VARS + v], value)
                picks.append(value if k == 0 else jnp.where(k < counts[side, b], value, 0.0))
            nears.append([[value] for value in picks])
        return nears

    def first(b, window):
        acc = couple(mlow, b, near(window, b, -1, lcols, 0))
        fresh = tuple(source[b, i] + acc[i][0] for i in range(VARS))
        return Kept(fresh + window[: STATE - VARS], [(ybuf, (b, i), fresh[i]) for i in range(VARS)])

    steps(blocks, 8, first, entering(0))

    def second(e, carry):
        c = blocks - 1 - e
        window, edges = carry[:STATE], list(carry[STATE:])
        acc = couple(mupp, c, near(window, c, 1, ucols, 1))
        fresh = tuple(ybuf[c, i] + acc[i][0] for i in range(VARS))
        here = (lane == 2 * c) | (lane == (2 * c + cells - 1) % cells)
        stores = []
        for i in range(VARS):
            stores += [(zout, (c, i), fresh[i]), (wout, (c, i), acc[i][0])]
            edges[i] = jnp.where(here, pltpu.roll(fresh[i], 2 * c, 1), edges[i])
        return Kept(fresh + window[: STATE - VARS] + tuple(edges), stores)

    carry = steps(blocks, 8, second, entering(128) + (zero,) * VARS)
    for v in range(VARS):
        edge[v] = carry[STATE + v]
    for m in range(REACH):
        for v in range(VARS):
            tail[m, v] = wout[blocks - REACH + m, v]
    for copy in copies:
        copy.wait()


def inner_kernel(z, w, low, side, lcols, counts, resid, coef, correction, wbuf, sem):
    store = pltpu.make_async_copy(z, correction, sem)
    store.start()
    blocks, _, nrhs, cells = z.shape
    base = lax.axis_index("chain") * blocks
    lane = lanes_of(cells)
    zero = jnp.zeros((nrhs, cells), jnp.float32)
    for v in range(VARS):
        for m in range(REACH):
            wbuf[m, v] = zero
            wbuf[m + REACH, v] = w[m, v]
        wbuf[2 * REACH, v] = zero
    pages = coef.shape[0]
    size = VARS * VARS * SLOTS
    row = lax.broadcasted_iota(jnp.int32, (8, cells), 0)

    def block(b, found, buf, shift, empty):
        nears = [read_block(buf, s) for s in slots(lcols, counts, 0, b, shift - base, empty)]
        acc = apply_coef(low, b, nears)
        left, right = [], []
        for v in range(VARS):
            here = z[b, v]
            left.append(jnp.where(lane == 0, 0.0, pltpu.roll(here, 1, 1)))
            right.append(jnp.where(lane == cells - 1, 0.0, pltpu.roll(here, cells - 1, 1)))
        beside = apply_coef(side, b, [left, right])
        here = (lane + row % 2) % cells == 2 * b
        found = tuple(
            jnp.where(here, pltpu.roll(side[pl.ds(b * size + 8 * r, 8), :], 2 * b, 1), found[r])
            for r in range(pages)
        )
        return Kept(found, [(resid, (b, i), acc[i] + beside[i]) for i in range(VARS)])

    found = (jnp.zeros((8, cells), jnp.float32),) * pages
    for b in range(REACH):
        kept = block(b, found, wbuf, REACH, 2 * REACH)
        store_all(kept.stores)
        found = kept.carry

    def inner(b, found):
        return block(b + REACH, found, w, 0, blocks)

    found = steps(blocks - REACH, 7, inner, found)
    for r in range(pages):
        coef[r] = found[r]
    store.wait()


def outer_kernel(
    inner, coef, low, tail, swap_a, swap_b, lcols, counts, resid, squares, wbuf
):
    blocks, _, nrhs, cells = inner.shape
    base = lax.axis_index("chain") * blocks
    first_block = lax.axis_index("chain") == 0
    place = lax.axis_index("sub")
    odd = place % 2 == 1
    first, last = place == 0, place == lax.axis_size("sub") - 1
    lane = lanes_of(cells)
    zero = jnp.zeros((nrhs, cells), jnp.float32)
    near = []
    for v in range(VARS):
        west = jnp.where(first, 0.0, jnp.where(odd, swap_a[v], swap_b[v]))
        east = jnp.where(last, 0.0, jnp.where(odd, swap_b[v], swap_a[v]))
        west, east = pltpu.roll(west, 1, 1), pltpu.roll(east, cells - 1, 1)
        near.append(jnp.where(lane % 2 == 0, west, east))
    edge = []
    for i in range(VARS):
        rows = []
        for j in range(VARS):
            k = (i * VARS + j) * SLOTS
            rows.append(coef[k // 8, pl.ds(k % 8, 1), :] + coef[(k + 1) // 8, pl.ds((k + 1) % 8, 1), :])
        edge.append(mul_rows(rows, near))
    for v in range(VARS):
        for m in range(REACH):
            wbuf[m, v] = jnp.where(first_block, 0.0, tail[m, v])
        wbuf[REACH, v] = zero
    ends = (lane == 0) | (lane == cells - 1)

    def add(b, values, totals):
        stores, fresh = [], []
        for i in range(VARS):
            other = pltpu.roll(edge[i], (cells - 2 * b) % cells, 1)
            value = values[i] + jnp.where(ends, other, 0.0)
            stores.append((resid, (b, i), value))
            fresh.append(totals[i] + value * value)
        return Kept(tuple(fresh), stores)

    totals = (zero,) * VARS
    stores = []
    for b in range(REACH):
        places = [
            jnp.where(s < REACH, s, REACH) for s in slots(lcols, counts, 0, b, REACH - base, REACH)
        ]
        acc = apply_coef(low, b, [read_block(wbuf, s) for s in places])
        kept = add(b, [inner[b, i] + acc[i] for i in range(VARS)], totals)
        stores += kept.stores
        totals = kept.carry
    store_all(stores)

    def rest(b, totals):
        return add(b + REACH, [inner[b + REACH, i] for i in range(VARS)], totals)

    totals = steps(blocks - REACH, 7, rest, totals)
    total = totals[0]
    for i in range(1, VARS):
        total = total + totals[i]
    sums = jnp.broadcast_to(jnp.sum(total, axis=1, keepdims=True), total.shape)
    row = lax.broadcasted_iota(jnp.int32, total.shape, 0)
    line = jnp.sum(jnp.where(lane == row, sums, 0.0), axis=0, keepdims=True)
    for p in range(squares.shape[0]):
        squares[p] = line


def scale_kernel(entries, resid, squares, out):
    blocks, _, nrhs, cells = resid.shape
    line = squares[0]
    for p in range(1, squares.shape[0]):
        line = line + squares[p]
    lane = lanes_of(cells)
    row = lax.broadcasted_iota(jnp.int32, (nrhs, cells), 0)
    line = jnp.where(lane == row, jnp.broadcast_to(line, (nrhs, cells)), 0.0)
    msq = jnp.sum(line, axis=1, keepdims=True) / entries
    factor = jnp.broadcast_to(-lax.rsqrt(msq + 1e-06), (nrhs, cells))

    def block(b, carry):
        return Kept(carry, [(out, (b, v), resid[b, v] * factor) for v in range(VARS)])

    steps(blocks, 12, block)


def call(kernel, outs, args, places, scratch):
    args = [
        pltpu.with_memory_space_constraint(a, p) if p is HBM else a for a, p in zip(args, places)
    ]
    return pl.pallas_call(
        kernel,
        out_shape=[jax.ShapeDtypeStruct(o[0], (o + (jnp.float32,))[2]) for o in outs],
        in_specs=[pl.BlockSpec(memory_space=p) for p in places],
        out_specs=[pl.BlockSpec(memory_space=p) for p in (o[1] for o in outs)],
        scratch_shapes=[VMEM(s, jnp.float32) if isinstance(s, tuple) else s for s in scratch],
        compiler_params=pltpu.CompilerParams(vmem_limit_bytes=VMEM_LIMIT),
    )(*args)


def shards(
    rhs, diag_block, diag_inverse, lower_coef, upper_coef, side_coef, lower_cols, upper_cols, counts
):
    blocks, nvars, nrhs, cells = rhs.shape
    n = lax.axis_size("chain")
    inv = jnp.transpose(diag_inverse, (1, 2, 0, 3))
    low, upp, side = (
        jnp.transpose(a, (0, 2, 3, 1, 4)).reshape(-1, cells)
        for a in (lower_coef, upper_coef, side_coef)
    )
    lcols, ucols, used = lower_cols.T, upper_cols.T, counts.T
    m = lax.axis_size("sub")
    rows = blocks + REACH + 1
    half = n // 2
    parts = -(-len(column_order(nrhs)) // half)
    back = -(-32 // half)
    packed = min(8, half)
    extra = 8 // packed
    wide = 2 * (extra + WIDE // packed)
    sides = [list(range(half)), list(range(half, n))]
    tile = (nrhs, cells)

    mats = (VARS, VARS, SLOTS, blocks + PAD, cells)
    padded = (low.shape[0] + PAD, cells)

    count = half if half <= DIRECT else 1

    def pieces(pages):
        return [((pages,) + tile, VMEM)] * count if count > 1 else [((half, pages) + tile, VMEM)]

    def whole(pages):
        return [(half, pages) + tile] if count > 1 else []

    *maps, source, mlow, mupp, lcols, ucols, used = call(
        functools.partial(parted, functools.partial(local_kernel, half), 7, count, half),
        pieces(parts)
        + [(rhs.shape, VMEM), (mats, VMEM), (mats, VMEM)]
        + [(lcols.shape, VMEM, jnp.int32)] * 3,
        (rhs, inv, low, upp, lcols, ucols, used),
        (HBM,) * 7,
        [rhs.shape, (VARS, VARS, blocks + PAD, cells), low.shape, upp.shape]
        + [pltpu.SMEM(lcols.shape, jnp.int32)] * 3
        + [(rows, VARS, nrhs + WIDE, cells), (rows, VARS, nrhs + 2 * WIDE, cells)]
        + [(WIDE * SPACE, cells), pltpu.SemaphoreType.DMA((10,))]
        + whole(parts),
    )
    maps = exchange(maps, half, sides)
    cols, ends, offer = call(
        functools.partial(joined, first_solve_kernel, count, half),
        [
            ((half * COLUMNS * 8, cells), VMEM),
            ((half, 4 * extra) + tile, VMEM),
            ((wide,) + tile, VMEM),
        ],
        tuple(maps),
        (VMEM,) * count,
        [(half, wide) + tile, (wide // 2 * WIDE + PAD, cells)] + whole(parts),
    )
    got = lax.ppermute(
        offer, "chain", [p for i in range(half) for p in ((i, i + half), (i + half, i))]
    )
    states = call(
        functools.partial(parted, second_solve_kernel, 4, count, half),
        pieces(back),
        (cols, ends, offer, got),
        (VMEM,) * 4,
        [(half, 2 * extra) + tile, (extra * WIDE + PAD, cells), (half, 4 * extra) + tile]
        + whole(back),
    )
    states = exchange(states, half, sides)
    z, w, tail, edge, low, side = call(
        functools.partial(joined, functools.partial(sweep_kernel, half), count, half),
        [
            (rhs.shape, VMEM),
            ((blocks + 1, VARS) + tile, VMEM),
            ((REACH, VARS) + tile, VMEM),
            ((VARS,) + tile, VMEM),
            (padded, VMEM),
            (padded, VMEM),
        ],
        (*states, source, mlow, mupp, lcols, ucols, used, low, side),
        (VMEM,) * (3 + count) + (SMEM,) * 3 + (HBM,) * 2,
        [rhs.shape, (32 * 8, cells), pltpu.SemaphoreType.DMA((2,))] + whole(back),
    )
    tail = lax.ppermute(tail, "chain", [(i, (i + 1) % n) for i in range(n)])
    swap_a, swap_b = (
        lax.ppermute(edge, "sub", [p for i, j in pairs for p in ((i, j), (j, i))])
        for pairs in (
            [(i, i + 1) for i in range(0, m - 1, 2)],
            [(i, i + 1) for i in range(1, m - 1, 2)] + [(0, m - 1)] * (m % 2 == 0),
        )
    )
    inner, coef, correction = call(
        inner_kernel,
        [
            (rhs.shape, VMEM),
            ((-(-VARS * VARS * SLOTS // 8),) + (8, cells), VMEM),
            (rhs.shape, HBM),
        ],
        (z, w, low, side, lcols, used),
        (VMEM,) * 4 + (SMEM,) * 2,
        [(2 * REACH + 1, VARS) + tile, pltpu.SemaphoreType.DMA],
    )
    resid, squares = call(
        outer_kernel,
        [(rhs.shape, VMEM), ((n * m, 1, cells), VMEM)],
        (inner, coef, low, tail, swap_a, swap_b, lcols, used),
        (VMEM,) * 6 + (SMEM,) * 2,
        [(REACH + 1, VARS) + tile],
    )
    squares = lax.all_to_all(squares, ("chain", "sub"), 0, 0, tiled=True)
    entries = blocks * VARS * cells * n * m
    (residual_unit,) = call(
        functools.partial(scale_kernel, entries),
        [(rhs.shape, VMEM)],
        (resid, squares),
        (VMEM, VMEM),
        [],
    )
    return (correction, residual_unit)


def solution(mesh):
    in_specs = (
        P("chain", None, None, "sub"),
        P("chain", None, None, "sub"),
        P("chain", None, None, "sub"),
        P("chain", None, None, None, "sub"),
        P("chain", None, None, None, "sub"),
        P("chain", None, None, None, "sub"),
        P("chain", None),
        P("chain", None),
        P("chain", None),
    )
    out_specs = (P("chain", None, None, "sub"), P("chain", None, None, "sub"))
    return jax.shard_map(shards, mesh=mesh, in_specs=in_specs, out_specs=out_specs, check_vma=False)
```

```python
import functools

import jax
import jax.numpy as jnp
from jax import lax
from jax.experimental import pallas as pl
from jax.experimental.pallas import tpu as pltpu
from jax.sharding import PartitionSpec as P

VARS = 5
REACH = 3
SLOTS = 2
STATE = REACH * VARS
WIDE = 16
PAD = 8
SPACE = 72
DIRECT = 4
VMEM_LIMIT = 40 * 1024 * 1024

VMEM = pltpu.VMEM
SMEM = pltpu.SMEM
HBM = pltpu.HBM


def lanes_of(cells):
    return lax.broadcasted_iota(jnp.int32, (8, cells), 1)


def block_transpose(items, width, cells):
    count = len(items)
    lane = lanes_of(cells)
    half = 1
    while half < count:
        bit = (lane // (half * width)) % 2 == 1
        out = list(items)
        for a in range(count):
            if a & half:
                continue
            b = a + half
            out[a] = jnp.where(bit, pltpu.roll(items[b], half * width, 1), items[a])
            out[b] = jnp.where(bit, items[b], pltpu.roll(items[a], cells - half * width, 1))
        items = out
        half *= 2
    return items


def spread(ref, place, row):
    return ref[place + (pl.ds(row, 8, stride=0), slice(None))]


def mul_rows(rows, near):
    total = rows[0] * near[0]
    for j in range(1, len(near)):
        total = total + rows[j] * near[j]
    return total


def mul_groups(rows, nears):
    return [mul_rows(rows, [near[g] for near in nears]) for g in range(len(nears[0]))]


def couple(mats, b, nears):
    out = []
    for i in range(VARS):
        parts = [
            mul_groups([spread(mats, (i, j, k), b) for j in range(VARS)], nears[k])
            for k in range(SLOTS)
        ]
        out.append([x + y for x, y in zip(*parts)])
    return out


def apply_coef(coef, b, nears):
    out = []
    for i in range(VARS):
        parts = []
        for k in range(SLOTS):
            place = (b * VARS + i) * VARS * SLOTS + k
            parts.append(
                mul_rows([spread(coef, (), place + SLOTS * j) for j in range(VARS)], nears[k])
            )
        out.append(parts[0] + parts[1])
    return out


def products(inv, coef, out):
    blocks = out.shape[3] - PAD
    stride = VARS * VARS * SLOTS

    def some(o, carry):
        start = o * 8
        left = [[-inv[i, m, pl.ds(start, 8), :] for m in range(VARS)] for i in range(VARS)]
        for k in range(SLOTS):
            stores = []
            for j in range(VARS):
                place = start * stride + j * SLOTS + k
                right = [
                    coef[pl.ds(place + m * VARS * SLOTS, 8, stride=stride), :] for m in range(VARS)
                ]
                for i in range(VARS):
                    here = (i, j, k, pl.ds(start, 8))
                    stores.append((out, here, mul_rows(left[i], right)))
            store_all(stores)
        return carry

    steps(blocks // 8, 3, some)


def slots(cols, counts, side, b, shift, empty):
    return [jnp.where(k < counts[side, b], cols[k, b] + shift, empty) for k in range(SLOTS)]


def read_block(buf, place):
    return [buf[place, v] for v in range(VARS)]


def read_groups(buf, place):
    count = buf.shape[2] // 8
    return [[buf[place, v, pl.ds(8 * g, 8), :] for g in range(count)] for v in range(VARS)]


class Kept:
    def __init__(self, carry, stores):
        self.carry, self.stores = carry, stores


def store_all(stores):
    for ref, place, value in stores:
        ref[place] = value


def steps(count, most, body, carry=0):
    unroll = max(u for u in range(1, most + 1) if count % u == 0)

    def chunk(o, carry):
        kept = []
        for u in range(unroll):
            carry = body(o * unroll + u, carry)
            if isinstance(carry, Kept):
                kept += carry.stores
                carry = carry.carry
        store_all(kept)
        return carry

    return lax.fori_loop(0, count // unroll, chunk, carry)


def column_order(nrhs):
    wide_y = nrhs + WIDE
    order = []
    for first, count in ((nrhs, STATE), (wide_y + nrhs, STATE - 1), (wide_y + nrhs + WIDE, STATE)):
        order += [(half, first + j) for half in range(2) for j in range(count)]
    for first in (0, wide_y):
        order += [(half, first + q) for half in range(2) for q in range(nrhs)]
    return order


def position(n):
    return lax.axis_index("chain") % n


def gather_parts(parts, buf):
    here = position(buf.shape[0])
    for x, part in enumerate(parts):
        for page in range(part.shape[0]):
            buf[here ^ x, page] = part[page]


def scatter_parts(buf, parts):
    here = position(buf.shape[0])
    for x, part in enumerate(parts):
        for page in range(part.shape[0]):
            part[page] = buf[here ^ x, page]


def parted(kernel, before, count, n, *refs):
    if count == 1:
        return kernel(*refs)
    outs, buf = refs[before : before + count], refs[-1]
    kernel(*refs[:before], buf, *refs[before + count : -1])
    scatter_parts(buf, outs)


def joined(kernel, count, n, *refs):
    if count == 1:
        return kernel(*refs)
    gather_parts(refs[:count], refs[-1])
    kernel(refs[-1], *refs[count:-1])


def exchange(parts, n, groups):
    if len(parts) == 1:
        return [lax.all_to_all(parts[0], "chain", 0, 0, tiled=True, axis_index_groups=groups)]
    count = lax.axis_size("chain")
    parts = list(parts)
    for x in [len(parts) - 1] + list(range(1, len(parts) - 1)):
        parts[x] = lax.ppermute(parts[x], "chain", [(i, i ^ x) for i in range(count)])
    return parts


def local_kernel(
    n,
    rhs_h,
    inv_h,
    low_h,
    upp_h,
    lcols_h,
    ucols_h,
    counts_h,
    out,
    source,
    mlow,
    mupp,
    lcols_v,
    ucols_v,
    counts_v,
    rhs,
    inv,
    low,
    upp,
    lcols,
    ucols,
    counts,
    ybuf,
    zbuf,
    stage,
    sems,
):
    copies = [
        pltpu.make_async_copy(src, dst, sems.at[k])
        for k, (src, dst) in enumerate(
            (
                (inv_h, inv.at[:, :, pl.ds(0, rhs.shape[0]), :]),
                (low_h, low),
                (lcols_h, lcols),
                (counts_h, counts),
                (ucols_h, ucols),
                (rhs_h, rhs),
                (upp_h, upp),
                (lcols_h, lcols_v),
                (ucols_h, ucols_v),
                (counts_h, counts_v),
            )
        )
    ]
    for copy in copies:
        copy.start()
    blocks, _, nrhs, cells = rhs.shape
    base = lax.axis_index("chain") * blocks
    wide_y = nrhs + WIDE
    wide_z = wide_y + WIDE
    row_y = lax.broadcasted_iota(jnp.int32, (wide_y, cells), 0)
    row_z = lax.broadcasted_iota(jnp.int32, (wide_z, cells), 0)
    for m in range(REACH):
        for v in range(VARS):
            q = VARS * m + v
            ybuf[REACH - 1 - m, v] = (row_y == nrhs + q).astype(jnp.float32)
            zbuf[blocks + m, v] = (row_z == wide_y + q).astype(jnp.float32)
    for v in range(VARS):
        ybuf[blocks + REACH, v] = jnp.zeros((wide_y, cells), jnp.float32)
        zbuf[blocks + REACH, v] = jnp.zeros((wide_z, cells), jnp.float32)
    empty = blocks + REACH
    copies[0].wait()
    copies[1].wait()
    products(inv, low, mlow)
    for copy in copies[2:6]:
        copy.wait()

    def first(b, carry):
        nears = [read_groups(ybuf, s) for s in slots(lcols, counts, 0, b, REACH - base, empty)]
        acc = couple(mlow, b, nears)
        right = [rhs[b, i] for i in range(VARS)]
        stores = []
        for i in range(VARS):
            own = mul_rows([spread(inv, (i, j), b) for j in range(VARS)], right)
            stores.append((source, (b, i), own))
            for g in range(len(acc[i])):
                value = own + acc[i][0] if g == 0 else acc[i][g]
                stores.append((ybuf, (b + REACH, i, pl.ds(8 * g, 8)), value))
        store_all(stores)
        return carry

    steps(blocks, 6, first)
    for copy in copies[6:]:
        copy.wait()
    products(inv, upp, mupp)

    def second(e, carry):
        c = blocks - 1 - e
        nears = [read_groups(zbuf, s) for s in slots(ucols, counts, 1, c, -base, empty)]
        acc = couple(mupp, c, nears)
        stores = []
        for i in range(VARS):
            for g in range(len(acc[i])):
                if g < wide_y // 8:
                    value = ybuf[c + REACH, i, 8 * g : 8 * g + 8] + acc[i][g]
                else:
                    value = acc[i][g]
                stores.append((zbuf, (c, i, pl.ds(8 * g, 8)), value))
        store_all(stores)
        return carry

    steps(blocks, 6, second)

    zero = jnp.zeros((8, cells), jnp.float32)
    for i in range(WIDE):
        m, v = i // VARS, i % VARS
        for g in range((wide_y + wide_z) // 8):
            if i == STATE:
                value = zero
            elif g < wide_y // 8:
                value = ybuf[blocks + REACH - 1 - m, v, 8 * g : 8 * g + 8]
            else:
                value = zbuf[m, v, 8 * g - wide_y : 8 * g - wide_y + 8]
            stage[pl.ds(i * SPACE + 8 * g, 8), :] = value

    def column(half, index):
        return stage[pl.ds(half * 8 * SPACE + index, 8, stride=SPACE), :]

    for half in range(2):
        place = STATE * SPACE + nrhs + 8 * half
        stage[pl.ds(place, 8), :] = column(half, wide_y + nrhs + STATE - 1)
    order = column_order(nrhs)
    width = cells // n
    for page in range(out.shape[1]):
        items = [column(*at) for at in order[page * n : (page + 1) * n]]
        items += [zero] * (n - len(items))
        for k, item in enumerate(block_transpose(items, width, cells)):
            out[k, page] = item


def split(value, period, stop, width, cells):
    items = [value]
    lane = lanes_of(cells)
    while period > stop:
        half = period // 2 * width
        bit = lane // half % 2 == 1
        fresh = []
        for item in items:
            other = pltpu.roll(item, half, 1)
            fresh += [jnp.where(bit, other, item), jnp.where(bit, item, other)]
        items = fresh
        period //= 2
    return items


def total_of(terms):
    while len(terms) > 1:
        pairs = [terms[k] + terms[k + 1] for k in range(0, len(terms) - 1, 2)]
        terms = pairs + terms[len(terms) - len(terms) % 2 :]
    return terms[0]


COLUMNS = 6 * STATE - 2


def store_state(buf, state):
    for half in range(2):
        for g, value in enumerate(state[half]):
            buf[pl.ds(g * WIDE + 8 * half, 8), :] = value


def state_rows(buf, count):
    return [[spread(buf, (), g * WIDE + j) for j in range(STATE)] for g in range(count)]


def pass_forward(d, cols, sides, state, buf, keep):
    groups, extra = len(state[0]), sides.shape[1] // 4
    store_state(buf, state)
    rows = state_rows(buf, groups)
    fresh = []
    for half in range(2):
        columns = [cols[pl.ds((d * COLUMNS + half * STATE + j) * 8, 8), :] for j in range(STATE)]
        fresh.append([])
        for g in range(groups):
            total = total_of([c * r for c, r in zip(columns, rows[g])])
            fresh[half].append(total + sides[d, half * extra + g] if g < extra else total)
        first = d * COLUMNS + 2 * STATE + half * (STATE - 1)
        columns = [cols[pl.ds((first + j) * 8, 8), :] for j in range(STATE - 1)]
        start = (d * COLUMNS + STATE + 8 * half) * 8 + 7
        columns.append(cols[pl.ds(start, 8, stride=8), :])
        for g in range(groups):
            total = total_of([c * r for c, r in zip(columns, rows[g])])
            if g < extra:
                total = total + sides[d, (2 + half) * extra + g]
            keep[d, half * groups + g] = total
    return fresh


def pass_back(d, cols, state, buf, keep):
    groups = len(state[0])
    store_state(buf, state)
    rows = state_rows(buf, groups)
    fresh = []
    for half in range(2):
        first = d * COLUMNS + 4 * STATE - 2 + half * STATE
        columns = [cols[pl.ds((first + j) * 8, 8), :] for j in range(STATE)]
        fresh.append(
            [
                total_of([c * r for c, r in zip(columns, rows[g])]) + keep[d, half * groups + g]
                for g in range(groups)
            ]
        )
    return fresh


def flat(state):
    return tuple(state[0] + state[1])


def folded(values):
    groups = len(values) // 2
    return [list(values[:groups]), list(values[groups:])]


def first_solve_kernel(x, cols, sides, offer, keep, buf):
    n, cells = x.shape[0], x.shape[3]
    width = cells // n
    packed = min(8, n)
    extra, groups = sides.shape[1] // 4, offer.shape[0] // 2
    zero = jnp.zeros((8, cells), jnp.float32)

    def unpack(d, carry):
        values = [x[d, page] for page in range(x.shape[1])]
        for page, value in enumerate(values):
            for k, block in enumerate(split(value, n, packed, width, cells)):
                e = page * n + k * packed
                if e < COLUMNS:
                    for g, item in enumerate(split(block, packed, 1, width, cells)):
                        cols[pl.ds((d * COLUMNS + e + g) * 8, 8), :] = item
                elif e < COLUMNS + 4 * 8:
                    sides[d, (e - COLUMNS) // packed] = block
        return carry

    steps(n, 2, unpack)
    lane = lanes_of(cells)
    row = lax.broadcasted_iota(jnp.int32, (8, cells), 0)
    start = []
    for half in range(2):
        start.append([zero] * extra)
        for g in range(groups - extra):
            column = lane // width % packed + g * packed
            start[half].append((column == row + 8 * half).astype(jnp.float32))

    def ahead(d, state):
        return flat(pass_forward(d, cols, sides, folded(state), buf, keep))

    leaving = steps(n, 2, ahead, flat(start))

    def back(e, state):
        return flat(pass_back(n - 1 - e, cols, folded(state), buf, keep))

    left = steps(n, 2, back, (zero,) * (2 * groups))
    is_left = lax.axis_index("chain") < n
    for e in range(2 * groups):
        offer[e] = jnp.where(is_left, leaving[e], left[e])


def second_solve_kernel(cols, sides, mine, got, out, keep, buf, states):
    n, cells = out.shape[0], out.shape[3]
    width = cells // n
    packed = min(8, n)
    extra, groups = sides.shape[1] // 4, mine.shape[0] // 2
    zero = jnp.zeros((8, cells), jnp.float32)
    is_left = lax.axis_index("chain") < n
    store_state(buf, [[mine[half * groups + g] for g in range(extra)] for half in range(2)])
    rows = state_rows(buf, extra)
    entering, far = [], []
    for half in range(2):
        columns = []
        for g in range(extra, groups):
            columns += split(got[half * groups + g], packed, 1, width, cells)
        for g in range(extra):
            known = got[half * groups + g]
            total = total_of([c * r for c, r in zip(columns, rows[g])])
            entering.append(jnp.where(is_left, 0.0, known))
            far.append(jnp.where(is_left, known + total, 0.0))

    def ahead(d, state):
        for e in range(2 * extra):
            states[d, e] = state[e]
        return flat(pass_forward(d, cols, sides, folded(state), buf, keep))

    steps(n, 4, ahead, tuple(entering))

    def back(e, state):
        d = n - 1 - e
        for e in range(2 * extra):
            states[d, 2 * extra + e] = state[e]
        return flat(pass_back(d, cols, folded(state), buf, keep))

    steps(n, 4, back, tuple(far))
    block = lanes_of(cells) // (packed * width)

    def pack(d, carry):
        for page in range(out.shape[1]):
            total = zero
            for r in range(4 * extra):
                if packed * r // n == page:
                    total = jnp.where(block == packed * r % n // packed, states[d, r], total)
            out[d, page] = total
        return carry

    steps(n, 4, pack)


def sweep_kernel(
    n,
    states,
    source,
    mlow,
    mupp,
    lcols,
    ucols,
    counts,
    low_h,
    side_h,
    zout,
    wout,
    tail,
    edge,
    low,
    side,
    ybuf,
    stage,
    sems,
):
    total = low_h.shape[0]
    copies = [
        pltpu.make_async_copy(src, dst.at[pl.ds(0, total), :], sems.at[k])
        for k, (src, dst) in enumerate(((low_h, low), (side_h, side)))
    ]
    for copy in copies:
        copy.start()
    blocks, _, nrhs, cells = source.shape
    base = lax.axis_index("chain") * blocks
    width = cells // n
    zero = jnp.zeros((nrhs, cells), jnp.float32)
    items = []
    for r in range(states.shape[1]):
        items += block_transpose([states[k, r] for k in range(n)], width, cells)
    for e in range(32):
        stage[pl.ds(8 * e, 8), :] = items[e]

    def entering(start):
        rows = [stage[pl.ds(start + q // 8 * 64 + q % 8, 8, stride=8), :] for q in range(STATE)]
        return tuple(rows)

    lane = lanes_of(cells)
    for v in range(VARS):
        wout[blocks, v] = zero

    def near(window, b, sign, cols, side):
        nears = []
        for k in range(SLOTS):
            off = sign * (cols[k, b] - base - b)
            picks = []
            for v in range(VARS):
                value = window[(REACH - 1) * VARS + v]
                for d in range(REACH - 1):
                    value = jnp.where(off == d + 1, window[d * VARS + v], value)
                picks.append(value if k == 0 else jnp.where(k < counts[side, b], value, 0.0))
            nears.append([[value] for value in picks])
        return nears

    def first(b, window):
        acc = couple(mlow, b, near(window, b, -1, lcols, 0))
        fresh = tuple(source[b, i] + acc[i][0] for i in range(VARS))
        return Kept(fresh + window[: STATE - VARS], [(ybuf, (b, i), fresh[i]) for i in range(VARS)])

    steps(blocks, 8, first, entering(0))

    def second(e, carry):
        c = blocks - 1 - e
        window, edges = carry[:STATE], list(carry[STATE:])
        acc = couple(mupp, c, near(window, c, 1, ucols, 1))
        fresh = tuple(ybuf[c, i] + acc[i][0] for i in range(VARS))
        here = (lane == 2 * c) | (lane == (2 * c + cells - 1) % cells)
        stores = []
        for i in range(VARS):
            stores += [(zout, (c, i), fresh[i]), (wout, (c, i), acc[i][0])]
            edges[i] = jnp.where(here, pltpu.roll(fresh[i], 2 * c, 1), edges[i])
        return Kept(fresh + window[: STATE - VARS] + tuple(edges), stores)

    carry = steps(blocks, 8, second, entering(128) + (zero,) * VARS)
    for v in range(VARS):
        edge[v] = carry[STATE + v]
    for m in range(REACH):
        for v in range(VARS):
            tail[m, v] = wout[blocks - REACH + m, v]
    for copy in copies:
        copy.wait()


def inner_kernel(z, w, low, side, lcols, counts, resid, coef, correction, wbuf, sem):
    store = pltpu.make_async_copy(z, correction, sem)
    store.start()
    blocks, _, nrhs, cells = z.shape
    base = lax.axis_index("chain") * blocks
    lane = lanes_of(cells)
    zero = jnp.zeros((nrhs, cells), jnp.float32)
    for v in range(VARS):
        for m in range(REACH):
            wbuf[m, v] = zero
            wbuf[m + REACH, v] = w[m, v]
        wbuf[2 * REACH, v] = zero
    pages = coef.shape[0]
    size = VARS * VARS * SLOTS
    row = lax.broadcasted_iota(jnp.int32, (8, cells), 0)

    def block(b, found, buf, shift, empty):
        nears = [read_block(buf, s) for s in slots(lcols, counts, 0, b, shift - base, empty)]
        acc = apply_coef(low, b, nears)
        left, right = [], []
        for v in range(VARS):
            here = z[b, v]
            left.append(jnp.where(lane == 0, 0.0, pltpu.roll(here, 1, 1)))
            right.append(jnp.where(lane == cells - 1, 0.0, pltpu.roll(here, cells - 1, 1)))
        beside = apply_coef(side, b, [left, right])
        here = (lane + row % 2) % cells == 2 * b
        found = tuple(
            jnp.where(here, pltpu.roll(side[pl.ds(b * size + 8 * r, 8), :], 2 * b, 1), found[r])
            for r in range(pages)
        )
        return Kept(found, [(resid, (b, i), acc[i] + beside[i]) for i in range(VARS)])

    found = (jnp.zeros((8, cells), jnp.float32),) * pages
    for b in range(REACH):
        kept = block(b, found, wbuf, REACH, 2 * REACH)
        store_all(kept.stores)
        found = kept.carry

    def inner(b, found):
        return block(b + REACH, found, w, 0, blocks)

    found = steps(blocks - REACH, 7, inner, found)
    for r in range(pages):
        coef[r] = found[r]
    store.wait()


def outer_kernel(
    inner, coef, low, tail, swap_a, swap_b, lcols, counts, resid, squares, wbuf
):
    blocks, _, nrhs, cells = inner.shape
    base = lax.axis_index("chain") * blocks
    first_block = lax.axis_index("chain") == 0
    place = lax.axis_index("sub")
    odd = place % 2 == 1
    first, last = place == 0, place == lax.axis_size("sub") - 1
    lane = lanes_of(cells)
    zero = jnp.zeros((nrhs, cells), jnp.float32)
    near = []
    for v in range(VARS):
        west = jnp.where(first, 0.0, jnp.where(odd, swap_a[v], swap_b[v]))
        east = jnp.where(last, 0.0, jnp.where(odd, swap_b[v], swap_a[v]))
        west, east = pltpu.roll(west, 1, 1), pltpu.roll(east, cells - 1, 1)
        near.append(jnp.where(lane % 2 == 0, west, east))
    edge = []
    for i in range(VARS):
        rows = []
        for j in range(VARS):
            k = (i * VARS + j) * SLOTS
            rows.append(coef[k // 8, pl.ds(k % 8, 1), :] + coef[(k + 1) // 8, pl.ds((k + 1) % 8, 1), :])
        edge.append(mul_rows(rows, near))
    for v in range(VARS):
        for m in range(REACH):
            wbuf[m, v] = jnp.where(first_block, 0.0, tail[m, v])
        wbuf[REACH, v] = zero
    ends = (lane == 0) | (lane == cells - 1)

    def add(b, values, totals):
        stores, fresh = [], []
        for i in range(VARS):
            other = pltpu.roll(edge[i], (cells - 2 * b) % cells, 1)
            value = values[i] + jnp.where(ends, other, 0.0)
            stores.append((resid, (b, i), value))
            fresh.append(totals[i] + value * value)
        return Kept(tuple(fresh), stores)

    totals = (zero,) * VARS
    stores = []
    for b in range(REACH):
        places = [
            jnp.where(s < REACH, s, REACH) for s in slots(lcols, counts, 0, b, REACH - base, REACH)
        ]
        acc = apply_coef(low, b, [read_block(wbuf, s) for s in places])
        kept = add(b, [inner[b, i] + acc[i] for i in range(VARS)], totals)
        stores += kept.stores
        totals = kept.carry
    store_all(stores)

    def rest(b, totals):
        return add(b + REACH, [inner[b + REACH, i] for i in range(VARS)], totals)

    totals = steps(blocks - REACH, 7, rest, totals)
    total = totals[0]
    for i in range(1, VARS):
        total = total + totals[i]
    sums = jnp.broadcast_to(jnp.sum(total, axis=1, keepdims=True), total.shape)
    row = lax.broadcasted_iota(jnp.int32, total.shape, 0)
    line = jnp.sum(jnp.where(lane == row, sums, 0.0), axis=0, keepdims=True)
    for p in range(squares.shape[0]):
        squares[p] = line


def scale_kernel(entries, resid, squares, out, scaled, sems):
    blocks, _, nrhs, cells = resid.shape
    line = squares[0]
    for p in range(1, squares.shape[0]):
        line = line + squares[p]
    lane = lanes_of(cells)
    row = lax.broadcasted_iota(jnp.int32, (nrhs, cells), 0)
    line = jnp.where(lane == row, jnp.broadcast_to(line, (nrhs, cells)), 0.0)
    msq = jnp.sum(line, axis=1, keepdims=True) / entries
    factor = jnp.broadcast_to(-lax.rsqrt(msq + 1e-06), (nrhs, cells))

    count = sems.shape[0]
    size = blocks // count
    copies = []
    for part in range(count):
        stores = [
            (scaled, (b, v), resid[b, v] * factor)
            for b in range(part * size, (part + 1) * size)
            for v in range(VARS)
        ]
        store_all(stores)
        here = pl.ds(part * size, size)
        copies.append(pltpu.make_async_copy(scaled.at[here], out.at[here], sems.at[part]))
        copies[part].start()
    for copy in copies:
        copy.wait()


def call(kernel, outs, args, places, scratch):
    args = [
        pltpu.with_memory_space_constraint(a, p) if p is HBM else a for a, p in zip(args, places)
    ]
    return pl.pallas_call(
        kernel,
        out_shape=[jax.ShapeDtypeStruct(o[0], (o + (jnp.float32,))[2]) for o in outs],
        in_specs=[pl.BlockSpec(memory_space=p) for p in places],
        out_specs=[pl.BlockSpec(memory_space=p) for p in (o[1] for o in outs)],
        scratch_shapes=[VMEM(s, jnp.float32) if isinstance(s, tuple) else s for s in scratch],
        compiler_params=pltpu.CompilerParams(vmem_limit_bytes=VMEM_LIMIT),
    )(*args)


def shards(
    rhs, diag_block, diag_inverse, lower_coef, upper_coef, side_coef, lower_cols, upper_cols, counts
):
    blocks, nvars, nrhs, cells = rhs.shape
    n = lax.axis_size("chain")
    inv = jnp.transpose(diag_inverse, (1, 2, 0, 3))
    low, upp, side = (
        jnp.transpose(a, (0, 2, 3, 1, 4)).reshape(-1, cells)
        for a in (lower_coef, upper_coef, side_coef)
    )
    lcols, ucols, used = lower_cols.T, upper_cols.T, counts.T
    m = lax.axis_size("sub")
    rows = blocks + REACH + 1
    half = n // 2
    parts = -(-len(column_order(nrhs)) // half)
    back = -(-32 // half)
    packed = min(8, half)
    extra = 8 // packed
    wide = 2 * (extra + WIDE // packed)
    sides = [list(range(half)), list(range(half, n))]
    tile = (nrhs, cells)

    mats = (VARS, VARS, SLOTS, blocks + PAD, cells)
    padded = (low.shape[0] + PAD, cells)

    count = half if half <= DIRECT else 1

    def pieces(pages):
        return [((pages,) + tile, VMEM)] * count if count > 1 else [((half, pages) + tile, VMEM)]

    def whole(pages):
        return [(half, pages) + tile] if count > 1 else []

    *maps, source, mlow, mupp, lcols, ucols, used = call(
        functools.partial(parted, functools.partial(local_kernel, half), 7, count, half),
        pieces(parts)
        + [(rhs.shape, VMEM), (mats, VMEM), (mats, VMEM)]
        + [(lcols.shape, VMEM, jnp.int32)] * 3,
        (rhs, inv, low, upp, lcols, ucols, used),
        (HBM,) * 7,
        [rhs.shape, (VARS, VARS, blocks + PAD, cells), low.shape, upp.shape]
        + [pltpu.SMEM(lcols.shape, jnp.int32)] * 3
        + [(rows, VARS, nrhs + WIDE, cells), (rows, VARS, nrhs + 2 * WIDE, cells)]
        + [(WIDE * SPACE, cells), pltpu.SemaphoreType.DMA((10,))]
        + whole(parts),
    )
    maps = exchange(maps, half, sides)
    cols, ends, offer = call(
        functools.partial(joined, first_solve_kernel, count, half),
        [
            ((half * COLUMNS * 8, cells), VMEM),
            ((half, 4 * extra) + tile, VMEM),
            ((wide,) + tile, VMEM),
        ],
        tuple(maps),
        (VMEM,) * count,
        [(half, wide) + tile, (wide // 2 * WIDE + PAD, cells)] + whole(parts),
    )
    got = lax.ppermute(
        offer, "chain", [p for i in range(half) for p in ((i, i + half), (i + half, i))]
    )
    states = call(
        functools.partial(parted, second_solve_kernel, 4, count, half),
        pieces(back),
        (cols, ends, offer, got),
        (VMEM,) * 4,
        [(half, 2 * extra) + tile, (extra * WIDE + PAD, cells), (half, 4 * extra) + tile]
        + whole(back),
    )
    states = exchange(states, half, sides)
    z, w, tail, edge, low, side = call(
        functools.partial(joined, functools.partial(sweep_kernel, half), count, half),
        [
            (rhs.shape, VMEM),
            ((blocks + 1, VARS) + tile, VMEM),
            ((REACH, VARS) + tile, VMEM),
            ((VARS,) + tile, VMEM),
            (padded, VMEM),
            (padded, VMEM),
        ],
        (*states, source, mlow, mupp, lcols, ucols, used, low, side),
        (VMEM,) * (3 + count) + (SMEM,) * 3 + (HBM,) * 2,
        [rhs.shape, (32 * 8, cells), pltpu.SemaphoreType.DMA((2,))] + whole(back),
    )
    tail = lax.ppermute(tail, "chain", [(i, (i + 1) % n) for i in range(n)])
    swap_a, swap_b = (
        lax.ppermute(edge, "sub", [p for i, j in pairs for p in ((i, j), (j, i))])
        for pairs in (
            [(i, i + 1) for i in range(0, m - 1, 2)],
            [(i, i + 1) for i in range(1, m - 1, 2)] + [(0, m - 1)] * (m % 2 == 0),
        )
    )
    inner, coef, correction = call(
        inner_kernel,
        [
            (rhs.shape, VMEM),
            ((-(-VARS * VARS * SLOTS // 8),) + (8, cells), VMEM),
            (rhs.shape, HBM),
        ],
        (z, w, low, side, lcols, used),
        (VMEM,) * 4 + (SMEM,) * 2,
        [(2 * REACH + 1, VARS) + tile, pltpu.SemaphoreType.DMA],
    )
    resid, squares = call(
        outer_kernel,
        [(rhs.shape, VMEM), ((n * m, 1, cells), VMEM)],
        (inner, coef, low, tail, swap_a, swap_b, lcols, used),
        (VMEM,) * 6 + (SMEM,) * 2,
        [(REACH + 1, VARS) + tile],
    )
    squares = lax.all_to_all(squares, ("chain", "sub"), 0, 0, tiled=True)
    entries = blocks * VARS * cells * n * m
    (residual_unit,) = call(
        functools.partial(scale_kernel, entries),
        [(rhs.shape, HBM)],
        (resid, squares),
        (VMEM, VMEM),
        [rhs.shape, pltpu.SemaphoreType.DMA((4 if blocks % 4 == 0 else 1,))],
    )
    return (correction, residual_unit)


def solution(mesh):
    in_specs = (
        P("chain", None, None, "sub"),
        P("chain", None, None, "sub"),
        P("chain", None, None, "sub"),
        P("chain", None, None, None, "sub"),
        P("chain", None, None, None, "sub"),
        P("chain", None, None, None, "sub"),
        P("chain", None),
        P("chain", None),
        P("chain", None),
    )
    out_specs = (P("chain", None, None, "sub"), P("chain", None, None, "sub"))
    return jax.shard_map(shards, mesh=mesh, in_specs=in_specs, out_specs=out_specs, check_vma=False)
```

```python
import functools

import jax
import jax.numpy as jnp
from jax import lax
from jax.experimental import pallas as pl
from jax.experimental.pallas import tpu as pltpu
from jax.sharding import PartitionSpec as P

VARS = 5
REACH = 3
SLOTS = 2
STATE = REACH * VARS
WIDE = 16
PAD = 8
SPACE = 72
DIRECT = 4
VMEM_LIMIT = 40 * 1024 * 1024

VMEM = pltpu.VMEM
SMEM = pltpu.SMEM
HBM = pltpu.HBM


def lanes_of(cells):
    return lax.broadcasted_iota(jnp.int32, (8, cells), 1)


def block_transpose(items, width, cells):
    count = len(items)
    lane = lanes_of(cells)
    half = 1
    while half < count:
        bit = (lane // (half * width)) % 2 == 1
        out = list(items)
        for a in range(count):
            if a & half:
                continue
            b = a + half
            out[a] = jnp.where(bit, pltpu.roll(items[b], half * width, 1), items[a])
            out[b] = jnp.where(bit, items[b], pltpu.roll(items[a], cells - half * width, 1))
        items = out
        half *= 2
    return items


def spread(ref, place, row):
    return ref[place + (pl.ds(row, 8, stride=0), slice(None))]


def mul_rows(rows, near):
    total = rows[0] * near[0]
    for j in range(1, len(near)):
        total = total + rows[j] * near[j]
    return total


def mul_groups(rows, nears):
    return [mul_rows(rows, [near[g] for near in nears]) for g in range(len(nears[0]))]


def couple(mats, b, nears):
    out = []
    for i in range(VARS):
        parts = [
            mul_groups([spread(mats, (i, j, k), b) for j in range(VARS)], nears[k])
            for k in range(SLOTS)
        ]
        out.append([x + y for x, y in zip(*parts)])
    return out


def apply_coef(coef, b, nears):
    out = []
    for i in range(VARS):
        parts = []
        for k in range(SLOTS):
            place = (b * VARS + i) * VARS * SLOTS + k
            parts.append(
                mul_rows([spread(coef, (), place + SLOTS * j) for j in range(VARS)], nears[k])
            )
        out.append(parts[0] + parts[1])
    return out


def products(inv, coef, out):
    blocks = out.shape[3] - PAD
    stride = VARS * VARS * SLOTS

    def some(o, carry):
        start = o * 8
        left = [[-inv[i, m, pl.ds(start, 8), :] for m in range(VARS)] for i in range(VARS)]
        for k in range(SLOTS):
            stores = []
            for j in range(VARS):
                place = start * stride + j * SLOTS + k
                right = [
                    coef[pl.ds(place + m * VARS * SLOTS, 8, stride=stride), :] for m in range(VARS)
                ]
                for i in range(VARS):
                    here = (i, j, k, pl.ds(start, 8))
                    stores.append((out, here, mul_rows(left[i], right)))
            store_all(stores)
        return carry

    steps(blocks // 8, 3, some)


def slots(cols, counts, side, b, shift, empty):
    return [jnp.where(k < counts[side, b], cols[k, b] + shift, empty) for k in range(SLOTS)]


def read_block(buf, place):
    return [buf[place, v] for v in range(VARS)]


def read_groups(buf, place):
    count = buf.shape[2] // 8
    return [[buf[place, v, pl.ds(8 * g, 8), :] for g in range(count)] for v in range(VARS)]


class Kept:
    def __init__(self, carry, stores):
        self.carry, self.stores = carry, stores


def store_all(stores):
    for ref, place, value in stores:
        ref[place] = value


def steps(count, most, body, carry=0):
    unroll = max(u for u in range(1, most + 1) if count % u == 0)

    def chunk(o, carry):
        kept = []
        for u in range(unroll):
            carry = body(o * unroll + u, carry)
            if isinstance(carry, Kept):
                kept += carry.stores
                carry = carry.carry
        store_all(kept)
        return carry

    return lax.fori_loop(0, count // unroll, chunk, carry)


def column_order(nrhs):
    wide_y = nrhs + WIDE
    order = []
    for first, count in ((nrhs, STATE), (wide_y + nrhs, STATE - 1), (wide_y + nrhs + WIDE, STATE)):
        order += [(half, first + j) for half in range(2) for j in range(count)]
    for first in (0, wide_y):
        order += [(half, first + q) for half in range(2) for q in range(nrhs)]
    return order


def position(n):
    return lax.axis_index("chain") % n


def distances(count):
    return [0, count - 1] + list(range(1, count - 1))


def gather_parts(parts, buf):
    here = position(buf.shape[0])
    for x, part in zip(distances(len(parts)), parts):
        for page in range(part.shape[0]):
            buf[here ^ x, page] = part[page]


def scatter_parts(buf, parts):
    here = position(buf.shape[0])
    for x, part in zip(distances(len(parts)), parts):
        for page in range(part.shape[0]):
            part[page] = buf[here ^ x, page]


def parted(kernel, before, count, n, *refs):
    if count == 1:
        return kernel(*refs)
    outs, buf = refs[before : before + count], refs[-1]
    kernel(*refs[:before], buf, *refs[before + count : -1])
    scatter_parts(buf, outs)


def joined(kernel, count, n, *refs):
    if count == 1:
        return kernel(*refs)
    gather_parts(refs[:count], refs[-1])
    kernel(refs[-1], *refs[count:-1])


def exchange(parts, n, groups):
    if len(parts) == 1:
        return [lax.all_to_all(parts[0], "chain", 0, 0, tiled=True, axis_index_groups=groups)]
    count = lax.axis_size("chain")
    return [
        part if x == 0 else lax.ppermute(part, "chain", [(i, i ^ x) for i in range(count)])
        for x, part in zip(distances(len(parts)), parts)
    ]


def local_kernel(
    n,
    rhs_h,
    inv_h,
    low_h,
    upp_h,
    lcols_h,
    ucols_h,
    counts_h,
    out,
    source,
    mlow,
    mupp,
    lcols_v,
    ucols_v,
    counts_v,
    rhs,
    inv,
    low,
    upp,
    lcols,
    ucols,
    counts,
    ybuf,
    zbuf,
    stage,
    sems,
):
    copies = [
        pltpu.make_async_copy(src, dst, sems.at[k])
        for k, (src, dst) in enumerate(
            (
                (inv_h, inv.at[:, :, pl.ds(0, rhs.shape[0]), :]),
                (low_h, low),
                (lcols_h, lcols),
                (counts_h, counts),
                (ucols_h, ucols),
                (rhs_h, rhs),
                (upp_h, upp),
                (lcols_h, lcols_v),
                (ucols_h, ucols_v),
                (counts_h, counts_v),
            )
        )
    ]
    for copy in copies:
        copy.start()
    blocks, _, nrhs, cells = rhs.shape
    base = lax.axis_index("chain") * blocks
    wide_y = nrhs + WIDE
    wide_z = wide_y + WIDE
    row_y = lax.broadcasted_iota(jnp.int32, (wide_y, cells), 0)
    row_z = lax.broadcasted_iota(jnp.int32, (wide_z, cells), 0)
    for m in range(REACH):
        for v in range(VARS):
            q = VARS * m + v
            ybuf[REACH - 1 - m, v] = (row_y == nrhs + q).astype(jnp.float32)
            zbuf[blocks + m, v] = (row_z == wide_y + q).astype(jnp.float32)
    for v in range(VARS):
        ybuf[blocks + REACH, v] = jnp.zeros((wide_y, cells), jnp.float32)
        zbuf[blocks + REACH, v] = jnp.zeros((wide_z, cells), jnp.float32)
    empty = blocks + REACH
    copies[0].wait()
    copies[1].wait()
    products(inv, low, mlow)
    for copy in copies[2:6]:
        copy.wait()

    def first(b, carry):
        nears = [read_groups(ybuf, s) for s in slots(lcols, counts, 0, b, REACH - base, empty)]
        acc = couple(mlow, b, nears)
        right = [rhs[b, i] for i in range(VARS)]
        stores = []
        for i in range(VARS):
            own = mul_rows([spread(inv, (i, j), b) for j in range(VARS)], right)
            stores.append((source, (b, i), own))
            for g in range(len(acc[i])):
                value = own + acc[i][0] if g == 0 else acc[i][g]
                stores.append((ybuf, (b + REACH, i, pl.ds(8 * g, 8)), value))
        store_all(stores)
        return carry

    steps(blocks, 6, first)
    for copy in copies[6:]:
        copy.wait()
    products(inv, upp, mupp)

    def second(e, carry):
        c = blocks - 1 - e
        nears = [read_groups(zbuf, s) for s in slots(ucols, counts, 1, c, -base, empty)]
        acc = couple(mupp, c, nears)
        stores = []
        for i in range(VARS):
            for g in range(len(acc[i])):
                if g < wide_y // 8:
                    value = ybuf[c + REACH, i, 8 * g : 8 * g + 8] + acc[i][g]
                else:
                    value = acc[i][g]
                stores.append((zbuf, (c, i, pl.ds(8 * g, 8)), value))
        store_all(stores)
        return carry

    steps(blocks, 6, second)

    zero = jnp.zeros((8, cells), jnp.float32)
    for i in range(WIDE):
        m, v = i // VARS, i % VARS
        for g in range((wide_y + wide_z) // 8):
            if i == STATE:
                value = zero
            elif g < wide_y // 8:
                value = ybuf[blocks + REACH - 1 - m, v, 8 * g : 8 * g + 8]
            else:
                value = zbuf[m, v, 8 * g - wide_y : 8 * g - wide_y + 8]
            stage[pl.ds(i * SPACE + 8 * g, 8), :] = value

    def column(half, index):
        return stage[pl.ds(half * 8 * SPACE + index, 8, stride=SPACE), :]

    for half in range(2):
        place = STATE * SPACE + nrhs + 8 * half
        stage[pl.ds(place, 8), :] = column(half, wide_y + nrhs + STATE - 1)
    order = column_order(nrhs)
    width = cells // n
    for page in range(out.shape[1]):
        items = [column(*at) for at in order[page * n : (page + 1) * n]]
        items += [zero] * (n - len(items))
        for k, item in enumerate(block_transpose(items, width, cells)):
            out[k, page] = item


def split(value, period, stop, width, cells):
    items = [value]
    lane = lanes_of(cells)
    while period > stop:
        half = period // 2 * width
        bit = lane // half % 2 == 1
        fresh = []
        for item in items:
            other = pltpu.roll(item, half, 1)
            fresh += [jnp.where(bit, other, item), jnp.where(bit, item, other)]
        items = fresh
        period //= 2
    return items


def total_of(terms):
    while len(terms) > 1:
        pairs = [terms[k] + terms[k + 1] for k in range(0, len(terms) - 1, 2)]
        terms = pairs + terms[len(terms) - len(terms) % 2 :]
    return terms[0]


COLUMNS = 6 * STATE - 2


def store_state(buf, state):
    for half in range(2):
        for g, value in enumerate(state[half]):
            buf[pl.ds(g * WIDE + 8 * half, 8), :] = value


def state_rows(buf, count):
    return [[spread(buf, (), g * WIDE + j) for j in range(STATE)] for g in range(count)]


def pass_forward(d, cols, sides, state, buf, keep):
    groups, extra = len(state[0]), sides.shape[1] // 4
    store_state(buf, state)
    rows = state_rows(buf, groups)
    fresh = []
    for half in range(2):
        columns = [cols[pl.ds((d * COLUMNS + half * STATE + j) * 8, 8), :] for j in range(STATE)]
        fresh.append([])
        for g in range(groups):
            total = total_of([c * r for c, r in zip(columns, rows[g])])
            fresh[half].append(total + sides[d, half * extra + g] if g < extra else total)
        first = d * COLUMNS + 2 * STATE + half * (STATE - 1)
        columns = [cols[pl.ds((first + j) * 8, 8), :] for j in range(STATE - 1)]
        start = (d * COLUMNS + STATE + 8 * half) * 8 + 7
        columns.append(cols[pl.ds(start, 8, stride=8), :])
        for g in range(groups):
            total = total_of([c * r for c, r in zip(columns, rows[g])])
            if g < extra:
                total = total + sides[d, (2 + half) * extra + g]
            keep[d, half * groups + g] = total
    return fresh


def pass_back(d, cols, state, buf, keep):
    groups = len(state[0])
    store_state(buf, state)
    rows = state_rows(buf, groups)
    fresh = []
    for half in range(2):
        first = d * COLUMNS + 4 * STATE - 2 + half * STATE
        columns = [cols[pl.ds((first + j) * 8, 8), :] for j in range(STATE)]
        fresh.append(
            [
                total_of([c * r for c, r in zip(columns, rows[g])]) + keep[d, half * groups + g]
                for g in range(groups)
            ]
        )
    return fresh


def flat(state):
    return tuple(state[0] + state[1])


def folded(values):
    groups = len(values) // 2
    return [list(values[:groups]), list(values[groups:])]


def first_solve_kernel(x, cols, sides, offer, keep, buf):
    n, cells = x.shape[0], x.shape[3]
    width = cells // n
    packed = min(8, n)
    extra, groups = sides.shape[1] // 4, offer.shape[0] // 2
    zero = jnp.zeros((8, cells), jnp.float32)

    def unpack(d, carry):
        values = [x[d, page] for page in range(x.shape[1])]
        for page, value in enumerate(values):
            for k, block in enumerate(split(value, n, packed, width, cells)):
                e = page * n + k * packed
                if e < COLUMNS:
                    for g, item in enumerate(split(block, packed, 1, width, cells)):
                        cols[pl.ds((d * COLUMNS + e + g) * 8, 8), :] = item
                elif e < COLUMNS + 4 * 8:
                    sides[d, (e - COLUMNS) // packed] = block
        return carry

    steps(n, 2, unpack)
    lane = lanes_of(cells)
    row = lax.broadcasted_iota(jnp.int32, (8, cells), 0)
    start = []
    for half in range(2):
        start.append([zero] * extra)
        for g in range(groups - extra):
            column = lane // width % packed + g * packed
            start[half].append((column == row + 8 * half).astype(jnp.float32))

    def ahead(d, state):
        return flat(pass_forward(d, cols, sides, folded(state), buf, keep))

    leaving = steps(n, 2, ahead, flat(start))

    def back(e, state):
        return flat(pass_back(n - 1 - e, cols, folded(state), buf, keep))

    left = steps(n, 2, back, (zero,) * (2 * groups))
    is_left = lax.axis_index("chain") < n
    for e in range(2 * groups):
        offer[e] = jnp.where(is_left, leaving[e], left[e])


def second_solve_kernel(cols, sides, mine, got, out, keep, buf, states):
    n, cells = out.shape[0], out.shape[3]
    width = cells // n
    packed = min(8, n)
    extra, groups = sides.shape[1] // 4, mine.shape[0] // 2
    zero = jnp.zeros((8, cells), jnp.float32)
    is_left = lax.axis_index("chain") < n
    store_state(buf, [[mine[half * groups + g] for g in range(extra)] for half in range(2)])
    rows = state_rows(buf, extra)
    entering, far = [], []
    for half in range(2):
        columns = []
        for g in range(extra, groups):
            columns += split(got[half * groups + g], packed, 1, width, cells)
        for g in range(extra):
            known = got[half * groups + g]
            total = total_of([c * r for c, r in zip(columns, rows[g])])
            entering.append(jnp.where(is_left, 0.0, known))
            far.append(jnp.where(is_left, known + total, 0.0))

    def ahead(d, state):
        for e in range(2 * extra):
            states[d, e] = state[e]
        return flat(pass_forward(d, cols, sides, folded(state), buf, keep))

    steps(n, 4, ahead, tuple(entering))

    def back(e, state):
        d = n - 1 - e
        for e in range(2 * extra):
            states[d, 2 * extra + e] = state[e]
        return flat(pass_back(d, cols, folded(state), buf, keep))

    steps(n, 4, back, tuple(far))
    block = lanes_of(cells) // (packed * width)

    def pack(d, carry):
        for page in range(out.shape[1]):
            total = zero
            for r in range(4 * extra):
                if packed * r // n == page:
                    total = jnp.where(block == packed * r % n // packed, states[d, r], total)
            out[d, page] = total
        return carry

    steps(n, 4, pack)


def sweep_kernel(
    n,
    states,
    source,
    mlow,
    mupp,
    lcols,
    ucols,
    counts,
    low_h,
    side_h,
    zout,
    wout,
    tail,
    edge,
    low,
    side,
    ybuf,
    stage,
    sems,
):
    total = low_h.shape[0]
    copies = [
        pltpu.make_async_copy(src, dst.at[pl.ds(0, total), :], sems.at[k])
        for k, (src, dst) in enumerate(((low_h, low), (side_h, side)))
    ]
    for copy in copies:
        copy.start()
    blocks, _, nrhs, cells = source.shape
    base = lax.axis_index("chain") * blocks
    width = cells // n
    zero = jnp.zeros((nrhs, cells), jnp.float32)
    items = []
    for r in range(states.shape[1]):
        items += block_transpose([states[k, r] for k in range(n)], width, cells)
    for e in range(32):
        stage[pl.ds(8 * e, 8), :] = items[e]

    def entering(start):
        rows = [stage[pl.ds(start + q // 8 * 64 + q % 8, 8, stride=8), :] for q in range(STATE)]
        return tuple(rows)

    lane = lanes_of(cells)
    for v in range(VARS):
        wout[blocks, v] = zero

    def near(window, b, sign, cols, side):
        nears = []
        for k in range(SLOTS):
            off = sign * (cols[k, b] - base - b)
            picks = []
            for v in range(VARS):
                value = window[(REACH - 1) * VARS + v]
                for d in range(REACH - 1):
                    value = jnp.where(off == d + 1, window[d * VARS + v], value)
                picks.append(value if k == 0 else jnp.where(k < counts[side, b], value, 0.0))
            nears.append([[value] for value in picks])
        return nears

    def first(b, window):
        acc = couple(mlow, b, near(window, b, -1, lcols, 0))
        fresh = tuple(source[b, i] + acc[i][0] for i in range(VARS))
        return Kept(fresh + window[: STATE - VARS], [(ybuf, (b, i), fresh[i]) for i in range(VARS)])

    steps(blocks, 8, first, entering(0))

    def second(e, carry):
        c = blocks - 1 - e
        window, edges = carry[:STATE], list(carry[STATE:])
        acc = couple(mupp, c, near(window, c, 1, ucols, 1))
        fresh = tuple(ybuf[c, i] + acc[i][0] for i in range(VARS))
        here = (lane == 2 * c) | (lane == (2 * c + cells - 1) % cells)
        stores = []
        for i in range(VARS):
            stores += [(zout, (c, i), fresh[i]), (wout, (c, i), acc[i][0])]
            edges[i] = jnp.where(here, pltpu.roll(fresh[i], 2 * c, 1), edges[i])
        return Kept(fresh + window[: STATE - VARS] + tuple(edges), stores)

    carry = steps(blocks, 8, second, entering(128) + (zero,) * VARS)
    for v in range(VARS):
        edge[v] = carry[STATE + v]
    for m in range(REACH):
        for v in range(VARS):
            tail[m, v] = wout[blocks - REACH + m, v]
    for copy in copies:
        copy.wait()


def inner_kernel(z, w, low, side, lcols, counts, resid, coef, correction, wbuf, sem):
    store = pltpu.make_async_copy(z, correction, sem)
    store.start()
    blocks, _, nrhs, cells = z.shape
    base = lax.axis_index("chain") * blocks
    lane = lanes_of(cells)
    zero = jnp.zeros((nrhs, cells), jnp.float32)
    for v in range(VARS):
        for m in range(REACH):
            wbuf[m, v] = zero
            wbuf[m + REACH, v] = w[m, v]
        wbuf[2 * REACH, v] = zero
    pages = coef.shape[0]
    size = VARS * VARS * SLOTS
    row = lax.broadcasted_iota(jnp.int32, (8, cells), 0)

    def block(b, found, buf, shift, empty):
        nears = [read_block(buf, s) for s in slots(lcols, counts, 0, b, shift - base, empty)]
        acc = apply_coef(low, b, nears)
        left, right = [], []
        for v in range(VARS):
            here = z[b, v]
            left.append(jnp.where(lane == 0, 0.0, pltpu.roll(here, 1, 1)))
            right.append(jnp.where(lane == cells - 1, 0.0, pltpu.roll(here, cells - 1, 1)))
        beside = apply_coef(side, b, [left, right])
        here = (lane + row % 2) % cells == 2 * b
        found = tuple(
            jnp.where(here, pltpu.roll(side[pl.ds(b * size + 8 * r, 8), :], 2 * b, 1), found[r])
            for r in range(pages)
        )
        return Kept(found, [(resid, (b, i), acc[i] + beside[i]) for i in range(VARS)])

    found = (jnp.zeros((8, cells), jnp.float32),) * pages
    for b in range(REACH):
        kept = block(b, found, wbuf, REACH, 2 * REACH)
        store_all(kept.stores)
        found = kept.carry

    def inner(b, found):
        return block(b + REACH, found, w, 0, blocks)

    found = steps(blocks - REACH, 7, inner, found)
    for r in range(pages):
        coef[r] = found[r]
    store.wait()


def outer_kernel(
    inner, coef, low, tail, swap_a, swap_b, lcols, counts, resid, squares, wbuf
):
    blocks, _, nrhs, cells = inner.shape
    base = lax.axis_index("chain") * blocks
    first_block = lax.axis_index("chain") == 0
    place = lax.axis_index("sub")
    odd = place % 2 == 1
    first, last = place == 0, place == lax.axis_size("sub") - 1
    lane = lanes_of(cells)
    zero = jnp.zeros((nrhs, cells), jnp.float32)
    near = []
    for v in range(VARS):
        west = jnp.where(first, 0.0, jnp.where(odd, swap_a[v], swap_b[v]))
        east = jnp.where(last, 0.0, jnp.where(odd, swap_b[v], swap_a[v]))
        west, east = pltpu.roll(west, 1, 1), pltpu.roll(east, cells - 1, 1)
        near.append(jnp.where(lane % 2 == 0, west, east))
    edge = []
    for i in range(VARS):
        rows = []
        for j in range(VARS):
            k = (i * VARS + j) * SLOTS
            rows.append(coef[k // 8, pl.ds(k % 8, 1), :] + coef[(k + 1) // 8, pl.ds((k + 1) % 8, 1), :])
        edge.append(mul_rows(rows, near))
    for v in range(VARS):
        for m in range(REACH):
            wbuf[m, v] = jnp.where(first_block, 0.0, tail[m, v])
        wbuf[REACH, v] = zero
    ends = (lane == 0) | (lane == cells - 1)

    def add(b, values, totals):
        stores, fresh = [], []
        for i in range(VARS):
            other = pltpu.roll(edge[i], (cells - 2 * b) % cells, 1)
            value = values[i] + jnp.where(ends, other, 0.0)
            stores.append((resid, (b, i), value))
            fresh.append(totals[i] + value * value)
        return Kept(tuple(fresh), stores)

    totals = (zero,) * VARS
    stores = []
    for b in range(REACH):
        places = [
            jnp.where(s < REACH, s, REACH) for s in slots(lcols, counts, 0, b, REACH - base, REACH)
        ]
        acc = apply_coef(low, b, [read_block(wbuf, s) for s in places])
        kept = add(b, [inner[b, i] + acc[i] for i in range(VARS)], totals)
        stores += kept.stores
        totals = kept.carry
    store_all(stores)

    def rest(b, totals):
        return add(b + REACH, [inner[b + REACH, i] for i in range(VARS)], totals)

    totals = steps(blocks - REACH, 7, rest, totals)
    total = totals[0]
    for i in range(1, VARS):
        total = total + totals[i]
    sums = jnp.broadcast_to(jnp.sum(total, axis=1, keepdims=True), total.shape)
    row = lax.broadcasted_iota(jnp.int32, total.shape, 0)
    line = jnp.sum(jnp.where(lane == row, sums, 0.0), axis=0, keepdims=True)
    for p in range(squares.shape[0]):
        squares[p] = line


def scale_kernel(entries, resid, squares, out, scaled, sems):
    blocks, _, nrhs, cells = resid.shape
    line = squares[0]
    for p in range(1, squares.shape[0]):
        line = line + squares[p]
    lane = lanes_of(cells)
    row = lax.broadcasted_iota(jnp.int32, (nrhs, cells), 0)
    line = jnp.where(lane == row, jnp.broadcast_to(line, (nrhs, cells)), 0.0)
    msq = jnp.sum(line, axis=1, keepdims=True) / entries
    factor = jnp.broadcast_to(-lax.rsqrt(msq + 1e-06), (nrhs, cells))

    count = sems.shape[0]
    size = blocks // count
    copies = []
    for part in range(count):
        stores = [
            (scaled, (b, v), resid[b, v] * factor)
            for b in range(part * size, (part + 1) * size)
            for v in range(VARS)
        ]
        store_all(stores)
        here = pl.ds(part * size, size)
        copies.append(pltpu.make_async_copy(scaled.at[here], out.at[here], sems.at[part]))
        copies[part].start()
    for copy in copies:
        copy.wait()


def call(kernel, outs, args, places, scratch):
    args = [
        pltpu.with_memory_space_constraint(a, p) if p is HBM else a for a, p in zip(args, places)
    ]
    return pl.pallas_call(
        kernel,
        out_shape=[jax.ShapeDtypeStruct(o[0], (o + (jnp.float32,))[2]) for o in outs],
        in_specs=[pl.BlockSpec(memory_space=p) for p in places],
        out_specs=[pl.BlockSpec(memory_space=p) for p in (o[1] for o in outs)],
        scratch_shapes=[VMEM(s, jnp.float32) if isinstance(s, tuple) else s for s in scratch],
        compiler_params=pltpu.CompilerParams(vmem_limit_bytes=VMEM_LIMIT),
    )(*args)


def shards(
    rhs, diag_block, diag_inverse, lower_coef, upper_coef, side_coef, lower_cols, upper_cols, counts
):
    blocks, nvars, nrhs, cells = rhs.shape
    n = lax.axis_size("chain")
    inv = jnp.transpose(diag_inverse, (1, 2, 0, 3))
    low, upp, side = (
        jnp.transpose(a, (0, 2, 3, 1, 4)).reshape(-1, cells)
        for a in (lower_coef, upper_coef, side_coef)
    )
    lcols, ucols, used = lower_cols.T, upper_cols.T, counts.T
    m = lax.axis_size("sub")
    rows = blocks + REACH + 1
    half = n // 2
    parts = -(-len(column_order(nrhs)) // half)
    back = -(-32 // half)
    packed = min(8, half)
    extra = 8 // packed
    wide = 2 * (extra + WIDE // packed)
    sides = [list(range(half)), list(range(half, n))]
    tile = (nrhs, cells)

    mats = (VARS, VARS, SLOTS, blocks + PAD, cells)
    padded = (low.shape[0] + PAD, cells)

    count = half if half <= DIRECT else 1

    def pieces(pages):
        return [((pages,) + tile, VMEM)] * count if count > 1 else [((half, pages) + tile, VMEM)]

    def whole(pages):
        return [(half, pages) + tile] if count > 1 else []

    *maps, source, mlow, mupp, lcols, ucols, used = call(
        functools.partial(parted, functools.partial(local_kernel, half), 7, count, half),
        pieces(parts)
        + [(rhs.shape, VMEM), (mats, VMEM), (mats, VMEM)]
        + [(lcols.shape, VMEM, jnp.int32)] * 3,
        (rhs, inv, low, upp, lcols, ucols, used),
        (HBM,) * 7,
        [rhs.shape, (VARS, VARS, blocks + PAD, cells), low.shape, upp.shape]
        + [pltpu.SMEM(lcols.shape, jnp.int32)] * 3
        + [(rows, VARS, nrhs + WIDE, cells), (rows, VARS, nrhs + 2 * WIDE, cells)]
        + [(WIDE * SPACE, cells), pltpu.SemaphoreType.DMA((10,))]
        + whole(parts),
    )
    maps = exchange(maps, half, sides)
    cols, ends, offer = call(
        functools.partial(joined, first_solve_kernel, count, half),
        [
            ((half * COLUMNS * 8, cells), VMEM),
            ((half, 4 * extra) + tile, VMEM),
            ((wide,) + tile, VMEM),
        ],
        tuple(maps),
        (VMEM,) * count,
        [(half, wide) + tile, (wide // 2 * WIDE + PAD, cells)] + whole(parts),
    )
    got = lax.ppermute(
        offer, "chain", [p for i in range(half) for p in ((i, i + half), (i + half, i))]
    )
    states = call(
        functools.partial(parted, second_solve_kernel, 4, count, half),
        pieces(back),
        (cols, ends, offer, got),
        (VMEM,) * 4,
        [(half, 2 * extra) + tile, (extra * WIDE + PAD, cells), (half, 4 * extra) + tile]
        + whole(back),
    )
    states = exchange(states, half, sides)
    z, w, tail, edge, low, side = call(
        functools.partial(joined, functools.partial(sweep_kernel, half), count, half),
        [
            (rhs.shape, VMEM),
            ((blocks + 1, VARS) + tile, VMEM),
            ((REACH, VARS) + tile, VMEM),
            ((VARS,) + tile, VMEM),
            (padded, VMEM),
            (padded, VMEM),
        ],
        (*states, source, mlow, mupp, lcols, ucols, used, low, side),
        (VMEM,) * (3 + count) + (SMEM,) * 3 + (HBM,) * 2,
        [rhs.shape, (32 * 8, cells), pltpu.SemaphoreType.DMA((2,))] + whole(back),
    )
    tail = lax.ppermute(tail, "chain", [(i, (i + 1) % n) for i in range(n)])
    swap_a, swap_b = (
        lax.ppermute(edge, "sub", [p for i, j in pairs for p in ((i, j), (j, i))])
        for pairs in (
            [(i, i + 1) for i in range(0, m - 1, 2)],
            [(i, i + 1) for i in range(1, m - 1, 2)] + [(0, m - 1)] * (m % 2 == 0),
        )
    )
    inner, coef, correction = call(
        inner_kernel,
        [
            (rhs.shape, VMEM),
            ((-(-VARS * VARS * SLOTS // 8),) + (8, cells), VMEM),
            (rhs.shape, HBM),
        ],
        (z, w, low, side, lcols, used),
        (VMEM,) * 4 + (SMEM,) * 2,
        [(2 * REACH + 1, VARS) + tile, pltpu.SemaphoreType.DMA],
    )
    resid, squares = call(
        outer_kernel,
        [(rhs.shape, VMEM), ((n * m, 1, cells), VMEM)],
        (inner, coef, low, tail, swap_a, swap_b, lcols, used),
        (VMEM,) * 6 + (SMEM,) * 2,
        [(REACH + 1, VARS) + tile],
    )
    squares = lax.all_to_all(squares, ("chain", "sub"), 0, 0, tiled=True)
    entries = blocks * VARS * cells * n * m
    (residual_unit,) = call(
        functools.partial(scale_kernel, entries),
        [(rhs.shape, HBM)],
        (resid, squares),
        (VMEM, VMEM),
        [rhs.shape, pltpu.SemaphoreType.DMA((4 if blocks % 4 == 0 else 1,))],
    )
    return (correction, residual_unit)


def solution(mesh):
    in_specs = (
        P("chain", None, None, "sub"),
        P("chain", None, None, "sub"),
        P("chain", None, None, "sub"),
        P("chain", None, None, None, "sub"),
        P("chain", None, None, None, "sub"),
        P("chain", None, None, None, "sub"),
        P("chain", None),
        P("chain", None),
        P("chain", None),
    )
    out_specs = (P("chain", None, None, "sub"), P("chain", None, None, "sub"))
    return jax.shard_map(shards, mesh=mesh, in_specs=in_specs, out_specs=out_specs, check_vma=False)
```

```python
import functools

import jax
import jax.numpy as jnp
from jax import lax
from jax.experimental import pallas as pl
from jax.experimental.pallas import tpu as pltpu
from jax.sharding import PartitionSpec as P

VARS = 5
REACH = 3
SLOTS = 2
STATE = REACH * VARS
WIDE = 16
PAD = 8
SPACE = 72
DIRECT = 4
VMEM_LIMIT = 40 * 1024 * 1024

VMEM = pltpu.VMEM
SMEM = pltpu.SMEM
HBM = pltpu.HBM


def lanes_of(cells):
    return lax.broadcasted_iota(jnp.int32, (8, cells), 1)


def block_transpose(items, width, cells):
    count = len(items)
    lane = lanes_of(cells)
    half = 1
    while half < count:
        bit = (lane // (half * width)) % 2 == 1
        out = list(items)
        for a in range(count):
            if a & half:
                continue
            b = a + half
            out[a] = jnp.where(bit, pltpu.roll(items[b], half * width, 1), items[a])
            out[b] = jnp.where(bit, items[b], pltpu.roll(items[a], cells - half * width, 1))
        items = out
        half *= 2
    return items


def spread(ref, place, row):
    return ref[place + (pl.ds(row, 8, stride=0), slice(None))]


def mul_rows(rows, near):
    total = rows[0] * near[0]
    for j in range(1, len(near)):
        total = total + rows[j] * near[j]
    return total


def mul_groups(rows, nears):
    return [mul_rows(rows, [near[g] for near in nears]) for g in range(len(nears[0]))]


def couple(mats, b, nears):
    out = []
    for i in range(VARS):
        parts = [
            mul_groups([spread(mats, (i, j, k), b) for j in range(VARS)], nears[k])
            for k in range(SLOTS)
        ]
        out.append([x + y for x, y in zip(*parts)])
    return out


def apply_coef(coef, b, nears):
    out = []
    for i in range(VARS):
        parts = []
        for k in range(SLOTS):
            place = (b * VARS + i) * VARS * SLOTS + k
            parts.append(
                mul_rows([spread(coef, (), place + SLOTS * j) for j in range(VARS)], nears[k])
            )
        out.append(parts[0] + parts[1])
    return out


def products(inv, coef, out):
    blocks = out.shape[3] - PAD
    stride = VARS * VARS * SLOTS

    def some(o, carry):
        start = o * 8
        left = [[-inv[i, m, pl.ds(start, 8), :] for m in range(VARS)] for i in range(VARS)]
        for k in range(SLOTS):
            stores = []
            for j in range(VARS):
                place = start * stride + j * SLOTS + k
                right = [
                    coef[pl.ds(place + m * VARS * SLOTS, 8, stride=stride), :] for m in range(VARS)
                ]
                for i in range(VARS):
                    here = (i, j, k, pl.ds(start, 8))
                    stores.append((out, here, mul_rows(left[i], right)))
            store_all(stores)
        return carry

    steps(blocks // 8, 3, some)


def slots(cols, counts, side, b, shift, empty):
    return [jnp.where(k < counts[side, b], cols[k, b] + shift, empty) for k in range(SLOTS)]


def read_block(buf, place):
    return [buf[place, v] for v in range(VARS)]


def read_groups(buf, place):
    count = buf.shape[2] // 8
    return [[buf[place, v, pl.ds(8 * g, 8), :] for g in range(count)] for v in range(VARS)]


class Kept:
    def __init__(self, carry, stores):
        self.carry, self.stores = carry, stores


def store_all(stores):
    for ref, place, value in stores:
        ref[place] = value


def steps(count, most, body, carry=0):
    unroll = max(u for u in range(1, most + 1) if count % u == 0)

    def chunk(o, carry):
        kept = []
        for u in range(unroll):
            carry = body(o * unroll + u, carry)
            if isinstance(carry, Kept):
                kept += carry.stores
                carry = carry.carry
        store_all(kept)
        return carry

    return lax.fori_loop(0, count // unroll, chunk, carry)


def column_order(nrhs):
    wide_y = nrhs + WIDE
    order = []
    for first, count in ((nrhs, STATE), (wide_y + nrhs, STATE - 1), (wide_y + nrhs + WIDE, STATE)):
        order += [(half, first + j) for half in range(2) for j in range(count)]
    for first in (0, wide_y):
        order += [(half, first + q) for half in range(2) for q in range(nrhs)]
    return order


def position(n):
    return lax.axis_index("chain") % n


def distances(count):
    return [0, count - 1] + list(range(1, count - 1))


def gather_parts(parts, buf):
    here = position(buf.shape[0])
    for x, part in zip(distances(len(parts)), parts):
        for page in range(part.shape[0]):
            buf[here ^ x, page] = part[page]


def scatter_parts(buf, parts):
    here = position(buf.shape[0])
    for x, part in zip(distances(len(parts)), parts):
        for page in range(part.shape[0]):
            part[page] = buf[here ^ x, page]


def parted(kernel, before, count, n, *refs):
    if count == 1:
        return kernel(*refs)
    outs, buf = refs[before : before + count], refs[-1]
    kernel(*refs[:before], buf, *refs[before + count : -1])
    scatter_parts(buf, outs)


def joined(kernel, count, n, *refs):
    if count == 1:
        return kernel(*refs)
    gather_parts(refs[:count], refs[-1])
    kernel(refs[-1], *refs[count:-1])


def exchange(parts, n, groups):
    if len(parts) == 1:
        return [lax.all_to_all(parts[0], "chain", 0, 0, tiled=True, axis_index_groups=groups)]
    count = lax.axis_size("chain")
    return [
        part if x == 0 else lax.ppermute(part, "chain", [(i, i ^ x) for i in range(count)])
        for x, part in zip(distances(len(parts)), parts)
    ]


def local_kernel(
    n,
    rhs_h,
    inv_h,
    low_h,
    upp_h,
    side_h,
    lcols_h,
    ucols_h,
    counts_h,
    out,
    source,
    mlow,
    mupp,
    lcols_v,
    ucols_v,
    counts_v,
    low,
    side,
    rhs,
    inv,
    upp,
    lcols,
    ucols,
    counts,
    ybuf,
    zbuf,
    stage,
    sems,
):
    copies = [
        pltpu.make_async_copy(src, dst, sems.at[k])
        for k, (src, dst) in enumerate(
            (
                (inv_h, inv.at[:, :, pl.ds(0, rhs.shape[0]), :]),
                (low_h, low.at[pl.ds(0, low_h.shape[0]), :]),
                (lcols_h, lcols),
                (counts_h, counts),
                (ucols_h, ucols),
                (rhs_h, rhs),
                (upp_h, upp.at[pl.ds(0, upp_h.shape[0]), :]),
                (lcols_h, lcols_v),
                (ucols_h, ucols_v),
                (counts_h, counts_v),
                (side_h, side.at[pl.ds(0, side_h.shape[0]), :]),
            )
        )
    ]
    for copy in copies:
        copy.start()
    blocks, _, nrhs, cells = rhs.shape
    base = lax.axis_index("chain") * blocks
    wide_y = nrhs + WIDE
    wide_z = wide_y + WIDE
    row_y = lax.broadcasted_iota(jnp.int32, (wide_y, cells), 0)
    row_z = lax.broadcasted_iota(jnp.int32, (wide_z, cells), 0)
    for m in range(REACH):
        for v in range(VARS):
            q = VARS * m + v
            ybuf[REACH - 1 - m, v] = (row_y == nrhs + q).astype(jnp.float32)
            zbuf[blocks + m, v] = (row_z == wide_y + q).astype(jnp.float32)
    for v in range(VARS):
        ybuf[blocks + REACH, v] = jnp.zeros((wide_y, cells), jnp.float32)
        zbuf[blocks + REACH, v] = jnp.zeros((wide_z, cells), jnp.float32)
    empty = blocks + REACH
    copies[0].wait()
    copies[1].wait()
    products(inv, low, mlow)
    for copy in copies[2:6]:
        copy.wait()

    def first(b, carry):
        nears = [read_groups(ybuf, s) for s in slots(lcols, counts, 0, b, REACH - base, empty)]
        acc = couple(mlow, b, nears)
        right = [rhs[b, i] for i in range(VARS)]
        stores = []
        for i in range(VARS):
            own = mul_rows([spread(inv, (i, j), b) for j in range(VARS)], right)
            stores.append((source, (b, i), own))
            for g in range(len(acc[i])):
                value = own + acc[i][0] if g == 0 else acc[i][g]
                stores.append((ybuf, (b + REACH, i, pl.ds(8 * g, 8)), value))
        store_all(stores)
        return carry

    steps(blocks, 6, first)
    for copy in copies[6:-1]:
        copy.wait()
    products(inv, upp, mupp)

    def second(e, carry):
        c = blocks - 1 - e
        nears = [read_groups(zbuf, s) for s in slots(ucols, counts, 1, c, -base, empty)]
        acc = couple(mupp, c, nears)
        stores = []
        for i in range(VARS):
            for g in range(len(acc[i])):
                if g < wide_y // 8:
                    value = ybuf[c + REACH, i, 8 * g : 8 * g + 8] + acc[i][g]
                else:
                    value = acc[i][g]
                stores.append((zbuf, (c, i, pl.ds(8 * g, 8)), value))
        store_all(stores)
        return carry

    steps(blocks, 6, second)

    zero = jnp.zeros((8, cells), jnp.float32)
    for i in range(WIDE):
        m, v = i // VARS, i % VARS
        for g in range((wide_y + wide_z) // 8):
            if i == STATE:
                value = zero
            elif g < wide_y // 8:
                value = ybuf[blocks + REACH - 1 - m, v, 8 * g : 8 * g + 8]
            else:
                value = zbuf[m, v, 8 * g - wide_y : 8 * g - wide_y + 8]
            stage[pl.ds(i * SPACE + 8 * g, 8), :] = value

    def column(half, index):
        return stage[pl.ds(half * 8 * SPACE + index, 8, stride=SPACE), :]

    for half in range(2):
        place = STATE * SPACE + nrhs + 8 * half
        stage[pl.ds(place, 8), :] = column(half, wide_y + nrhs + STATE - 1)
    order = column_order(nrhs)
    width = cells // n
    for page in range(out.shape[1]):
        items = [column(*at) for at in order[page * n : (page + 1) * n]]
        items += [zero] * (n - len(items))
        for k, item in enumerate(block_transpose(items, width, cells)):
            out[k, page] = item
    copies[-1].wait()


def split(value, period, stop, width, cells):
    items = [value]
    lane = lanes_of(cells)
    while period > stop:
        half = period // 2 * width
        bit = lane // half % 2 == 1
        fresh = []
        for item in items:
            other = pltpu.roll(item, half, 1)
            fresh += [jnp.where(bit, other, item), jnp.where(bit, item, other)]
        items = fresh
        period //= 2
    return items


def total_of(terms):
    while len(terms) > 1:
        pairs = [terms[k] + terms[k + 1] for k in range(0, len(terms) - 1, 2)]
        terms = pairs + terms[len(terms) - len(terms) % 2 :]
    return terms[0]


COLUMNS = 6 * STATE - 2


def store_state(buf, state):
    for half in range(2):
        for g, value in enumerate(state[half]):
            buf[pl.ds(g * WIDE + 8 * half, 8), :] = value


def state_rows(buf, count):
    return [[spread(buf, (), g * WIDE + j) for j in range(STATE)] for g in range(count)]


def pass_forward(d, cols, sides, state, buf, keep):
    groups, extra = len(state[0]), sides.shape[1] // 4
    store_state(buf, state)
    rows = state_rows(buf, groups)
    fresh = []
    for half in range(2):
        columns = [cols[pl.ds((d * COLUMNS + half * STATE + j) * 8, 8), :] for j in range(STATE)]
        fresh.append([])
        for g in range(groups):
            total = total_of([c * r for c, r in zip(columns, rows[g])])
            fresh[half].append(total + sides[d, half * extra + g] if g < extra else total)
        first = d * COLUMNS + 2 * STATE + half * (STATE - 1)
        columns = [cols[pl.ds((first + j) * 8, 8), :] for j in range(STATE - 1)]
        start = (d * COLUMNS + STATE + 8 * half) * 8 + 7
        columns.append(cols[pl.ds(start, 8, stride=8), :])
        for g in range(groups):
            total = total_of([c * r for c, r in zip(columns, rows[g])])
            if g < extra:
                total = total + sides[d, (2 + half) * extra + g]
            keep[d, half * groups + g] = total
    return fresh


def pass_back(d, cols, state, buf, keep):
    groups = len(state[0])
    store_state(buf, state)
    rows = state_rows(buf, groups)
    fresh = []
    for half in range(2):
        first = d * COLUMNS + 4 * STATE - 2 + half * STATE
        columns = [cols[pl.ds((first + j) * 8, 8), :] for j in range(STATE)]
        fresh.append(
            [
                total_of([c * r for c, r in zip(columns, rows[g])]) + keep[d, half * groups + g]
                for g in range(groups)
            ]
        )
    return fresh


def flat(state):
    return tuple(state[0] + state[1])


def folded(values):
    groups = len(values) // 2
    return [list(values[:groups]), list(values[groups:])]


def first_solve_kernel(x, cols, sides, offer, keep, buf):
    n, cells = x.shape[0], x.shape[3]
    width = cells // n
    packed = min(8, n)
    extra, groups = sides.shape[1] // 4, offer.shape[0] // 2
    zero = jnp.zeros((8, cells), jnp.float32)

    def unpack(d, carry):
        values = [x[d, page] for page in range(x.shape[1])]
        for page, value in enumerate(values):
            for k, block in enumerate(split(value, n, packed, width, cells)):
                e = page * n + k * packed
                if e < COLUMNS:
                    for g, item in enumerate(split(block, packed, 1, width, cells)):
                        cols[pl.ds((d * COLUMNS + e + g) * 8, 8), :] = item
                elif e < COLUMNS + 4 * 8:
                    sides[d, (e - COLUMNS) // packed] = block
        return carry

    steps(n, 2, unpack)
    lane = lanes_of(cells)
    row = lax.broadcasted_iota(jnp.int32, (8, cells), 0)
    start = []
    for half in range(2):
        start.append([zero] * extra)
        for g in range(groups - extra):
            column = lane // width % packed + g * packed
            start[half].append((column == row + 8 * half).astype(jnp.float32))

    def ahead(d, state):
        return flat(pass_forward(d, cols, sides, folded(state), buf, keep))

    leaving = steps(n, 2, ahead, flat(start))

    def back(e, state):
        return flat(pass_back(n - 1 - e, cols, folded(state), buf, keep))

    left = steps(n, 2, back, (zero,) * (2 * groups))
    is_left = lax.axis_index("chain") < n
    for e in range(2 * groups):
        offer[e] = jnp.where(is_left, leaving[e], left[e])


def second_solve_kernel(cols, sides, mine, got, out, keep, buf, states):
    n, cells = out.shape[0], out.shape[3]
    width = cells // n
    packed = min(8, n)
    extra, groups = sides.shape[1] // 4, mine.shape[0] // 2
    zero = jnp.zeros((8, cells), jnp.float32)
    is_left = lax.axis_index("chain") < n
    store_state(buf, [[mine[half * groups + g] for g in range(extra)] for half in range(2)])
    rows = state_rows(buf, extra)
    entering, far = [], []
    for half in range(2):
        columns = []
        for g in range(extra, groups):
            columns += split(got[half * groups + g], packed, 1, width, cells)
        for g in range(extra):
            known = got[half * groups + g]
            total = total_of([c * r for c, r in zip(columns, rows[g])])
            entering.append(jnp.where(is_left, 0.0, known))
            far.append(jnp.where(is_left, known + total, 0.0))

    def ahead(d, state):
        for e in range(2 * extra):
            states[d, e] = state[e]
        return flat(pass_forward(d, cols, sides, folded(state), buf, keep))

    steps(n, 4, ahead, tuple(entering))

    def back(e, state):
        d = n - 1 - e
        for e in range(2 * extra):
            states[d, 2 * extra + e] = state[e]
        return flat(pass_back(d, cols, folded(state), buf, keep))

    steps(n, 4, back, tuple(far))
    block = lanes_of(cells) // (packed * width)

    def pack(d, carry):
        for page in range(out.shape[1]):
            total = zero
            for r in range(4 * extra):
                if packed * r // n == page:
                    total = jnp.where(block == packed * r % n // packed, states[d, r], total)
            out[d, page] = total
        return carry

    steps(n, 4, pack)


def near_blocks(window, b, base, sign, cols, counts, side):
    nears = []
    for k in range(SLOTS):
        off = sign * (cols[k, b] - base - b)
        picks = []
        for v in range(VARS):
            value = window[(REACH - 1) * VARS + v]
            for d in range(REACH - 1):
                value = jnp.where(off == d + 1, window[d * VARS + v], value)
            picks.append(value if k == 0 else jnp.where(k < counts[side, b], value, 0.0))
        nears.append([[value] for value in picks])
    return nears


def forward_kernel(
    n, states, source, mlow, mupp, lcols, ucols, counts, yout, start, tail, stage
):
    blocks, _, nrhs, cells = source.shape
    base = lax.axis_index("chain") * blocks
    width = cells // n
    items = []
    for r in range(states.shape[1]):
        items += block_transpose([states[k, r] for k in range(n)], width, cells)
    for e in range(32):
        stage[pl.ds(8 * e, 8), :] = items[e]

    def entering(start):
        rows = [stage[pl.ds(start + q // 8 * 64 + q % 8, 8, stride=8), :] for q in range(STATE)]
        return tuple(rows)

    def first(b, window):
        acc = couple(mlow, b, near_blocks(window, b, base, -1, lcols, counts, 0))
        fresh = tuple(source[b, i] + acc[i][0] for i in range(VARS))
        return Kept(fresh + window[: STATE - VARS], [(yout, (b, i), fresh[i]) for i in range(VARS)])

    steps(blocks, 8, first, entering(0))

    window = entering(128)
    for q in range(STATE):
        start[q] = window[q]
    for m in reversed(range(REACH)):
        c = blocks - REACH + m
        acc = couple(mupp, c, near_blocks(window, c, base, 1, ucols, counts, 1))
        fresh = tuple(yout[c, i] + acc[i][0] for i in range(VARS))
        for i in range(VARS):
            tail[m, i] = acc[i][0]
        window = fresh + window[: STATE - VARS]


def sweep_kernel(ybuf, start, mupp, ucols, counts, zout, wout, edge):
    blocks, _, nrhs, cells = ybuf.shape
    base = lax.axis_index("chain") * blocks
    zero = jnp.zeros((nrhs, cells), jnp.float32)
    lane = lanes_of(cells)
    for v in range(VARS):
        wout[blocks, v] = zero

    def second(e, carry):
        c = blocks - 1 - e
        window, edges = carry[:STATE], list(carry[STATE:])
        acc = couple(mupp, c, near_blocks(window, c, base, 1, ucols, counts, 1))
        fresh = tuple(ybuf[c, i] + acc[i][0] for i in range(VARS))
        here = (lane == 2 * c) | (lane == (2 * c + cells - 1) % cells)
        stores = []
        for i in range(VARS):
            stores += [(zout, (c, i), fresh[i]), (wout, (c, i), acc[i][0])]
            edges[i] = jnp.where(here, pltpu.roll(fresh[i], 2 * c, 1), edges[i])
        return Kept(fresh + window[: STATE - VARS] + tuple(edges), stores)

    carry = steps(blocks, 8, second, tuple(start[q] for q in range(STATE)) + (zero,) * VARS)
    for v in range(VARS):
        edge[v] = carry[STATE + v]


def inner_kernel(z, w, low, side, lcols, counts, resid, coef, correction, wbuf, sem):
    store = pltpu.make_async_copy(z, correction, sem)
    store.start()
    blocks, _, nrhs, cells = z.shape
    base = lax.axis_index("chain") * blocks
    lane = lanes_of(cells)
    zero = jnp.zeros((nrhs, cells), jnp.float32)
    for v in range(VARS):
        for m in range(REACH):
            wbuf[m, v] = zero
            wbuf[m + REACH, v] = w[m, v]
        wbuf[2 * REACH, v] = zero
    pages = coef.shape[0]
    size = VARS * VARS * SLOTS
    row = lax.broadcasted_iota(jnp.int32, (8, cells), 0)

    def block(b, found, buf, shift, empty):
        nears = [read_block(buf, s) for s in slots(lcols, counts, 0, b, shift - base, empty)]
        acc = apply_coef(low, b, nears)
        left, right = [], []
        for v in range(VARS):
            here = z[b, v]
            left.append(jnp.where(lane == 0, 0.0, pltpu.roll(here, 1, 1)))
            right.append(jnp.where(lane == cells - 1, 0.0, pltpu.roll(here, cells - 1, 1)))
        beside = apply_coef(side, b, [left, right])
        here = (lane + row % 2) % cells == 2 * b
        found = tuple(
            jnp.where(here, pltpu.roll(side[pl.ds(b * size + 8 * r, 8), :], 2 * b, 1), found[r])
            for r in range(pages)
        )
        return Kept(found, [(resid, (b, i), acc[i] + beside[i]) for i in range(VARS)])

    found = (jnp.zeros((8, cells), jnp.float32),) * pages
    for b in range(REACH):
        kept = block(b, found, wbuf, REACH, 2 * REACH)
        store_all(kept.stores)
        found = kept.carry

    def inner(b, found):
        return block(b + REACH, found, w, 0, blocks)

    found = steps(blocks - REACH, 7, inner, found)
    for r in range(pages):
        coef[r] = found[r]
    store.wait()


def outer_kernel(
    inner, coef, low, tail, swap_a, swap_b, lcols, counts, resid, squares, wbuf
):
    blocks, _, nrhs, cells = inner.shape
    base = lax.axis_index("chain") * blocks
    first_block = lax.axis_index("chain") == 0
    place = lax.axis_index("sub")
    odd = place % 2 == 1
    first, last = place == 0, place == lax.axis_size("sub") - 1
    lane = lanes_of(cells)
    zero = jnp.zeros((nrhs, cells), jnp.float32)
    near = []
    for v in range(VARS):
        west = jnp.where(first, 0.0, jnp.where(odd, swap_a[v], swap_b[v]))
        east = jnp.where(last, 0.0, jnp.where(odd, swap_b[v], swap_a[v]))
        west, east = pltpu.roll(west, 1, 1), pltpu.roll(east, cells - 1, 1)
        near.append(jnp.where(lane % 2 == 0, west, east))
    edge = []
    for i in range(VARS):
        rows = []
        for j in range(VARS):
            k = (i * VARS + j) * SLOTS
            rows.append(coef[k // 8, pl.ds(k % 8, 1), :] + coef[(k + 1) // 8, pl.ds((k + 1) % 8, 1), :])
        edge.append(mul_rows(rows, near))
    for v in range(VARS):
        for m in range(REACH):
            wbuf[m, v] = jnp.where(first_block, 0.0, tail[m, v])
        wbuf[REACH, v] = zero
    ends = (lane == 0) | (lane == cells - 1)

    def add(b, values, totals):
        stores, fresh = [], []
        for i in range(VARS):
            other = pltpu.roll(edge[i], (cells - 2 * b) % cells, 1)
            value = values[i] + jnp.where(ends, other, 0.0)
            stores.append((resid, (b, i), value))
            fresh.append(totals[i] + value * value)
        return Kept(tuple(fresh), stores)

    totals = (zero,) * VARS
    stores = []
    for b in range(REACH):
        places = [
            jnp.where(s < REACH, s, REACH) for s in slots(lcols, counts, 0, b, REACH - base, REACH)
        ]
        acc = apply_coef(low, b, [read_block(wbuf, s) for s in places])
        kept = add(b, [inner[b, i] + acc[i] for i in range(VARS)], totals)
        stores += kept.stores
        totals = kept.carry
    store_all(stores)

    def rest(b, totals):
        return add(b + REACH, [inner[b + REACH, i] for i in range(VARS)], totals)

    totals = steps(blocks - REACH, 7, rest, totals)
    total = totals[0]
    for i in range(1, VARS):
        total = total + totals[i]
    sums = jnp.broadcast_to(jnp.sum(total, axis=1, keepdims=True), total.shape)
    row = lax.broadcasted_iota(jnp.int32, total.shape, 0)
    line = jnp.sum(jnp.where(lane == row, sums, 0.0), axis=0, keepdims=True)
    for p in range(squares.shape[0]):
        squares[p] = line


def scale_kernel(entries, resid, squares, out, scaled, sems):
    blocks, _, nrhs, cells = resid.shape
    line = squares[0]
    for p in range(1, squares.shape[0]):
        line = line + squares[p]
    lane = lanes_of(cells)
    row = lax.broadcasted_iota(jnp.int32, (nrhs, cells), 0)
    line = jnp.where(lane == row, jnp.broadcast_to(line, (nrhs, cells)), 0.0)
    msq = jnp.sum(line, axis=1, keepdims=True) / entries
    factor = jnp.broadcast_to(-lax.rsqrt(msq + 1e-06), (nrhs, cells))

    count = sems.shape[0]
    size = blocks // count
    copies = []
    for part in range(count):
        stores = [
            (scaled, (b, v), resid[b, v] * factor)
            for b in range(part * size, (part + 1) * size)
            for v in range(VARS)
        ]
        store_all(stores)
        here = pl.ds(part * size, size)
        copies.append(pltpu.make_async_copy(scaled.at[here], out.at[here], sems.at[part]))
        copies[part].start()
    for copy in copies:
        copy.wait()


def call(kernel, outs, args, places, scratch):
    args = [
        pltpu.with_memory_space_constraint(a, p) if p is HBM else a for a, p in zip(args, places)
    ]
    return pl.pallas_call(
        kernel,
        out_shape=[jax.ShapeDtypeStruct(o[0], (o + (jnp.float32,))[2]) for o in outs],
        in_specs=[pl.BlockSpec(memory_space=p) for p in places],
        out_specs=[pl.BlockSpec(memory_space=p) for p in (o[1] for o in outs)],
        scratch_shapes=[VMEM(s, jnp.float32) if isinstance(s, tuple) else s for s in scratch],
        compiler_params=pltpu.CompilerParams(vmem_limit_bytes=VMEM_LIMIT),
    )(*args)


def shards(
    rhs, diag_block, diag_inverse, lower_coef, upper_coef, side_coef, lower_cols, upper_cols, counts
):
    blocks, nvars, nrhs, cells = rhs.shape
    n = lax.axis_size("chain")
    inv = jnp.transpose(diag_inverse, (1, 2, 0, 3))
    low, upp, side = (
        jnp.transpose(a, (0, 2, 3, 1, 4)).reshape(-1, cells)
        for a in (lower_coef, upper_coef, side_coef)
    )
    lcols, ucols, used = lower_cols.T, upper_cols.T, counts.T
    m = lax.axis_size("sub")
    rows = blocks + REACH + 1
    half = n // 2
    parts = -(-len(column_order(nrhs)) // half)
    back = -(-32 // half)
    packed = min(8, half)
    extra = 8 // packed
    wide = 2 * (extra + WIDE // packed)
    sides = [list(range(half)), list(range(half, n))]
    tile = (nrhs, cells)

    mats = (VARS, VARS, SLOTS, blocks + PAD, cells)
    padded = (low.shape[0] + VARS * VARS * SLOTS, cells)

    count = half if half <= DIRECT else 1

    def pieces(pages):
        return [((pages,) + tile, VMEM)] * count if count > 1 else [((half, pages) + tile, VMEM)]

    def whole(pages):
        return [(half, pages) + tile] if count > 1 else []

    *maps, source, mlow, mupp, lcols, ucols, used, low, side = call(
        functools.partial(parted, functools.partial(local_kernel, half), 8, count, half),
        pieces(parts)
        + [(rhs.shape, VMEM), (mats, VMEM), (mats, VMEM)]
        + [(lcols.shape, VMEM, jnp.int32)] * 3
        + [(padded, VMEM)] * 2,
        (rhs, inv, low, upp, side, lcols, ucols, used),
        (HBM,) * 8,
        [rhs.shape, (VARS, VARS, blocks + PAD, cells), padded]
        + [pltpu.SMEM(lcols.shape, jnp.int32)] * 3
        + [(rows, VARS, nrhs + WIDE, cells), (rows, VARS, nrhs + 2 * WIDE, cells)]
        + [(WIDE * SPACE + SPACE, cells), pltpu.SemaphoreType.DMA((11,))]
        + whole(parts),
    )
    maps = exchange(maps, half, sides)
    cols, ends, offer = call(
        functools.partial(joined, first_solve_kernel, count, half),
        [
            ((half * COLUMNS * 8, cells), VMEM),
            ((half, 4 * extra) + tile, VMEM),
            ((wide,) + tile, VMEM),
        ],
        tuple(maps),
        (VMEM,) * count,
        [(half, wide) + tile, (wide // 2 * WIDE + PAD, cells)] + whole(parts),
    )
    got = lax.ppermute(
        offer, "chain", [p for i in range(half) for p in ((i, i + half), (i + half, i))]
    )
    states = call(
        functools.partial(parted, second_solve_kernel, 4, count, half),
        pieces(back),
        (cols, ends, offer, got),
        (VMEM,) * 4,
        [(half, 2 * extra) + tile, (extra * WIDE + PAD, cells), (half, 4 * extra) + tile]
        + whole(back),
    )
    states = exchange(states, half, sides)
    y, start, tail = call(
        functools.partial(joined, functools.partial(forward_kernel, half), count, half),
        [(rhs.shape, VMEM), ((STATE,) + tile, VMEM), ((REACH, VARS) + tile, VMEM)],
        (*states, source, mlow, mupp, lcols, ucols, used),
        (VMEM,) * (3 + count) + (SMEM,) * 3,
        [(33 * 8, cells)] + whole(back),
    )
    z, w, edge = call(
        sweep_kernel,
        [(rhs.shape, VMEM), ((blocks + 1, VARS) + tile, VMEM), ((VARS,) + tile, VMEM)],
        (y, start, mupp, ucols, used),
        (VMEM,) * 3 + (SMEM,) * 2,
        [],
    )
    tail = lax.ppermute(tail, "chain", [(i, (i + 1) % n) for i in range(n)])
    swap_a, swap_b = (
        lax.ppermute(edge, "sub", [p for i, j in pairs for p in ((i, j), (j, i))])
        for pairs in (
            [(i, i + 1) for i in range(0, m - 1, 2)],
            [(i, i + 1) for i in range(1, m - 1, 2)] + [(0, m - 1)] * (m % 2 == 0),
        )
    )
    inner, coef, correction = call(
        inner_kernel,
        [
            (rhs.shape, VMEM),
            ((-(-VARS * VARS * SLOTS // 8),) + (8, cells), VMEM),
            (rhs.shape, HBM),
        ],
        (z, w, low, side, lcols, used),
        (VMEM,) * 4 + (SMEM,) * 2,
        [(2 * REACH + 1, VARS) + tile, pltpu.SemaphoreType.DMA],
    )
    resid, squares = call(
        outer_kernel,
        [(rhs.shape, VMEM), ((n * m, 1, cells), VMEM)],
        (inner, coef, low, tail, swap_a, swap_b, lcols, used),
        (VMEM,) * 6 + (SMEM,) * 2,
        [(REACH + 1, VARS) + tile],
    )
    squares = lax.all_to_all(squares, ("chain", "sub"), 0, 0, tiled=True)
    entries = blocks * VARS * cells * n * m
    (residual_unit,) = call(
        functools.partial(scale_kernel, entries),
        [(rhs.shape, HBM)],
        (resid, squares),
        (VMEM, VMEM),
        [rhs.shape, pltpu.SemaphoreType.DMA((4 if blocks % 4 == 0 else 1,))],
    )
    return (correction, residual_unit)


def solution(mesh):
    in_specs = (
        P("chain", None, None, "sub"),
        P("chain", None, None, "sub"),
        P("chain", None, None, "sub"),
        P("chain", None, None, None, "sub"),
        P("chain", None, None, None, "sub"),
        P("chain", None, None, None, "sub"),
        P("chain", None),
        P("chain", None),
        P("chain", None),
    )
    out_specs = (P("chain", None, None, "sub"), P("chain", None, None, "sub"))
    return jax.shard_map(shards, mesh=mesh, in_specs=in_specs, out_specs=out_specs, check_vma=False)
```

```python
import functools

import jax
import jax.numpy as jnp
from jax import lax
from jax.experimental import pallas as pl
from jax.experimental.pallas import tpu as pltpu
from jax.sharding import PartitionSpec as P

VARS = 5
REACH = 3
SLOTS = 2
STATE = REACH * VARS
WIDE = 16
PAD = 8
SPACE = 72
DIRECT = 4
VMEM_LIMIT = 40 * 1024 * 1024

VMEM = pltpu.VMEM
SMEM = pltpu.SMEM
HBM = pltpu.HBM


def lanes_of(cells):
    return lax.broadcasted_iota(jnp.int32, (8, cells), 1)


def block_transpose(items, width, cells):
    count = len(items)
    lane = lanes_of(cells)
    half = 1
    while half < count:
        bit = (lane // (half * width)) % 2 == 1
        out = list(items)
        for a in range(count):
            if a & half:
                continue
            b = a + half
            out[a] = jnp.where(bit, pltpu.roll(items[b], half * width, 1), items[a])
            out[b] = jnp.where(bit, items[b], pltpu.roll(items[a], cells - half * width, 1))
        items = out
        half *= 2
    return items


def spread(ref, place, row):
    return ref[place + (pl.ds(row, 8, stride=0), slice(None))]


def mul_rows(rows, near):
    total = rows[0] * near[0]
    for j in range(1, len(near)):
        total = total + rows[j] * near[j]
    return total


def mul_groups(rows, nears):
    return [mul_rows(rows, [near[g] for near in nears]) for g in range(len(nears[0]))]


def couple(mats, b, nears):
    out = []
    for i in range(VARS):
        parts = [
            mul_groups([spread(mats, (i, j, k), b) for j in range(VARS)], nears[k])
            for k in range(SLOTS)
        ]
        out.append([x + y for x, y in zip(*parts)])
    return out


def apply_coef(coef, b, nears):
    out = []
    for i in range(VARS):
        parts = []
        for k in range(SLOTS):
            place = (b * VARS + i) * VARS * SLOTS + k
            parts.append(
                mul_rows([spread(coef, (), place + SLOTS * j) for j in range(VARS)], nears[k])
            )
        out.append(parts[0] + parts[1])
    return out


def products(inv, coef, out):
    blocks = out.shape[3] - PAD
    stride = VARS * VARS * SLOTS

    def some(o, carry):
        start = o * 8
        left = [[-inv[i, m, pl.ds(start, 8), :] for m in range(VARS)] for i in range(VARS)]
        for k in range(SLOTS):
            stores = []
            for j in range(VARS):
                place = start * stride + j * SLOTS + k
                right = [
                    coef[pl.ds(place + m * VARS * SLOTS, 8, stride=stride), :] for m in range(VARS)
                ]
                for i in range(VARS):
                    here = (i, j, k, pl.ds(start, 8))
                    stores.append((out, here, mul_rows(left[i], right)))
            store_all(stores)
        return carry

    steps(blocks // 8, 3, some)


def slots(cols, counts, side, b, shift, empty):
    return [jnp.where(k < counts[side, b], cols[k, b] + shift, empty) for k in range(SLOTS)]


def read_block(buf, place):
    return [buf[place, v] for v in range(VARS)]


def read_groups(buf, place):
    count = buf.shape[2] // 8
    return [[buf[place, v, pl.ds(8 * g, 8), :] for g in range(count)] for v in range(VARS)]


class Kept:
    def __init__(self, carry, stores):
        self.carry, self.stores = carry, stores


def store_all(stores):
    for ref, place, value in stores:
        ref[place] = value


def steps(count, most, body, carry=0):
    unroll = max(u for u in range(1, most + 1) if count % u == 0)

    def chunk(o, carry):
        kept = []
        for u in range(unroll):
            carry = body(o * unroll + u, carry)
            if isinstance(carry, Kept):
                kept += carry.stores
                carry = carry.carry
        store_all(kept)
        return carry

    return lax.fori_loop(0, count // unroll, chunk, carry)


def column_order(nrhs):
    wide_y = nrhs + WIDE
    order = []
    for first, count in ((nrhs, STATE), (wide_y + nrhs, STATE - 1), (wide_y + nrhs + WIDE, STATE)):
        order += [(half, first + j) for half in range(2) for j in range(count)]
    for first in (0, wide_y):
        order += [(half, first + q) for half in range(2) for q in range(nrhs)]
    return order


def position(n):
    return lax.axis_index("chain") % n


def distances(count):
    return [0, count - 1] + list(range(1, count - 1))


def gather_parts(parts, buf):
    here = position(buf.shape[0])
    for x, part in zip(distances(len(parts)), parts):
        for page in range(part.shape[0]):
            buf[here ^ x, page] = part[page]


def scatter_parts(buf, parts):
    here = position(buf.shape[0])
    for x, part in zip(distances(len(parts)), parts):
        for page in range(part.shape[0]):
            part[page] = buf[here ^ x, page]


def parted(kernel, before, count, n, *refs):
    if count == 1:
        return kernel(*refs)
    outs, buf = refs[before : before + count], refs[-1]
    kernel(*refs[:before], buf, *refs[before + count : -1])
    scatter_parts(buf, outs)


def joined(kernel, count, n, *refs):
    if count == 1:
        return kernel(*refs)
    gather_parts(refs[:count], refs[-1])
    kernel(refs[-1], *refs[count:-1])


def exchange(parts, n, groups):
    if len(parts) == 1:
        return [lax.all_to_all(parts[0], "chain", 0, 0, tiled=True, axis_index_groups=groups)]
    count = lax.axis_size("chain")
    return [
        part if x == 0 else lax.ppermute(part, "chain", [(i, i ^ x) for i in range(count)])
        for x, part in zip(distances(len(parts)), parts)
    ]


def local_kernel(
    n,
    rhs_h,
    inv_h,
    low_h,
    upp_h,
    lcols_h,
    ucols_h,
    counts_h,
    out,
    source,
    mlow,
    mupp,
    lcols_v,
    ucols_v,
    counts_v,
    rhs,
    inv,
    low,
    upp,
    lcols,
    ucols,
    counts,
    ybuf,
    zbuf,
    stage,
    sems,
):
    copies = [
        pltpu.make_async_copy(src, dst, sems.at[k])
        for k, (src, dst) in enumerate(
            (
                (inv_h, inv.at[:, :, pl.ds(0, rhs.shape[0]), :]),
                (low_h, low.at[pl.ds(0, low_h.shape[0]), :]),
                (lcols_h, lcols),
                (counts_h, counts),
                (ucols_h, ucols),
                (rhs_h, rhs),
                (upp_h, upp.at[pl.ds(0, upp_h.shape[0]), :]),
                (lcols_h, lcols_v),
                (ucols_h, ucols_v),
                (counts_h, counts_v),
            )
        )
    ]
    for copy in copies:
        copy.start()
    blocks, _, nrhs, cells = rhs.shape
    base = lax.axis_index("chain") * blocks
    wide_y = nrhs + WIDE
    wide_z = wide_y + WIDE
    row_y = lax.broadcasted_iota(jnp.int32, (wide_y, cells), 0)
    row_z = lax.broadcasted_iota(jnp.int32, (wide_z, cells), 0)
    for m in range(REACH):
        for v in range(VARS):
            q = VARS * m + v
            ybuf[REACH - 1 - m, v] = (row_y == nrhs + q).astype(jnp.float32)
            zbuf[blocks + m, v] = (row_z == wide_y + q).astype(jnp.float32)
    for v in range(VARS):
        ybuf[blocks + REACH, v] = jnp.zeros((wide_y, cells), jnp.float32)
        zbuf[blocks + REACH, v] = jnp.zeros((wide_z, cells), jnp.float32)
    empty = blocks + REACH
    copies[0].wait()
    copies[1].wait()
    products(inv, low, mlow)
    for copy in copies[2:6]:
        copy.wait()

    def first(b, carry):
        nears = [read_groups(ybuf, s) for s in slots(lcols, counts, 0, b, REACH - base, empty)]
        acc = couple(mlow, b, nears)
        right = [rhs[b, i] for i in range(VARS)]
        stores = []
        for i in range(VARS):
            own = mul_rows([spread(inv, (i, j), b) for j in range(VARS)], right)
            stores.append((source, (b, i), own))
            for g in range(len(acc[i])):
                value = own + acc[i][0] if g == 0 else acc[i][g]
                stores.append((ybuf, (b + REACH, i, pl.ds(8 * g, 8)), value))
        store_all(stores)
        return carry

    steps(blocks, 6, first)
    for copy in copies[6:]:
        copy.wait()
    products(inv, upp, mupp)

    def second(e, carry):
        c = blocks - 1 - e
        nears = [read_groups(zbuf, s) for s in slots(ucols, counts, 1, c, -base, empty)]
        acc = couple(mupp, c, nears)
        stores = []
        for i in range(VARS):
            for g in range(len(acc[i])):
                if g < wide_y // 8:
                    value = ybuf[c + REACH, i, 8 * g : 8 * g + 8] + acc[i][g]
                else:
                    value = acc[i][g]
                stores.append((zbuf, (c, i, pl.ds(8 * g, 8)), value))
        store_all(stores)
        return carry

    steps(blocks, 6, second)

    zero = jnp.zeros((8, cells), jnp.float32)
    for i in range(WIDE):
        m, v = i // VARS, i % VARS
        for g in range((wide_y + wide_z) // 8):
            if i == STATE:
                value = zero
            elif g < wide_y // 8:
                value = ybuf[blocks + REACH - 1 - m, v, 8 * g : 8 * g + 8]
            else:
                value = zbuf[m, v, 8 * g - wide_y : 8 * g - wide_y + 8]
            stage[pl.ds(i * SPACE + 8 * g, 8), :] = value

    def column(half, index):
        return stage[pl.ds(half * 8 * SPACE + index, 8, stride=SPACE), :]

    for half in range(2):
        place = STATE * SPACE + nrhs + 8 * half
        stage[pl.ds(place, 8), :] = column(half, wide_y + nrhs + STATE - 1)
    order = column_order(nrhs)
    width = cells // n
    for page in range(out.shape[1]):
        items = [column(*at) for at in order[page * n : (page + 1) * n]]
        items += [zero] * (n - len(items))
        for k, item in enumerate(block_transpose(items, width, cells)):
            out[k, page] = item


def split(value, period, stop, width, cells):
    items = [value]
    lane = lanes_of(cells)
    while period > stop:
        half = period // 2 * width
        bit = lane // half % 2 == 1
        fresh = []
        for item in items:
            other = pltpu.roll(item, half, 1)
            fresh += [jnp.where(bit, other, item), jnp.where(bit, item, other)]
        items = fresh
        period //= 2
    return items


def total_of(terms):
    while len(terms) > 1:
        pairs = [terms[k] + terms[k + 1] for k in range(0, len(terms) - 1, 2)]
        terms = pairs + terms[len(terms) - len(terms) % 2 :]
    return terms[0]


COLUMNS = 6 * STATE - 2


def store_state(buf, state):
    for half in range(2):
        for g, value in enumerate(state[half]):
            buf[pl.ds(g * WIDE + 8 * half, 8), :] = value


def state_rows(buf, count):
    return [[spread(buf, (), g * WIDE + j) for j in range(STATE)] for g in range(count)]


def pass_forward(d, cols, sides, state, buf, keep):
    groups, extra = len(state[0]), sides.shape[1] // 4
    store_state(buf, state)
    rows = state_rows(buf, groups)
    fresh = []
    for half in range(2):
        columns = [cols[pl.ds((d * COLUMNS + half * STATE + j) * 8, 8), :] for j in range(STATE)]
        fresh.append([])
        for g in range(groups):
            total = total_of([c * r for c, r in zip(columns, rows[g])])
            fresh[half].append(total + sides[d, half * extra + g] if g < extra else total)
        first = d * COLUMNS + 2 * STATE + half * (STATE - 1)
        columns = [cols[pl.ds((first + j) * 8, 8), :] for j in range(STATE - 1)]
        start = (d * COLUMNS + STATE + 8 * half) * 8 + 7
        columns.append(cols[pl.ds(start, 8, stride=8), :])
        for g in range(groups):
            total = total_of([c * r for c, r in zip(columns, rows[g])])
            if g < extra:
                total = total + sides[d, (2 + half) * extra + g]
            keep[d, half * groups + g] = total
    return fresh


def pass_back(d, cols, state, buf, keep):
    groups = len(state[0])
    store_state(buf, state)
    rows = state_rows(buf, groups)
    fresh = []
    for half in range(2):
        first = d * COLUMNS + 4 * STATE - 2 + half * STATE
        columns = [cols[pl.ds((first + j) * 8, 8), :] for j in range(STATE)]
        fresh.append(
            [
                total_of([c * r for c, r in zip(columns, rows[g])]) + keep[d, half * groups + g]
                for g in range(groups)
            ]
        )
    return fresh


def flat(state):
    return tuple(state[0] + state[1])


def folded(values):
    groups = len(values) // 2
    return [list(values[:groups]), list(values[groups:])]


def first_solve_kernel(x, cols, sides, offer, keep, buf):
    n, cells = x.shape[0], x.shape[3]
    width = cells // n
    packed = min(8, n)
    extra, groups = sides.shape[1] // 4, offer.shape[0] // 2
    zero = jnp.zeros((8, cells), jnp.float32)

    def unpack(d, carry):
        values = [x[d, page] for page in range(x.shape[1])]
        for page, value in enumerate(values):
            for k, block in enumerate(split(value, n, packed, width, cells)):
                e = page * n + k * packed
                if e < COLUMNS:
                    for g, item in enumerate(split(block, packed, 1, width, cells)):
                        cols[pl.ds((d * COLUMNS + e + g) * 8, 8), :] = item
                elif e < COLUMNS + 4 * 8:
                    sides[d, (e - COLUMNS) // packed] = block
        return carry

    steps(n, 2, unpack)
    lane = lanes_of(cells)
    row = lax.broadcasted_iota(jnp.int32, (8, cells), 0)
    start = []
    for half in range(2):
        start.append([zero] * extra)
        for g in range(groups - extra):
            column = lane // width % packed + g * packed
            start[half].append((column == row + 8 * half).astype(jnp.float32))

    def ahead(d, state):
        return flat(pass_forward(d, cols, sides, folded(state), buf, keep))

    leaving = steps(n, 2, ahead, flat(start))

    def back(e, state):
        return flat(pass_back(n - 1 - e, cols, folded(state), buf, keep))

    left = steps(n, 2, back, (zero,) * (2 * groups))
    is_left = lax.axis_index("chain") < n
    for e in range(2 * groups):
        offer[e] = jnp.where(is_left, leaving[e], left[e])


def second_solve_kernel(cols, sides, mine, got, out, keep, buf, states):
    n, cells = out.shape[0], out.shape[3]
    width = cells // n
    packed = min(8, n)
    extra, groups = sides.shape[1] // 4, mine.shape[0] // 2
    zero = jnp.zeros((8, cells), jnp.float32)
    is_left = lax.axis_index("chain") < n
    store_state(buf, [[mine[half * groups + g] for g in range(extra)] for half in range(2)])
    rows = state_rows(buf, extra)
    entering, far = [], []
    for half in range(2):
        columns = []
        for g in range(extra, groups):
            columns += split(got[half * groups + g], packed, 1, width, cells)
        for g in range(extra):
            known = got[half * groups + g]
            total = total_of([c * r for c, r in zip(columns, rows[g])])
            entering.append(jnp.where(is_left, 0.0, known))
            far.append(jnp.where(is_left, known + total, 0.0))

    def ahead(d, state):
        for e in range(2 * extra):
            states[d, e] = state[e]
        return flat(pass_forward(d, cols, sides, folded(state), buf, keep))

    steps(n, 4, ahead, tuple(entering))

    def back(e, state):
        d = n - 1 - e
        for e in range(2 * extra):
            states[d, 2 * extra + e] = state[e]
        return flat(pass_back(d, cols, folded(state), buf, keep))

    steps(n, 4, back, tuple(far))
    block = lanes_of(cells) // (packed * width)

    def pack(d, carry):
        for page in range(out.shape[1]):
            total = zero
            for r in range(4 * extra):
                if packed * r // n == page:
                    total = jnp.where(block == packed * r % n // packed, states[d, r], total)
            out[d, page] = total
        return carry

    steps(n, 4, pack)


def sweep_kernel(
    n,
    states,
    source,
    mlow,
    mupp,
    lcols,
    ucols,
    counts,
    low_h,
    side_h,
    zout,
    wout,
    tail,
    edge,
    low,
    side,
    ybuf,
    stage,
    sems,
):
    total = low_h.shape[0]
    copies = [
        pltpu.make_async_copy(src, dst.at[pl.ds(0, total), :], sems.at[k])
        for k, (src, dst) in enumerate(((low_h, low), (side_h, side)))
    ]
    for copy in copies:
        copy.start()
    blocks, _, nrhs, cells = source.shape
    base = lax.axis_index("chain") * blocks
    width = cells // n
    zero = jnp.zeros((nrhs, cells), jnp.float32)
    items = []
    for r in range(states.shape[1]):
        items += block_transpose([states[k, r] for k in range(n)], width, cells)
    for e in range(32):
        stage[pl.ds(8 * e, 8), :] = items[e]

    def entering(start):
        rows = [stage[pl.ds(start + q // 8 * 64 + q % 8, 8, stride=8), :] for q in range(STATE)]
        return tuple(rows)

    lane = lanes_of(cells)
    for v in range(VARS):
        wout[blocks, v] = zero

    def near(window, b, sign, cols, side):
        nears = []
        for k in range(SLOTS):
            off = sign * (cols[k, b] - base - b)
            picks = []
            for v in range(VARS):
                value = window[(REACH - 1) * VARS + v]
                for d in range(REACH - 1):
                    value = jnp.where(off == d + 1, window[d * VARS + v], value)
                picks.append(value if k == 0 else jnp.where(k < counts[side, b], value, 0.0))
            nears.append([[value] for value in picks])
        return nears

    def first(b, window):
        acc = couple(mlow, b, near(window, b, -1, lcols, 0))
        fresh = tuple(source[b, i] + acc[i][0] for i in range(VARS))
        return Kept(fresh + window[: STATE - VARS], [(ybuf, (b, i), fresh[i]) for i in range(VARS)])

    steps(blocks, 12, first, entering(0))

    def second(e, carry):
        c = blocks - 1 - e
        window, edges = carry[:STATE], list(carry[STATE:])
        acc = couple(mupp, c, near(window, c, 1, ucols, 1))
        fresh = tuple(ybuf[c, i] + acc[i][0] for i in range(VARS))
        here = (lane == 2 * c) | (lane == (2 * c + cells - 1) % cells)
        stores = []
        for i in range(VARS):
            stores += [(zout, (c, i), fresh[i]), (wout, (c, i), acc[i][0])]
            edges[i] = jnp.where(here, pltpu.roll(fresh[i], 2 * c, 1), edges[i])
        return Kept(fresh + window[: STATE - VARS] + tuple(edges), stores)

    carry = steps(blocks, 12, second, entering(128) + (zero,) * VARS)
    for v in range(VARS):
        edge[v] = carry[STATE + v]
    for m in range(REACH):
        for v in range(VARS):
            tail[m, v] = wout[blocks - REACH + m, v]
    for copy in copies:
        copy.wait()


def inner_kernel(z, w, low, side, lcols, counts, resid, coef, correction, wbuf, sem):
    store = pltpu.make_async_copy(z, correction, sem)
    store.start()
    blocks, _, nrhs, cells = z.shape
    base = lax.axis_index("chain") * blocks
    lane = lanes_of(cells)
    zero = jnp.zeros((nrhs, cells), jnp.float32)
    for v in range(VARS):
        for m in range(REACH):
            wbuf[m, v] = zero
            wbuf[m + REACH, v] = w[m, v]
        wbuf[2 * REACH, v] = zero
    pages = coef.shape[0]
    size = VARS * VARS * SLOTS
    row = lax.broadcasted_iota(jnp.int32, (8, cells), 0)

    def block(b, found, buf, shift, empty):
        nears = [read_block(buf, s) for s in slots(lcols, counts, 0, b, shift - base, empty)]
        acc = apply_coef(low, b, nears)
        left, right = [], []
        for v in range(VARS):
            here = z[b, v]
            left.append(jnp.where(lane == 0, 0.0, pltpu.roll(here, 1, 1)))
            right.append(jnp.where(lane == cells - 1, 0.0, pltpu.roll(here, cells - 1, 1)))
        beside = apply_coef(side, b, [left, right])
        here = (lane + row % 2) % cells == 2 * b
        found = tuple(
            jnp.where(here, pltpu.roll(side[pl.ds(b * size + 8 * r, 8), :], 2 * b, 1), found[r])
            for r in range(pages)
        )
        return Kept(found, [(resid, (b, i), acc[i] + beside[i]) for i in range(VARS)])

    found = (jnp.zeros((8, cells), jnp.float32),) * pages
    for b in range(REACH):
        kept = block(b, found, wbuf, REACH, 2 * REACH)
        store_all(kept.stores)
        found = kept.carry

    def inner(b, found):
        return block(b + REACH, found, w, 0, blocks)

    found = steps(blocks - REACH, 7, inner, found)
    for r in range(pages):
        coef[r] = found[r]
    store.wait()


def outer_kernel(
    inner, coef, low, tail, swap_a, swap_b, lcols, counts, resid, squares, wbuf
):
    blocks, _, nrhs, cells = inner.shape
    base = lax.axis_index("chain") * blocks
    first_block = lax.axis_index("chain") == 0
    place = lax.axis_index("sub")
    odd = place % 2 == 1
    first, last = place == 0, place == lax.axis_size("sub") - 1
    lane = lanes_of(cells)
    zero = jnp.zeros((nrhs, cells), jnp.float32)
    near = []
    for v in range(VARS):
        west = jnp.where(first, 0.0, jnp.where(odd, swap_a[v], swap_b[v]))
        east = jnp.where(last, 0.0, jnp.where(odd, swap_b[v], swap_a[v]))
        west, east = pltpu.roll(west, 1, 1), pltpu.roll(east, cells - 1, 1)
        near.append(jnp.where(lane % 2 == 0, west, east))
    edge = []
    for i in range(VARS):
        rows = []
        for j in range(VARS):
            k = (i * VARS + j) * SLOTS
            rows.append(coef[k // 8, pl.ds(k % 8, 1), :] + coef[(k + 1) // 8, pl.ds((k + 1) % 8, 1), :])
        edge.append(mul_rows(rows, near))
    for v in range(VARS):
        for m in range(REACH):
            wbuf[m, v] = jnp.where(first_block, 0.0, tail[m, v])
        wbuf[REACH, v] = zero
    ends = (lane == 0) | (lane == cells - 1)

    def add(b, values, totals):
        stores, fresh = [], []
        for i in range(VARS):
            other = pltpu.roll(edge[i], (cells - 2 * b) % cells, 1)
            value = values[i] + jnp.where(ends, other, 0.0)
            stores.append((resid, (b, i), value))
            fresh.append(totals[i] + value * value)
        return Kept(tuple(fresh), stores)

    totals = (zero,) * VARS
    stores = []
    for b in range(REACH):
        places = [
            jnp.where(s < REACH, s, REACH) for s in slots(lcols, counts, 0, b, REACH - base, REACH)
        ]
        acc = apply_coef(low, b, [read_block(wbuf, s) for s in places])
        kept = add(b, [inner[b, i] + acc[i] for i in range(VARS)], totals)
        stores += kept.stores
        totals = kept.carry
    store_all(stores)

    def rest(b, totals):
        return add(b + REACH, [inner[b + REACH, i] for i in range(VARS)], totals)

    totals = steps(blocks - REACH, 7, rest, totals)
    total = totals[0]
    for i in range(1, VARS):
        total = total + totals[i]
    sums = jnp.broadcast_to(jnp.sum(total, axis=1, keepdims=True), total.shape)
    row = lax.broadcasted_iota(jnp.int32, total.shape, 0)
    line = jnp.sum(jnp.where(lane == row, sums, 0.0), axis=0, keepdims=True)
    for p in range(squares.shape[0]):
        squares[p] = line


def scale_kernel(entries, resid, squares, out, scaled, sems):
    blocks, _, nrhs, cells = resid.shape
    line = squares[0]
    for p in range(1, squares.shape[0]):
        line = line + squares[p]
    lane = lanes_of(cells)
    row = lax.broadcasted_iota(jnp.int32, (nrhs, cells), 0)
    line = jnp.where(lane == row, jnp.broadcast_to(line, (nrhs, cells)), 0.0)
    msq = jnp.sum(line, axis=1, keepdims=True) / entries
    factor = jnp.broadcast_to(-lax.rsqrt(msq + 1e-06), (nrhs, cells))

    count = sems.shape[0]
    size = blocks // count
    copies = []
    for part in range(count):
        stores = [
            (scaled, (b, v), resid[b, v] * factor)
            for b in range(part * size, (part + 1) * size)
            for v in range(VARS)
        ]
        store_all(stores)
        here = pl.ds(part * size, size)
        copies.append(pltpu.make_async_copy(scaled.at[here], out.at[here], sems.at[part]))
        copies[part].start()
    for copy in copies:
        copy.wait()


def call(kernel, outs, args, places, scratch):
    args = [
        pltpu.with_memory_space_constraint(a, p) if p is HBM else a for a, p in zip(args, places)
    ]
    return pl.pallas_call(
        kernel,
        out_shape=[jax.ShapeDtypeStruct(o[0], (o + (jnp.float32,))[2]) for o in outs],
        in_specs=[pl.BlockSpec(memory_space=p) for p in places],
        out_specs=[pl.BlockSpec(memory_space=p) for p in (o[1] for o in outs)],
        scratch_shapes=[VMEM(s, jnp.float32) if isinstance(s, tuple) else s for s in scratch],
        compiler_params=pltpu.CompilerParams(vmem_limit_bytes=VMEM_LIMIT),
    )(*args)


def shards(
    rhs, diag_block, diag_inverse, lower_coef, upper_coef, side_coef, lower_cols, upper_cols, counts
):
    blocks, nvars, nrhs, cells = rhs.shape
    n = lax.axis_size("chain")
    inv = jnp.transpose(diag_inverse, (1, 2, 0, 3))
    low, upp, side = (
        jnp.transpose(a, (0, 2, 3, 1, 4)).reshape(-1, cells)
        for a in (lower_coef, upper_coef, side_coef)
    )
    lcols, ucols, used = lower_cols.T, upper_cols.T, counts.T
    m = lax.axis_size("sub")
    rows = blocks + REACH + 1
    half = n // 2
    parts = -(-len(column_order(nrhs)) // half)
    back = -(-32 // half)
    packed = min(8, half)
    extra = 8 // packed
    wide = 2 * (extra + WIDE // packed)
    sides = [list(range(half)), list(range(half, n))]
    tile = (nrhs, cells)

    mats = (VARS, VARS, SLOTS, blocks + PAD, cells)
    padded = (low.shape[0] + VARS * VARS * SLOTS, cells)

    count = half if half <= DIRECT else 1

    def pieces(pages):
        return [((pages,) + tile, VMEM)] * count if count > 1 else [((half, pages) + tile, VMEM)]

    def whole(pages):
        return [(half, pages) + tile] if count > 1 else []

    *maps, source, mlow, mupp, lcols, ucols, used = call(
        functools.partial(parted, functools.partial(local_kernel, half), 7, count, half),
        pieces(parts)
        + [(rhs.shape, VMEM), (mats, VMEM), (mats, VMEM)]
        + [(lcols.shape, VMEM, jnp.int32)] * 3,
        (rhs, inv, low, upp, lcols, ucols, used),
        (HBM,) * 7,
        [rhs.shape, (VARS, VARS, blocks + PAD, cells), padded, padded]
        + [pltpu.SMEM(lcols.shape, jnp.int32)] * 3
        + [(rows, VARS, nrhs + WIDE, cells), (rows, VARS, nrhs + 2 * WIDE, cells)]
        + [(WIDE * SPACE + SPACE, cells), pltpu.SemaphoreType.DMA((10,))]
        + whole(parts),
    )
    maps = exchange(maps, half, sides)
    cols, ends, offer = call(
        functools.partial(joined, first_solve_kernel, count, half),
        [
            ((half * COLUMNS * 8, cells), VMEM),
            ((half, 4 * extra) + tile, VMEM),
            ((wide,) + tile, VMEM),
        ],
        tuple(maps),
        (VMEM,) * count,
        [(half, wide) + tile, (wide // 2 * WIDE + PAD, cells)] + whole(parts),
    )
    got = lax.ppermute(
        offer, "chain", [p for i in range(half) for p in ((i, i + half), (i + half, i))]
    )
    states = call(
        functools.partial(parted, second_solve_kernel, 4, count, half),
        pieces(back),
        (cols, ends, offer, got),
        (VMEM,) * 4,
        [(half, 2 * extra) + tile, (extra * WIDE + PAD, cells), (half, 4 * extra) + tile]
        + whole(back),
    )
    states = exchange(states, half, sides)
    z, w, tail, edge, low, side = call(
        functools.partial(joined, functools.partial(sweep_kernel, half), count, half),
        [
            (rhs.shape, VMEM),
            ((blocks + 1, VARS) + tile, VMEM),
            ((REACH, VARS) + tile, VMEM),
            ((VARS,) + tile, VMEM),
            (padded, VMEM),
            (padded, VMEM),
        ],
        (*states, source, mlow, mupp, lcols, ucols, used, low, side),
        (VMEM,) * (3 + count) + (SMEM,) * 3 + (HBM,) * 2,
        [rhs.shape, (33 * 8, cells), pltpu.SemaphoreType.DMA((2,))] + whole(back),
    )
    tail = lax.ppermute(tail, "chain", [(i, (i + 1) % n) for i in range(n)])
    swap_a, swap_b = (
        lax.ppermute(edge, "sub", [p for i, j in pairs for p in ((i, j), (j, i))])
        for pairs in (
            [(i, i + 1) for i in range(0, m - 1, 2)],
            [(i, i + 1) for i in range(1, m - 1, 2)] + [(0, m - 1)] * (m % 2 == 0),
        )
    )
    inner, coef, correction = call(
        inner_kernel,
        [
            (rhs.shape, VMEM),
            ((-(-VARS * VARS * SLOTS // 8),) + (8, cells), VMEM),
            (rhs.shape, HBM),
        ],
        (z, w, low, side, lcols, used),
        (VMEM,) * 4 + (SMEM,) * 2,
        [(2 * REACH + 1, VARS) + tile, pltpu.SemaphoreType.DMA],
    )
    resid, squares = call(
        outer_kernel,
        [(rhs.shape, VMEM), ((n * m, 1, cells), VMEM)],
        (inner, coef, low, tail, swap_a, swap_b, lcols, used),
        (VMEM,) * 6 + (SMEM,) * 2,
        [(REACH + 1, VARS) + tile],
    )
    squares = lax.all_to_all(squares, ("chain", "sub"), 0, 0, tiled=True)
    entries = blocks * VARS * cells * n * m
    (residual_unit,) = call(
        functools.partial(scale_kernel, entries),
        [(rhs.shape, HBM)],
        (resid, squares),
        (VMEM, VMEM),
        [rhs.shape, pltpu.SemaphoreType.DMA((4 if blocks % 4 == 0 else 1,))],
    )
    return (correction, residual_unit)


def solution(mesh):
    in_specs = (
        P("chain", None, None, "sub"),
        P("chain", None, None, "sub"),
        P("chain", None, None, "sub"),
        P("chain", None, None, None, "sub"),
        P("chain", None, None, None, "sub"),
        P("chain", None, None, None, "sub"),
        P("chain", None),
        P("chain", None),
        P("chain", None),
    )
    out_specs = (P("chain", None, None, "sub"), P("chain", None, None, "sub"))
    return jax.shard_map(shards, mesh=mesh, in_specs=in_specs, out_specs=out_specs, check_vma=False)
```

```python
import functools

import jax
import jax.numpy as jnp
from jax import lax
from jax.experimental import pallas as pl
from jax.experimental.pallas import tpu as pltpu
from jax.sharding import PartitionSpec as P

VARS = 5
REACH = 3
SLOTS = 2
STATE = REACH * VARS
WIDE = 16
PAD = 8
SPACE = 72
DIRECT = 4
VMEM_LIMIT = 40 * 1024 * 1024

VMEM = pltpu.VMEM
SMEM = pltpu.SMEM
HBM = pltpu.HBM


def lanes_of(cells):
    return lax.broadcasted_iota(jnp.int32, (8, cells), 1)


def block_transpose(items, width, cells):
    count = len(items)
    lane = lanes_of(cells)
    half = 1
    while half < count:
        bit = (lane // (half * width)) % 2 == 1
        out = list(items)
        for a in range(count):
            if a & half:
                continue
            b = a + half
            out[a] = jnp.where(bit, pltpu.roll(items[b], half * width, 1), items[a])
            out[b] = jnp.where(bit, items[b], pltpu.roll(items[a], cells - half * width, 1))
        items = out
        half *= 2
    return items


def spread(ref, place, row):
    return ref[place + (pl.ds(row, 8, stride=0), slice(None))]


def mul_rows(rows, near):
    total = rows[0] * near[0]
    for j in range(1, len(near)):
        total = total + rows[j] * near[j]
    return total


def mul_groups(rows, nears):
    return [mul_rows(rows, [near[g] for near in nears]) for g in range(len(nears[0]))]


def couple(mats, b, nears):
    out = []
    for i in range(VARS):
        parts = [
            mul_groups([spread(mats, (i, j, k), b) for j in range(VARS)], nears[k])
            for k in range(SLOTS)
        ]
        out.append([x + y for x, y in zip(*parts)])
    return out


def apply_coef(coef, b, nears):
    out = []
    for i in range(VARS):
        parts = []
        for k in range(SLOTS):
            place = (b * VARS + i) * VARS * SLOTS + k
            parts.append(
                mul_rows([spread(coef, (), place + SLOTS * j) for j in range(VARS)], nears[k])
            )
        out.append(parts[0] + parts[1])
    return out


def products(inv, coef, out):
    blocks = out.shape[3] - PAD
    stride = VARS * VARS * SLOTS

    def some(o, carry):
        start = o * 8
        left = [[-inv[i, m, pl.ds(start, 8), :] for m in range(VARS)] for i in range(VARS)]
        for k in range(SLOTS):
            stores = []
            for j in range(VARS):
                place = start * stride + j * SLOTS + k
                right = [
                    coef[pl.ds(place + m * VARS * SLOTS, 8, stride=stride), :] for m in range(VARS)
                ]
                for i in range(VARS):
                    here = (i, j, k, pl.ds(start, 8))
                    stores.append((out, here, mul_rows(left[i], right)))
            store_all(stores)
        return carry

    steps(blocks // 8, 3, some)


def slots(cols, counts, side, b, shift, empty):
    return [jnp.where(k < counts[side, b], cols[k, b] + shift, empty) for k in range(SLOTS)]


def read_block(buf, place):
    return [buf[place, v] for v in range(VARS)]


def read_groups(buf, place):
    count = buf.shape[2] // 8
    return [[buf[place, v, pl.ds(8 * g, 8), :] for g in range(count)] for v in range(VARS)]


class Kept:
    def __init__(self, carry, stores):
        self.carry, self.stores = carry, stores


def store_all(stores):
    for ref, place, value in stores:
        ref[place] = value


def steps(count, most, body, carry=0):
    unroll = max(u for u in range(1, most + 1) if count % u == 0)

    def chunk(o, carry):
        kept = []
        for u in range(unroll):
            carry = body(o * unroll + u, carry)
            if isinstance(carry, Kept):
                kept += carry.stores
                carry = carry.carry
        store_all(kept)
        return carry

    return lax.fori_loop(0, count // unroll, chunk, carry)


def column_order(nrhs):
    wide_y = nrhs + WIDE
    order = []
    for first, count in ((nrhs, STATE), (wide_y + nrhs, STATE - 1), (wide_y + nrhs + WIDE, STATE)):
        order += [(half, first + j) for half in range(2) for j in range(count)]
    for first in (0, wide_y):
        order += [(half, first + q) for half in range(2) for q in range(nrhs)]
    return order


def position(n):
    return lax.axis_index("chain") % n


def distances(count):
    return [0] + list(range(count - 1, 0, -1))


def gather_parts(parts, buf):
    here = position(buf.shape[0])
    for x, part in zip(distances(len(parts)), parts):
        for page in range(part.shape[0]):
            buf[here ^ x, page] = part[page]


def scatter_parts(buf, parts):
    here = position(buf.shape[0])
    for x, part in zip(distances(len(parts)), parts):
        for page in range(part.shape[0]):
            part[page] = buf[here ^ x, page]


def parted(kernel, before, count, n, *refs):
    if count == 1:
        return kernel(*refs)
    outs, buf = refs[before : before + count], refs[-1]
    kernel(*refs[:before], buf, *refs[before + count : -1])
    scatter_parts(buf, outs)


def joined(kernel, count, n, *refs):
    if count == 1:
        return kernel(*refs)
    gather_parts(refs[:count], refs[-1])
    kernel(refs[-1], *refs[count:-1])


def exchange(parts, n, groups):
    if len(parts) == 1:
        return [lax.all_to_all(parts[0], "chain", 0, 0, tiled=True, axis_index_groups=groups)]
    count = lax.axis_size("chain")
    return [
        part if x == 0 else lax.ppermute(part, "chain", [(i, i ^ x) for i in range(count)])
        for x, part in zip(distances(len(parts)), parts)
    ]


def local_kernel(
    n,
    rhs_h,
    inv_h,
    low_h,
    upp_h,
    lcols_h,
    ucols_h,
    counts_h,
    out,
    source,
    mlow,
    mupp,
    lcols_v,
    ucols_v,
    counts_v,
    rhs,
    inv,
    low,
    upp,
    lcols,
    ucols,
    counts,
    ybuf,
    zbuf,
    stage,
    sems,
):
    copies = [
        pltpu.make_async_copy(src, dst, sems.at[k])
        for k, (src, dst) in enumerate(
            (
                (inv_h, inv.at[:, :, pl.ds(0, rhs.shape[0]), :]),
                (low_h, low.at[pl.ds(0, low_h.shape[0]), :]),
                (lcols_h, lcols),
                (counts_h, counts),
                (ucols_h, ucols),
                (rhs_h, rhs),
                (upp_h, upp.at[pl.ds(0, upp_h.shape[0]), :]),
                (lcols_h, lcols_v),
                (ucols_h, ucols_v),
                (counts_h, counts_v),
            )
        )
    ]
    for copy in copies:
        copy.start()
    blocks, _, nrhs, cells = rhs.shape
    base = lax.axis_index("chain") * blocks
    wide_y = nrhs + WIDE
    wide_z = wide_y + WIDE
    row_y = lax.broadcasted_iota(jnp.int32, (wide_y, cells), 0)
    row_z = lax.broadcasted_iota(jnp.int32, (wide_z, cells), 0)
    for m in range(REACH):
        for v in range(VARS):
            q = VARS * m + v
            ybuf[REACH - 1 - m, v] = (row_y == nrhs + q).astype(jnp.float32)
            zbuf[blocks + m, v] = (row_z == wide_y + q).astype(jnp.float32)
    for v in range(VARS):
        ybuf[blocks + REACH, v] = jnp.zeros((wide_y, cells), jnp.float32)
        zbuf[blocks + REACH, v] = jnp.zeros((wide_z, cells), jnp.float32)
    empty = blocks + REACH
    copies[0].wait()
    copies[1].wait()
    products(inv, low, mlow)
    for copy in copies[2:6]:
        copy.wait()

    def first(b, carry):
        nears = [read_groups(ybuf, s) for s in slots(lcols, counts, 0, b, REACH - base, empty)]
        acc = couple(mlow, b, nears)
        right = [rhs[b, i] for i in range(VARS)]
        stores = []
        for i in range(VARS):
            own = mul_rows([spread(inv, (i, j), b) for j in range(VARS)], right)
            stores.append((source, (b, i), own))
            for g in range(len(acc[i])):
                value = own + acc[i][0] if g == 0 else acc[i][g]
                stores.append((ybuf, (b + REACH, i, pl.ds(8 * g, 8)), value))
        store_all(stores)
        return carry

    steps(blocks, 6, first)
    for copy in copies[6:]:
        copy.wait()
    products(inv, upp, mupp)

    def second(e, carry):
        c = blocks - 1 - e
        nears = [read_groups(zbuf, s) for s in slots(ucols, counts, 1, c, -base, empty)]
        acc = couple(mupp, c, nears)
        stores = []
        for i in range(VARS):
            for g in range(len(acc[i])):
                if g < wide_y // 8:
                    value = ybuf[c + REACH, i, 8 * g : 8 * g + 8] + acc[i][g]
                else:
                    value = acc[i][g]
                stores.append((zbuf, (c, i, pl.ds(8 * g, 8)), value))
        store_all(stores)
        return carry

    steps(blocks, 6, second)

    zero = jnp.zeros((8, cells), jnp.float32)
    for i in range(WIDE):
        m, v = i // VARS, i % VARS
        for g in range((wide_y + wide_z) // 8):
            if i == STATE:
                value = zero
            elif g < wide_y // 8:
                value = ybuf[blocks + REACH - 1 - m, v, 8 * g : 8 * g + 8]
            else:
                value = zbuf[m, v, 8 * g - wide_y : 8 * g - wide_y + 8]
            stage[pl.ds(i * SPACE + 8 * g, 8), :] = value

    def column(half, index):
        return stage[pl.ds(half * 8 * SPACE + index, 8, stride=SPACE), :]

    for half in range(2):
        place = STATE * SPACE + nrhs + 8 * half
        stage[pl.ds(place, 8), :] = column(half, wide_y + nrhs + STATE - 1)
    order = column_order(nrhs)
    width = cells // n
    for page in range(out.shape[1]):
        items = [column(*at) for at in order[page * n : (page + 1) * n]]
        items += [zero] * (n - len(items))
        for k, item in enumerate(block_transpose(items, width, cells)):
            out[k, page] = item


def split(value, period, stop, width, cells):
    items = [value]
    lane = lanes_of(cells)
    while period > stop:
        half = period // 2 * width
        bit = lane // half % 2 == 1
        fresh = []
        for item in items:
            other = pltpu.roll(item, half, 1)
            fresh += [jnp.where(bit, other, item), jnp.where(bit, item, other)]
        items = fresh
        period //= 2
    return items


def total_of(terms):
    while len(terms) > 1:
        pairs = [terms[k] + terms[k + 1] for k in range(0, len(terms) - 1, 2)]
        terms = pairs + terms[len(terms) - len(terms) % 2 :]
    return terms[0]


COLUMNS = 6 * STATE - 2


def store_state(buf, state):
    for half in range(2):
        for g, value in enumerate(state[half]):
            buf[pl.ds(g * WIDE + 8 * half, 8), :] = value


def state_rows(buf, count):
    return [[spread(buf, (), g * WIDE + j) for j in range(STATE)] for g in range(count)]


def pass_forward(d, cols, sides, state, buf, keep):
    groups, extra = len(state[0]), sides.shape[1] // 4
    store_state(buf, state)
    rows = state_rows(buf, groups)
    fresh = []
    for half in range(2):
        columns = [cols[pl.ds((d * COLUMNS + half * STATE + j) * 8, 8), :] for j in range(STATE)]
        fresh.append([])
        for g in range(groups):
            total = total_of([c * r for c, r in zip(columns, rows[g])])
            fresh[half].append(total + sides[d, half * extra + g] if g < extra else total)
        first = d * COLUMNS + 2 * STATE + half * (STATE - 1)
        columns = [cols[pl.ds((first + j) * 8, 8), :] for j in range(STATE - 1)]
        start = (d * COLUMNS + STATE + 8 * half) * 8 + 7
        columns.append(cols[pl.ds(start, 8, stride=8), :])
        for g in range(groups):
            total = total_of([c * r for c, r in zip(columns, rows[g])])
            if g < extra:
                total = total + sides[d, (2 + half) * extra + g]
            keep[d, half * groups + g] = total
    return fresh


def pass_back(d, cols, state, buf, keep):
    groups = len(state[0])
    store_state(buf, state)
    rows = state_rows(buf, groups)
    fresh = []
    for half in range(2):
        first = d * COLUMNS + 4 * STATE - 2 + half * STATE
        columns = [cols[pl.ds((first + j) * 8, 8), :] for j in range(STATE)]
        fresh.append(
            [
                total_of([c * r for c, r in zip(columns, rows[g])]) + keep[d, half * groups + g]
                for g in range(groups)
            ]
        )
    return fresh


def flat(state):
    return tuple(state[0] + state[1])


def folded(values):
    groups = len(values) // 2
    return [list(values[:groups]), list(values[groups:])]


def first_solve_kernel(x, cols, sides, offer, keep, buf):
    n, cells = x.shape[0], x.shape[3]
    width = cells // n
    packed = min(8, n)
    extra, groups = sides.shape[1] // 4, offer.shape[0] // 2
    zero = jnp.zeros((8, cells), jnp.float32)

    def unpack(d, carry):
        values = [x[d, page] for page in range(x.shape[1])]
        for page, value in enumerate(values):
            for k, block in enumerate(split(value, n, packed, width, cells)):
                e = page * n + k * packed
                if e < COLUMNS:
                    for g, item in enumerate(split(block, packed, 1, width, cells)):
                        cols[pl.ds((d * COLUMNS + e + g) * 8, 8), :] = item
                elif e < COLUMNS + 4 * 8:
                    sides[d, (e - COLUMNS) // packed] = block
        return carry

    steps(n, 2, unpack)
    lane = lanes_of(cells)
    row = lax.broadcasted_iota(jnp.int32, (8, cells), 0)
    start = []
    for half in range(2):
        start.append([zero] * extra)
        for g in range(groups - extra):
            column = lane // width % packed + g * packed
            start[half].append((column == row + 8 * half).astype(jnp.float32))

    def ahead(d, state):
        return flat(pass_forward(d, cols, sides, folded(state), buf, keep))

    leaving = steps(n, 2, ahead, flat(start))

    def back(e, state):
        return flat(pass_back(n - 1 - e, cols, folded(state), buf, keep))

    left = steps(n, 2, back, (zero,) * (2 * groups))
    is_left = lax.axis_index("chain") < n
    for e in range(2 * groups):
        offer[e] = jnp.where(is_left, leaving[e], left[e])


def second_solve_kernel(cols, sides, mine, got, out, keep, buf, states):
    n, cells = out.shape[0], out.shape[3]
    width = cells // n
    packed = min(8, n)
    extra, groups = sides.shape[1] // 4, mine.shape[0] // 2
    zero = jnp.zeros((8, cells), jnp.float32)
    is_left = lax.axis_index("chain") < n
    store_state(buf, [[mine[half * groups + g] for g in range(extra)] for half in range(2)])
    rows = state_rows(buf, extra)
    entering, far = [], []
    for half in range(2):
        columns = []
        for g in range(extra, groups):
            columns += split(got[half * groups + g], packed, 1, width, cells)
        for g in range(extra):
            known = got[half * groups + g]
            total = total_of([c * r for c, r in zip(columns, rows[g])])
            entering.append(jnp.where(is_left, 0.0, known))
            far.append(jnp.where(is_left, known + total, 0.0))

    def ahead(d, state):
        for e in range(2 * extra):
            states[d, e] = state[e]
        return flat(pass_forward(d, cols, sides, folded(state), buf, keep))

    steps(n, 4, ahead, tuple(entering))

    def back(e, state):
        d = n - 1 - e
        for e in range(2 * extra):
            states[d, 2 * extra + e] = state[e]
        return flat(pass_back(d, cols, folded(state), buf, keep))

    steps(n, 4, back, tuple(far))
    block = lanes_of(cells) // (packed * width)

    def pack(d, carry):
        for page in range(out.shape[1]):
            total = zero
            for r in range(4 * extra):
                if packed * r // n == page:
                    total = jnp.where(block == packed * r % n // packed, states[d, r], total)
            out[d, page] = total
        return carry

    steps(n, 4, pack)


def sweep_kernel(
    n,
    states,
    source,
    mlow,
    mupp,
    lcols,
    ucols,
    counts,
    low_h,
    side_h,
    zout,
    wout,
    tail,
    edge,
    low,
    side,
    ybuf,
    stage,
    sems,
):
    total = low_h.shape[0]
    copies = [
        pltpu.make_async_copy(src, dst.at[pl.ds(0, total), :], sems.at[k])
        for k, (src, dst) in enumerate(((low_h, low), (side_h, side)))
    ]
    for copy in copies:
        copy.start()
    blocks, _, nrhs, cells = source.shape
    base = lax.axis_index("chain") * blocks
    width = cells // n
    zero = jnp.zeros((nrhs, cells), jnp.float32)
    items = []
    for r in range(states.shape[1]):
        items += block_transpose([states[k, r] for k in range(n)], width, cells)
    for e in range(32):
        stage[pl.ds(8 * e, 8), :] = items[e]

    def entering(start):
        rows = [stage[pl.ds(start + q // 8 * 64 + q % 8, 8, stride=8), :] for q in range(STATE)]
        return tuple(rows)

    lane = lanes_of(cells)
    for v in range(VARS):
        wout[blocks, v] = zero

    def near(window, b, sign, cols, side):
        nears = []
        for k in range(SLOTS):
            off = sign * (cols[k, b] - base - b)
            picks = []
            for v in range(VARS):
                value = window[(REACH - 1) * VARS + v]
                for d in range(REACH - 1):
                    value = jnp.where(off == d + 1, window[d * VARS + v], value)
                picks.append(value if k == 0 else jnp.where(k < counts[side, b], value, 0.0))
            nears.append([[value] for value in picks])
        return nears

    def first(b, window):
        acc = couple(mlow, b, near(window, b, -1, lcols, 0))
        fresh = tuple(source[b, i] + acc[i][0] for i in range(VARS))
        return Kept(fresh + window[: STATE - VARS], [(ybuf, (b, i), fresh[i]) for i in range(VARS)])

    steps(blocks, 12, first, entering(0))

    def second(e, carry):
        c = blocks - 1 - e
        window, edges = carry[:STATE], list(carry[STATE:])
        acc = couple(mupp, c, near(window, c, 1, ucols, 1))
        fresh = tuple(ybuf[c, i] + acc[i][0] for i in range(VARS))
        here = (lane == 2 * c) | (lane == (2 * c + cells - 1) % cells)
        stores = []
        for i in range(VARS):
            stores += [(zout, (c, i), fresh[i]), (wout, (c, i), acc[i][0])]
            edges[i] = jnp.where(here, pltpu.roll(fresh[i], 2 * c, 1), edges[i])
        return Kept(fresh + window[: STATE - VARS] + tuple(edges), stores)

    carry = steps(blocks, 12, second, entering(128) + (zero,) * VARS)
    for v in range(VARS):
        edge[v] = carry[STATE + v]
    for m in range(REACH):
        for v in range(VARS):
            tail[m, v] = wout[blocks - REACH + m, v]
    for copy in copies:
        copy.wait()


def inner_kernel(z, w, low, side, lcols, counts, resid, coef, correction, wbuf, sem):
    store = pltpu.make_async_copy(z, correction, sem)
    store.start()
    blocks, _, nrhs, cells = z.shape
    base = lax.axis_index("chain") * blocks
    lane = lanes_of(cells)
    zero = jnp.zeros((nrhs, cells), jnp.float32)
    for v in range(VARS):
        for m in range(REACH):
            wbuf[m, v] = zero
            wbuf[m + REACH, v] = w[m, v]
        wbuf[2 * REACH, v] = zero
    pages = coef.shape[0]
    size = VARS * VARS * SLOTS
    row = lax.broadcasted_iota(jnp.int32, (8, cells), 0)

    def block(b, found, buf, shift, empty):
        nears = [read_block(buf, s) for s in slots(lcols, counts, 0, b, shift - base, empty)]
        acc = apply_coef(low, b, nears)
        left, right = [], []
        for v in range(VARS):
            here = z[b, v]
            left.append(jnp.where(lane == 0, 0.0, pltpu.roll(here, 1, 1)))
            right.append(jnp.where(lane == cells - 1, 0.0, pltpu.roll(here, cells - 1, 1)))
        beside = apply_coef(side, b, [left, right])
        here = (lane + row % 2) % cells == 2 * b
        found = tuple(
            jnp.where(here, pltpu.roll(side[pl.ds(b * size + 8 * r, 8), :], 2 * b, 1), found[r])
            for r in range(pages)
        )
        return Kept(found, [(resid, (b, i), acc[i] + beside[i]) for i in range(VARS)])

    found = (jnp.zeros((8, cells), jnp.float32),) * pages
    for b in range(REACH):
        kept = block(b, found, wbuf, REACH, 2 * REACH)
        store_all(kept.stores)
        found = kept.carry

    def inner(b, found):
        return block(b + REACH, found, w, 0, blocks)

    found = steps(blocks - REACH, 7, inner, found)
    for r in range(pages):
        coef[r] = found[r]
    store.wait()


def outer_kernel(
    inner, coef, low, tail, swap_a, swap_b, lcols, counts, resid, squares, wbuf
):
    blocks, _, nrhs, cells = inner.shape
    base = lax.axis_index("chain") * blocks
    first_block = lax.axis_index("chain") == 0
    place = lax.axis_index("sub")
    odd = place % 2 == 1
    first, last = place == 0, place == lax.axis_size("sub") - 1
    lane = lanes_of(cells)
    zero = jnp.zeros((nrhs, cells), jnp.float32)
    near = []
    for v in range(VARS):
        west = jnp.where(first, 0.0, jnp.where(odd, swap_a[v], swap_b[v]))
        east = jnp.where(last, 0.0, jnp.where(odd, swap_b[v], swap_a[v]))
        west, east = pltpu.roll(west, 1, 1), pltpu.roll(east, cells - 1, 1)
        near.append(jnp.where(lane % 2 == 0, west, east))
    edge = []
    for i in range(VARS):
        rows = []
        for j in range(VARS):
            k = (i * VARS + j) * SLOTS
            rows.append(coef[k // 8, pl.ds(k % 8, 1), :] + coef[(k + 1) // 8, pl.ds((k + 1) % 8, 1), :])
        edge.append(mul_rows(rows, near))
    for v in range(VARS):
        for m in range(REACH):
            wbuf[m, v] = jnp.where(first_block, 0.0, tail[m, v])
        wbuf[REACH, v] = zero
    ends = (lane == 0) | (lane == cells - 1)

    def add(b, values, totals):
        stores, fresh = [], []
        for i in range(VARS):
            other = pltpu.roll(edge[i], (cells - 2 * b) % cells, 1)
            value = values[i] + jnp.where(ends, other, 0.0)
            stores.append((resid, (b, i), value))
            fresh.append(totals[i] + value * value)
        return Kept(tuple(fresh), stores)

    totals = (zero,) * VARS
    stores = []
    for b in range(REACH):
        places = [
            jnp.where(s < REACH, s, REACH) for s in slots(lcols, counts, 0, b, REACH - base, REACH)
        ]
        acc = apply_coef(low, b, [read_block(wbuf, s) for s in places])
        kept = add(b, [inner[b, i] + acc[i] for i in range(VARS)], totals)
        stores += kept.stores
        totals = kept.carry
    store_all(stores)

    def rest(b, totals):
        return add(b + REACH, [inner[b + REACH, i] for i in range(VARS)], totals)

    totals = steps(blocks - REACH, 7, rest, totals)
    total = totals[0]
    for i in range(1, VARS):
        total = total + totals[i]
    sums = jnp.broadcast_to(jnp.sum(total, axis=1, keepdims=True), total.shape)
    row = lax.broadcasted_iota(jnp.int32, total.shape, 0)
    line = jnp.sum(jnp.where(lane == row, sums, 0.0), axis=0, keepdims=True)
    for p in range(squares.shape[0]):
        squares[p] = line


def scale_kernel(entries, resid, squares, out, scaled, sems):
    blocks, _, nrhs, cells = resid.shape
    line = squares[0]
    for p in range(1, squares.shape[0]):
        line = line + squares[p]
    lane = lanes_of(cells)
    row = lax.broadcasted_iota(jnp.int32, (nrhs, cells), 0)
    line = jnp.where(lane == row, jnp.broadcast_to(line, (nrhs, cells)), 0.0)
    msq = jnp.sum(line, axis=1, keepdims=True) / entries
    factor = jnp.broadcast_to(-lax.rsqrt(msq + 1e-06), (nrhs, cells))

    count = sems.shape[0]
    size = blocks // count
    copies = []
    for part in range(count):
        stores = [
            (scaled, (b, v), resid[b, v] * factor)
            for b in range(part * size, (part + 1) * size)
            for v in range(VARS)
        ]
        store_all(stores)
        here = pl.ds(part * size, size)
        copies.append(pltpu.make_async_copy(scaled.at[here], out.at[here], sems.at[part]))
        copies[part].start()
    for copy in copies:
        copy.wait()


def call(kernel, outs, args, places, scratch):
    args = [
        pltpu.with_memory_space_constraint(a, p) if p is HBM else a for a, p in zip(args, places)
    ]
    return pl.pallas_call(
        kernel,
        out_shape=[jax.ShapeDtypeStruct(o[0], (o + (jnp.float32,))[2]) for o in outs],
        in_specs=[pl.BlockSpec(memory_space=p) for p in places],
        out_specs=[pl.BlockSpec(memory_space=p) for p in (o[1] for o in outs)],
        scratch_shapes=[VMEM(s, jnp.float32) if isinstance(s, tuple) else s for s in scratch],
        compiler_params=pltpu.CompilerParams(vmem_limit_bytes=VMEM_LIMIT),
    )(*args)


def shards(
    rhs, diag_block, diag_inverse, lower_coef, upper_coef, side_coef, lower_cols, upper_cols, counts
):
    blocks, nvars, nrhs, cells = rhs.shape
    n = lax.axis_size("chain")
    inv = jnp.transpose(diag_inverse, (1, 2, 0, 3))
    low, upp, side = (
        jnp.transpose(a, (0, 2, 3, 1, 4)).reshape(-1, cells)
        for a in (lower_coef, upper_coef, side_coef)
    )
    lcols, ucols, used = lower_cols.T, upper_cols.T, counts.T
    m = lax.axis_size("sub")
    rows = blocks + REACH + 1
    half = n // 2
    parts = -(-len(column_order(nrhs)) // half)
    back = -(-32 // half)
    packed = min(8, half)
    extra = 8 // packed
    wide = 2 * (extra + WIDE // packed)
    sides = [list(range(half)), list(range(half, n))]
    tile = (nrhs, cells)

    mats = (VARS, VARS, SLOTS, blocks + PAD, cells)
    padded = (low.shape[0] + VARS * VARS * SLOTS, cells)

    count = half if half <= DIRECT else 1

    def pieces(pages):
        return [((pages,) + tile, VMEM)] * count if count > 1 else [((half, pages) + tile, VMEM)]

    def whole(pages):
        return [(half, pages) + tile] if count > 1 else []

    *maps, source, mlow, mupp, lcols, ucols, used = call(
        functools.partial(parted, functools.partial(local_kernel, half), 7, count, half),
        pieces(parts)
        + [(rhs.shape, VMEM), (mats, VMEM), (mats, VMEM)]
        + [(lcols.shape, VMEM, jnp.int32)] * 3,
        (rhs, inv, low, upp, lcols, ucols, used),
        (HBM,) * 7,
        [rhs.shape, (VARS, VARS, blocks + PAD, cells), padded, padded]
        + [pltpu.SMEM(lcols.shape, jnp.int32)] * 3
        + [(rows, VARS, nrhs + WIDE, cells), (rows, VARS, nrhs + 2 * WIDE, cells)]
        + [(WIDE * SPACE + SPACE, cells), pltpu.SemaphoreType.DMA((10,))]
        + whole(parts),
    )
    maps = exchange(maps, half, sides)
    cols, ends, offer = call(
        functools.partial(joined, first_solve_kernel, count, half),
        [
            ((half * COLUMNS * 8, cells), VMEM),
            ((half, 4 * extra) + tile, VMEM),
            ((wide,) + tile, VMEM),
        ],
        tuple(maps),
        (VMEM,) * count,
        [(half, wide) + tile, (wide // 2 * WIDE + PAD, cells)] + whole(parts),
    )
    got = lax.ppermute(
        offer, "chain", [p for i in range(half) for p in ((i, i + half), (i + half, i))]
    )
    states = call(
        functools.partial(parted, second_solve_kernel, 4, count, half),
        pieces(back),
        (cols, ends, offer, got),
        (VMEM,) * 4,
        [(half, 2 * extra) + tile, (extra * WIDE + PAD, cells), (half, 4 * extra) + tile]
        + whole(back),
    )
    states = exchange(states, half, sides)
    z, w, tail, edge, low, side = call(
        functools.partial(joined, functools.partial(sweep_kernel, half), count, half),
        [
            (rhs.shape, VMEM),
            ((blocks + 1, VARS) + tile, VMEM),
            ((REACH, VARS) + tile, VMEM),
            ((VARS,) + tile, VMEM),
            (padded, VMEM),
            (padded, VMEM),
        ],
        (*states, source, mlow, mupp, lcols, ucols, used, low, side),
        (VMEM,) * (3 + count) + (SMEM,) * 3 + (HBM,) * 2,
        [rhs.shape, (33 * 8, cells), pltpu.SemaphoreType.DMA((2,))] + whole(back),
    )
    tail = lax.ppermute(tail, "chain", [(i, (i + 1) % n) for i in range(n)])
    swap_a, swap_b = (
        lax.ppermute(edge, "sub", [p for i, j in pairs for p in ((i, j), (j, i))])
        for pairs in (
            [(i, i + 1) for i in range(0, m - 1, 2)],
            [(i, i + 1) for i in range(1, m - 1, 2)] + [(0, m - 1)] * (m % 2 == 0),
        )
    )
    inner, coef, correction = call(
        inner_kernel,
        [
            (rhs.shape, VMEM),
            ((-(-VARS * VARS * SLOTS // 8),) + (8, cells), VMEM),
            (rhs.shape, HBM),
        ],
        (z, w, low, side, lcols, used),
        (VMEM,) * 4 + (SMEM,) * 2,
        [(2 * REACH + 1, VARS) + tile, pltpu.SemaphoreType.DMA],
    )
    resid, squares = call(
        outer_kernel,
        [(rhs.shape, VMEM), ((n * m, 1, cells), VMEM)],
        (inner, coef, low, tail, swap_a, swap_b, lcols, used),
        (VMEM,) * 6 + (SMEM,) * 2,
        [(REACH + 1, VARS) + tile],
    )
    squares = lax.all_to_all(squares, ("chain", "sub"), 0, 0, tiled=True)
    entries = blocks * VARS * cells * n * m
    (residual_unit,) = call(
        functools.partial(scale_kernel, entries),
        [(rhs.shape, HBM)],
        (resid, squares),
        (VMEM, VMEM),
        [rhs.shape, pltpu.SemaphoreType.DMA((4 if blocks % 4 == 0 else 1,))],
    )
    return (correction, residual_unit)


def solution(mesh):
    in_specs = (
        P("chain", None, None, "sub"),
        P("chain", None, None, "sub"),
        P("chain", None, None, "sub"),
        P("chain", None, None, None, "sub"),
        P("chain", None, None, None, "sub"),
        P("chain", None, None, None, "sub"),
        P("chain", None),
        P("chain", None),
        P("chain", None),
    )
    out_specs = (P("chain", None, None, "sub"), P("chain", None, None, "sub"))
    return jax.shard_map(shards, mesh=mesh, in_specs=in_specs, out_specs=out_specs, check_vma=False)
```
